32 devices in a mesh: dp: 2 (over x), seq: 16 (over z, y, core).
Axes of the slice: x: 2, y: 2, z: 4, core: 2. Of those that a mesh axis runs over, the one named last changes fastest.
Arguments:
- inputs: bfloat16 [2, 2, 1024, 1152], P(None, 'dp', 'seq'), may hold values from -8 to 8
- segments: int32 [2, 2, 1024], P(None, 'dp', 'seq'), may hold values from 0 to 9, as said below
- weight_query: bfloat16 [1152, 1152], P('seq', 'dp'), may hold values from -0.1875 to 0.1875
- key_weight_matrix: bfloat16 [1152, 384], P('seq', 'dp'), may hold values from -0.1875 to 0.1875
- value_weight_matrix: bfloat16 [1152, 384], P('seq', 'dp'), may hold values from -0.1875 to 0.1875
- weight_out: bfloat16 [1152, 1152], P('seq', 'dp'), may hold values from -0.75 to 0.75
- weight_gate: bfloat16 [1152, 3072], P('seq', 'dp'), may hold values from -0.1875 to 0.1875
- weight_up: bfloat16 [1152, 3072], P('seq', 'dp'), may hold values from -0.1875 to 0.1875
- weight_down: bfloat16 [3072, 1152], P('seq', 'dp'), may hold values from -0.109375 to 0.109375
- gain_attention: bfloat16 [1152], P('seq'), may hold values from 0.25 to 1.75
- gain_feed: bfloat16 [1152], P('seq'), may hold values from 0.25 to 1.75
- cotangent: bfloat16 [2, 2, 1024, 1152], P(None, 'dp', 'seq'), may hold values from -6 to 6
Outputs:
- output: bfloat16 [2, 2, 1024, 1152], P(None, 'dp', 'seq')
- grad_inputs: bfloat16 [2, 2, 1024, 1152], P(None, 'dp', 'seq')
- grad_query: float32 [1152, 1152], P('seq', 'dp')
- grad_key: float32 [1152, 384], P('seq', 'dp')
- grad_value: float32 [1152, 384], P('seq', 'dp')
- grad_out: float32 [1152, 1152], P('seq', 'dp')
- grad_gate: float32 [1152, 3072], P('seq', 'dp')
- grad_up: float32 [1152, 3072], P('seq', 'dp')
- grad_down: float32 [3072, 1152], P('seq', 'dp')
- grad_gain_attention: float32 [1152], P('seq')
- grad_gain_feed: float32 [1152], P('seq')
- root_means: float32 [3], replicated
The draws below stay inside these ranges and needn't reach their ends.
Inputs may be any that keep to these rules, and one draw needn't show every extreme that they name: `segments`: within a sequence the numbers never fall; 0 marks padding, which only ends a sequence; for every index of dp, one of its 2 sequences over all micro-batches, drawn from the seed, is a single document that ends within the last 64 positions.
All inputs are finite; a program needn't handle non-finite values.
Results may differ from the reference program's by a relative error of at most 0.015.
Values may be sent and summed in bfloat16 or wider, within the bound.
A program may use at most 256 MiB of HBM per device.

```python
import math
import jax
import jax.numpy as jnp
from jax import lax

MODEL_DIMENSION = 1152
QUERY_HEADS = 18
KEY_VALUE_HEADS = 6
HEAD_DIMENSION = 64
FF = 3072
MICRO = 2
SEQ_MB = 1
TOK_SEQ = 64
NBREAK = 8
SEQ_ALL = 2
LENGTH = 1024


def draw_inputs(key, part):
    key_noise = jax.random.fold_in(key, 0)
    full_shape = (MICRO, SEQ_ALL, LENGTH, MODEL_DIMENSION)
    position = jnp.arange(LENGTH, dtype=jnp.float32) / LENGTH
    ramp_scale = (0.5 + position)[None, None, :, None]
    values = jax.random.normal(key_noise, full_shape, jnp.float32) * ramp_scale
    return jnp.clip(values, -8.0, 8.0).astype(jnp.bfloat16)


def draw_segments(key, part):
    key_cut, key_pad, key_whole = jax.random.split(key, 3)
    total_seqs = MICRO * SEQ_ALL
    dp_count = SEQ_ALL // SEQ_MB
    left_part = jax.random.randint(key_cut, (total_seqs, NBREAK), 0, 1024)
    right_part = jax.random.randint(jax.random.fold_in(key_cut, 7), (total_seqs, NBREAK), 0, 1024)
    padding = jax.random.randint(key_pad, (total_seqs,), 0, max(LENGTH // 4, 1))
    short_pad = jax.random.randint(jax.random.fold_in(key_pad, 3), (total_seqs,), 0, max(TOK_SEQ // 2, 1))
    whole_pick = jax.random.randint(key_whole, (dp_count,), 0, MICRO * SEQ_MB)
    micro_index = jnp.arange(MICRO, dtype=jnp.int32)[:, None]
    seq_index = jnp.arange(SEQ_ALL, dtype=jnp.int32)[None, :]
    local_index = micro_index * SEQ_MB + seq_index % SEQ_MB
    chosen = local_index == whole_pick[seq_index // SEQ_MB]
    chosen = chosen.reshape(total_seqs)
    valid_len = LENGTH - jnp.where(chosen, short_pad, padding)
    cuts = left_part * right_part // 1024 * valid_len[:, None] // 1024
    cuts = jnp.where(chosen[:, None], LENGTH, cuts)
    place = jnp.arange(LENGTH, dtype=jnp.int32)
    doc_ids = 1 + jnp.sum((cuts[:, None, :] <= place[None, :, None]).astype(jnp.int32), axis=-1)
    doc_ids = jnp.where(place[None, :] < valid_len[:, None], doc_ids, 0)
    return doc_ids.reshape(MICRO, SEQ_ALL, LENGTH).astype(jnp.int32)


def block_scale(key, shape, cuts, low, top_value):
    def one(dim, shards_of):
        heights = jax.random.uniform(jax.random.fold_in(jax.random.fold_in(key, 6), dim), (shards_of,), jnp.float32, low / len(cuts), top_value / len(cuts))
        return jnp.repeat(jnp.exp(heights), shape[dim] // shards_of).reshape((-1,) + (1,) * (len(shape) - dim - 1))

    level = one(*cuts[0])
    for cut in cuts[1:]:
        level = level * one(*cut)
    return level


def normal_values(key, extent, deviation, most, pieces=(), kind=jnp.bfloat16):
    factor_of = block_scale(key, extent, pieces, -0.22, 0.18) if pieces else 1.0
    values = jax.random.normal(key, extent, jnp.float32) * deviation * factor_of
    return jnp.minimum(jnp.maximum(values, -most), most).astype(kind)


def setup_inputs(seed: int = 0) -> dict:
    key_of = jax.random.split(jax.random.key(seed), 13)
    return {
        "inputs": draw_inputs(jax.random.fold_in(key_of[12], 71), 0),
        "segments": draw_segments(jax.random.fold_in(key_of[12], 71), 0),
        "weight_query": normal_values(key_of[2], (MODEL_DIMENSION, QUERY_HEADS * HEAD_DIMENSION), MODEL_DIMENSION ** -0.5, 0.1875, ((0, 16), (1, 2))),
        "key_weight_matrix": normal_values(key_of[3], (MODEL_DIMENSION, KEY_VALUE_HEADS * HEAD_DIMENSION), MODEL_DIMENSION ** -0.5, 0.1875, ((0, 16), (1, 2))),
        "value_weight_matrix": normal_values(key_of[4], (MODEL_DIMENSION, KEY_VALUE_HEADS * HEAD_DIMENSION), MODEL_DIMENSION ** -0.5, 0.1875, ((0, 16), (1, 2))),
        "weight_out": normal_values(key_of[5], (QUERY_HEADS * HEAD_DIMENSION, MODEL_DIMENSION), (MODEL_DIMENSION // 16) ** -0.5, 0.75, ((0, 16), (1, 2))),
        "weight_gate": normal_values(key_of[6], (MODEL_DIMENSION, FF), MODEL_DIMENSION ** -0.5, 0.1875, ((0, 16), (1, 2))),
        "weight_up": normal_values(key_of[7], (MODEL_DIMENSION, FF), MODEL_DIMENSION ** -0.5, 0.1875, ((0, 16), (1, 2))),
        "weight_down": normal_values(key_of[8], (FF, MODEL_DIMENSION), FF ** -0.5, 0.109375, ((0, 16), (1, 2))),
        "gain_attention": jnp.clip(1.0 + 0.15 * jax.random.normal(key_of[9], (MODEL_DIMENSION,), jnp.float32), 0.25, 1.75).astype(jnp.bfloat16),
        "gain_feed": jnp.clip(1.0 + 0.15 * jax.random.normal(key_of[10], (MODEL_DIMENSION,), jnp.float32), 0.25, 1.75).astype(jnp.bfloat16),
        "cotangent": normal_values(key_of[11], (MICRO, SEQ_ALL, LENGTH, MODEL_DIMENSION), 1.0, 6.0, ((1, 2), (2, 16))),
    }


@jax.custom_vjp
def low(v):
    return lax.optimization_barrier(v.astype(jnp.bfloat16)).astype(jnp.float32)

@jax.custom_vjp
def low_back(v):
    return v

def low_keep(v):
    return (low(v), None)

def low_pass(kept, grad):
    return (grad,)

def back_keep(v):
    return (v, None)

def back_low(kept, grad):
    return (low(grad),)
low.defvjp(low_keep, low_pass)
low_back.defvjp(back_keep, back_low)
EPS = 1e-05
THETA = 10000.0
NEGATIVE = -1e+30
TOP_PRECISION = lax.Precision.HIGHEST

def rope_tables(positions, head_size):
    half_size = head_size // 2
    frequency = THETA ** (-jnp.arange(half_size, dtype=jnp.float32) * 2.0 / head_size)
    angles = positions.astype(jnp.float32)[:, None] * frequency[None, :]
    angles = jnp.concatenate([angles, angles], axis=1)
    return (jnp.cos(angles), jnp.sin(angles))

def turn_half(values_in):
    half_size = values_in.shape[-1] // 2
    return jnp.concatenate([-values_in[..., half_size:], values_in[..., :half_size]], axis=-1)

def apply_rotation(values_in, cosine_table, sine_values):
    return values_in * cosine_table[:, None, :] + turn_half(values_in) * sine_values[:, None, :]

def rms_norm(values_in, gain):
    row_scale = lax.rsqrt(lax.optimization_barrier(jnp.mean(values_in * values_in, axis=-1, keepdims=True)) + EPS)
    return values_in * row_scale * gain

def sequence_forward(tokens, segment_ids, weights):
    weight_query, key_weight_matrix, value_weight_matrix, weight_out, weight_gate, weight_up, weight_down, gain_attention, gain_feed = weights
    token_length = tokens.shape[0]
    positions = jnp.arange(token_length, dtype=jnp.int32)
    cosine_table, sine_values = rope_tables(positions, HEAD_DIMENSION)
    normalized = low(rms_norm(tokens, gain_attention))
    query_raw = low_back(jnp.dot(normalized, weight_query, precision=TOP_PRECISION))
    query_matrix = low(apply_rotation(query_raw.reshape(token_length, QUERY_HEADS, HEAD_DIMENSION), cosine_table, sine_values))
    key_unrotated = low_back(jnp.dot(normalized, key_weight_matrix, precision=TOP_PRECISION))
    key_matrix_rows = low(apply_rotation(key_unrotated.reshape(token_length, KEY_VALUE_HEADS, HEAD_DIMENSION), cosine_table, sine_values))
    value_matrix_rows = low(low_back(jnp.dot(normalized, value_weight_matrix, precision=TOP_PRECISION))).reshape(token_length, KEY_VALUE_HEADS, HEAD_DIMENSION)
    group_width = QUERY_HEADS // KEY_VALUE_HEADS
    query_matrix = query_matrix.reshape(token_length, KEY_VALUE_HEADS, group_width, HEAD_DIMENSION)
    block_size = min(512, token_length)
    score_scale = 1.0 / math.sqrt(HEAD_DIMENSION)

    def attend_block(block_offset):
        query_rows = lax.dynamic_slice_in_dim(query_matrix, block_offset, block_size, 0)
        row_segments = lax.dynamic_slice_in_dim(segment_ids, block_offset, block_size, 0)
        row_positions = block_offset + jnp.arange(block_size, dtype=jnp.int32)
        raw_scores = jnp.einsum('tkgd,jkd->kgtj', query_rows, key_matrix_rows, precision=TOP_PRECISION)
        scores = low_back(raw_scores) * score_scale
        allowed = (row_segments[:, None] == segment_ids[None, :]) & (positions[None, :] <= row_positions[:, None])
        scores = jnp.where(allowed[None, None], scores, NEGATIVE)
        row_top = lax.optimization_barrier(jnp.max(scores, axis=-1, keepdims=True))
        exponent = jnp.where(allowed[None, None], jnp.exp(scores - row_top), 0.0)
        probabilities = exponent / lax.optimization_barrier(jnp.sum(exponent, axis=-1, keepdims=True))
        return jnp.einsum('kgtj,jkd->tkgd', low(probabilities), value_matrix_rows, precision=TOP_PRECISION)
    starts = jnp.arange(0, token_length, block_size, dtype=jnp.int32)
    mixed_heads = lax.map(jax.checkpoint(attend_block), starts).reshape(token_length, QUERY_HEADS * HEAD_DIMENSION)
    attn_low = low(low_back(mixed_heads))
    branch_attn = low_back(jnp.dot(attn_low, weight_out, precision=TOP_PRECISION))
    hidden = tokens + branch_attn
    normed_second = low(rms_norm(hidden, gain_feed))
    gate_values = low_back(jnp.dot(normed_second, weight_gate, precision=TOP_PRECISION))
    up_values = low_back(jnp.dot(normed_second, weight_up, precision=TOP_PRECISION))
    inner_low = low(jax.nn.silu(gate_values) * up_values)
    branch_feed = low_back(jnp.dot(inner_low, weight_down, precision=TOP_PRECISION))
    result = hidden + branch_feed
    return (result, (branch_attn, branch_feed))

def reference(inputs, segments, weight_query, key_weight_matrix, value_weight_matrix, weight_out, weight_gate, weight_up, weight_down, gain_attention, gain_feed, cotangent):
    weights = tuple((weight_item.astype(jnp.float32) for weight_item in (weight_query, key_weight_matrix, value_weight_matrix, weight_out, weight_gate, weight_up, weight_down, gain_attention, gain_feed)))
    flat_inputs = inputs.reshape(-1, LENGTH, MODEL_DIMENSION)
    flat_segments = segments.reshape(-1, LENGTH)
    flat_cot = cotangent.reshape(-1, LENGTH, MODEL_DIMENSION)
    zero_grads = tuple((jnp.zeros(weight_item.shape, jnp.float32) for weight_item in weights))

    def per_sequence(carried, item_in):
        grad_sums, totals = carried
        tokens, segment_ids, cot_rows = item_in

        def forward(token_values, weight_values):
            return sequence_forward(token_values, segment_ids, weight_values)
        result, pullback, branches = jax.vjp(forward, tokens.astype(jnp.float32), weights, has_aux=True)
        grad_tokens, grad_weights = pullback(cot_rows.astype(jnp.float32))
        valid_rows = (segment_ids != 0).astype(jnp.float32)[:, None]
        new_totals = totals + jnp.stack([jnp.sum(valid_rows * branches[0] * branches[0]), jnp.sum(valid_rows * branches[1] * branches[1]), jnp.sum(valid_rows * result * result), jnp.sum(valid_rows)])
        new_sums = jax.tree.map(jnp.add, grad_sums, grad_weights)
        return ((new_sums, new_totals), (result.astype(jnp.bfloat16), grad_tokens.astype(jnp.bfloat16)))
    (grad_sums, totals), (outputs, grad_rows) = lax.scan(per_sequence, (zero_grads, jnp.zeros((4,), jnp.float32)), (flat_inputs, flat_segments, flat_cot))
    root_means = jnp.sqrt(totals[:3] / (totals[3] * MODEL_DIMENSION))
    return (outputs.reshape(inputs.shape), grad_rows.reshape(inputs.shape), grad_sums[0], grad_sums[1], grad_sums[2], grad_sums[3], grad_sums[4], grad_sums[5], grad_sums[6], grad_sums[7], grad_sums[8], root_means)
```

```python
import math

import jax
import jax.numpy as jnp
from jax import lax
from jax.sharding import PartitionSpec as P

QUERY_HEADS = 18
KEY_VALUE_HEADS = 6
HEAD_DIMENSION = 64


EPS = 1e-05
THETA = 10000.0
NEGATIVE = -1e30


def rope_tables(positions, head_size):
    half_size = head_size // 2
    frequency = THETA ** (-jnp.arange(half_size, dtype=jnp.float32) * 2.0 / head_size)
    angles = positions.astype(jnp.float32)[:, None] * frequency[None, :]
    angles = jnp.concatenate([angles, angles], axis=1)
    return (jnp.cos(angles), jnp.sin(angles))


def turn_half(values_in):
    half_size = values_in.shape[-1] // 2
    return jnp.concatenate([-values_in[..., half_size:], values_in[..., :half_size]], axis=-1)


def apply_rotation(values_in, cosine_table, sine_values):
    return values_in * cosine_table[:, None, :] + turn_half(values_in) * sine_values[:, None, :]


def reverse_rotation(grads_in, cosine_table, sine_values):
    return grads_in * cosine_table[:, None, :] - turn_half(grads_in * sine_values[:, None, :])


def norm_forward(values_in, gain):
    row_scale = lax.rsqrt(jnp.mean(values_in * values_in, axis=-1, keepdims=True) + EPS)
    return (values_in * row_scale * gain, row_scale)


def norm_backward(values_in, row_scale, gain, grad_normed):
    scaled = grad_normed * gain
    inner_mean = jnp.mean(scaled * values_in, axis=-1, keepdims=True)
    value_gradient_rows = row_scale * scaled - values_in * row_scale**3 * inner_mean
    grad_gain = jnp.sum(grad_normed * values_in * row_scale, axis=(0, 1))
    return (value_gradient_rows, grad_gain)


def apply_projection(acts_low, weight_full):
    return jnp.einsum("std,df->stf", acts_low, weight_full, preferred_element_type=jnp.float32)


def project_back(grads_low, weight_full):
    return jnp.einsum("sta,ba->stb", grads_low, weight_full, preferred_element_type=jnp.float32)


def weight_grad(acts_low, grads_low):
    return jnp.einsum("std,stf->df", acts_low, grads_low, preferred_element_type=jnp.float32)


def gather_all(shards, gain_shards):
    wide = (
        lax.all_gather(shards[0], "dp", axis=1, tiled=True),
        lax.all_gather(shards[1], "dp", axis=1, tiled=True),
        lax.all_gather(shards[2], "dp", axis=1, tiled=True),
        lax.all_gather(shards[3], "dp", axis=1, tiled=True),
        lax.all_gather(shards[4], "dp", axis=1, tiled=True),
        lax.all_gather(shards[5], "dp", axis=1, tiled=True),
        lax.all_gather(shards[6], "dp", axis=1, tiled=True),
    )
    return (
        lax.all_gather(wide[0], "seq", axis=0, tiled=True),
        lax.all_gather(wide[1], "seq", axis=0, tiled=True),
        lax.all_gather(wide[2], "seq", axis=0, tiled=True),
        lax.all_gather(wide[3], "seq", axis=0, tiled=True),
        lax.all_gather(wide[4], "seq", axis=0, tiled=True),
        lax.all_gather(wide[5], "seq", axis=0, tiled=True),
        lax.all_gather(wide[6], "seq", axis=0, tiled=True),
        lax.all_gather(gain_shards[0], "seq", axis=0, tiled=True),
        lax.all_gather(gain_shards[1], "seq", axis=0, tiled=True),
    )


def gather_keys(key_low, value_low, seg_low):
    return (
        lax.all_gather(key_low, "seq", axis=1, tiled=True),
        lax.all_gather(value_low, "seq", axis=1, tiled=True),
        lax.all_gather(seg_low, "seq", axis=1, tiled=True),
    )


def reduce_grads(grads):
    rows = [
        lax.psum_scatter(g.astype(jnp.bfloat16), "seq", scatter_dimension=0, tiled=True)
        for g in grads
    ]
    return tuple(
        lax.psum_scatter(r, "dp", scatter_dimension=1, tiled=True).astype(jnp.float32)
        for r in rows
    )


def block_view(gathered, block_index, key_tile_block):
    block_offset = block_index * key_tile_block
    key_portion = lax.dynamic_slice_in_dim(gathered[0], block_offset, key_tile_block, 1)
    value_portion = lax.dynamic_slice_in_dim(gathered[1], block_offset, key_tile_block, 1)
    seg_part = lax.dynamic_slice_in_dim(gathered[2], block_offset, key_tile_block, 1).astype(
        jnp.float32
    )
    sequence_count = key_portion.shape[0]
    key_portion = key_portion.reshape(
        sequence_count, key_tile_block, KEY_VALUE_HEADS, HEAD_DIMENSION
    )
    value_portion = value_portion.reshape(
        sequence_count, key_tile_block, KEY_VALUE_HEADS, HEAD_DIMENSION
    )
    col_pos = block_offset + jnp.arange(key_tile_block, dtype=jnp.int32)
    return (key_portion, value_portion, seg_part, col_pos)


def masked_scores(query_block_list, key_portion, seg_rows, seg_part, row_pos, col_pos, score_scale):
    raw_scores = jnp.einsum(
        "skgtd,sjkd->skgtj", query_block_list, key_portion, preferred_element_type=jnp.float32
    )
    allowed = (seg_rows[:, :, None] == seg_part[:, None, :]) & (
        col_pos[None, None, :] <= row_pos[None, :, None]
    )
    allowed = allowed[:, None, None, :, :]
    return (jnp.where(allowed, raw_scores * score_scale, NEGATIVE), allowed)


def log_sum(
    query_block_list, gathered, seg_rows, row_pos, block_count, key_tile_block, score_scale
):
    lead_shape = query_block_list.shape[:4]

    def log_step_fn(block_index, carried):
        row_top, row_total = carried
        key_portion, value_portion, seg_part, col_pos = block_view(
            gathered, block_index, key_tile_block
        )
        scores, allowed = masked_scores(
            query_block_list, key_portion, seg_rows, seg_part, row_pos, col_pos, score_scale
        )
        new_top = jnp.maximum(row_top, jnp.max(scores, axis=-1))
        exponent = jnp.where(allowed, jnp.exp(scores - new_top[..., None]), 0.0)
        row_total = row_total * jnp.exp(row_top - new_top) + jnp.sum(exponent, axis=-1)
        return (new_top, row_total)

    start_state = (jnp.full(lead_shape, NEGATIVE, jnp.float32), jnp.zeros(lead_shape, jnp.float32))
    row_top, row_total = lax.fori_loop(0, block_count, log_step_fn, start_state)
    return row_top + jnp.log(row_total)


def attend(
    query_block_list,
    gathered,
    seg_rows,
    row_pos,
    block_count,
    key_tile_block,
    score_scale,
    log_total,
):

    def attend_step_fn(block_index, mixed_heads):
        key_portion, value_portion, seg_part, col_pos = block_view(
            gathered, block_index, key_tile_block
        )
        scores, allowed = masked_scores(
            query_block_list, key_portion, seg_rows, seg_part, row_pos, col_pos, score_scale
        )
        probabilities = jnp.where(allowed, jnp.exp(scores - log_total[..., None]), 0.0).astype(
            jnp.bfloat16
        )
        return mixed_heads + jnp.einsum(
            "skgtj,sjkd->skgtd", probabilities, value_portion, preferred_element_type=jnp.float32
        )

    return lax.fori_loop(
        0, block_count, attend_step_fn, jnp.zeros(query_block_list.shape, jnp.float32)
    )


def query_back(
    query_block_list,
    gathered,
    seg_rows,
    row_pos,
    block_count,
    key_tile_block,
    score_scale,
    log_total,
    gradient_reduced,
    row_delta,
):

    def query_step_fn(block_index, grad_query):
        key_portion, value_portion, seg_part, col_pos = block_view(
            gathered, block_index, key_tile_block
        )
        scores, allowed = masked_scores(
            query_block_list, key_portion, seg_rows, seg_part, row_pos, col_pos, score_scale
        )
        probabilities = jnp.where(allowed, jnp.exp(scores - log_total[..., None]), 0.0)
        grad_probs = jnp.einsum(
            "skgtd,sjkd->skgtj", gradient_reduced, value_portion, preferred_element_type=jnp.float32
        )
        grad_scores = (probabilities * (grad_probs - row_delta[..., None]) * score_scale).astype(
            jnp.bfloat16
        )
        return grad_query + jnp.einsum(
            "skgtj,sjkd->skgtd", grad_scores, key_portion, preferred_element_type=jnp.float32
        )

    return lax.fori_loop(
        0, block_count, query_step_fn, jnp.zeros(query_block_list.shape, jnp.float32)
    )


def key_back(
    key_local,
    value_local,
    seg_rows,
    row_pos,
    query_whole,
    grads_whole,
    stats_whole,
    seg_whole,
    first_block,
    block_count,
    query_tile,
    score_scale,
):
    sequence_count = key_local.shape[0]
    group_width = QUERY_HEADS // KEY_VALUE_HEADS

    def key_step_fn(block_index, carried):
        key_total, value_total = carried
        block_offset = block_index * query_tile
        query_rows = lax.dynamic_slice_in_dim(query_whole, block_offset, query_tile, 1).reshape(
            sequence_count, query_tile, KEY_VALUE_HEADS, group_width, HEAD_DIMENSION
        )
        grad_rows = lax.dynamic_slice_in_dim(grads_whole, block_offset, query_tile, 1).reshape(
            sequence_count, query_tile, KEY_VALUE_HEADS, group_width, HEAD_DIMENSION
        )
        log_rows = lax.dynamic_slice_in_dim(stats_whole[0], block_offset, query_tile, 3)
        delta_rows = lax.dynamic_slice_in_dim(stats_whole[1], block_offset, query_tile, 3)
        seg_query = lax.dynamic_slice_in_dim(seg_whole, block_offset, query_tile, 1).astype(
            jnp.float32
        )
        query_pos = block_offset + jnp.arange(query_tile, dtype=jnp.int32)
        raw_scores = jnp.einsum(
            "stkgd,sjkd->skgtj", query_rows, key_local, preferred_element_type=jnp.float32
        )
        allowed = (seg_query[:, :, None] == seg_rows[:, None, :]) & (
            row_pos[None, None, :] <= query_pos[None, :, None]
        )
        allowed = allowed[:, None, None, :, :]
        scores = jnp.where(allowed, raw_scores * score_scale, NEGATIVE)
        probabilities = jnp.where(allowed, jnp.exp(scores - log_rows[..., None]), 0.0)
        grad_probs = jnp.einsum(
            "stkgd,sjkd->skgtj", grad_rows, value_local, preferred_element_type=jnp.float32
        )
        grad_scores = (probabilities * (grad_probs - delta_rows[..., None]) * score_scale).astype(
            jnp.bfloat16
        )
        key_total = key_total + jnp.einsum(
            "skgtj,stkgd->sjkd", grad_scores, query_rows, preferred_element_type=jnp.float32
        )
        value_total = value_total + jnp.einsum(
            "skgtj,stkgd->sjkd",
            probabilities.astype(jnp.bfloat16),
            grad_rows,
            preferred_element_type=jnp.float32,
        )
        return (key_total, value_total)

    start_state = (jnp.zeros(key_local.shape, jnp.float32), jnp.zeros(key_local.shape, jnp.float32))
    return lax.fori_loop(first_block, block_count, key_step_fn, start_state)


def per_device(
    inputs,
    segments,
    weight_query,
    key_weight_matrix,
    value_weight_matrix,
    weight_out,
    weight_gate,
    weight_up,
    weight_down,
    gain_attention,
    gain_feed,
    cotangent,
):
    shards = (
        weight_query,
        key_weight_matrix,
        value_weight_matrix,
        weight_out,
        weight_gate,
        weight_up,
        weight_down,
    )
    gain_shards = (gain_attention, gain_feed)
    micro_count, sequence_count, token_count, model_width = inputs.shape
    group_width = QUERY_HEADS // KEY_VALUE_HEADS
    score_scale = 1.0 / math.sqrt(HEAD_DIMENSION)
    row_pos = lax.axis_index("seq") * token_count + jnp.arange(token_count, dtype=jnp.int32)
    cosine_table, sine_values = rope_tables(row_pos, HEAD_DIMENSION)
    key_span_length = token_count * lax.axis_size("seq")
    key_tile_block = min(512, key_span_length)
    total_blocks = key_span_length // key_tile_block
    block_count = row_pos[token_count - 1] // key_tile_block + 1
    first_block = row_pos[0] // key_tile_block
    outputs = []
    grad_list = []
    totals = jnp.zeros((4,), jnp.float32)
    gain_grads = jnp.zeros((2, model_width), jnp.float32)
    summed = None
    weights_complete = gather_all(shards, gain_shards)
    for batch_index in range(micro_count):
        tokens = inputs[batch_index].astype(jnp.float32)
        seg_local = segments[batch_index]
        seg_rows = seg_local.astype(jnp.float32)
        seg_low = seg_local.astype(jnp.bfloat16)
        gain_first = weights_complete[7].astype(jnp.float32)
        gain_second = weights_complete[8].astype(jnp.float32)
        norm_first, scale_first = norm_forward(tokens, gain_first)
        normalized = norm_first.astype(jnp.bfloat16)
        query_raw = apply_projection(normalized, weights_complete[0]).reshape(
            sequence_count, token_count, QUERY_HEADS, HEAD_DIMENSION
        )
        query_reduced = apply_rotation(query_raw, cosine_table, sine_values).astype(jnp.bfloat16)
        key_unrotated = apply_projection(normalized, weights_complete[1]).reshape(
            sequence_count, token_count, KEY_VALUE_HEADS, HEAD_DIMENSION
        )
        key_low = (
            apply_rotation(key_unrotated, cosine_table, sine_values)
            .astype(jnp.bfloat16)
            .reshape(sequence_count, token_count, KEY_VALUE_HEADS * HEAD_DIMENSION)
        )
        value_low = apply_projection(normalized, weights_complete[2]).astype(jnp.bfloat16)
        gathered = gather_keys(key_low, value_low, seg_low)
        query_block_list = query_reduced.reshape(
            sequence_count, token_count, KEY_VALUE_HEADS, group_width, HEAD_DIMENSION
        ).transpose(0, 2, 3, 1, 4)
        log_total = log_sum(
            query_block_list, gathered, seg_rows, row_pos, block_count, key_tile_block, score_scale
        )
        mixed_heads = attend(
            query_block_list,
            gathered,
            seg_rows,
            row_pos,
            block_count,
            key_tile_block,
            score_scale,
            log_total,
        )
        attn_low = (
            mixed_heads.transpose(0, 3, 1, 2, 4)
            .reshape(sequence_count, token_count, QUERY_HEADS * HEAD_DIMENSION)
            .astype(jnp.bfloat16)
        )
        branch_attn = apply_projection(attn_low, weights_complete[3])
        hidden = tokens + branch_attn
        norm_second, scale_second = norm_forward(hidden, gain_second)
        normed_second = norm_second.astype(jnp.bfloat16)
        gate_values = apply_projection(normed_second, weights_complete[4])
        up_values = apply_projection(normed_second, weights_complete[5])
        gate_sigmoid = jax.nn.sigmoid(gate_values)
        inner_low = (gate_values * gate_sigmoid * up_values).astype(jnp.bfloat16)
        branch_feed = apply_projection(inner_low, weights_complete[6])
        result = hidden + branch_feed
        outputs.append(result.astype(jnp.bfloat16))
        valid_rows = (seg_local != 0).astype(jnp.float32)[:, :, None]
        totals = totals + jnp.stack(
            [
                jnp.sum(valid_rows * branch_attn * branch_attn),
                jnp.sum(valid_rows * branch_feed * branch_feed),
                jnp.sum(valid_rows * result * result),
                jnp.sum(valid_rows),
            ]
        )
        back_weights = weights_complete
        back_keys = gathered
        grad_result = cotangent[batch_index].astype(jnp.float32)
        grad_feed = grad_result.astype(jnp.bfloat16)
        grad_down = weight_grad(inner_low, grad_feed)
        grad_inner = project_back(grad_feed, back_weights[6])
        grad_up = (grad_inner * gate_values * gate_sigmoid).astype(jnp.bfloat16)
        grad_gate = (
            grad_inner * up_values * gate_sigmoid * (1.0 + gate_values * (1.0 - gate_sigmoid))
        ).astype(jnp.bfloat16)
        grad_gate_w = weight_grad(normed_second, grad_gate)
        grad_up_w = weight_grad(normed_second, grad_up)
        grad_normed_second = project_back(grad_gate, back_weights[4]) + project_back(
            grad_up, back_weights[5]
        )
        grad_hidden_norm, grad_gain_second = norm_backward(
            hidden, scale_second, gain_second, grad_normed_second
        )
        grad_hidden = grad_result + grad_hidden_norm
        grad_branch = grad_hidden.astype(jnp.bfloat16)
        grad_out_w = weight_grad(attn_low, grad_branch)
        mixed_gradient = project_back(grad_branch, back_weights[3]).astype(jnp.bfloat16)
        gradient_reduced = mixed_gradient.reshape(
            sequence_count, token_count, KEY_VALUE_HEADS, group_width, HEAD_DIMENSION
        ).transpose(0, 2, 3, 1, 4)
        row_delta = jnp.sum(gradient_reduced.astype(jnp.float32) * mixed_heads, axis=-1)
        grad_query = query_back(
            query_block_list,
            back_keys,
            seg_rows,
            row_pos,
            block_count,
            key_tile_block,
            score_scale,
            log_total,
            gradient_reduced,
            row_delta,
        )
        query_flat = query_reduced.reshape(
            sequence_count, token_count, QUERY_HEADS * HEAD_DIMENSION
        )
        query_whole, grads_whole = (
            lax.all_gather(query_flat, "seq", axis=1, tiled=True),
            lax.all_gather(mixed_gradient, "seq", axis=1, tiled=True),
        )
        stats_whole = (
            lax.all_gather(log_total, "seq", axis=3, tiled=True),
            lax.all_gather(row_delta, "seq", axis=3, tiled=True),
        )
        key_local = key_low.reshape(sequence_count, token_count, KEY_VALUE_HEADS, HEAD_DIMENSION)
        value_local = value_low.reshape(
            sequence_count, token_count, KEY_VALUE_HEADS, HEAD_DIMENSION
        )
        key_total, value_total = key_back(
            key_local,
            value_local,
            seg_rows,
            row_pos,
            query_whole,
            grads_whole,
            stats_whole,
            back_keys[2],
            first_block,
            total_blocks,
            key_tile_block,
            score_scale,
        )
        key_grad_low = (
            reverse_rotation(key_total, cosine_table, sine_values)
            .reshape(sequence_count, token_count, KEY_VALUE_HEADS * HEAD_DIMENSION)
            .astype(jnp.bfloat16)
        )
        value_grad_low = value_total.reshape(
            sequence_count, token_count, KEY_VALUE_HEADS * HEAD_DIMENSION
        ).astype(jnp.bfloat16)
        query_grad = grad_query.transpose(0, 3, 1, 2, 4).reshape(
            sequence_count, token_count, QUERY_HEADS, HEAD_DIMENSION
        )
        query_grad_low = (
            reverse_rotation(query_grad, cosine_table, sine_values)
            .reshape(sequence_count, token_count, QUERY_HEADS * HEAD_DIMENSION)
            .astype(jnp.bfloat16)
        )
        grad_normed = (
            project_back(query_grad_low, back_weights[0])
            + project_back(key_grad_low, back_weights[1])
            + project_back(value_grad_low, back_weights[2])
        )
        grad_token_norm, grad_gain_first = norm_backward(
            tokens, scale_first, gain_first, grad_normed
        )
        grad_list.append((grad_hidden + grad_token_norm).astype(jnp.bfloat16))
        gain_grads = gain_grads + jnp.stack([grad_gain_first, grad_gain_second])
        batch_grads = (
            weight_grad(normalized, query_grad_low),
            weight_grad(normalized, key_grad_low),
            weight_grad(normalized, value_grad_low),
            grad_out_w,
            grad_gate_w,
            grad_up_w,
            grad_down,
        )
        summed = batch_grads if summed is None else jax.tree.map(jnp.add, summed, batch_grads)
    reduced = reduce_grads(summed)
    gain_total, totals = lax.psum((gain_grads, totals), ("dp", "seq"))
    piece_width = model_width // lax.axis_size("seq")
    gain_part = lax.dynamic_slice_in_dim(
        gain_total, lax.axis_index("seq") * piece_width, piece_width, 1
    )
    root_means = jnp.sqrt(totals[:3] / (totals[3] * model_width))
    return (
        jnp.stack(outputs),
        jnp.stack(grad_list),
        reduced[0],
        reduced[1],
        reduced[2],
        reduced[3],
        reduced[4],
        reduced[5],
        reduced[6],
        gain_part[0],
        gain_part[1],
        root_means,
    )


def solution(mesh):
    placed = (
        P(None, "dp", "seq", None),
        P(None, "dp", "seq"),
        P("seq", "dp"),
        P("seq", "dp"),
        P("seq", "dp"),
        P("seq", "dp"),
        P("seq", "dp"),
        P("seq", "dp"),
        P("seq", "dp"),
        P("seq"),
        P("seq"),
        P(None, "dp", "seq", None),
    )
    return jax.shard_map(
        per_device,
        mesh=mesh,
        in_specs=placed,
        out_specs=(
            P(None, "dp", "seq", None),
            P(None, "dp", "seq", None),
            P("seq", "dp"),
            P("seq", "dp"),
            P("seq", "dp"),
            P("seq", "dp"),
            P("seq", "dp"),
            P("seq", "dp"),
            P("seq", "dp"),
            P("seq"),
            P("seq"),
            P(),
        ),
        check_vma=False,
    )
```

```python
import functools
import math

import jax
import jax.numpy as jnp
import numpy as np
from jax import lax
from jax.experimental import pallas as pl
from jax.experimental.pallas import tpu as pltpu
from jax.sharding import PartitionSpec as P

QUERY_HEADS = 18
KEY_VALUE_HEADS = 6
HEAD_DIMENSION = 64


EPS = 1e-05
THETA = 10000.0
NEGATIVE = -1e30


def rope_tables(positions, head_size):
    half_size = head_size // 2
    frequency = THETA ** (-jnp.arange(half_size, dtype=jnp.float32) * 2.0 / head_size)
    angles = positions.astype(jnp.float32)[:, None] * frequency[None, :]
    angles = jnp.concatenate([angles, angles], axis=1)
    return (jnp.cos(angles), jnp.sin(angles))


def turn_half(values_in):
    half_size = values_in.shape[-1] // 2
    return jnp.concatenate([-values_in[..., half_size:], values_in[..., :half_size]], axis=-1)


def apply_rotation(values_in, cosine_table, sine_values):
    return values_in * cosine_table[:, None, :] + turn_half(values_in) * sine_values[:, None, :]


def reverse_rotation(grads_in, cosine_table, sine_values):
    return grads_in * cosine_table[:, None, :] - turn_half(grads_in * sine_values[:, None, :])


def norm_forward(values_in, gain):
    row_scale = lax.rsqrt(jnp.mean(values_in * values_in, axis=-1, keepdims=True) + EPS)
    return (values_in * row_scale * gain, row_scale)


def norm_backward(values_in, row_scale, gain, grad_normed):
    scaled = grad_normed * gain
    inner_mean = jnp.mean(scaled * values_in, axis=-1, keepdims=True)
    value_gradient_rows = row_scale * scaled - values_in * row_scale**3 * inner_mean
    grad_gain = jnp.sum(grad_normed * values_in * row_scale, axis=(0, 1))
    return (value_gradient_rows, grad_gain)


def apply_projection(acts_low, weight_full):
    return jnp.einsum("std,df->stf", acts_low, weight_full, preferred_element_type=jnp.float32)


def project_back(grads_low, weight_full):
    return jnp.einsum("sta,ba->stb", grads_low, weight_full, preferred_element_type=jnp.float32)


def weight_grad(acts_low, grads_low):
    return jnp.einsum("std,stf->df", acts_low, grads_low, preferred_element_type=jnp.float32)


def gather_all(shards, gain_shards):
    wide = (
        lax.all_gather(shards[0], "dp", axis=1, tiled=True),
        lax.all_gather(shards[1], "dp", axis=1, tiled=True),
        lax.all_gather(shards[2], "dp", axis=1, tiled=True),
        lax.all_gather(shards[3], "dp", axis=1, tiled=True),
        lax.all_gather(shards[4], "dp", axis=1, tiled=True),
        lax.all_gather(shards[5], "dp", axis=1, tiled=True),
        lax.all_gather(shards[6], "dp", axis=1, tiled=True),
    )
    return (
        lax.all_gather(wide[0], "seq", axis=0, tiled=True),
        lax.all_gather(wide[1], "seq", axis=0, tiled=True),
        lax.all_gather(wide[2], "seq", axis=0, tiled=True),
        lax.all_gather(wide[3], "seq", axis=0, tiled=True),
        lax.all_gather(wide[4], "seq", axis=0, tiled=True),
        lax.all_gather(wide[5], "seq", axis=0, tiled=True),
        lax.all_gather(wide[6], "seq", axis=0, tiled=True),
        lax.all_gather(gain_shards[0], "seq", axis=0, tiled=True),
        lax.all_gather(gain_shards[1], "seq", axis=0, tiled=True),
    )


def gather_keys(key_low, value_low, seg_low):
    return (
        lax.all_gather(key_low, "seq", axis=1, tiled=True),
        lax.all_gather(value_low, "seq", axis=1, tiled=True),
        lax.all_gather(seg_low, "seq", axis=1, tiled=True),
    )


def reduce_grads(grads):
    rows = [
        lax.psum_scatter(g.astype(jnp.bfloat16), "seq", scatter_dimension=0, tiled=True)
        for g in grads
    ]
    return tuple(
        lax.psum_scatter(r, "dp", scatter_dimension=1, tiled=True).astype(jnp.float32)
        for r in rows
    )


def block_view(gathered, block_index, key_tile_block):
    block_offset = block_index * key_tile_block
    key_portion = lax.dynamic_slice_in_dim(gathered[0], block_offset, key_tile_block, 1)
    value_portion = lax.dynamic_slice_in_dim(gathered[1], block_offset, key_tile_block, 1)
    seg_part = lax.dynamic_slice_in_dim(gathered[2], block_offset, key_tile_block, 1).astype(
        jnp.float32
    )
    sequence_count = key_portion.shape[0]
    key_portion = key_portion.reshape(
        sequence_count, key_tile_block, KEY_VALUE_HEADS, HEAD_DIMENSION
    )
    value_portion = value_portion.reshape(
        sequence_count, key_tile_block, KEY_VALUE_HEADS, HEAD_DIMENSION
    )
    col_pos = block_offset + jnp.arange(key_tile_block, dtype=jnp.int32)
    return (key_portion, value_portion, seg_part, col_pos)


def masked_scores(query_block_list, key_portion, seg_rows, seg_part, row_pos, col_pos, score_scale):
    raw_scores = jnp.einsum(
        "skgtd,sjkd->skgtj", query_block_list, key_portion, preferred_element_type=jnp.float32
    )
    allowed = (seg_rows[:, :, None] == seg_part[:, None, :]) & (
        col_pos[None, None, :] <= row_pos[None, :, None]
    )
    allowed = allowed[:, None, None, :, :]
    return (jnp.where(allowed, raw_scores * score_scale, NEGATIVE), allowed)


def log_sum(
    query_block_list, gathered, seg_rows, row_pos, block_count, key_tile_block, score_scale
):
    lead_shape = query_block_list.shape[:4]

    def log_step_fn(block_index, carried):
        row_top, row_total = carried
        key_portion, value_portion, seg_part, col_pos = block_view(
            gathered, block_index, key_tile_block
        )
        scores, allowed = masked_scores(
            query_block_list, key_portion, seg_rows, seg_part, row_pos, col_pos, score_scale
        )
        new_top = jnp.maximum(row_top, jnp.max(scores, axis=-1))
        exponent = jnp.where(allowed, jnp.exp(scores - new_top[..., None]), 0.0)
        row_total = row_total * jnp.exp(row_top - new_top) + jnp.sum(exponent, axis=-1)
        return (new_top, row_total)

    start_state = (jnp.full(lead_shape, NEGATIVE, jnp.float32), jnp.zeros(lead_shape, jnp.float32))
    row_top, row_total = lax.fori_loop(0, block_count, log_step_fn, start_state)
    return row_top + jnp.log(row_total)


def attend(
    query_block_list,
    gathered,
    seg_rows,
    row_pos,
    block_count,
    key_tile_block,
    score_scale,
    log_total,
):

    def attend_step_fn(block_index, mixed_heads):
        key_portion, value_portion, seg_part, col_pos = block_view(
            gathered, block_index, key_tile_block
        )
        scores, allowed = masked_scores(
            query_block_list, key_portion, seg_rows, seg_part, row_pos, col_pos, score_scale
        )
        probabilities = jnp.where(allowed, jnp.exp(scores - log_total[..., None]), 0.0).astype(
            jnp.bfloat16
        )
        return mixed_heads + jnp.einsum(
            "skgtj,sjkd->skgtd", probabilities, value_portion, preferred_element_type=jnp.float32
        )

    return lax.fori_loop(
        0, block_count, attend_step_fn, jnp.zeros(query_block_list.shape, jnp.float32)
    )


def query_back(
    query_block_list,
    gathered,
    seg_rows,
    row_pos,
    block_count,
    key_tile_block,
    score_scale,
    log_total,
    gradient_reduced,
    row_delta,
):

    def query_step_fn(block_index, grad_query):
        key_portion, value_portion, seg_part, col_pos = block_view(
            gathered, block_index, key_tile_block
        )
        scores, allowed = masked_scores(
            query_block_list, key_portion, seg_rows, seg_part, row_pos, col_pos, score_scale
        )
        probabilities = jnp.where(allowed, jnp.exp(scores - log_total[..., None]), 0.0)
        grad_probs = jnp.einsum(
            "skgtd,sjkd->skgtj", gradient_reduced, value_portion, preferred_element_type=jnp.float32
        )
        grad_scores = (probabilities * (grad_probs - row_delta[..., None]) * score_scale).astype(
            jnp.bfloat16
        )
        return grad_query + jnp.einsum(
            "skgtj,sjkd->skgtd", grad_scores, key_portion, preferred_element_type=jnp.float32
        )

    return lax.fori_loop(
        0, block_count, query_step_fn, jnp.zeros(query_block_list.shape, jnp.float32)
    )


def key_back(
    key_local,
    value_local,
    seg_rows,
    row_pos,
    query_whole,
    grads_whole,
    stats_whole,
    seg_whole,
    first_block,
    block_count,
    query_tile,
    score_scale,
):
    sequence_count = key_local.shape[0]
    group_width = QUERY_HEADS // KEY_VALUE_HEADS

    def key_step_fn(block_index, carried):
        key_total, value_total = carried
        block_offset = block_index * query_tile
        query_rows = lax.dynamic_slice_in_dim(query_whole, block_offset, query_tile, 1).reshape(
            sequence_count, query_tile, KEY_VALUE_HEADS, group_width, HEAD_DIMENSION
        )
        grad_rows = lax.dynamic_slice_in_dim(grads_whole, block_offset, query_tile, 1).reshape(
            sequence_count, query_tile, KEY_VALUE_HEADS, group_width, HEAD_DIMENSION
        )
        log_rows = lax.dynamic_slice_in_dim(stats_whole[0], block_offset, query_tile, 3)
        delta_rows = lax.dynamic_slice_in_dim(stats_whole[1], block_offset, query_tile, 3)
        seg_query = lax.dynamic_slice_in_dim(seg_whole, block_offset, query_tile, 1).astype(
            jnp.float32
        )
        query_pos = block_offset + jnp.arange(query_tile, dtype=jnp.int32)
        raw_scores = jnp.einsum(
            "stkgd,sjkd->skgtj", query_rows, key_local, preferred_element_type=jnp.float32
        )
        allowed = (seg_query[:, :, None] == seg_rows[:, None, :]) & (
            row_pos[None, None, :] <= query_pos[None, :, None]
        )
        allowed = allowed[:, None, None, :, :]
        scores = jnp.where(allowed, raw_scores * score_scale, NEGATIVE)
        probabilities = jnp.where(allowed, jnp.exp(scores - log_rows[..., None]), 0.0)
        grad_probs = jnp.einsum(
            "stkgd,sjkd->skgtj", grad_rows, value_local, preferred_element_type=jnp.float32
        )
        grad_scores = (probabilities * (grad_probs - delta_rows[..., None]) * score_scale).astype(
            jnp.bfloat16
        )
        key_total = key_total + jnp.einsum(
            "skgtj,stkgd->sjkd", grad_scores, query_rows, preferred_element_type=jnp.float32
        )
        value_total = value_total + jnp.einsum(
            "skgtj,stkgd->sjkd",
            probabilities.astype(jnp.bfloat16),
            grad_rows,
            preferred_element_type=jnp.float32,
        )
        return (key_total, value_total)

    start_state = (jnp.zeros(key_local.shape, jnp.float32), jnp.zeros(key_local.shape, jnp.float32))
    return lax.fori_loop(first_block, block_count, key_step_fn, start_state)


def per_device(
    inputs,
    segments,
    weight_query,
    key_weight_matrix,
    value_weight_matrix,
    weight_out,
    weight_gate,
    weight_up,
    weight_down,
    gain_attention,
    gain_feed,
    cotangent,
):
    shards = (
        weight_query,
        key_weight_matrix,
        value_weight_matrix,
        weight_out,
        weight_gate,
        weight_up,
        weight_down,
    )
    gain_shards = (gain_attention, gain_feed)
    micro_count, sequence_count, token_count, model_width = inputs.shape
    group_width = QUERY_HEADS // KEY_VALUE_HEADS
    score_scale = 1.0 / math.sqrt(HEAD_DIMENSION)
    row_pos = lax.axis_index("seq") * token_count + jnp.arange(token_count, dtype=jnp.int32)
    cosine_table, sine_values = rope_tables(row_pos, HEAD_DIMENSION)
    key_span_length = token_count * lax.axis_size("seq")
    key_tile_block = min(512, key_span_length)
    total_blocks = key_span_length // key_tile_block
    block_count = row_pos[token_count - 1] // key_tile_block + 1
    first_block = row_pos[0] // key_tile_block
    outputs = []
    grad_list = []
    totals = jnp.zeros((4,), jnp.float32)
    gain_grads = jnp.zeros((2, model_width), jnp.float32)
    summed = None
    weights_complete = gather_all(shards, gain_shards)
    for batch_index in range(micro_count):
        tokens = inputs[batch_index].astype(jnp.float32)
        seg_local = segments[batch_index]
        seg_rows = seg_local.astype(jnp.float32)
        seg_low = seg_local.astype(jnp.bfloat16)
        gain_first = weights_complete[7].astype(jnp.float32)
        gain_second = weights_complete[8].astype(jnp.float32)
        norm_first, scale_first = norm_forward(tokens, gain_first)
        normalized = norm_first.astype(jnp.bfloat16)
        query_raw = apply_projection(normalized, weights_complete[0]).reshape(
            sequence_count, token_count, QUERY_HEADS, HEAD_DIMENSION
        )
        query_reduced = apply_rotation(query_raw, cosine_table, sine_values).astype(jnp.bfloat16)
        key_unrotated = apply_projection(normalized, weights_complete[1]).reshape(
            sequence_count, token_count, KEY_VALUE_HEADS, HEAD_DIMENSION
        )
        key_low = (
            apply_rotation(key_unrotated, cosine_table, sine_values)
            .astype(jnp.bfloat16)
            .reshape(sequence_count, token_count, KEY_VALUE_HEADS * HEAD_DIMENSION)
        )
        value_low = apply_projection(normalized, weights_complete[2]).astype(jnp.bfloat16)
        gathered = gather_keys(key_low, value_low, seg_low)
        query_block_list = query_reduced.reshape(
            sequence_count, token_count, KEY_VALUE_HEADS, group_width, HEAD_DIMENSION
        ).transpose(0, 2, 3, 1, 4)
        log_total = log_sum(
            query_block_list, gathered, seg_rows, row_pos, block_count, key_tile_block, score_scale
        )
        mixed_heads = attend(
            query_block_list,
            gathered,
            seg_rows,
            row_pos,
            block_count,
            key_tile_block,
            score_scale,
            log_total,
        )
        attn_low = (
            mixed_heads.transpose(0, 3, 1, 2, 4)
            .reshape(sequence_count, token_count, QUERY_HEADS * HEAD_DIMENSION)
            .astype(jnp.bfloat16)
        )
        branch_attn = apply_projection(attn_low, weights_complete[3])
        hidden = tokens + branch_attn
        norm_second, scale_second = norm_forward(hidden, gain_second)
        normed_second = norm_second.astype(jnp.bfloat16)
        gate_values = apply_projection(normed_second, weights_complete[4])
        up_values = apply_projection(normed_second, weights_complete[5])
        gate_sigmoid = jax.nn.sigmoid(gate_values)
        inner_low = (gate_values * gate_sigmoid * up_values).astype(jnp.bfloat16)
        branch_feed = apply_projection(inner_low, weights_complete[6])
        result = hidden + branch_feed
        outputs.append(result.astype(jnp.bfloat16))
        valid_rows = (seg_local != 0).astype(jnp.float32)[:, :, None]
        totals = totals + jnp.stack(
            [
                jnp.sum(valid_rows * branch_attn * branch_attn),
                jnp.sum(valid_rows * branch_feed * branch_feed),
                jnp.sum(valid_rows * result * result),
                jnp.sum(valid_rows),
            ]
        )
        back_weights = weights_complete
        back_keys = gathered
        grad_result = cotangent[batch_index].astype(jnp.float32)
        grad_feed = grad_result.astype(jnp.bfloat16)
        grad_down = weight_grad(inner_low, grad_feed)
        grad_inner = project_back(grad_feed, back_weights[6])
        grad_up = (grad_inner * gate_values * gate_sigmoid).astype(jnp.bfloat16)
        grad_gate = (
            grad_inner * up_values * gate_sigmoid * (1.0 + gate_values * (1.0 - gate_sigmoid))
        ).astype(jnp.bfloat16)
        grad_gate_w = weight_grad(normed_second, grad_gate)
        grad_up_w = weight_grad(normed_second, grad_up)
        grad_normed_second = project_back(grad_gate, back_weights[4]) + project_back(
            grad_up, back_weights[5]
        )
        grad_hidden_norm, grad_gain_second = norm_backward(
            hidden, scale_second, gain_second, grad_normed_second
        )
        grad_hidden = grad_result + grad_hidden_norm
        grad_branch = grad_hidden.astype(jnp.bfloat16)
        grad_out_w = weight_grad(attn_low, grad_branch)
        mixed_gradient = project_back(grad_branch, back_weights[3]).astype(jnp.bfloat16)
        gradient_reduced = mixed_gradient.reshape(
            sequence_count, token_count, KEY_VALUE_HEADS, group_width, HEAD_DIMENSION
        ).transpose(0, 2, 3, 1, 4)
        row_delta = jnp.sum(gradient_reduced.astype(jnp.float32) * mixed_heads, axis=-1)
        grad_query = query_back(
            query_block_list,
            back_keys,
            seg_rows,
            row_pos,
            block_count,
            key_tile_block,
            score_scale,
            log_total,
            gradient_reduced,
            row_delta,
        )
        query_flat = query_reduced.reshape(
            sequence_count, token_count, QUERY_HEADS * HEAD_DIMENSION
        )
        query_whole, grads_whole = (
            lax.all_gather(query_flat, "seq", axis=1, tiled=True),
            lax.all_gather(mixed_gradient, "seq", axis=1, tiled=True),
        )
        stats_whole = (
            lax.all_gather(log_total, "seq", axis=3, tiled=True),
            lax.all_gather(row_delta, "seq", axis=3, tiled=True),
        )
        key_local = key_low.reshape(sequence_count, token_count, KEY_VALUE_HEADS, HEAD_DIMENSION)
        value_local = value_low.reshape(
            sequence_count, token_count, KEY_VALUE_HEADS, HEAD_DIMENSION
        )
        key_total, value_total = key_back(
            key_local,
            value_local,
            seg_rows,
            row_pos,
            query_whole,
            grads_whole,
            stats_whole,
            back_keys[2],
            first_block,
            total_blocks,
            key_tile_block,
            score_scale,
        )
        key_grad_low = (
            reverse_rotation(key_total, cosine_table, sine_values)
            .reshape(sequence_count, token_count, KEY_VALUE_HEADS * HEAD_DIMENSION)
            .astype(jnp.bfloat16)
        )
        value_grad_low = value_total.reshape(
            sequence_count, token_count, KEY_VALUE_HEADS * HEAD_DIMENSION
        ).astype(jnp.bfloat16)
        query_grad = grad_query.transpose(0, 3, 1, 2, 4).reshape(
            sequence_count, token_count, QUERY_HEADS, HEAD_DIMENSION
        )
        query_grad_low = (
            reverse_rotation(query_grad, cosine_table, sine_values)
            .reshape(sequence_count, token_count, QUERY_HEADS * HEAD_DIMENSION)
            .astype(jnp.bfloat16)
        )
        grad_normed = (
            project_back(query_grad_low, back_weights[0])
            + project_back(key_grad_low, back_weights[1])
            + project_back(value_grad_low, back_weights[2])
        )
        grad_token_norm, grad_gain_first = norm_backward(
            tokens, scale_first, gain_first, grad_normed
        )
        grad_list.append((grad_hidden + grad_token_norm).astype(jnp.bfloat16))
        gain_grads = gain_grads + jnp.stack([grad_gain_first, grad_gain_second])
        batch_grads = (
            weight_grad(normalized, query_grad_low),
            weight_grad(normalized, key_grad_low),
            weight_grad(normalized, value_grad_low),
            grad_out_w,
            grad_gate_w,
            grad_up_w,
            grad_down,
        )
        summed = batch_grads if summed is None else jax.tree.map(jnp.add, summed, batch_grads)
    reduced = reduce_grads(summed)
    gain_total, totals = lax.psum((gain_grads, totals), ("dp", "seq"))
    piece_width = model_width // lax.axis_size("seq")
    gain_part = lax.dynamic_slice_in_dim(
        gain_total, lax.axis_index("seq") * piece_width, piece_width, 1
    )
    root_means = jnp.sqrt(totals[:3] / (totals[3] * model_width))
    return (
        jnp.stack(outputs),
        jnp.stack(grad_list),
        reduced[0],
        reduced[1],
        reduced[2],
        reduced[3],
        reduced[4],
        reduced[5],
        reduced[6],
        gain_part[0],
        gain_part[1],
        root_means,
    )


LANES = 128


def fast_kernel(
    meta_in,
    x_in,
    cot_in,
    wq_in,
    wo_in,
    gu_in,
    wd_in,
    cos_in,
    sin_in,
    out_o,
    gin_o,
    gq_o,
    go_o,
    ggu_o,
    gd_o,
    small_o,
    meta_r,
    xo,
    co,
    n1g,
    gfg,
    n2g,
    wq_r,
    wq_w,
    wo_r,
    wo_w,
    gu_r,
    gu_w,
    wd_r,
    wd_w,
    acc,
    qk,
    qt,
    dat,
    kw,
    vw,
    pb0,
    pb1,
    pb2,
    pb3,
    mx,
    segr,
    segc,
    gains,
    at_s,
    at_r,
    hid,
    dhid,
    inner_s,
    dgu_s,
    part_e,
    e2r1,
    e2r2,
    bfr1,
    bfr2,
    da_s,
    da_r,
    d_s,
    dkvt,
    gux_r,
    guz_r,
    guf_r,
    gd_s,
    gdx_r,
    gdz_r,
    gor1,
    gox_r,
    goq_r,
    goz_r,
    gq_r,
    small_s,
    small_r,
    rows_s,
    rows_r,
    ssem,
    rsem,
):
    f32, bf16 = jnp.float32, jnp.bfloat16
    part_f = n2g
    e1r1, e1r2 = gfg.at[0], gfg.at[1]
    x = lax.axis_index("dp")
    s = lax.axis_index("seq")
    zh, j = s // 8, s % 8
    zl, y, c = j // 4, (j // 2) % 2, j % 2
    own_chip = zl * 2 + y
    attends = (j != 3) & (j != 5)

    def head_of(device_index):
        high = device_index // 4
        return device_index - high * (1 + (device_index - 2) // 3)

    head_own = head_of(j)
    width = x_in.shape[2]
    counter = [0]
    pending = []

    def index_of(mask):
        return (
            ((1 - zl) if mask & 4 else zl) * 4
            + ((1 - y) if mask & 2 else y) * 2
            + ((1 - c) if mask & 1 else c)
        )

    def device(mask=0, flip_x=False, flip_z=False):
        return (
            (1 - x) if flip_x else x,
            ((1 - zh) if flip_z else zh) * 8 + index_of(mask),
        )

    def fresh():
        counter[0] += 1
        return counter[0] - 1

    def send(src, dst, target, keep=True):
        n = fresh()
        copy = pltpu.make_async_remote_copy(
            src_ref=src,
            dst_ref=dst,
            send_sem=ssem.at[n],
            recv_sem=rsem.at[n],
            device_id=target,
            device_id_type=pl.DeviceIdType.MESH,
        )
        copy.start()
        if keep:
            pending.append(copy)
        return copy

    def mm(a, b):
        return jnp.dot(a, b, preferred_element_type=f32)

    def mm_t(a, b):
        return lax.dot_general(a, b, (((1,), (1,)), ((), ())), preferred_element_type=f32)

    def mm_w(a, b):
        return lax.dot_general(a, b, (((0,), (0,)), ((), ())), preferred_element_type=f32)

    chip_y, chip_z, chip_d = zl * 2 + 1 - y, (1 - zl) * 2 + y, (1 - zl) * 2 + 1 - y

    class Gather:
        def __init__(self, view, pair=True, halves=(True, True)):
            self.view, self.pair, self.halves = view, pair, halves
            self.copies, self.cores = [], []

        def start(self, source=None):
            own = self.view(own_chip)
            source = own if source is None else source
            self.z = self.put(source, own, 4)
            self.y = self.put(source, own, 2)
            if self.pair:
                self.cores.append(self.put(source, own, 1))

        def put(self, source, place, mask):
            copy = send(source, place, device(mask))
            self.copies.append(copy)
            return copy

        def part(self, chip, half):
            view = self.view(chip)
            return view if self.halves[0] != self.halves[1] else view.at[half]

        def from_z(self):
            self.z.wait_recv()
            if self.halves[0]:
                self.zy = self.put(self.part(chip_z, 0), self.part(chip_z, 0), 2)
            if self.pair:
                self.cores.append(self.put(self.view(chip_z), self.view(chip_z), 1))

        def from_y(self):
            self.y.wait_recv()
            if self.halves[1]:
                self.yz = self.put(self.part(chip_y, 1), self.part(chip_y, 1), 4)
            if self.pair:
                self.cores.append(self.put(self.view(chip_y), self.view(chip_y), 1))

        def from_far(self):
            if self.halves[0]:
                self.zy.wait_recv()
            if self.halves[1]:
                self.yz.wait_recv()
            if self.pair:
                self.cores.append(self.put(self.view(chip_d), self.view(chip_d), 1))

        def finish(self):
            for copy in self.cores:
                copy.wait_recv()

        def sent(self):
            for copy in self.copies:
                copy.wait_send()

    def tokens_of(half):
        return lambda chip: n1g.at[half, chip, c]

    x_a = Gather(tokens_of(zh), True, (True, False))
    x_b = Gather(tokens_of(1 - zh), True, (False, True))
    x_a.start(x_in.at[zh])
    x_copy = send(x_in.at[1 - zh], n1g.at[zh, own_chip, c], device(0, False, True))
    meta_copies = []
    for mask in range(8):
        for far in (False, True):
            if mask or far:
                meta_copies.append(send(meta_in, meta_r.at[s], device(mask, False, far)))

    qkv_sem = fresh()
    qkv_first = []
    for far_x in (False, True):
        for far_z in (False, True):
            for piece in range(3):
                n = fresh()
                tx = (1 - x) if far_x else x
                tz = (1 - zh) if far_z else zh
                target = (tx, tz * 8 + 4 * x + piece + x * ((piece + 1) // 2))
                copy = pltpu.make_async_remote_copy(
                    src_ref=wq_in.at[piece],
                    dst_ref=wq_r.at[s],
                    send_sem=ssem.at[n],
                    recv_sem=rsem.at[qkv_sem],
                    device_id=target,
                    device_id_type=pl.DeviceIdType.MESH,
                )
                if far_x or far_z:
                    copy.start()
                    pending.append(copy)
                else:
                    here = j == 4 * x + piece + x * ((piece + 1) // 2)
                    local = pltpu.make_async_copy(
                        wq_in.at[piece], wq_r.at[s], rsem.at[qkv_sem]
                    )
                    pl.when(here)(local.start)
                    pl.when(jnp.logical_not(here))(copy.start)
                    qkv_first.append((here, copy))
    wo_z = send(wo_in, wo_r.at[x, zh, own_chip, c], device(0, False, True))
    wo_r[x, zh, own_chip, c] = wo_in[...]
    wd_r[x, zh] = wd_in[...]
    gu_r[x, zh, j] = gu_in[j]
    meta_r[s] = meta_in[...]
    n1g[zh, own_chip, c] = x_in[zh]
    xo[zh] = x_in[zh]
    co[zh] = cot_in[zh]
    gfg[zh, own_chip, c] = cot_in[zh]
    da_s[...] = jnp.zeros(da_s.shape, bf16)
    wd_w[...] = jnp.zeros(wd_w.shape, bf16)

    def norm_rows(values, gain):
        scale = lax.rsqrt(jnp.mean(values * values, axis=-1, keepdims=True) + EPS)
        return values * scale * gain, scale

    x_copy.wait_recv()
    x_b.start()
    xo[1 - zh] = n1g[1 - zh, own_chip, c]
    x_a.from_z()
    x_a.from_y()
    for copy in meta_copies:
        copy.wait_recv()
    gain_rows = jnp.zeros((8, width), f32)
    seg_rows = jnp.zeros((8, 1024), f32)
    for slot in range(16):
        piece = meta_r[slot]
        wide = jnp.concatenate([piece, jnp.zeros((8, width - LANES), f32)], axis=1)
        gain_rows = gain_rows + pltpu.roll(wide, 72 * slot, 1)
        wide = jnp.concatenate([piece, jnp.zeros((8, 1024 - LANES), f32)], axis=1)
        seg_rows = seg_rows + pltpu.roll(wide, 64 * slot, 1)
    gains[...] = gain_rows
    seg_own = jnp.where(zh == 0, seg_rows[2:3, :], seg_rows[3:4, :])
    seg_wide = jnp.broadcast_to(seg_own, (8, 1024))
    segr[...] = seg_wide
    segc[...] = seg_wide.T

    x_a.from_far()
    x_b.from_z()
    x_b.from_y()
    x_b.from_far()

    def wo_view(chip):
        return wo_r.at[x, :, chip, c]

    def gf_view(chip):
        return gfg.at[:, chip, c]

    def n2_view(chip):
        return n2g.at[:, chip, c]

    wo_z.wait_recv()
    wo_q = Gather(wo_view, False)
    wo_q.start()
    wo_x = [send(wo_view(own_chip), wo_view(own_chip), device(0, True))]

    def spread_rows(read, columns):
        def step(slot, carry):
            acc[pl.ds(pl.multiple_of(slot * 72, 8), 72), 0:columns] = read(slot).astype(f32)
            return carry

        lax.fori_loop(0, 16, step, 0)

    def to_low(store, columns):
        def step(block, carry):
            at = pl.multiple_of(block * 128, 128)
            store(at, acc[pl.ds(at, 128), 0:columns].astype(bf16))
            return carry

        lax.fori_loop(0, 9, step, 0)

    def from_rows(store):
        def step(slot, carry):
            store(slot, pl.multiple_of(slot * 72, 8))
            return carry

        lax.fori_loop(0, 16, step, 0)


    @pl.when(attends)
    def _():
        pltpu.make_async_copy(wq_r, wq_r, rsem.at[qkv_sem]).wait()
        spread_rows(lambda slot: wq_r[slot], 384)

        def store(at, value):
            wq_w[pl.ds(at, 128), :] = value

        to_low(store, 384)

    x_a.finish()
    x_b.finish()
    x_a.sent()
    x_b.sent()
    cot_copy = send(cot_in.at[1 - zh], co.at[zh], device(0, False, True))
    gu_first = []
    for mask in range(1, 8):
        gu_first.append(send(gu_in.at[index_of(mask)], gu_r.at[x, zh, j], device(mask)))
    wd_z = send(wd_in, wd_r.at[x, zh], device(0, False, True))
    wd_x = send(wd_in, wd_r.at[x, zh], device(0, True))

    lane256 = lax.broadcasted_iota(jnp.int32, (1, 256), 1)
    low_half = (lane256 % 64) < 32

    def swap_half(values):
        return jnp.where(low_half, pltpu.roll(values, 256 - 32, 1), pltpu.roll(values, 32, 1))

    def tables(at, rows):
        cosine = cos_in[pl.ds(at, rows), :]
        sine = sin_in[pl.ds(at, rows), :]
        return (
            jnp.concatenate([cosine, cosine], axis=1),
            jnp.concatenate([sine, sine], axis=1),
        )

    @pl.when(attends)
    def _():
        def step(block, carry):
            at = pl.multiple_of(block * 256, 256)
            rows = n1g[block // 2, pl.ds((block % 2) * 2, 2)].reshape(256, width)
            rows, _ = norm_rows(rows.astype(f32), gains[0:1, :])
            rows = rows.astype(bf16)
            n1g[block // 2, pl.ds((block % 2) * 2, 2)] = rows.reshape(2, 2, 64, width)
            raw = mm(rows, wq_w[...])
            cosine, sine = tables(at, 256)
            pair = raw[:, 0:256]
            turned = pair * cosine + swap_half(pair) * sine
            turned = turned.astype(bf16).astype(f32)
            qk[pl.ds(at, 256), :] = turned.astype(bf16)
            qt[:, pl.ds(at, 256)] = turned.T[0:192].astype(bf16)
            values = raw[:, 256:384].astype(bf16).astype(f32)
            values = jnp.concatenate([values, jnp.zeros((256, 128), f32)], axis=1)
            for head in range(3):
                mine = (lane256 // 64) == head
                shift = (64 * (head + 1)) % 256
                kw[head, pl.ds(at, 256), :] = jnp.where(
                    mine, pltpu.roll(turned, shift, 1), 0.0
                ).astype(bf16)
                placed = pltpu.roll(values, 64 * head, 1) if head else values
                vw[head, pl.ds(at, 256), :] = placed.astype(bf16)
            return carry

        lax.fori_loop(0, 4, step, 0)

    pbs = (pb0, pb1, pb2, pb3)
    scale = 1.0 / math.sqrt(HEAD_DIMENSION)

    def attend_block(quarter):
        length = 256 * (quarter + 1)

        def step(sub, carry):
            at = pl.multiple_of(quarter * 256 + sub * 128, 128)
            query = qk[pl.ds(at, 128), :]
            key_pos = lax.broadcasted_iota(jnp.int32, (128, length), 1)
            row_pos = lax.broadcasted_iota(jnp.int32, (128, length), 0) + at
            allowed = (segc[pl.ds(at, 128), 0:1] == segr[0:1, 0:length]) & (key_pos <= row_pos)
            mixed = jnp.zeros((128, 256), f32)
            for head in range(3):
                scores = mm_t(query, kw[head, 0:length, :])
                scores = jnp.where(allowed, scores * scale, NEGATIVE)
                top = jnp.max(scores, axis=-1, keepdims=True)
                weight = jnp.exp(scores - top)
                weight = weight / jnp.sum(weight, axis=-1, keepdims=True)
                low_p = weight.astype(bf16)
                pbs[quarter][head, pl.ds(pl.multiple_of(sub * 128, 128), 128), :] = low_p
                mixed = mixed + mm(low_p, vw[head, 0:length, :])
            mx[pl.ds(at, 128), :] = mixed
            at_s[quarter // 2, pl.ds((quarter % 2) * 4 + sub * 2, 2)] = mixed.astype(
                bf16
            ).reshape(2, 64, 256)
            return carry

        lax.fori_loop(0, 2, step, 0)

    wo_q.from_z()
    wo_x.append(send(wo_view(chip_z), wo_view(chip_z), device(0, True)))
    pl.when(attends)(lambda: attend_block(0))
    wo_q.from_y()
    wo_x.append(send(wo_view(chip_y), wo_view(chip_y), device(0, True)))
    pl.when(attends)(lambda: attend_block(1))
    for copy in gu_first:
        copy.wait_recv()
    gu_z = []
    for part in range(2):
        rows = gu_r.at[x, zh, 4 * part : 4 * part + 4]
        gu_z.append(send(rows, rows, device(0, False, True)))
    gu_x = [send(gu_r.at[x, zh], gu_r.at[x, zh], device(0, True))]
    pl.when(attends)(lambda: attend_block(2))
    wo_q.from_far()
    wo_x.append(send(wo_view(chip_d), wo_view(chip_d), device(0, True)))
    wo_c = [send(wo_r.at[x, :, :, c], wo_r.at[x, :, :, c], device(1))]
    pl.when(attends)(lambda: attend_block(3))

    at_copies = []
    for mask in range(1, 8):
        n = fresh()
        there = index_of(mask)
        copy = pltpu.make_async_remote_copy(
            src_ref=at_s.at[:, there],
            dst_ref=at_r.at[head_own],
            send_sem=ssem.at[n],
            recv_sem=rsem.at[n],
            device_id=device(mask),
            device_id_type=pl.DeviceIdType.MESH,
        )
        pl.when(attends)(copy.start)
        at_copies.append(((there != 3) & (there != 5), copy))

    @pl.when(attends)
    def _():
        at_r[head_own] = at_s[:, j]

    cot_copy.wait_recv()
    gfg[1 - zh, own_chip, c] = co[1 - zh]
    gf_all = Gather(gf_view)
    gf_all.start()
    for copy in wo_x:
        copy.wait_recv()
    wo_c.append(send(wo_r.at[1 - x, :, :, c], wo_r.at[1 - x, :, :, c], device(1)))
    wd_z.wait_recv()
    wd_f = send(wd_r.at[x, 1 - zh], wd_r.at[x, 1 - zh], device(0, True))
    for copy in wo_c:
        copy.wait_recv()

    def spread_left(slot):
        z_half, chip, core = slot // 8, (slot % 8) // 2, slot % 2
        left = wo_r[0, z_half, chip, core].astype(f32)
        right = wo_r[1, z_half, chip, core, :, 0:128].astype(f32)
        return jnp.concatenate([left[:, 0:512], left[:, 512:640] + right], axis=1)

    def store_left(at, value):
        wo_w[pl.ds(at, 128), 0:640] = value

    spread_rows(spread_left, 640)
    to_low(store_left, 640)

    def store_right(at, value):
        wo_w[pl.ds(at, 128), 640:1152] = value

    spread_rows(lambda slot: wo_r[1, slot // 8, (slot % 8) // 2, slot % 2, :, 128:640], 512)
    to_low(store_right, 512)

    for theirs, copy in at_copies:
        pl.when(theirs)(copy.wait_recv)

    def branch_of():
        total = jnp.zeros((128, width), f32)
        for head in range(6):
            piece = at_r[head].reshape(128, 256)[:, 0:192]
            total = total + mm(piece, wo_w[192 * head : 192 * head + 192, :])
        return total

    branch = branch_of()
    valid = jnp.concatenate(
        [
            (segc[pl.ds(pl.multiple_of(64 * j, 64), 64), 0:1] != 0).astype(f32),
            (segc[pl.ds(pl.multiple_of(512 + 64 * j, 64), 64), 0:1] != 0).astype(f32),
        ],
        axis=0,
    )
    lane1 = lax.broadcasted_iota(jnp.int32, (1, LANES), 1)
    square_attn = jnp.sum(jnp.sum(valid * branch * branch, axis=0, keepdims=True), axis=1, keepdims=True)
    count = jnp.sum(valid, axis=0, keepdims=True)
    hidden = xo[...].reshape(128, width).astype(f32) + branch
    hid[...] = hidden
    normed, _ = norm_rows(hidden, gains[1:2, :])
    n2g[:, own_chip, c] = normed.astype(bf16).reshape(2, 64, width)
    n2_all = Gather(n2_view)
    n2_all.start()
    gf_all.from_z()
    gf_all.from_y()
    for part in range(2):
        gu_z[part].wait_recv()
        rows = gu_r.at[x, 1 - zh, 4 * part : 4 * part + 4]
        gu_x.append(send(rows, rows, device(0, True)))
    gf_all.from_far()
    n2_all.from_z()
    n2_all.from_y()

    wd_x.wait_recv()
    wd_f.wait_recv()
    for copy in gu_x:
        copy.wait_recv()
    for chunk in range(2):
        spread_rows(lambda slot: gu_r[chunk, slot // 8, slot % 8], 384)

        def store_gu(at, value):
            gu_w[chunk, pl.ds(at, 128), :] = value

        to_low(store_gu, 384)
        left, right = wd_r[0, chunk], wd_r[1, chunk]
        wd_w[chunk, 0:192, 0:512] = left[:, 0:512]
        wd_w[chunk, 0:192, 512:640] = (
            left[:, 512:640].astype(f32) + right[:, 0:128].astype(f32)
        ).astype(bf16)
        wd_w[chunk, 0:192, 640:1152] = right[:, 128:640]
    n2_all.from_far()
    gf_all.finish()
    n2_all.finish()

    def chip_at(step):
        return ((zl + step + 1) % 2) * 2 + (y + (3 - step) // 2) % 2

    def pair_copy(ref, got, base, step):
        chip = chip_at(step)
        return pltpu.make_async_remote_copy(
            src_ref=ref.at[:, chip, 1 - c],
            dst_ref=got.at[step],
            send_sem=ssem.at[base + step],
            recv_sem=rsem.at[base + step],
            device_id=device(1),
            device_id_type=pl.DeviceIdType.MESH,
        )

    def side_copy(ref, got2, base, kind):
        step, half, slot, mask = (
            (0, 0, 0, 2),
            (0, 1, 0, 4),
            (1, 0, 1, 2),
            (2, 1, 2, 4),
            (1, 1, 1, 2),
            (2, 0, 2, 4),
        )[kind]
        return pltpu.make_async_remote_copy(
            src_ref=ref.at[half, chip_at(step), c],
            dst_ref=got2.at[slot, half],
            send_sem=ssem.at[base + 4 + kind],
            recv_sem=rsem.at[base + 4 + kind],
            device_id=device(mask),
            device_id_type=pl.DeviceIdType.MESH,
        )

    def pair_sum(ref, got, step):
        chip = chip_at(step)
        return ref[:, chip, c].astype(f32) + got[step].astype(f32)

    def scatter_side(ref, got, got2, base, step):
        pair_copy(ref, got, base, step).wait_recv()
        ref[:, chip_at(step), c] = pair_sum(ref, got, step).astype(bf16)
        for kind in ((0, 1), (2,), (3,))[step]:
            side_copy(ref, got2, base, kind).start()

    def scatter_first(ref, got, got2, compute):
        base = counter[0]
        counter[0] += 10

        def step_fn(step, carry):
            chip = chip_at(step)
            block = compute(chip).astype(bf16).reshape(2, 2, 64, width)
            ref[:, chip] = block
            pair_copy(ref, got, base, step).start()
            for done in range(3):
                pl.when(step == done + 1)(
                    functools.partial(scatter_side, ref, got, got2, base, done)
                )
            return carry

        lax.fori_loop(0, 4, step_fn, 0)
        return base

    def scatter_second(ref, got, got2, base):
        for kind, step, half in ((5, 2, 0), (4, 1, 1)):
            side_copy(ref, got2, base, half).wait_recv()
            chip = chip_at(step)
            total = ref[half, chip, c].astype(f32) + got2[0, half].astype(f32)
            ref[half, chip, c] = total.astype(bf16)
            side_copy(ref, got2, base, kind).start()

    def scatter_finish(ref, got, got2, base):
        pair_copy(ref, got, base, 3).wait_recv()
        total = pair_sum(ref, got, 3)
        for kind in (2, 3, 4, 5):
            side_copy(ref, got2, base, kind).wait_recv()
        total = total + got2[1].astype(f32) + got2[2].astype(f32)
        return total.reshape(128, width)

    def scatter_sent(ref, got, got2, base):
        for step in range(4):
            pair_copy(ref, got, base, step).wait_send()
        for kind in range(6):
            side_copy(ref, got2, base, kind).wait_send()

    lane128 = lax.broadcasted_iota(jnp.int32, (1, LANES), 1)

    def feed_block(chip):
        rows = n2g[:, chip].reshape(256, width)
        grads = gfg[:, chip].reshape(256, width)
        total = jnp.zeros((256, width), f32)
        for chunk in range(2):
            both = mm(rows, gu_w[chunk])
            d_inner = mm_t(grads, wd_w[chunk])
            gate_a, mid, up_a = both[:, 0:128], both[:, 128:256], both[:, 256:384]
            turned = pltpu.roll(mid, 64, 1)
            pieces = []
            for gate, up, back in (
                (gate_a, up_a, d_inner[:, 0:128]),
                (mid, turned, d_inner[:, 128:256]),
            ):
                sig = jax.nn.sigmoid(gate)
                silu = gate * sig
                pieces.append(
                    (silu * up, back * silu, back * up * sig * (1.0 + gate * (1.0 - sig)))
                )
            inner_s[chunk, :, pl.ds(chip * 2, 2), :, 0:128] = (
                pieces[0][0].astype(bf16).reshape(2, 2, 64, 128)
            )
            inner_s[chunk, :, pl.ds(chip * 2, 2), :, 128:256] = (
                jnp.where(lane128 < 64, pieces[1][0], 0.0).astype(bf16).reshape(2, 2, 64, 128)
            )
            gate_low = jnp.where(lane128 < 64, pieces[1][2], 0.0)
            up_low = jnp.where(lane128 < 64, pieces[1][1], 0.0)
            middle = (gate_low + pltpu.roll(up_low, 64, 1)).astype(bf16)
            d_both = jnp.concatenate(
                [pieces[0][2].astype(bf16), middle, pieces[0][1].astype(bf16)], axis=1
            )
            dgu_s[chunk, :, pl.ds(chip * 2, 2)] = d_both.reshape(2, 2, 64, 384)
            total = total + mm_t(d_both, gu_w[chunk])
        return total

    e2_base = scatter_first(part_e, e2r1, e2r2, feed_block)
    scatter_second(part_e, e2r1, e2r2, e2_base)

    for copy in gu_x + gu_z:
        copy.wait_send()
    gf_all.sent()
    for chunk in range(2):
        grads = dgu_s[chunk].reshape(1024, 384)

        def wide_step(block, carry):
            at = pl.multiple_of(block * 128, 128)
            rows = n2g[:, :, :, :, pl.ds(at, 128)].reshape(1024, 128)
            acc[pl.ds(at, 128), 0:384] = mm_w(rows, grads)
            return carry

        lax.fori_loop(0, 9, wide_step, 0)

        def cut(slot, at):
            gu_r[chunk, slot // 8, slot % 8] = acc[pl.ds(at, 72), 0:384].astype(bf16)

        from_rows(cut)
    ggu_x = send(gu_r.at[1 - x], gux_r, device(0, True))

    def down_step(chunk, carry):
        grads = gfg[...].reshape(1024, width)
        piece = mm_w(inner_s[chunk].reshape(1024, 256), grads)
        gd_s[chunk, 0] = piece[0:192, 0:640].astype(bf16)
        gd_s[chunk, 1] = piece[0:192, 512:1152].astype(bf16)
        return carry

    lax.fori_loop(0, 2, down_step, 0)
    ggd_x = send(gd_s.at[:, 1 - x], gdx_r, device(0, True))

    def result_block(chip):
        total = mm(
            inner_s[0, :, pl.ds(chip * 2, 2)].reshape(256, 256), wd_w[0]
        )
        return total + mm(inner_s[1, :, pl.ds(chip * 2, 2)].reshape(256, 256), wd_w[1])

    n2_all.sent()
    bf_base = scatter_first(part_f, bfr1, bfr2, result_block)

    e2 = scatter_finish(part_e, e2r1, e2r2, e2_base)
    hidden = hid[...]
    scale2 = lax.rsqrt(jnp.mean(hidden * hidden, axis=-1, keepdims=True) + EPS)
    scaled = e2 * gains[1:2, :]
    inner_mean = jnp.mean(scaled * hidden, axis=-1, keepdims=True)
    gain_feed_row = jnp.sum(e2 * hidden * scale2, axis=0, keepdims=True)
    d_hidden = (
        co[...].reshape(128, width).astype(f32)
        + scale2 * scaled
        - hidden * (scale2 * scale2 * scale2) * inner_mean
    )
    dhid[...] = d_hidden
    d_low = d_hidden.astype(bf16)
    for head in range(6):
        piece = mm_t(d_low, wo_w[192 * head : 192 * head + 192, :])
        da_s[head, :, :, 0:192] = piece.astype(bf16).reshape(2, 64, 192)
    da_copies = []
    for mask in range(1, 8):
        n = fresh()
        there = index_of(mask)
        copy = pltpu.make_async_remote_copy(
            src_ref=da_s.at[head_of(there)],
            dst_ref=da_r.at[:, j],
            send_sem=ssem.at[n],
            recv_sem=rsem.at[n],
            device_id=device(mask),
            device_id_type=pl.DeviceIdType.MESH,
        )
        pl.when((there != 3) & (there != 5))(copy.start)
        da_copies.append(((there != 3) & (there != 5), copy))

    @pl.when(attends)
    def _():
        da_r[:, j] = da_s[head_own]

    for copy in wo_c + wo_x:
        copy.wait_send()
    wo_q.sent()
    for plane in range(2):
        for head in range(6):
            piece = at_r[head].reshape(128, 256)[:, 0:192]
            acc[192 * head : 192 * head + 192, :] = mm_w(
                piece, d_low[:, 512 * plane : 512 * plane + 640]
            )

        def cut_out(slot, at):
            wo_r[plane, slot // 8, (slot % 8) // 2, slot % 2] = acc[pl.ds(at, 72), :].astype(bf16)

        from_rows(cut_out)
    go_c = send(wo_r.at[:, :, :, 1 - c], gor1, device(1))

    dkvt[...] = jnp.zeros(dkvt.shape, f32)
    for _, copy in da_copies:
        pl.when(attends)(copy.wait_recv)

    @pl.when(attends)
    def _():
        def step(block, carry):
            at = pl.multiple_of(block * 256, 256)
            rows = da_r[block // 2, pl.ds((block % 2) * 4, 4)].reshape(256, 256)
            dat[:, pl.ds(at, 256)] = rows.astype(f32).T[0:192].astype(bf16)
            return carry

        lax.fori_loop(0, 4, step, 0)

    def back_block(quarter):
        length = 256 * (quarter + 1)

        def step(sub, carry):
            at = pl.multiple_of(quarter * 256 + sub * 128, 128)
            grads = da_r[quarter // 2, pl.ds((quarter % 2) * 4 + sub * 2, 2)].reshape(128, 256)
            products = grads.astype(f32) * mx[pl.ds(at, 128), :]
            d_query = jnp.zeros((128, 256), f32)
            d_key = jnp.zeros((64, length), f32)
            d_value = jnp.zeros((64, length), f32)
            for head in range(3):
                delta = jnp.sum(
                    jnp.where((lane256 // 64) == head, products, 0.0), axis=-1, keepdims=True
                )
                low_p = pbs[quarter][head, pl.ds(pl.multiple_of(sub * 128, 128), 128), :]
                d_p = mm_t(grads, vw[head, 0:length, :])
                d_s_low = (low_p.astype(f32) * (d_p - delta) * scale).astype(bf16)
                d_query = d_query + mm(d_s_low, kw[head, 0:length, :])
                d_key = d_key + mm(qt[64 * head : 64 * head + 64, pl.ds(at, 128)], d_s_low)
                d_value = d_value + mm(dat[64 * head : 64 * head + 64, pl.ds(at, 128)], low_p)
            mx[pl.ds(at, 128), :] = d_query
            dkvt[0:64, 0:length] += d_value
            dkvt[64:128, 0:length] += d_key
            return carry

        lax.fori_loop(0, 2, step, 0)

    pl.when(attends)(lambda: back_block(0))
    scatter_second(part_f, bfr1, bfr2, bf_base)
    go_c.wait_recv()

    def go_add(chip, carry):
        for half in range(2):
            for plane in range(2):
                wo_r[plane, half, chip, c] = (
                    wo_r[plane, half, chip, c].astype(f32) + gor1[plane, half, chip].astype(f32)
                ).astype(bf16)
        return carry

    lax.fori_loop(0, 4, go_add, 0)

    def go_side(chip, half, slot, mask):
        return send(wo_r.at[:, half, chip, c], goq_r.at[slot, half], device(mask))

    def go_sum(half, chip, slot):
        for plane in range(2):
            wo_r[plane, half, chip, c] = (
                wo_r[plane, half, chip, c].astype(f32) + goq_r[slot, half, plane].astype(f32)
            ).astype(bf16)

    go_first = [
        go_side(chip_d, 0, 0, 2),
        go_side(chip_d, 1, 0, 4),
        go_side(chip_y, 0, 1, 2),
        go_side(chip_z, 1, 2, 4),
    ]
    pl.when(attends)(lambda: back_block(1))
    ggu_x.wait_recv()

    def gu_add(slot, carry):
        gu_r[x, slot // 8, slot % 8] = (
            gu_r[x, slot // 8, slot % 8].astype(f32) + gux_r[slot // 8, slot % 8].astype(f32)
        ).astype(bf16)
        return carry

    lax.fori_loop(0, 16, gu_add, 0)
    ggu_z = send(gu_r.at[x, 1 - zh], guz_r, device(0, False, True))
    pl.when(attends)(lambda: back_block(2))
    pl.when(attends)(lambda: back_block(3))

    @pl.when(attends)
    def _():
        def step(block, carry):
            at = pl.multiple_of(block * 256, 256)
            cosine, sine = tables(at, 256)
            turned = dkvt[:, pl.ds(at, 256)].T
            query = mx[pl.ds(at, 256), :]
            pair = jnp.concatenate(
                [query[:, 0:128], jnp.where(lane128 < 64, query[:, 128:256], turned)], axis=1
            )
            back = pair * cosine - swap_half(pair) * sine
            values = jnp.where(lane128 < 64, turned, 0.0)
            both = jnp.concatenate([back.astype(bf16), values.astype(bf16)], axis=1)
            d_s[block // 2, pl.ds((block % 2) * 4, 4)] = both.reshape(4, 64, 384)
            return carry

        lax.fori_loop(0, 4, step, 0)

    @pl.when(jnp.logical_not(attends))
    def _():
        d_s[...] = jnp.zeros(d_s.shape, bf16)
        wq_w[...] = jnp.zeros(wq_w.shape, bf16)

    def input_block(chip):
        return mm_t(d_s[:, pl.ds(chip * 2, 2)].reshape(256, 384), wq_w[...])

    scatter_sent(part_e, e2r1, e2r2, e2_base)
    e1_base = scatter_first(part_e, e1r1, e1r2, input_block)
    scatter_second(part_e, e1r1, e1r2, e1_base)

    ggd_x.wait_recv()
    for half in range(2):
        gd_s[half, x] = (gd_s[half, x].astype(f32) + gdx_r[half].astype(f32)).astype(bf16)
    ggd_z = send(gd_s.at[1 - zh, x], gdz_r, device(0, False, True))
    for n, half, chip, mask, slot in ((0, 0, chip_z, 4, 2), (1, 1, chip_y, 2, 1)):
        go_first[n].wait_recv()
        go_sum(half, chip, 0)
        go_first.append(go_side(chip, half, slot, mask))

    branch_feed = scatter_finish(part_f, bfr1, bfr2, bf_base)
    result = hid[...] + branch_feed
    square_feed = jnp.sum(
        jnp.sum(valid * branch_feed * branch_feed, axis=0, keepdims=True), axis=1, keepdims=True
    )
    square_out = jnp.sum(
        jnp.sum(valid * result * result, axis=0, keepdims=True), axis=1, keepdims=True
    )
    rows_s[0] = result.astype(bf16).reshape(2, 64, width)
    ret_out = send(rows_s.at[0, 1 - zh], rows_r.at[0], device(0, False, True))
    out_o[zh] = rows_s[0, zh]

    gq_send, gq_sem = fresh(), fresh()
    plane_to = zl
    piece_own = head_own - 3 * zl

    def gq_copy(slot):
        return pltpu.make_async_remote_copy(
            src_ref=wq_r.at[slot],
            dst_ref=gq_r.at[x * 2 + zh, piece_own],
            send_sem=ssem.at[gq_send],
            recv_sem=rsem.at[gq_sem],
            device_id=(plane_to, slot),
            device_id_type=pl.DeviceIdType.MESH,
        )

    @pl.when(attends)
    def _():
        grads = d_s[...].reshape(1024, 384)

        def wide_step(block, carry):
            at = pl.multiple_of(block * 128, 128)
            rows = n1g[:, :, :, :, pl.ds(at, 128)].reshape(1024, 128)
            acc[pl.ds(at, 128), 0:384] = mm_w(rows, grads)
            return carry

        lax.fori_loop(0, 9, wide_step, 0)

        def step(slot, carry):
            wq_r[slot] = acc[pl.ds(pl.multiple_of(slot * 72, 8), 72), 0:384].astype(bf16)
            here = (plane_to == x) & (slot == s)

            @pl.when(here)
            def _():
                pltpu.make_async_copy(
                    wq_r.at[slot], gq_r.at[x * 2 + zh, piece_own], rsem.at[gq_sem]
                ).start()

            pl.when(jnp.logical_not(here))(lambda: gq_copy(slot).start())
            return carry

        lax.fori_loop(0, 16, step, 0)

    ggu_z.wait_recv()

    def gu_add2(slot, carry):
        gu_r[x, zh, slot] = (
            gu_r[x, zh, slot].astype(f32) + guz_r[slot].astype(f32)
        ).astype(bf16)
        return carry

    lax.fori_loop(0, 8, gu_add2, 0)
    ggu_q = [
        send(gu_r.at[x, zh, index_of(mask)], guf_r.at[j], device(mask)) for mask in range(1, 8)
    ]
    guf_r[j] = gu_r[x, zh, j]
    e1 = scatter_finish(part_e, e1r1, e1r2, e1_base)
    tokens = xo[...].reshape(128, width).astype(f32)
    scale1 = lax.rsqrt(jnp.mean(tokens * tokens, axis=-1, keepdims=True) + EPS)
    scaled = e1 * gains[0:1, :]
    inner_mean = jnp.mean(scaled * tokens, axis=-1, keepdims=True)
    gain_attn_row = jnp.sum(e1 * tokens * scale1, axis=0, keepdims=True)
    grad_rows = (
        dhid[...] + scale1 * scaled - tokens * (scale1 * scale1 * scale1) * inner_mean
    )
    rows_s[1] = grad_rows.astype(bf16).reshape(2, 64, width)
    ret_in = send(rows_s.at[1, 1 - zh], rows_r.at[1], device(0, False, True))
    gin_o[zh] = rows_s[1, zh]

    total_row = jnp.where(
        lane1 == 0,
        square_attn,
        jnp.where(lane1 == 1, square_feed, jnp.where(lane1 == 2, square_out, count)),
    )
    row8 = lax.broadcasted_iota(jnp.int32, (8, 1), 0)
    both_gains = jnp.where(
        row8 == 0,
        jnp.broadcast_to(gain_attn_row, (8, width)),
        jnp.broadcast_to(gain_feed_row, (8, width)),
    )
    for slot in range(16):
        moved = pltpu.roll(both_gains, (width - 72 * slot) % width, 1) if slot else both_gains
        small_s[slot] = jnp.where(row8 == 2, total_row, moved[:, 0:LANES])
    small_copies = []
    for flip_x in (False, True):
        for flip_z in (False, True):
            for mask in range(8):
                if flip_x or flip_z or mask:
                    target = device(mask, flip_x, flip_z)
                    small_copies.append(
                        send(small_s.at[target[1]], small_r.at[x * 16 + s], target)
                    )
    small_r[x * 16 + s] = small_s[s]

    for copy in go_first[2:]:
        copy.wait_recv()
    for slot in (1, 2):
        for half in range(2):
            go_sum(half, own_chip, slot)
    go_x = send(wo_r.at[1 - x, :, own_chip, c], gox_r, device(0, True))

    go_x.wait_recv()
    for half in range(2):
        wo_r[x, half, own_chip, c] = (
            wo_r[x, half, own_chip, c].astype(f32) + gox_r[half].astype(f32)
        ).astype(bf16)
    go_z = send(wo_r.at[x, 1 - zh, own_chip, c], goz_r, device(0, False, True))
    ggd_z.wait_recv()
    gd_o[...] = gd_s[zh, x].astype(f32) + gdz_r[...].astype(f32)
    for copy in ggu_q:
        copy.wait_recv()
    ggu_o[...] = guf_r[...]
    go_z.wait_recv()
    go_o[...] = wo_r[x, zh, own_chip, c].astype(f32) + goz_r[...].astype(f32)
    ret_out.wait_recv()
    out_o[1 - zh] = rows_r[0]
    pltpu.make_async_copy(gq_r, gq_r, rsem.at[gq_sem]).wait()
    gq_o[...] = (
        (gq_r[0].astype(f32) + gq_r[1].astype(f32)) + (gq_r[2].astype(f32) + gq_r[3].astype(f32))
    )
    for copy in small_copies:
        copy.wait_recv()
    total = small_r[0]
    for slot in range(1, 32):
        total = total + small_r[slot]
    small_o[...] = total
    ret_in.wait_recv()
    gin_o[1 - zh] = rows_r[1]

    waited = {id(copy) for copy in wo_c + wo_x + gu_x + gu_z}
    for gather in (wo_q, gf_all, n2_all, x_a, x_b):
        waited |= {id(copy) for copy in gather.copies}
    for copy in pending:
        if id(copy) not in waited:
            copy.wait_send()
    for here, copy in qkv_first:
        pl.when(jnp.logical_not(here))(copy.wait_send)
    for theirs, copy in at_copies:
        pl.when(attends)(copy.wait_send)
    for theirs, copy in da_copies:
        pl.when(theirs)(copy.wait_send)
    scatter_sent(part_f, bfr1, bfr2, bf_base)
    scatter_sent(part_e, e1r1, e1r2, e1_base)

    @pl.when(attends)
    def _():
        def step(slot, carry):
            here = (plane_to == x) & (slot == s)
            pl.when(jnp.logical_not(here))(lambda: gq_copy(slot).wait_send())
            return carry

        lax.fori_loop(0, 16, step, 0)


def roll64(values):
    return pltpu.roll(values, 64, 1)


def prepare_kernel(
    ga, gf, seg, wq, wk, wv, wo, gate, up, wd, meta_o, wq_o, wo_o, gu_o, wd_o
):
    f32, bf16 = jnp.float32, jnp.bfloat16
    first = lax.axis_index("dp") == 0
    rows = wq.shape[0]
    low = lax.broadcasted_iota(jnp.int32, (1, LANES), 1) < 64
    meta_o[...] = jnp.zeros(meta_o.shape, f32)
    meta_o[0:1, 0:rows] = ga[...].astype(f32)
    meta_o[1:2, 0:rows] = gf[...].astype(f32)
    meta_o[2:4, 0:64] = seg[...].astype(f32)

    def part(ref, at, size=LANES):
        values = ref[:, at : at + size].astype(f32)
        if size < LANES:
            values = jnp.concatenate(
                [values, jnp.zeros((values.shape[0], LANES - size), f32)], axis=1
            )
        return values

    q = [part(wq, LANES * n) for n in range(4)] + [part(wq, 512, 64)]
    k = [part(wk, 0), part(wk, LANES, 64)]
    v = [part(wv, 0), part(wv, LANES, 64)]
    slabs = (
        (q[0], jnp.where(low, q[1], roll64(k[0])), jnp.where(low, v[0], 0.0)),
        (
            jnp.where(low, roll64(q[1]), roll64(q[2])),
            jnp.where(low, roll64(q[2]), k[0]),
            jnp.where(low, roll64(v[0]), 0.0),
        ),
        (q[3], jnp.where(low, q[4], roll64(k[1])), v[1]),
    )
    for head in range(3):
        for place in range(3):
            wq_o[head, :, LANES * place : LANES * (place + 1)] = slabs[head][place].astype(bf16)

    def window(ref, out):
        pieces = [part(ref, LANES * n) for n in range(4)] + [part(ref, 512, 64)]
        before = jnp.zeros_like(pieces[0])
        for n in range(5):
            moved = jnp.where(low, roll64(before), roll64(pieces[n]))
            out[:, LANES * n : LANES * (n + 1)] = jnp.where(first, pieces[n], moved).astype(bf16)
            before = pieces[n]

    window(wo, wo_o)
    window(wd, wd_o)
    for pair in range(4):
        g = [part(gate, 384 * pair + LANES * n) for n in range(3)]
        u = [part(up, 384 * pair + LANES * n) for n in range(3)]
        slabs = (
            (g[0], jnp.where(low, g[1], roll64(u[1])), u[0]),
            (
                jnp.where(low, roll64(g[1]), roll64(g[2])),
                jnp.where(low, roll64(g[2]), u[2]),
                jnp.where(low, roll64(u[1]), roll64(u[2])),
            ),
        )
        for odd in range(2):
            for place in range(3):
                gu_o[2 * pair + odd, :, LANES * place : LANES * (place + 1)] = slabs[odd][
                    place
                ].astype(bf16)


def finish_kernel(
    out, gin, gq, go, ggu, gd, small,
    out_o, gin_o, gq_o, gk_o, gv_o, go_o, gg_o, gu_o, gd_o, ga_o, gf_o, rm_o,
):
    f32 = jnp.float32
    first = lax.axis_index("dp") == 0
    rows = gq.shape[1]
    low = lax.broadcasted_iota(jnp.int32, (1, LANES), 1) < 64
    out_o[...] = out[...]
    gin_o[...] = gin[...]
    p = [[gq[head, :, LANES * n : LANES * (n + 1)].astype(f32) for n in range(3)] for head in range(3)]
    gq_o[:, 0:128] = p[0][0]
    gq_o[:, 128:256] = jnp.where(low, p[0][1], roll64(p[1][0]))
    gq_o[:, 256:384] = jnp.where(low, roll64(p[1][0]), roll64(p[1][1]))
    gq_o[:, 384:512] = p[2][0]
    gq_o[:, 512:576] = p[2][1][:, 0:64]
    gk_o[:, 0:128] = jnp.where(low, roll64(p[0][1]), p[1][1])
    gk_o[:, 128:192] = roll64(p[2][1])[:, 0:64]
    gv_o[:, 0:128] = jnp.where(low, p[0][2], roll64(p[1][2]))
    gv_o[:, 128:192] = p[2][2][:, 0:64]

    def unwindow(ref, res):
        pieces = [ref[:, LANES * n : LANES * (n + 1)].astype(f32) for n in range(5)]
        for n in range(5):
            after = pieces[min(n + 1, 4)]
            moved = jnp.where(low, roll64(pieces[n]), roll64(after))
            value = jnp.where(first, pieces[n], moved)
            if n < 4:
                res[:, LANES * n : LANES * (n + 1)] = value
            else:
                res[:, 512:576] = value[:, 0:64]

    unwindow(go, go_o)
    unwindow(gd, gd_o)
    for pair in range(4):
        a, b = [
            [ggu[2 * pair + odd, :, LANES * n : LANES * (n + 1)].astype(f32) for n in range(3)]
            for odd in range(2)
        ]
        at = 384 * pair
        gg_o[:, at : at + 128] = a[0]
        gg_o[:, at + 128 : at + 256] = jnp.where(low, a[1], roll64(b[0]))
        gg_o[:, at + 256 : at + 384] = jnp.where(low, roll64(b[0]), roll64(b[1]))
        gu_o[:, at : at + 128] = a[2]
        gu_o[:, at + 128 : at + 256] = jnp.where(low, roll64(a[1]), roll64(b[2]))
        gu_o[:, at + 256 : at + 384] = jnp.where(low, roll64(b[2]), b[1])
    ga_o[...] = small[0:1, 0:rows]
    gf_o[...] = small[1:2, 0:rows]
    width = out.shape[2]
    rm_o[...] = jnp.sqrt(small[2:3, 0:3] / (small[2:3, 3:4] * width))


def fast_device(
    inputs,
    segments,
    weight_query,
    key_weight_matrix,
    value_weight_matrix,
    weight_out,
    weight_gate,
    weight_up,
    weight_down,
    gain_attention,
    gain_feed,
    cotangent,
):
    f32, bf16 = jnp.float32, jnp.bfloat16
    micro, _, rows, width = inputs.shape
    dp = lax.axis_index("dp")
    length = rows * 16
    piece = width // 16

    whole = pl.BlockSpec(memory_space=pltpu.VMEM)
    meta, wq, wo, gu, wd = pl.pallas_call(
        prepare_kernel,
        out_shape=(
            jax.ShapeDtypeStruct((8, LANES), f32),
            jax.ShapeDtypeStruct((3, piece, 384), bf16),
            jax.ShapeDtypeStruct((piece, 640), bf16),
            jax.ShapeDtypeStruct((8, piece, 384), bf16),
            jax.ShapeDtypeStruct((192, 640), bf16),
        ),
        in_specs=[whole] * 10,
        out_specs=[whole] * 5,
        name="prepare",
    )(
        gain_attention.reshape(1, piece),
        gain_feed.reshape(1, piece),
        segments[:, 0],
        weight_query,
        key_weight_matrix,
        value_weight_matrix,
        weight_out,
        weight_gate,
        weight_up,
        weight_down,
    )
    half = HEAD_DIMENSION // 2
    frequency = THETA ** (-np.arange(half, dtype=np.float32) * np.float32(2.0) / HEAD_DIMENSION)
    angles = np.arange(length, dtype=np.float32)[:, None] * frequency.astype(np.float32)[None, :]
    cosine, sine = np.cos(angles), np.sin(angles)
    cosine = np.concatenate([cosine] * 4, axis=1).astype(np.float32)
    sine = np.concatenate([-sine, sine, -sine, sine], axis=1).astype(np.float32)

    v = pltpu.VMEM
    tok = (2, 4, 2, 64, width)
    scratch = [
        v((16, 8, LANES), f32),
        v((2, 64, width), bf16),
        v((2, 64, width), bf16),
        v(tok, bf16),
        v(tok, bf16),
        v(tok, bf16),
        v((16, 72, 384), bf16),
        v((width, 384), bf16),
        v((2, 2, 4, 2, 72, 640), bf16),
        v((width, width), bf16),
        v((2, 2, 8, 72, 384), bf16),
        v((2, width, 384), bf16),
        v((2, 2, 192, 640), bf16),
        v((2, 256, width), bf16),
        v((width, 640), f32),
        v((1024, 256), bf16),
        v((192, 1024), bf16),
        v((192, 1024), bf16),
        v((3, 1024, 256), bf16),
        v((3, 1024, 256), bf16),
        v((3, 256, 256), bf16),
        v((3, 256, 512), bf16),
        v((3, 256, 768), bf16),
        v((3, 256, 1024), bf16),
        v((1024, 256), f32),
        v((8, 1024), f32),
        v((1024, 8), f32),
        v((8, width), f32),
        v((2, 8, 64, 256), bf16),
        v((6, 2, 64, 256), bf16),
        v((128, width), f32),
        v((128, width), f32),
        v((2, 2, 8, 64, 256), bf16),
        v((2, 2, 8, 64, 384), bf16),
        v((2, 4, 2, 64, width), bf16),
        v((4, 2, 64, width), bf16),
        v((3, 2, 64, width), bf16),
        v((4, 2, 64, width), bf16),
        v((3, 2, 64, width), bf16),
        v((6, 2, 64, 256), bf16),
        v((2, 8, 64, 256), bf16),
        v((2, 8, 64, 384), bf16),
        v((128, 1024), f32),
        v((2, 8, 72, 384), bf16),
        v((8, 72, 384), bf16),
        v((8, 72, 384), bf16),
        v((2, 2, 192, 640), bf16),
        v((2, 192, 640), bf16),
        v((192, 640), bf16),
        v((2, 2, 4, 72, 640), bf16),
        v((2, 72, 640), bf16),
        v((3, 2, 2, 72, 640), bf16),
        v((72, 640), bf16),
        v((4, 3, 72, 384), bf16),
        v((16, 8, LANES), f32),
        v((32, 8, LANES), f32),
        v((2, 2, 64, width), bf16),
        v((2, 64, width), bf16),
        pltpu.SemaphoreType.DMA((256,)),
        pltpu.SemaphoreType.DMA((256,)),
    ]
    out, gin, gq, go, ggu, gd, small = pl.pallas_call(
        fast_kernel,
        out_shape=(
            jax.ShapeDtypeStruct((2, rows, width), bf16),
            jax.ShapeDtypeStruct((2, rows, width), bf16),
            jax.ShapeDtypeStruct((3, piece, 384), f32),
            jax.ShapeDtypeStruct((piece, 640), f32),
            jax.ShapeDtypeStruct((8, piece, 384), bf16),
            jax.ShapeDtypeStruct((192, 640), f32),
            jax.ShapeDtypeStruct((8, LANES), f32),
        ),
        in_specs=[whole] * 9,
        out_specs=[whole] * 7,
        scratch_shapes=scratch,
        compiler_params=pltpu.CompilerParams(
            has_side_effects=True, vmem_limit_bytes=62 * 1024 * 1024
        ),
        name="layer",
    )(
        meta,
        inputs[:, 0],
        cotangent[:, 0],
        wq,
        wo,
        gu,
        wd,
        jnp.asarray(cosine),
        jnp.asarray(sine),
    )

    grads = pl.pallas_call(
        finish_kernel,
        out_shape=(
            jax.ShapeDtypeStruct((2, rows, width), bf16),
            jax.ShapeDtypeStruct((2, rows, width), bf16),
            jax.ShapeDtypeStruct(weight_query.shape, f32),
            jax.ShapeDtypeStruct(key_weight_matrix.shape, f32),
            jax.ShapeDtypeStruct(value_weight_matrix.shape, f32),
            jax.ShapeDtypeStruct(weight_out.shape, f32),
            jax.ShapeDtypeStruct(weight_gate.shape, f32),
            jax.ShapeDtypeStruct(weight_up.shape, f32),
            jax.ShapeDtypeStruct(weight_down.shape, f32),
            jax.ShapeDtypeStruct((1, piece), f32),
            jax.ShapeDtypeStruct((1, piece), f32),
            jax.ShapeDtypeStruct((1, 3), f32),
        ),
        in_specs=[whole] * 7,
        out_specs=[whole] * 12,
        name="finish",
    )(out, gin, gq, go, ggu, gd, small)
    return (
        grads[0][:, None],
        grads[1][:, None],
        *grads[2:9],
        grads[9].reshape(piece),
        grads[10].reshape(piece),
        grads[11].reshape(3),
    )


def solution(mesh):
    placed = (
        P(None, "dp", "seq", None),
        P(None, "dp", "seq"),
        P("seq", "dp"),
        P("seq", "dp"),
        P("seq", "dp"),
        P("seq", "dp"),
        P("seq", "dp"),
        P("seq", "dp"),
        P("seq", "dp"),
        P("seq"),
        P("seq"),
        P(None, "dp", "seq", None),
    )
    body = fast_device if dict(mesh.shape) == {"dp": 2, "seq": 16} else per_device
    return jax.shard_map(
        body,
        mesh=mesh,
        in_specs=placed,
        out_specs=(
            P(None, "dp", "seq", None),
            P(None, "dp", "seq", None),
            P("seq", "dp"),
            P("seq", "dp"),
            P("seq", "dp"),
            P("seq", "dp"),
            P("seq", "dp"),
            P("seq", "dp"),
            P("seq", "dp"),
            P("seq"),
            P("seq"),
            P(),
        ),
        check_vma=False,
    )
```

```python
import functools
import math

import jax
import jax.numpy as jnp
import numpy as np
from jax import lax
from jax.experimental import pallas as pl
from jax.experimental.pallas import tpu as pltpu
from jax.sharding import PartitionSpec as P

QUERY_HEADS = 18
KEY_VALUE_HEADS = 6
HEAD_DIMENSION = 64


EPS = 1e-05
THETA = 10000.0
NEGATIVE = -1e30


def rope_tables(positions, head_size):
    half_size = head_size // 2
    frequency = THETA ** (-jnp.arange(half_size, dtype=jnp.float32) * 2.0 / head_size)
    angles = positions.astype(jnp.float32)[:, None] * frequency[None, :]
    angles = jnp.concatenate([angles, angles], axis=1)
    return (jnp.cos(angles), jnp.sin(angles))


def turn_half(values_in):
    half_size = values_in.shape[-1] // 2
    return jnp.concatenate([-values_in[..., half_size:], values_in[..., :half_size]], axis=-1)


def apply_rotation(values_in, cosine_table, sine_values):
    return values_in * cosine_table[:, None, :] + turn_half(values_in) * sine_values[:, None, :]


def reverse_rotation(grads_in, cosine_table, sine_values):
    return grads_in * cosine_table[:, None, :] - turn_half(grads_in * sine_values[:, None, :])


def norm_forward(values_in, gain):
    row_scale = lax.rsqrt(jnp.mean(values_in * values_in, axis=-1, keepdims=True) + EPS)
    return (values_in * row_scale * gain, row_scale)


def norm_backward(values_in, row_scale, gain, grad_normed):
    scaled = grad_normed * gain
    inner_mean = jnp.mean(scaled * values_in, axis=-1, keepdims=True)
    value_gradient_rows = row_scale * scaled - values_in * row_scale**3 * inner_mean
    grad_gain = jnp.sum(grad_normed * values_in * row_scale, axis=(0, 1))
    return (value_gradient_rows, grad_gain)


def apply_projection(acts_low, weight_full):
    return jnp.einsum("std,df->stf", acts_low, weight_full, preferred_element_type=jnp.float32)


def project_back(grads_low, weight_full):
    return jnp.einsum("sta,ba->stb", grads_low, weight_full, preferred_element_type=jnp.float32)


def weight_grad(acts_low, grads_low):
    return jnp.einsum("std,stf->df", acts_low, grads_low, preferred_element_type=jnp.float32)


def gather_all(shards, gain_shards):
    wide = (
        lax.all_gather(shards[0], "dp", axis=1, tiled=True),
        lax.all_gather(shards[1], "dp", axis=1, tiled=True),
        lax.all_gather(shards[2], "dp", axis=1, tiled=True),
        lax.all_gather(shards[3], "dp", axis=1, tiled=True),
        lax.all_gather(shards[4], "dp", axis=1, tiled=True),
        lax.all_gather(shards[5], "dp", axis=1, tiled=True),
        lax.all_gather(shards[6], "dp", axis=1, tiled=True),
    )
    return (
        lax.all_gather(wide[0], "seq", axis=0, tiled=True),
        lax.all_gather(wide[1], "seq", axis=0, tiled=True),
        lax.all_gather(wide[2], "seq", axis=0, tiled=True),
        lax.all_gather(wide[3], "seq", axis=0, tiled=True),
        lax.all_gather(wide[4], "seq", axis=0, tiled=True),
        lax.all_gather(wide[5], "seq", axis=0, tiled=True),
        lax.all_gather(wide[6], "seq", axis=0, tiled=True),
        lax.all_gather(gain_shards[0], "seq", axis=0, tiled=True),
        lax.all_gather(gain_shards[1], "seq", axis=0, tiled=True),
    )


def gather_keys(key_low, value_low, seg_low):
    return (
        lax.all_gather(key_low, "seq", axis=1, tiled=True),
        lax.all_gather(value_low, "seq", axis=1, tiled=True),
        lax.all_gather(seg_low, "seq", axis=1, tiled=True),
    )


def reduce_grads(grads):
    rows = [
        lax.psum_scatter(g.astype(jnp.bfloat16), "seq", scatter_dimension=0, tiled=True)
        for g in grads
    ]
    return tuple(
        lax.psum_scatter(r, "dp", scatter_dimension=1, tiled=True).astype(jnp.float32)
        for r in rows
    )


def block_view(gathered, block_index, key_tile_block):
    block_offset = block_index * key_tile_block
    key_portion = lax.dynamic_slice_in_dim(gathered[0], block_offset, key_tile_block, 1)
    value_portion = lax.dynamic_slice_in_dim(gathered[1], block_offset, key_tile_block, 1)
    seg_part = lax.dynamic_slice_in_dim(gathered[2], block_offset, key_tile_block, 1).astype(
        jnp.float32
    )
    sequence_count = key_portion.shape[0]
    key_portion = key_portion.reshape(
        sequence_count, key_tile_block, KEY_VALUE_HEADS, HEAD_DIMENSION
    )
    value_portion = value_portion.reshape(
        sequence_count, key_tile_block, KEY_VALUE_HEADS, HEAD_DIMENSION
    )
    col_pos = block_offset + jnp.arange(key_tile_block, dtype=jnp.int32)
    return (key_portion, value_portion, seg_part, col_pos)


def masked_scores(query_block_list, key_portion, seg_rows, seg_part, row_pos, col_pos, score_scale):
    raw_scores = jnp.einsum(
        "skgtd,sjkd->skgtj", query_block_list, key_portion, preferred_element_type=jnp.float32
    )
    allowed = (seg_rows[:, :, None] == seg_part[:, None, :]) & (
        col_pos[None, None, :] <= row_pos[None, :, None]
    )
    allowed = allowed[:, None, None, :, :]
    return (jnp.where(allowed, raw_scores * score_scale, NEGATIVE), allowed)


def log_sum(
    query_block_list, gathered, seg_rows, row_pos, block_count, key_tile_block, score_scale
):
    lead_shape = query_block_list.shape[:4]

    def log_step_fn(block_index, carried):
        row_top, row_total = carried
        key_portion, value_portion, seg_part, col_pos = block_view(
            gathered, block_index, key_tile_block
        )
        scores, allowed = masked_scores(
            query_block_list, key_portion, seg_rows, seg_part, row_pos, col_pos, score_scale
        )
        new_top = jnp.maximum(row_top, jnp.max(scores, axis=-1))
        exponent = jnp.where(allowed, jnp.exp(scores - new_top[..., None]), 0.0)
        row_total = row_total * jnp.exp(row_top - new_top) + jnp.sum(exponent, axis=-1)
        return (new_top, row_total)

    start_state = (jnp.full(lead_shape, NEGATIVE, jnp.float32), jnp.zeros(lead_shape, jnp.float32))
    row_top, row_total = lax.fori_loop(0, block_count, log_step_fn, start_state)
    return row_top + jnp.log(row_total)


def attend(
    query_block_list,
    gathered,
    seg_rows,
    row_pos,
    block_count,
    key_tile_block,
    score_scale,
    log_total,
):

    def attend_step_fn(block_index, mixed_heads):
        key_portion, value_portion, seg_part, col_pos = block_view(
            gathered, block_index, key_tile_block
        )
        scores, allowed = masked_scores(
            query_block_list, key_portion, seg_rows, seg_part, row_pos, col_pos, score_scale
        )
        probabilities = jnp.where(allowed, jnp.exp(scores - log_total[..., None]), 0.0).astype(
            jnp.bfloat16
        )
        return mixed_heads + jnp.einsum(
            "skgtj,sjkd->skgtd", probabilities, value_portion, preferred_element_type=jnp.float32
        )

    return lax.fori_loop(
        0, block_count, attend_step_fn, jnp.zeros(query_block_list.shape, jnp.float32)
    )


def query_back(
    query_block_list,
    gathered,
    seg_rows,
    row_pos,
    block_count,
    key_tile_block,
    score_scale,
    log_total,
    gradient_reduced,
    row_delta,
):

    def query_step_fn(block_index, grad_query):
        key_portion, value_portion, seg_part, col_pos = block_view(
            gathered, block_index, key_tile_block
        )
        scores, allowed = masked_scores(
            query_block_list, key_portion, seg_rows, seg_part, row_pos, col_pos, score_scale
        )
        probabilities = jnp.where(allowed, jnp.exp(scores - log_total[..., None]), 0.0)
        grad_probs = jnp.einsum(
            "skgtd,sjkd->skgtj", gradient_reduced, value_portion, preferred_element_type=jnp.float32
        )
        grad_scores = (probabilities * (grad_probs - row_delta[..., None]) * score_scale).astype(
            jnp.bfloat16
        )
        return grad_query + jnp.einsum(
            "skgtj,sjkd->skgtd", grad_scores, key_portion, preferred_element_type=jnp.float32
        )

    return lax.fori_loop(
        0, block_count, query_step_fn, jnp.zeros(query_block_list.shape, jnp.float32)
    )


def key_back(
    key_local,
    value_local,
    seg_rows,
    row_pos,
    query_whole,
    grads_whole,
    stats_whole,
    seg_whole,
    first_block,
    block_count,
    query_tile,
    score_scale,
):
    sequence_count = key_local.shape[0]
    group_width = QUERY_HEADS // KEY_VALUE_HEADS

    def key_step_fn(block_index, carried):
        key_total, value_total = carried
        block_offset = block_index * query_tile
        query_rows = lax.dynamic_slice_in_dim(query_whole, block_offset, query_tile, 1).reshape(
            sequence_count, query_tile, KEY_VALUE_HEADS, group_width, HEAD_DIMENSION
        )
        grad_rows = lax.dynamic_slice_in_dim(grads_whole, block_offset, query_tile, 1).reshape(
            sequence_count, query_tile, KEY_VALUE_HEADS, group_width, HEAD_DIMENSION
        )
        log_rows = lax.dynamic_slice_in_dim(stats_whole[0], block_offset, query_tile, 3)
        delta_rows = lax.dynamic_slice_in_dim(stats_whole[1], block_offset, query_tile, 3)
        seg_query = lax.dynamic_slice_in_dim(seg_whole, block_offset, query_tile, 1).astype(
            jnp.float32
        )
        query_pos = block_offset + jnp.arange(query_tile, dtype=jnp.int32)
        raw_scores = jnp.einsum(
            "stkgd,sjkd->skgtj", query_rows, key_local, preferred_element_type=jnp.float32
        )
        allowed = (seg_query[:, :, None] == seg_rows[:, None, :]) & (
            row_pos[None, None, :] <= query_pos[None, :, None]
        )
        allowed = allowed[:, None, None, :, :]
        scores = jnp.where(allowed, raw_scores * score_scale, NEGATIVE)
        probabilities = jnp.where(allowed, jnp.exp(scores - log_rows[..., None]), 0.0)
        grad_probs = jnp.einsum(
            "stkgd,sjkd->skgtj", grad_rows, value_local, preferred_element_type=jnp.float32
        )
        grad_scores = (probabilities * (grad_probs - delta_rows[..., None]) * score_scale).astype(
            jnp.bfloat16
        )
        key_total = key_total + jnp.einsum(
            "skgtj,stkgd->sjkd", grad_scores, query_rows, preferred_element_type=jnp.float32
        )
        value_total = value_total + jnp.einsum(
            "skgtj,stkgd->sjkd",
            probabilities.astype(jnp.bfloat16),
            grad_rows,
            preferred_element_type=jnp.float32,
        )
        return (key_total, value_total)

    start_state = (jnp.zeros(key_local.shape, jnp.float32), jnp.zeros(key_local.shape, jnp.float32))
    return lax.fori_loop(first_block, block_count, key_step_fn, start_state)


def per_device(
    inputs,
    segments,
    weight_query,
    key_weight_matrix,
    value_weight_matrix,
    weight_out,
    weight_gate,
    weight_up,
    weight_down,
    gain_attention,
    gain_feed,
    cotangent,
):
    shards = (
        weight_query,
        key_weight_matrix,
        value_weight_matrix,
        weight_out,
        weight_gate,
        weight_up,
        weight_down,
    )
    gain_shards = (gain_attention, gain_feed)
    micro_count, sequence_count, token_count, model_width = inputs.shape
    group_width = QUERY_HEADS // KEY_VALUE_HEADS
    score_scale = 1.0 / math.sqrt(HEAD_DIMENSION)
    row_pos = lax.axis_index("seq") * token_count + jnp.arange(token_count, dtype=jnp.int32)
    cosine_table, sine_values = rope_tables(row_pos, HEAD_DIMENSION)
    key_span_length = token_count * lax.axis_size("seq")
    key_tile_block = min(512, key_span_length)
    total_blocks = key_span_length // key_tile_block
    block_count = row_pos[token_count - 1] // key_tile_block + 1
    first_block = row_pos[0] // key_tile_block
    outputs = []
    grad_list = []
    totals = jnp.zeros((4,), jnp.float32)
    gain_grads = jnp.zeros((2, model_width), jnp.float32)
    summed = None
    weights_complete = gather_all(shards, gain_shards)
    for batch_index in range(micro_count):
        tokens = inputs[batch_index].astype(jnp.float32)
        seg_local = segments[batch_index]
        seg_rows = seg_local.astype(jnp.float32)
        seg_low = seg_local.astype(jnp.bfloat16)
        gain_first = weights_complete[7].astype(jnp.float32)
        gain_second = weights_complete[8].astype(jnp.float32)
        norm_first, scale_first = norm_forward(tokens, gain_first)
        normalized = norm_first.astype(jnp.bfloat16)
        query_raw = apply_projection(normalized, weights_complete[0]).reshape(
            sequence_count, token_count, QUERY_HEADS, HEAD_DIMENSION
        )
        query_reduced = apply_rotation(query_raw, cosine_table, sine_values).astype(jnp.bfloat16)
        key_unrotated = apply_projection(normalized, weights_complete[1]).reshape(
            sequence_count, token_count, KEY_VALUE_HEADS, HEAD_DIMENSION
        )
        key_low = (
            apply_rotation(key_unrotated, cosine_table, sine_values)
            .astype(jnp.bfloat16)
            .reshape(sequence_count, token_count, KEY_VALUE_HEADS * HEAD_DIMENSION)
        )
        value_low = apply_projection(normalized, weights_complete[2]).astype(jnp.bfloat16)
        gathered = gather_keys(key_low, value_low, seg_low)
        query_block_list = query_reduced.reshape(
            sequence_count, token_count, KEY_VALUE_HEADS, group_width, HEAD_DIMENSION
        ).transpose(0, 2, 3, 1, 4)
        log_total = log_sum(
            query_block_list, gathered, seg_rows, row_pos, block_count, key_tile_block, score_scale
        )
        mixed_heads = attend(
            query_block_list,
            gathered,
            seg_rows,
            row_pos,
            block_count,
            key_tile_block,
            score_scale,
            log_total,
        )
        attn_low = (
            mixed_heads.transpose(0, 3, 1, 2, 4)
            .reshape(sequence_count, token_count, QUERY_HEADS * HEAD_DIMENSION)
            .astype(jnp.bfloat16)
        )
        branch_attn = apply_projection(attn_low, weights_complete[3])
        hidden = tokens + branch_attn
        norm_second, scale_second = norm_forward(hidden, gain_second)
        normed_second = norm_second.astype(jnp.bfloat16)
        gate_values = apply_projection(normed_second, weights_complete[4])
        up_values = apply_projection(normed_second, weights_complete[5])
        gate_sigmoid = jax.nn.sigmoid(gate_values)
        inner_low = (gate_values * gate_sigmoid * up_values).astype(jnp.bfloat16)
        branch_feed = apply_projection(inner_low, weights_complete[6])
        result = hidden + branch_feed
        outputs.append(result.astype(jnp.bfloat16))
        valid_rows = (seg_local != 0).astype(jnp.float32)[:, :, None]
        totals = totals + jnp.stack(
            [
                jnp.sum(valid_rows * branch_attn * branch_attn),
                jnp.sum(valid_rows * branch_feed * branch_feed),
                jnp.sum(valid_rows * result * result),
                jnp.sum(valid_rows),
            ]
        )
        back_weights = weights_complete
        back_keys = gathered
        grad_result = cotangent[batch_index].astype(jnp.float32)
        grad_feed = grad_result.astype(jnp.bfloat16)
        grad_down = weight_grad(inner_low, grad_feed)
        grad_inner = project_back(grad_feed, back_weights[6])
        grad_up = (grad_inner * gate_values * gate_sigmoid).astype(jnp.bfloat16)
        grad_gate = (
            grad_inner * up_values * gate_sigmoid * (1.0 + gate_values * (1.0 - gate_sigmoid))
        ).astype(jnp.bfloat16)
        grad_gate_w = weight_grad(normed_second, grad_gate)
        grad_up_w = weight_grad(normed_second, grad_up)
        grad_normed_second = project_back(grad_gate, back_weights[4]) + project_back(
            grad_up, back_weights[5]
        )
        grad_hidden_norm, grad_gain_second = norm_backward(
            hidden, scale_second, gain_second, grad_normed_second
        )
        grad_hidden = grad_result + grad_hidden_norm
        grad_branch = grad_hidden.astype(jnp.bfloat16)
        grad_out_w = weight_grad(attn_low, grad_branch)
        mixed_gradient = project_back(grad_branch, back_weights[3]).astype(jnp.bfloat16)
        gradient_reduced = mixed_gradient.reshape(
            sequence_count, token_count, KEY_VALUE_HEADS, group_width, HEAD_DIMENSION
        ).transpose(0, 2, 3, 1, 4)
        row_delta = jnp.sum(gradient_reduced.astype(jnp.float32) * mixed_heads, axis=-1)
        grad_query = query_back(
            query_block_list,
            back_keys,
            seg_rows,
            row_pos,
            block_count,
            key_tile_block,
            score_scale,
            log_total,
            gradient_reduced,
            row_delta,
        )
        query_flat = query_reduced.reshape(
            sequence_count, token_count, QUERY_HEADS * HEAD_DIMENSION
        )
        query_whole, grads_whole = (
            lax.all_gather(query_flat, "seq", axis=1, tiled=True),
            lax.all_gather(mixed_gradient, "seq", axis=1, tiled=True),
        )
        stats_whole = (
            lax.all_gather(log_total, "seq", axis=3, tiled=True),
            lax.all_gather(row_delta, "seq", axis=3, tiled=True),
        )
        key_local = key_low.reshape(sequence_count, token_count, KEY_VALUE_HEADS, HEAD_DIMENSION)
        value_local = value_low.reshape(
            sequence_count, token_count, KEY_VALUE_HEADS, HEAD_DIMENSION
        )
        key_total, value_total = key_back(
            key_local,
            value_local,
            seg_rows,
            row_pos,
            query_whole,
            grads_whole,
            stats_whole,
            back_keys[2],
            first_block,
            total_blocks,
            key_tile_block,
            score_scale,
        )
        key_grad_low = (
            reverse_rotation(key_total, cosine_table, sine_values)
            .reshape(sequence_count, token_count, KEY_VALUE_HEADS * HEAD_DIMENSION)
            .astype(jnp.bfloat16)
        )
        value_grad_low = value_total.reshape(
            sequence_count, token_count, KEY_VALUE_HEADS * HEAD_DIMENSION
        ).astype(jnp.bfloat16)
        query_grad = grad_query.transpose(0, 3, 1, 2, 4).reshape(
            sequence_count, token_count, QUERY_HEADS, HEAD_DIMENSION
        )
        query_grad_low = (
            reverse_rotation(query_grad, cosine_table, sine_values)
            .reshape(sequence_count, token_count, QUERY_HEADS * HEAD_DIMENSION)
            .astype(jnp.bfloat16)
        )
        grad_normed = (
            project_back(query_grad_low, back_weights[0])
            + project_back(key_grad_low, back_weights[1])
            + project_back(value_grad_low, back_weights[2])
        )
        grad_token_norm, grad_gain_first = norm_backward(
            tokens, scale_first, gain_first, grad_normed
        )
        grad_list.append((grad_hidden + grad_token_norm).astype(jnp.bfloat16))
        gain_grads = gain_grads + jnp.stack([grad_gain_first, grad_gain_second])
        batch_grads = (
            weight_grad(normalized, query_grad_low),
            weight_grad(normalized, key_grad_low),
            weight_grad(normalized, value_grad_low),
            grad_out_w,
            grad_gate_w,
            grad_up_w,
            grad_down,
        )
        summed = batch_grads if summed is None else jax.tree.map(jnp.add, summed, batch_grads)
    reduced = reduce_grads(summed)
    gain_total, totals = lax.psum((gain_grads, totals), ("dp", "seq"))
    piece_width = model_width // lax.axis_size("seq")
    gain_part = lax.dynamic_slice_in_dim(
        gain_total, lax.axis_index("seq") * piece_width, piece_width, 1
    )
    root_means = jnp.sqrt(totals[:3] / (totals[3] * model_width))
    return (
        jnp.stack(outputs),
        jnp.stack(grad_list),
        reduced[0],
        reduced[1],
        reduced[2],
        reduced[3],
        reduced[4],
        reduced[5],
        reduced[6],
        gain_part[0],
        gain_part[1],
        root_means,
    )


LANES = 128


def roll64(values):
    return pltpu.roll(values, 64, 1)


def prepare(
    ga, gf, seg, wq, wk, wv, wo, gate, up, wd, meta_o, wq_o, wo_o, gu_o, wd_o
):
    f32, bf16 = jnp.float32, jnp.bfloat16
    first = lax.axis_index("dp") == 0
    rows = wq.shape[0]
    low = lax.broadcasted_iota(jnp.int32, (1, LANES), 1) < 64
    meta_o[...] = jnp.zeros(meta_o.shape, f32)
    meta_o[0:1, 0:rows] = ga[...].astype(f32)
    meta_o[1:2, 0:rows] = gf[...].astype(f32)
    meta_o[2:4, 0:64] = seg[...].astype(f32)

    def part(ref, at, size=LANES):
        values = ref[:, at : at + size].astype(f32)
        if size < LANES:
            values = jnp.concatenate(
                [values, jnp.zeros((values.shape[0], LANES - size), f32)], axis=1
            )
        return values

    q = [part(wq, LANES * n) for n in range(4)] + [part(wq, 512, 64)]
    k = [part(wk, 0), part(wk, LANES, 64)]
    v = [part(wv, 0), part(wv, LANES, 64)]
    slabs = (
        (q[0], jnp.where(low, q[1], roll64(k[0])), jnp.where(low, v[0], 0.0)),
        (
            jnp.where(low, roll64(q[1]), roll64(q[2])),
            jnp.where(low, roll64(q[2]), k[0]),
            jnp.where(low, roll64(v[0]), 0.0),
        ),
        (q[3], jnp.where(low, q[4], roll64(k[1])), v[1]),
    )
    for head in range(3):
        for place in range(3):
            wq_o[head, :, LANES * place : LANES * (place + 1)] = slabs[head][place].astype(bf16)

    def window(ref, out):
        pieces = [part(ref, LANES * n) for n in range(4)] + [part(ref, 512, 64)]
        before = jnp.zeros_like(pieces[0])
        for n in range(5):
            moved = jnp.where(low, roll64(before), roll64(pieces[n]))
            out[:, LANES * n : LANES * (n + 1)] = jnp.where(first, pieces[n], moved).astype(bf16)
            before = pieces[n]

    window(wo, wo_o)
    window(wd, wd_o)
    for pair in range(4):
        g = [part(gate, 384 * pair + LANES * n) for n in range(3)]
        u = [part(up, 384 * pair + LANES * n) for n in range(3)]
        slabs = (
            (g[0], jnp.where(low, g[1], roll64(u[1])), u[0]),
            (
                jnp.where(low, roll64(g[1]), roll64(g[2])),
                jnp.where(low, roll64(g[2]), u[2]),
                jnp.where(low, roll64(u[1]), roll64(u[2])),
            ),
        )
        for odd in range(2):
            for place in range(3):
                gu_o[2 * pair + odd, :, LANES * place : LANES * (place + 1)] = slabs[odd][
                    place
                ].astype(bf16)


def fast_kernel(
    x_in,
    cot_in,
    ga,
    gf,
    seg,
    wq,
    wk,
    wv,
    wo,
    gate,
    up,
    wd,
    turn_in,
    out_o,
    gin_o,
    gq_o,
    go_o,
    ggu_o,
    gd_o,
    small_o,
    meta_in,
    wq_in,
    wo_in,
    meta_r,
    xo,
    co,
    n1g,
    gfg,
    n2g,
    wq_r,
    wq_w,
    wo_r,
    wo_w,
    gu_r,
    gu_w,
    wd_r,
    wd_w,
    acc,
    qk,
    qt,
    dat,
    kw,
    vw,
    pb0,
    pb1,
    pb2,
    pb3,
    mx,
    segr,
    segc,
    gains,
    at_s,
    at_r,
    hid,
    dhid,
    inner_s,
    dgu_s,
    part_e,
    e2r1,
    e2r2,
    bfr1,
    bfr2,
    da_s,
    da_r,
    d_s,
    dkvt,
    gux_r,
    guz_r,
    guf_r,
    gd_s,
    gdx_r,
    gdz_r,
    gor1,
    gox_r,
    goq_r,
    goz_r,
    gq_r,
    small_s,
    small_r,
    rows_s,
    rows_r,
    ssem,
    rsem,
):
    f32, bf16 = jnp.float32, jnp.bfloat16
    part_f = n2g
    gu_in, wd_in = guf_r, gd_s.at[0, 0]
    e1r1, e1r2 = gfg.at[0], gfg.at[1]
    x = lax.axis_index("dp")
    s = lax.axis_index("seq")
    zh, j = s // 8, s % 8
    zl, y, c = j // 4, (j // 2) % 2, j % 2
    own_chip = zl * 2 + y
    attends = (j != 3) & (j != 5)

    def head_of(device_index):
        high = device_index // 4
        return device_index - high * (1 + (device_index - 2) // 3)

    head_own = head_of(j)
    width = x_in.shape[2]
    counter = [0]
    everyone = pltpu.get_barrier_semaphore()
    for other in range(1, 32):
        there = (x * 16 + s + other) % 32
        pl.semaphore_signal(
            everyone,
            inc=1,
            device_id=(there // 16, there % 16),
            device_id_type=pl.DeviceIdType.MESH,
        )
    prepare(ga, gf, seg, wq, wk, wv, wo, gate, up, wd, meta_in, wq_in, wo_in, gu_in, wd_in)
    pl.semaphore_wait(everyone, 31)
    pending = []

    def index_of(mask):
        return (
            ((1 - zl) if mask & 4 else zl) * 4
            + ((1 - y) if mask & 2 else y) * 2
            + ((1 - c) if mask & 1 else c)
        )

    def device(mask=0, flip_x=False, flip_z=False):
        return (
            (1 - x) if flip_x else x,
            ((1 - zh) if flip_z else zh) * 8 + index_of(mask),
        )

    def fresh():
        counter[0] += 1
        return counter[0] - 1

    def send(src, dst, target, keep=True):
        n = fresh()
        copy = pltpu.make_async_remote_copy(
            src_ref=src,
            dst_ref=dst,
            send_sem=ssem.at[n],
            recv_sem=rsem.at[n],
            device_id=target,
            device_id_type=pl.DeviceIdType.MESH,
        )
        copy.start()
        if keep:
            pending.append(copy)
        return copy

    def mm(a, b):
        return jnp.dot(a, b, preferred_element_type=f32)

    def mm_t(a, b):
        return lax.dot_general(a, b, (((1,), (1,)), ((), ())), preferred_element_type=f32)

    def mm_w(a, b):
        return lax.dot_general(a, b, (((0,), (0,)), ((), ())), preferred_element_type=f32)

    chip_y, chip_z, chip_d = zl * 2 + 1 - y, (1 - zl) * 2 + y, (1 - zl) * 2 + 1 - y

    class Gather:
        def __init__(self, view, pair=True, halves=(True, True)):
            self.view, self.pair, self.halves = view, pair, halves
            self.copies, self.cores = [], []

        def start(self, source=None):
            own = self.view(own_chip)
            source = own if source is None else source
            self.z = self.put(source, own, 4)
            self.y = self.put(source, own, 2)
            if self.pair:
                self.cores.append(self.put(source, own, 1))

        def put(self, source, place, mask):
            copy = send(source, place, device(mask))
            self.copies.append(copy)
            return copy

        def part(self, chip, half):
            view = self.view(chip)
            return view if self.halves[0] != self.halves[1] else view.at[half]

        def from_z(self):
            self.z.wait_recv()
            if self.halves[0]:
                self.zy = self.put(self.part(chip_z, 0), self.part(chip_z, 0), 2)
            if self.pair:
                self.cores.append(self.put(self.view(chip_z), self.view(chip_z), 1))

        def from_y(self):
            self.y.wait_recv()
            if self.halves[1]:
                self.yz = self.put(self.part(chip_y, 1), self.part(chip_y, 1), 4)
            if self.pair:
                self.cores.append(self.put(self.view(chip_y), self.view(chip_y), 1))

        def from_far(self):
            if self.halves[0]:
                self.zy.wait_recv()
            if self.halves[1]:
                self.yz.wait_recv()
            if self.pair:
                self.cores.append(self.put(self.view(chip_d), self.view(chip_d), 1))

        def finish(self):
            for copy in self.cores:
                copy.wait_recv()

        def sent(self):
            for copy in self.copies:
                copy.wait_send()

    def tokens_of(half):
        return lambda chip: n1g.at[half, chip, c]

    x_a = Gather(tokens_of(zh), True, (True, False))
    x_b = Gather(tokens_of(1 - zh), True, (True, False))
    x_a.start(x_in.at[zh])
    x_copy = send(x_in.at[1 - zh], n1g.at[zh, own_chip, c], device(0, False, True))
    meta_copies = []
    for mask in range(8):
        for far in (False, True):
            if mask or far:
                meta_copies.append(send(meta_in, meta_r.at[s], device(mask, False, far)))

    qkv_sem = fresh()
    qkv_first = []
    for far_x in (False, True):
        for far_z in (False, True):
            for piece in range(3):
                n = fresh()
                tx = (1 - x) if far_x else x
                tz = (1 - zh) if far_z else zh
                target = (tx, tz * 8 + 4 * x + piece + x * ((piece + 1) // 2))
                copy = pltpu.make_async_remote_copy(
                    src_ref=wq_in.at[piece],
                    dst_ref=wq_r.at[s],
                    send_sem=ssem.at[n],
                    recv_sem=rsem.at[qkv_sem],
                    device_id=target,
                    device_id_type=pl.DeviceIdType.MESH,
                )
                if far_x or far_z:
                    copy.start()
                    pending.append(copy)
                else:
                    here = j == 4 * x + piece + x * ((piece + 1) // 2)
                    local = pltpu.make_async_copy(
                        wq_in.at[piece], wq_r.at[s], rsem.at[qkv_sem]
                    )
                    pl.when(here)(local.start)
                    pl.when(jnp.logical_not(here))(copy.start)
                    qkv_first.append((here, copy))
    wo_z = send(wo_in, wo_r.at[x, zh, own_chip, c], device(0, False, True))
    wo_r[x, zh, own_chip, c] = wo_in[...]
    wd_r[x, zh] = wd_in[...]
    gu_r[x, zh, j] = gu_in[j]
    meta_r[s] = meta_in[...]
    n1g[zh, own_chip, c] = x_in[zh]
    xo[zh] = x_in[zh]
    co[zh] = cot_in[zh]
    gfg[zh, own_chip, c] = cot_in[zh]
    da_s[...] = jnp.zeros(da_s.shape, bf16)
    wd_w[...] = jnp.zeros(wd_w.shape, bf16)

    def norm_rows(values, gain):
        scale = lax.rsqrt(jnp.mean(values * values, axis=-1, keepdims=True) + EPS)
        return values * scale * gain, scale

    x_copy.wait_recv()
    x_b.start()
    xo[1 - zh] = n1g[1 - zh, own_chip, c]
    x_a.from_z()
    x_a.from_y()
    for copy in meta_copies:
        copy.wait_recv()
    gain_rows = jnp.zeros((8, width), f32)
    seg_rows = jnp.zeros((8, 1024), f32)
    for slot in range(16):
        piece = meta_r[slot]
        wide = jnp.concatenate([piece, jnp.zeros((8, width - LANES), f32)], axis=1)
        gain_rows = gain_rows + pltpu.roll(wide, 72 * slot, 1)
        wide = jnp.concatenate([piece, jnp.zeros((8, 1024 - LANES), f32)], axis=1)
        seg_rows = seg_rows + pltpu.roll(wide, 64 * slot, 1)
    gains[...] = gain_rows
    seg_own = jnp.where(zh == 0, seg_rows[2:3, :], seg_rows[3:4, :])
    seg_wide = jnp.broadcast_to(seg_own, (8, 1024))
    segr[...] = seg_wide
    segc[...] = seg_wide.T

    x_a.from_far()
    x_b.from_z()
    x_b.from_y()
    x_b.from_far()

    def wo_view(chip):
        return wo_r.at[x, :, chip, c]

    def gf_view(chip):
        return gfg.at[:, chip, c]

    def n2_view(chip):
        return n2g.at[:, chip, c]

    wo_z.wait_recv()
    wo_q = Gather(wo_view, False)
    wo_q.start()
    wo_x = [send(wo_view(own_chip), wo_view(own_chip), device(0, True))]

    def spread_rows(read, columns):
        def step(slot, carry):
            acc[pl.ds(pl.multiple_of(slot * 72, 8), 72), 0:columns] = read(slot).astype(f32)
            return carry

        lax.fori_loop(0, 16, step, 0)

    def to_low(store, columns):
        def step(block, carry):
            at = pl.multiple_of(block * 128, 128)
            store(at, acc[pl.ds(at, 128), 0:columns].astype(bf16))
            return carry

        lax.fori_loop(0, 9, step, 0)

    def from_rows(store):
        def step(slot, carry):
            store(slot, pl.multiple_of(slot * 72, 8))
            return carry

        lax.fori_loop(0, 16, step, 0)


    @pl.when(attends)
    def _():
        pltpu.make_async_copy(wq_r, wq_r, rsem.at[qkv_sem]).wait()
        spread_rows(lambda slot: wq_r[slot], 384)

        def store(at, value):
            wq_w[pl.ds(at, 128), :] = value

        to_low(store, 384)

    x_a.finish()
    x_b.finish()
    x_a.sent()
    x_b.sent()
    cot_copy = send(cot_in.at[1 - zh], co.at[zh], device(0, False, True))
    gu_first = []
    for mask in range(1, 8):
        gu_first.append(send(gu_in.at[index_of(mask)], gu_r.at[x, zh, j], device(mask)))
    wd_z = send(wd_in, wd_r.at[x, zh], device(0, False, True))
    wd_x = send(wd_in, wd_r.at[x, zh], device(0, True))

    lane256 = lax.broadcasted_iota(jnp.int32, (1, 256), 1)
    low_half = (lane256 % 64) < 32

    def swap_half(values):
        return jnp.where(low_half, pltpu.roll(values, 256 - 32, 1), pltpu.roll(values, 32, 1))

    def tables(at, rows):
        both = turn_in[pl.ds(at, rows), :]
        first_half = lane256[:, 0:128] < 64
        cosine = jnp.where(first_half, both, roll64(both))
        sine = jnp.where(first_half, roll64(both), both)
        return (
            jnp.concatenate([cosine, cosine], axis=1),
            jnp.concatenate([sine, sine], axis=1),
        )

    @pl.when(attends)
    def _():
        def step(block, carry):
            at = pl.multiple_of(block * 256, 256)
            rows = n1g[block // 2, pl.ds((block % 2) * 2, 2)].reshape(256, width)
            rows, _ = norm_rows(rows.astype(f32), gains[0:1, :])
            rows = rows.astype(bf16)
            n1g[block // 2, pl.ds((block % 2) * 2, 2)] = rows.reshape(2, 2, 64, width)
            raw = mm(rows, wq_w[...])
            cosine, sine = tables(at, 256)
            pair = raw[:, 0:256]
            turned = pair * cosine + swap_half(pair) * sine
            turned = turned.astype(bf16).astype(f32)
            qk[pl.ds(at, 256), :] = turned.astype(bf16)
            qt[:, pl.ds(at, 256)] = turned.T[0:192].astype(bf16)
            values = raw[:, 256:384].astype(bf16).astype(f32)
            values = jnp.concatenate([values, jnp.zeros((256, 128), f32)], axis=1)
            for head in range(3):
                mine = (lane256 // 64) == head
                shift = (64 * (head + 1)) % 256
                kw[head, pl.ds(at, 256), :] = jnp.where(
                    mine, pltpu.roll(turned, shift, 1), 0.0
                ).astype(bf16)
                placed = pltpu.roll(values, 64 * head, 1) if head else values
                vw[head, pl.ds(at, 256), :] = placed.astype(bf16)
            return carry

        lax.fori_loop(0, 4, step, 0)

    pbs = (pb0, pb1, pb2, pb3)
    scale = 1.0 / math.sqrt(HEAD_DIMENSION)

    def attend_block(quarter):
        length = 256 * (quarter + 1)

        def step(sub, carry):
            at = pl.multiple_of(quarter * 256 + sub * 128, 128)
            query = qk[pl.ds(at, 128), :]
            key_pos = lax.broadcasted_iota(jnp.int32, (128, length), 1)
            row_pos = lax.broadcasted_iota(jnp.int32, (128, length), 0) + at
            allowed = (segc[pl.ds(at, 128), 0:1] == segr[0:1, 0:length]) & (key_pos <= row_pos)
            mixed = jnp.zeros((128, 256), f32)
            for head in range(3):
                scores = mm_t(query, kw[head, 0:length, :])
                scores = jnp.where(allowed, scores * scale, NEGATIVE)
                top = jnp.max(scores, axis=-1, keepdims=True)
                weight = jnp.exp(scores - top)
                weight = weight / jnp.sum(weight, axis=-1, keepdims=True)
                low_p = weight.astype(bf16)
                pbs[quarter][head, pl.ds(pl.multiple_of(sub * 128, 128), 128), :] = low_p
                mixed = mixed + mm(low_p, vw[head, 0:length, :])
            mx[pl.ds(at, 128), :] = mixed
            at_s[quarter // 2, pl.ds((quarter % 2) * 4 + sub * 2, 2)] = mixed.astype(
                bf16
            ).reshape(2, 64, 256)
            return carry

        lax.fori_loop(0, 2, step, 0)

    wo_q.from_z()
    wo_x.append(send(wo_view(chip_z), wo_view(chip_z), device(0, True)))
    pl.when(attends)(lambda: attend_block(0))
    wo_q.from_y()
    wo_x.append(send(wo_view(chip_y), wo_view(chip_y), device(0, True)))
    pl.when(attends)(lambda: attend_block(1))
    for copy in gu_first:
        copy.wait_recv()
        copy.wait_send()
    gu_z = []
    for part in range(2):
        rows = gu_r.at[x, zh, 4 * part : 4 * part + 4]
        gu_z.append(send(rows, rows, device(0, False, True)))
    gu_x = [send(gu_r.at[x, zh], gu_r.at[x, zh], device(0, True))]
    pl.when(attends)(lambda: attend_block(2))
    wo_q.from_far()
    wo_x.append(send(wo_view(chip_d), wo_view(chip_d), device(0, True)))
    wo_c = [send(wo_r.at[x, :, :, c], wo_r.at[x, :, :, c], device(1))]
    pl.when(attends)(lambda: attend_block(3))

    at_copies = []
    for mask in range(1, 8):
        n = fresh()
        there = index_of(mask)
        copy = pltpu.make_async_remote_copy(
            src_ref=at_s.at[:, there],
            dst_ref=at_r.at[head_own],
            send_sem=ssem.at[n],
            recv_sem=rsem.at[n],
            device_id=device(mask),
            device_id_type=pl.DeviceIdType.MESH,
        )
        pl.when(attends)(copy.start)
        at_copies.append(((there != 3) & (there != 5), copy))

    @pl.when(attends)
    def _():
        at_r[head_own] = at_s[:, j]

    cot_copy.wait_recv()
    gfg[1 - zh, own_chip, c] = co[1 - zh]
    gf_all = Gather(gf_view)
    gf_all.start()
    for copy in wo_x:
        copy.wait_recv()
    wo_c.append(send(wo_r.at[1 - x, :, :, c], wo_r.at[1 - x, :, :, c], device(1)))
    wd_z.wait_recv()
    wd_f = send(wd_r.at[x, 1 - zh], wd_r.at[x, 1 - zh], device(0, True))
    for copy in wo_c:
        copy.wait_recv()

    def spread_left(slot):
        z_half, chip, core = slot // 8, (slot % 8) // 2, slot % 2
        left = wo_r[0, z_half, chip, core].astype(f32)
        right = wo_r[1, z_half, chip, core, :, 0:128].astype(f32)
        return jnp.concatenate([left[:, 0:512], left[:, 512:640] + right], axis=1)

    def store_left(at, value):
        wo_w[pl.ds(at, 128), 0:640] = value

    spread_rows(spread_left, 640)
    to_low(store_left, 640)

    def store_right(at, value):
        wo_w[pl.ds(at, 128), 640:1152] = value

    spread_rows(lambda slot: wo_r[1, slot // 8, (slot % 8) // 2, slot % 2, :, 128:640], 512)
    to_low(store_right, 512)

    for theirs, copy in at_copies:
        pl.when(theirs)(copy.wait_recv)

    def branch_of():
        total = jnp.zeros((128, width), f32)
        for head in range(6):
            piece = at_r[head].reshape(128, 256)[:, 0:192]
            total = total + mm(piece, wo_w[192 * head : 192 * head + 192, :])
        return total

    branch = branch_of()
    valid = jnp.concatenate(
        [
            (segc[pl.ds(pl.multiple_of(64 * j, 64), 64), 0:1] != 0).astype(f32),
            (segc[pl.ds(pl.multiple_of(512 + 64 * j, 64), 64), 0:1] != 0).astype(f32),
        ],
        axis=0,
    )
    lane1 = lax.broadcasted_iota(jnp.int32, (1, LANES), 1)
    square_attn = jnp.sum(jnp.sum(valid * branch * branch, axis=0, keepdims=True), axis=1, keepdims=True)
    count = jnp.sum(valid, axis=0, keepdims=True)
    hidden = xo[...].reshape(128, width).astype(f32) + branch
    hid[...] = hidden
    normed, _ = norm_rows(hidden, gains[1:2, :])
    n2g[:, own_chip, c] = normed.astype(bf16).reshape(2, 64, width)
    n2_all = Gather(n2_view)
    n2_all.start()
    gf_all.from_z()
    gf_all.from_y()
    for part in range(2):
        gu_z[part].wait_recv()
        rows = gu_r.at[x, 1 - zh, 4 * part : 4 * part + 4]
        gu_x.append(send(rows, rows, device(0, True)))
    gf_all.from_far()
    n2_all.from_z()
    n2_all.from_y()

    wd_x.wait_recv()
    wd_f.wait_recv()
    for copy in gu_x:
        copy.wait_recv()
    for chunk in range(2):
        spread_rows(lambda slot: gu_r[chunk, slot // 8, slot % 8], 384)

        def store_gu(at, value):
            gu_w[chunk, pl.ds(at, 128), :] = value

        to_low(store_gu, 384)
        left, right = wd_r[0, chunk], wd_r[1, chunk]
        wd_w[chunk, 0:192, 0:512] = left[:, 0:512]
        wd_w[chunk, 0:192, 512:640] = (
            left[:, 512:640].astype(f32) + right[:, 0:128].astype(f32)
        ).astype(bf16)
        wd_w[chunk, 0:192, 640:1152] = right[:, 128:640]
    n2_all.from_far()
    gf_all.finish()
    n2_all.finish()

    def chip_at(step):
        return ((zl + step + 1) % 2) * 2 + (y + (3 - step) // 2) % 2

    def pair_copy(ref, got, base, step):
        chip = chip_at(step)
        return pltpu.make_async_remote_copy(
            src_ref=ref.at[:, chip, 1 - c],
            dst_ref=got.at[step],
            send_sem=ssem.at[base + step],
            recv_sem=rsem.at[base + step],
            device_id=device(1),
            device_id_type=pl.DeviceIdType.MESH,
        )

    def side_copy(ref, got2, base, kind):
        step, half, slot, mask = (
            (0, 0, 0, 2),
            (0, 1, 0, 4),
            (1, 0, 1, 2),
            (2, 1, 2, 4),
            (1, 1, 1, 2),
            (2, 0, 2, 4),
        )[kind]
        return pltpu.make_async_remote_copy(
            src_ref=ref.at[half, chip_at(step), c],
            dst_ref=got2.at[slot, half],
            send_sem=ssem.at[base + 4 + kind],
            recv_sem=rsem.at[base + 4 + kind],
            device_id=device(mask),
            device_id_type=pl.DeviceIdType.MESH,
        )

    def pair_sum(ref, got, step):
        chip = chip_at(step)
        return ref[:, chip, c].astype(f32) + got[step].astype(f32)

    def scatter_side(ref, got, got2, base, step):
        pair_copy(ref, got, base, step).wait_recv()
        ref[:, chip_at(step), c] = pair_sum(ref, got, step).astype(bf16)
        for kind in ((0, 1), (2,), (3,))[step]:
            side_copy(ref, got2, base, kind).start()

    def scatter_first(ref, got, got2, compute):
        base = counter[0]
        counter[0] += 10

        def step_fn(step, carry):
            chip = chip_at(step)
            block = compute(chip).astype(bf16).reshape(2, 2, 64, width)
            ref[:, chip] = block
            pair_copy(ref, got, base, step).start()
            for done in range(3):
                pl.when(step == done + 1)(
                    functools.partial(scatter_side, ref, got, got2, base, done)
                )
            return carry

        lax.fori_loop(0, 4, step_fn, 0)
        return base

    def scatter_second(ref, got, got2, base):
        for kind, step, half in ((5, 2, 0), (4, 1, 1)):
            side_copy(ref, got2, base, half).wait_recv()
            chip = chip_at(step)
            total = ref[half, chip, c].astype(f32) + got2[0, half].astype(f32)
            ref[half, chip, c] = total.astype(bf16)
            side_copy(ref, got2, base, kind).start()

    def scatter_finish(ref, got, got2, base):
        pair_copy(ref, got, base, 3).wait_recv()
        total = pair_sum(ref, got, 3)
        for kind in (2, 3, 4, 5):
            side_copy(ref, got2, base, kind).wait_recv()
        total = total + got2[1].astype(f32) + got2[2].astype(f32)
        return total.reshape(128, width)

    def scatter_sent(ref, got, got2, base):
        for step in range(4):
            pair_copy(ref, got, base, step).wait_send()
        for kind in range(6):
            side_copy(ref, got2, base, kind).wait_send()

    lane128 = lax.broadcasted_iota(jnp.int32, (1, LANES), 1)

    def feed_block(chip):
        rows = n2g[:, chip].reshape(256, width)
        grads = gfg[:, chip].reshape(256, width)
        total = jnp.zeros((256, width), f32)
        for chunk in range(2):
            both = mm(rows, gu_w[chunk])
            d_inner = mm_t(grads, wd_w[chunk])
            gate_a, mid, up_a = both[:, 0:128], both[:, 128:256], both[:, 256:384]
            turned = pltpu.roll(mid, 64, 1)
            pieces = []
            for gate, up, back in (
                (gate_a, up_a, d_inner[:, 0:128]),
                (mid, turned, d_inner[:, 128:256]),
            ):
                sig = jax.nn.sigmoid(gate)
                silu = gate * sig
                pieces.append(
                    (silu * up, back * silu, back * up * sig * (1.0 + gate * (1.0 - sig)))
                )
            inner_s[chunk, :, pl.ds(chip * 2, 2), :, 0:128] = (
                pieces[0][0].astype(bf16).reshape(2, 2, 64, 128)
            )
            inner_s[chunk, :, pl.ds(chip * 2, 2), :, 128:256] = (
                jnp.where(lane128 < 64, pieces[1][0], 0.0).astype(bf16).reshape(2, 2, 64, 128)
            )
            gate_low = jnp.where(lane128 < 64, pieces[1][2], 0.0)
            up_low = jnp.where(lane128 < 64, pieces[1][1], 0.0)
            middle = (gate_low + pltpu.roll(up_low, 64, 1)).astype(bf16)
            d_both = jnp.concatenate(
                [pieces[0][2].astype(bf16), middle, pieces[0][1].astype(bf16)], axis=1
            )
            dgu_s[chunk, :, pl.ds(chip * 2, 2)] = d_both.reshape(2, 2, 64, 384)
            total = total + mm_t(d_both, gu_w[chunk])
        return total

    e2_base = scatter_first(part_e, e2r1, e2r2, feed_block)
    scatter_second(part_e, e2r1, e2r2, e2_base)

    for copy in gu_x + gu_z:
        copy.wait_send()
    gf_all.sent()
    for chunk in range(2):
        grads = dgu_s[chunk].reshape(1024, 384)

        def wide_step(block, carry):
            at = pl.multiple_of(block * 128, 128)
            rows = n2g[:, :, :, :, pl.ds(at, 128)].reshape(1024, 128)
            acc[pl.ds(at, 128), 0:384] = mm_w(rows, grads)
            return carry

        lax.fori_loop(0, 9, wide_step, 0)

        def cut(slot, at):
            gu_r[chunk, slot // 8, slot % 8] = acc[pl.ds(at, 72), 0:384].astype(bf16)

        from_rows(cut)
    ggu_x = send(gu_r.at[1 - x], gux_r, device(0, True))

    wd_z.wait_send()
    wd_x.wait_send()

    def down_step(chunk, carry):
        grads = gfg[...].reshape(1024, width)
        piece = mm_w(inner_s[chunk].reshape(1024, 256), grads)
        gd_s[chunk, 0] = piece[0:192, 0:640].astype(bf16)
        gd_s[chunk, 1] = piece[0:192, 512:1152].astype(bf16)
        return carry

    lax.fori_loop(0, 2, down_step, 0)
    ggd_x = send(gd_s.at[:, 1 - x], gdx_r, device(0, True))

    def result_block(chip):
        total = mm(
            inner_s[0, :, pl.ds(chip * 2, 2)].reshape(256, 256), wd_w[0]
        )
        return total + mm(inner_s[1, :, pl.ds(chip * 2, 2)].reshape(256, 256), wd_w[1])

    n2_all.sent()
    bf_base = scatter_first(part_f, bfr1, bfr2, result_block)

    e2 = scatter_finish(part_e, e2r1, e2r2, e2_base)
    hidden = hid[...]
    scale2 = lax.rsqrt(jnp.mean(hidden * hidden, axis=-1, keepdims=True) + EPS)
    scaled = e2 * gains[1:2, :]
    inner_mean = jnp.mean(scaled * hidden, axis=-1, keepdims=True)
    gain_feed_row = jnp.sum(e2 * hidden * scale2, axis=0, keepdims=True)
    d_hidden = (
        co[...].reshape(128, width).astype(f32)
        + scale2 * scaled
        - hidden * (scale2 * scale2 * scale2) * inner_mean
    )
    dhid[...] = d_hidden
    d_low = d_hidden.astype(bf16)
    for head in range(6):
        piece = mm_t(d_low, wo_w[192 * head : 192 * head + 192, :])
        da_s[head, :, :, 0:192] = piece.astype(bf16).reshape(2, 64, 192)
    da_copies = []
    for mask in range(1, 8):
        n = fresh()
        there = index_of(mask)
        copy = pltpu.make_async_remote_copy(
            src_ref=da_s.at[head_of(there)],
            dst_ref=da_r.at[:, j],
            send_sem=ssem.at[n],
            recv_sem=rsem.at[n],
            device_id=device(mask),
            device_id_type=pl.DeviceIdType.MESH,
        )
        pl.when((there != 3) & (there != 5))(copy.start)
        da_copies.append(((there != 3) & (there != 5), copy))

    @pl.when(attends)
    def _():
        da_r[:, j] = da_s[head_own]

    for copy in wo_c + wo_x:
        copy.wait_send()
    wo_q.sent()
    for plane in range(2):
        for head in range(6):
            piece = at_r[head].reshape(128, 256)[:, 0:192]
            acc[192 * head : 192 * head + 192, :] = mm_w(
                piece, d_low[:, 512 * plane : 512 * plane + 640]
            )

        def cut_out(slot, at):
            wo_r[plane, slot // 8, (slot % 8) // 2, slot % 2] = acc[pl.ds(at, 72), :].astype(bf16)

        from_rows(cut_out)
    go_c = send(wo_r.at[:, :, :, 1 - c], gor1, device(1))

    dkvt[...] = jnp.zeros(dkvt.shape, f32)
    for _, copy in da_copies:
        pl.when(attends)(copy.wait_recv)

    @pl.when(attends)
    def _():
        def step(block, carry):
            at = pl.multiple_of(block * 256, 256)
            rows = da_r[block // 2, pl.ds((block % 2) * 4, 4)].reshape(256, 256)
            dat[:, pl.ds(at, 256)] = rows.astype(f32).T[0:192].astype(bf16)
            return carry

        lax.fori_loop(0, 4, step, 0)

    def back_block(quarter):
        length = 256 * (quarter + 1)

        def step(sub, carry):
            at = pl.multiple_of(quarter * 256 + sub * 128, 128)
            grads = da_r[quarter // 2, pl.ds((quarter % 2) * 4 + sub * 2, 2)].reshape(128, 256)
            products = grads.astype(f32) * mx[pl.ds(at, 128), :]
            d_query = jnp.zeros((128, 256), f32)
            d_key = jnp.zeros((64, length), f32)
            d_value = jnp.zeros((64, length), f32)
            for head in range(3):
                delta = jnp.sum(
                    jnp.where((lane256 // 64) == head, products, 0.0), axis=-1, keepdims=True
                )
                low_p = pbs[quarter][head, pl.ds(pl.multiple_of(sub * 128, 128), 128), :]
                d_p = mm_t(grads, vw[head, 0:length, :])
                d_s_low = (low_p.astype(f32) * (d_p - delta) * scale).astype(bf16)
                d_query = d_query + mm(d_s_low, kw[head, 0:length, :])
                d_key = d_key + mm(qt[64 * head : 64 * head + 64, pl.ds(at, 128)], d_s_low)
                d_value = d_value + mm(dat[64 * head : 64 * head + 64, pl.ds(at, 128)], low_p)
            mx[pl.ds(at, 128), :] = d_query
            dkvt[0:64, 0:length] += d_value
            dkvt[64:128, 0:length] += d_key
            return carry

        lax.fori_loop(0, 2, step, 0)

    pl.when(attends)(lambda: back_block(0))
    scatter_second(part_f, bfr1, bfr2, bf_base)
    go_c.wait_recv()

    def go_add(chip, carry):
        for half in range(2):
            for plane in range(2):
                wo_r[plane, half, chip, c] = (
                    wo_r[plane, half, chip, c].astype(f32) + gor1[plane, half, chip].astype(f32)
                ).astype(bf16)
        return carry

    lax.fori_loop(0, 4, go_add, 0)

    def go_side(chip, half, slot, mask):
        return send(wo_r.at[:, half, chip, c], goq_r.at[slot, half], device(mask))

    def go_sum(half, chip, slot):
        for plane in range(2):
            wo_r[plane, half, chip, c] = (
                wo_r[plane, half, chip, c].astype(f32) + goq_r[slot, half, plane].astype(f32)
            ).astype(bf16)

    go_first = [
        go_side(chip_d, 0, 0, 2),
        go_side(chip_d, 1, 0, 4),
        go_side(chip_y, 0, 1, 2),
        go_side(chip_z, 1, 2, 4),
    ]
    pl.when(attends)(lambda: back_block(1))
    ggu_x.wait_recv()

    def gu_add(slot, carry):
        gu_r[x, slot // 8, slot % 8] = (
            gu_r[x, slot // 8, slot % 8].astype(f32) + gux_r[slot // 8, slot % 8].astype(f32)
        ).astype(bf16)
        return carry

    lax.fori_loop(0, 16, gu_add, 0)
    ggu_z = send(gu_r.at[x, 1 - zh], guz_r, device(0, False, True))
    pl.when(attends)(lambda: back_block(2))
    pl.when(attends)(lambda: back_block(3))

    @pl.when(attends)
    def _():
        def step(block, carry):
            at = pl.multiple_of(block * 256, 256)
            cosine, sine = tables(at, 256)
            turned = dkvt[:, pl.ds(at, 256)].T
            query = mx[pl.ds(at, 256), :]
            pair = jnp.concatenate(
                [query[:, 0:128], jnp.where(lane128 < 64, query[:, 128:256], turned)], axis=1
            )
            back = pair * cosine - swap_half(pair) * sine
            values = jnp.where(lane128 < 64, turned, 0.0)
            both = jnp.concatenate([back.astype(bf16), values.astype(bf16)], axis=1)
            d_s[block // 2, pl.ds((block % 2) * 4, 4)] = both.reshape(4, 64, 384)
            return carry

        lax.fori_loop(0, 4, step, 0)

    @pl.when(jnp.logical_not(attends))
    def _():
        d_s[...] = jnp.zeros(d_s.shape, bf16)
        wq_w[...] = jnp.zeros(wq_w.shape, bf16)

    def input_block(chip):
        return mm_t(d_s[:, pl.ds(chip * 2, 2)].reshape(256, 384), wq_w[...])

    scatter_sent(part_e, e2r1, e2r2, e2_base)
    e1_base = scatter_first(part_e, e1r1, e1r2, input_block)
    scatter_second(part_e, e1r1, e1r2, e1_base)

    ggd_x.wait_recv()
    for half in range(2):
        gd_s[half, x] = (gd_s[half, x].astype(f32) + gdx_r[half].astype(f32)).astype(bf16)
    ggd_z = send(gd_s.at[1 - zh, x], gdz_r, device(0, False, True))
    for n, half, chip, mask, slot in ((0, 0, chip_z, 4, 2), (1, 1, chip_y, 2, 1)):
        go_first[n].wait_recv()
        go_sum(half, chip, 0)
        go_first.append(go_side(chip, half, slot, mask))

    branch_feed = scatter_finish(part_f, bfr1, bfr2, bf_base)
    result = hid[...] + branch_feed
    square_feed = jnp.sum(
        jnp.sum(valid * branch_feed * branch_feed, axis=0, keepdims=True), axis=1, keepdims=True
    )
    square_out = jnp.sum(
        jnp.sum(valid * result * result, axis=0, keepdims=True), axis=1, keepdims=True
    )
    rows_s[0] = result.astype(bf16).reshape(2, 64, width)
    ret_out = send(rows_s.at[0, 1 - zh], rows_r.at[0], device(0, False, True))
    out_o[zh] = rows_s[0, zh]

    gq_send, gq_sem = fresh(), fresh()
    plane_to = zl
    piece_own = head_own - 3 * zl

    def gq_copy(slot):
        return pltpu.make_async_remote_copy(
            src_ref=wq_r.at[slot],
            dst_ref=gq_r.at[x * 2 + zh, piece_own],
            send_sem=ssem.at[gq_send],
            recv_sem=rsem.at[gq_sem],
            device_id=(plane_to, slot),
            device_id_type=pl.DeviceIdType.MESH,
        )

    @pl.when(attends)
    def _():
        grads = d_s[...].reshape(1024, 384)

        def wide_step(block, carry):
            at = pl.multiple_of(block * 128, 128)
            rows = n1g[:, :, :, :, pl.ds(at, 128)].reshape(1024, 128)
            acc[pl.ds(at, 128), 0:384] = mm_w(rows, grads)
            return carry

        lax.fori_loop(0, 9, wide_step, 0)

        def step(slot, carry):
            wq_r[slot] = acc[pl.ds(pl.multiple_of(slot * 72, 8), 72), 0:384].astype(bf16)
            here = (plane_to == x) & (slot == s)

            @pl.when(here)
            def _():
                pltpu.make_async_copy(
                    wq_r.at[slot], gq_r.at[x * 2 + zh, piece_own], rsem.at[gq_sem]
                ).start()

            pl.when(jnp.logical_not(here))(lambda: gq_copy(slot).start())
            return carry

        lax.fori_loop(0, 16, step, 0)

    ggu_z.wait_recv()

    def gu_add2(slot, carry):
        gu_r[x, zh, slot] = (
            gu_r[x, zh, slot].astype(f32) + guz_r[slot].astype(f32)
        ).astype(bf16)
        return carry

    lax.fori_loop(0, 8, gu_add2, 0)
    ggu_q = [
        send(gu_r.at[x, zh, index_of(mask)], guf_r.at[j], device(mask)) for mask in range(1, 8)
    ]
    guf_r[j] = gu_r[x, zh, j]
    e1 = scatter_finish(part_e, e1r1, e1r2, e1_base)
    tokens = xo[...].reshape(128, width).astype(f32)
    scale1 = lax.rsqrt(jnp.mean(tokens * tokens, axis=-1, keepdims=True) + EPS)
    scaled = e1 * gains[0:1, :]
    inner_mean = jnp.mean(scaled * tokens, axis=-1, keepdims=True)
    gain_attn_row = jnp.sum(e1 * tokens * scale1, axis=0, keepdims=True)
    grad_rows = (
        dhid[...] + scale1 * scaled - tokens * (scale1 * scale1 * scale1) * inner_mean
    )
    rows_s[1] = grad_rows.astype(bf16).reshape(2, 64, width)
    ret_in = send(rows_s.at[1, 1 - zh], rows_r.at[1], device(0, False, True))
    gin_o[zh] = rows_s[1, zh]

    total_row = jnp.where(
        lane1 == 0,
        square_attn,
        jnp.where(lane1 == 1, square_feed, jnp.where(lane1 == 2, square_out, count)),
    )
    row8 = lax.broadcasted_iota(jnp.int32, (8, 1), 0)
    both_gains = jnp.where(
        row8 == 0,
        jnp.broadcast_to(gain_attn_row, (8, width)),
        jnp.broadcast_to(gain_feed_row, (8, width)),
    )
    for slot in range(16):
        moved = pltpu.roll(both_gains, (width - 72 * slot) % width, 1) if slot else both_gains
        small_s[slot] = jnp.where(row8 == 2, total_row, moved[:, 0:LANES])
    small_copies = []
    for flip_x in (False, True):
        for flip_z in (False, True):
            for mask in range(8):
                if flip_x or flip_z or mask:
                    target = device(mask, flip_x, flip_z)
                    small_copies.append(
                        send(small_s.at[target[1]], small_r.at[x * 16 + s], target)
                    )
    small_r[x * 16 + s] = small_s[s]

    for copy in go_first[2:]:
        copy.wait_recv()
    for slot in (1, 2):
        for half in range(2):
            go_sum(half, own_chip, slot)
    go_x = send(wo_r.at[1 - x, :, own_chip, c], gox_r, device(0, True))

    go_x.wait_recv()
    for half in range(2):
        wo_r[x, half, own_chip, c] = (
            wo_r[x, half, own_chip, c].astype(f32) + gox_r[half].astype(f32)
        ).astype(bf16)
    go_z = send(wo_r.at[x, 1 - zh, own_chip, c], goz_r, device(0, False, True))
    ggd_z.wait_recv()
    gd_o[...] = gd_s[zh, x].astype(f32) + gdz_r[...].astype(f32)
    for copy in ggu_q:
        copy.wait_recv()
    ggu_o[...] = guf_r[...]
    go_z.wait_recv()
    go_o[...] = wo_r[x, zh, own_chip, c].astype(f32) + goz_r[...].astype(f32)
    ret_out.wait_recv()
    out_o[1 - zh] = rows_r[0]
    pltpu.make_async_copy(gq_r, gq_r, rsem.at[gq_sem]).wait()
    gq_o[...] = (
        (gq_r[0].astype(f32) + gq_r[1].astype(f32)) + (gq_r[2].astype(f32) + gq_r[3].astype(f32))
    )
    for copy in small_copies:
        copy.wait_recv()
    total = small_r[0]
    for slot in range(1, 32):
        total = total + small_r[slot]
    small_o[...] = total
    ret_in.wait_recv()
    gin_o[1 - zh] = rows_r[1]

    waited = {id(copy) for copy in wo_c + wo_x + gu_x + gu_z + gu_first + [wd_z, wd_x]}
    for gather in (wo_q, gf_all, n2_all, x_a, x_b):
        waited |= {id(copy) for copy in gather.copies}
    for copy in pending:
        if id(copy) not in waited:
            copy.wait_send()
    for here, copy in qkv_first:
        pl.when(jnp.logical_not(here))(copy.wait_send)
    for theirs, copy in at_copies:
        pl.when(attends)(copy.wait_send)
    for theirs, copy in da_copies:
        pl.when(theirs)(copy.wait_send)
    scatter_sent(part_f, bfr1, bfr2, bf_base)
    scatter_sent(part_e, e1r1, e1r2, e1_base)

    @pl.when(attends)
    def _():
        def step(slot, carry):
            here = (plane_to == x) & (slot == s)
            pl.when(jnp.logical_not(here))(lambda: gq_copy(slot).wait_send())
            return carry

        lax.fori_loop(0, 16, step, 0)


def finish_kernel(
    out, gin, gq, go, ggu, gd, small,
    out_o, gin_o, gq_o, gk_o, gv_o, go_o, gg_o, gu_o, gd_o, ga_o, gf_o, rm_o,
):
    f32 = jnp.float32
    first = lax.axis_index("dp") == 0
    rows = gq.shape[1]
    low = lax.broadcasted_iota(jnp.int32, (1, LANES), 1) < 64
    out_o[...] = out[...]
    gin_o[...] = gin[...]
    p = [[gq[head, :, LANES * n : LANES * (n + 1)].astype(f32) for n in range(3)] for head in range(3)]
    gq_o[:, 0:128] = p[0][0]
    gq_o[:, 128:256] = jnp.where(low, p[0][1], roll64(p[1][0]))
    gq_o[:, 256:384] = jnp.where(low, roll64(p[1][0]), roll64(p[1][1]))
    gq_o[:, 384:512] = p[2][0]
    gq_o[:, 512:576] = p[2][1][:, 0:64]
    gk_o[:, 0:128] = jnp.where(low, roll64(p[0][1]), p[1][1])
    gk_o[:, 128:192] = roll64(p[2][1])[:, 0:64]
    gv_o[:, 0:128] = jnp.where(low, p[0][2], roll64(p[1][2]))
    gv_o[:, 128:192] = p[2][2][:, 0:64]

    def unwindow(ref, res):
        pieces = [ref[:, LANES * n : LANES * (n + 1)].astype(f32) for n in range(5)]
        for n in range(5):
            after = pieces[min(n + 1, 4)]
            moved = jnp.where(low, roll64(pieces[n]), roll64(after))
            value = jnp.where(first, pieces[n], moved)
            if n < 4:
                res[:, LANES * n : LANES * (n + 1)] = value
            else:
                res[:, 512:576] = value[:, 0:64]

    unwindow(go, go_o)
    unwindow(gd, gd_o)
    for pair in range(4):
        a, b = [
            [ggu[2 * pair + odd, :, LANES * n : LANES * (n + 1)].astype(f32) for n in range(3)]
            for odd in range(2)
        ]
        at = 384 * pair
        gg_o[:, at : at + 128] = a[0]
        gg_o[:, at + 128 : at + 256] = jnp.where(low, a[1], roll64(b[0]))
        gg_o[:, at + 256 : at + 384] = jnp.where(low, roll64(b[0]), roll64(b[1]))
        gu_o[:, at : at + 128] = a[2]
        gu_o[:, at + 128 : at + 256] = jnp.where(low, roll64(a[1]), roll64(b[2]))
        gu_o[:, at + 256 : at + 384] = jnp.where(low, roll64(b[2]), b[1])
    ga_o[...] = small[0:1, 0:rows]
    gf_o[...] = small[1:2, 0:rows]
    width = out.shape[2]
    rm_o[...] = jnp.sqrt(small[2:3, 0:3] / (small[2:3, 3:4] * width))


def fast_device(
    inputs,
    segments,
    weight_query,
    key_weight_matrix,
    value_weight_matrix,
    weight_out,
    weight_gate,
    weight_up,
    weight_down,
    gain_attention,
    gain_feed,
    cotangent,
):
    f32, bf16 = jnp.float32, jnp.bfloat16
    micro, _, rows, width = inputs.shape
    dp = lax.axis_index("dp")
    length = rows * 16
    piece = width // 16

    whole = pl.BlockSpec(memory_space=pltpu.VMEM)
    half = HEAD_DIMENSION // 2
    frequency = THETA ** (-np.arange(half, dtype=np.float32) * np.float32(2.0) / HEAD_DIMENSION)
    angles = np.arange(length, dtype=np.float32)[:, None] * frequency.astype(np.float32)[None, :]
    cosine, sine = np.cos(angles), np.sin(angles)
    turns = np.concatenate([cosine, cosine, -sine, sine], axis=1).astype(np.float32)

    v = pltpu.VMEM
    tok = (2, 4, 2, 64, width)
    scratch = [
        v((8, LANES), f32),
        v((3, piece, 384), bf16),
        v((piece, 640), bf16),
        v((16, 8, LANES), f32),
        v((2, 64, width), bf16),
        v((2, 64, width), bf16),
        v(tok, bf16),
        v(tok, bf16),
        v(tok, bf16),
        v((16, 72, 384), bf16),
        v((width, 384), bf16),
        v((2, 2, 4, 2, 72, 640), bf16),
        v((width, width), bf16),
        v((2, 2, 8, 72, 384), bf16),
        v((2, width, 384), bf16),
        v((2, 2, 192, 640), bf16),
        v((2, 256, width), bf16),
        v((width, 640), f32),
        v((1024, 256), bf16),
        v((192, 1024), bf16),
        v((192, 1024), bf16),
        v((3, 1024, 256), bf16),
        v((3, 1024, 256), bf16),
        v((3, 256, 256), bf16),
        v((3, 256, 512), bf16),
        v((3, 256, 768), bf16),
        v((3, 256, 1024), bf16),
        v((1024, 256), f32),
        v((8, 1024), f32),
        v((1024, 8), f32),
        v((8, width), f32),
        v((2, 8, 64, 256), bf16),
        v((6, 2, 64, 256), bf16),
        v((128, width), f32),
        v((128, width), f32),
        v((2, 2, 8, 64, 256), bf16),
        v((2, 2, 8, 64, 384), bf16),
        v((2, 4, 2, 64, width), bf16),
        v((4, 2, 64, width), bf16),
        v((3, 2, 64, width), bf16),
        v((4, 2, 64, width), bf16),
        v((3, 2, 64, width), bf16),
        v((6, 2, 64, 256), bf16),
        v((2, 8, 64, 256), bf16),
        v((2, 8, 64, 384), bf16),
        v((128, 1024), f32),
        v((2, 8, 72, 384), bf16),
        v((8, 72, 384), bf16),
        v((8, 72, 384), bf16),
        v((2, 2, 192, 640), bf16),
        v((2, 192, 640), bf16),
        v((192, 640), bf16),
        v((2, 2, 4, 72, 640), bf16),
        v((2, 72, 640), bf16),
        v((3, 2, 2, 72, 640), bf16),
        v((72, 640), bf16),
        v((4, 3, 72, 384), bf16),
        v((16, 8, LANES), f32),
        v((32, 8, LANES), f32),
        v((2, 2, 64, width), bf16),
        v((2, 64, width), bf16),
        pltpu.SemaphoreType.DMA((256,)),
        pltpu.SemaphoreType.DMA((256,)),
    ]
    out, gin, gq, go, ggu, gd, small = pl.pallas_call(
        fast_kernel,
        out_shape=(
            jax.ShapeDtypeStruct((2, rows, width), bf16),
            jax.ShapeDtypeStruct((2, rows, width), bf16),
            jax.ShapeDtypeStruct((3, piece, 384), f32),
            jax.ShapeDtypeStruct((piece, 640), f32),
            jax.ShapeDtypeStruct((8, piece, 384), bf16),
            jax.ShapeDtypeStruct((192, 640), f32),
            jax.ShapeDtypeStruct((8, LANES), f32),
        ),
        in_specs=[whole] * 13,
        out_specs=[whole] * 7,
        scratch_shapes=scratch,
        compiler_params=pltpu.CompilerParams(
            has_side_effects=True, collective_id=0, vmem_limit_bytes=62 * 1024 * 1024
        ),
        name="layer",
    )(
        inputs[:, 0],
        cotangent[:, 0],
        gain_attention.reshape(1, piece),
        gain_feed.reshape(1, piece),
        segments[:, 0],
        weight_query,
        key_weight_matrix,
        value_weight_matrix,
        weight_out,
        weight_gate,
        weight_up,
        weight_down,
        jnp.asarray(turns),
    )

    grads = pl.pallas_call(
        finish_kernel,
        out_shape=(
            jax.ShapeDtypeStruct((2, rows, width), bf16),
            jax.ShapeDtypeStruct((2, rows, width), bf16),
            jax.ShapeDtypeStruct(weight_query.shape, f32),
            jax.ShapeDtypeStruct(key_weight_matrix.shape, f32),
            jax.ShapeDtypeStruct(value_weight_matrix.shape, f32),
            jax.ShapeDtypeStruct(weight_out.shape, f32),
            jax.ShapeDtypeStruct(weight_gate.shape, f32),
            jax.ShapeDtypeStruct(weight_up.shape, f32),
            jax.ShapeDtypeStruct(weight_down.shape, f32),
            jax.ShapeDtypeStruct((1, piece), f32),
            jax.ShapeDtypeStruct((1, piece), f32),
            jax.ShapeDtypeStruct((1, 3), f32),
        ),
        in_specs=[whole] * 7,
        out_specs=[whole] * 12,
        name="finish",
    )(out, gin, gq, go, ggu, gd, small)
    return (
        grads[0][:, None],
        grads[1][:, None],
        *grads[2:9],
        grads[9].reshape(piece),
        grads[10].reshape(piece),
        grads[11].reshape(3),
    )


def solution(mesh):
    placed = (
        P(None, "dp", "seq", None),
        P(None, "dp", "seq"),
        P("seq", "dp"),
        P("seq", "dp"),
        P("seq", "dp"),
        P("seq", "dp"),
        P("seq", "dp"),
        P("seq", "dp"),
        P("seq", "dp"),
        P("seq"),
        P("seq"),
        P(None, "dp", "seq", None),
    )
    body = fast_device if dict(mesh.shape) == {"dp": 2, "seq": 16} else per_device
    return jax.shard_map(
        body,
        mesh=mesh,
        in_specs=placed,
        out_specs=(
            P(None, "dp", "seq", None),
            P(None, "dp", "seq", None),
            P("seq", "dp"),
            P("seq", "dp"),
            P("seq", "dp"),
            P("seq", "dp"),
            P("seq", "dp"),
            P("seq", "dp"),
            P("seq", "dp"),
            P("seq"),
            P("seq"),
            P(),
        ),
        check_vma=False,
    )
```

```python
import functools
import math

import jax
import jax.numpy as jnp
import numpy as np
from jax import lax
from jax.experimental import pallas as pl
from jax.experimental.pallas import tpu as pltpu
from jax.sharding import PartitionSpec as P

QUERY_HEADS = 18
KEY_VALUE_HEADS = 6
HEAD_DIMENSION = 64


EPS = 1e-05
THETA = 10000.0
NEGATIVE = -1e30


def rope_tables(positions, head_size):
    half_size = head_size // 2
    frequency = THETA ** (-jnp.arange(half_size, dtype=jnp.float32) * 2.0 / head_size)
    angles = positions.astype(jnp.float32)[:, None] * frequency[None, :]
    angles = jnp.concatenate([angles, angles], axis=1)
    return (jnp.cos(angles), jnp.sin(angles))


def turn_half(values_in):
    half_size = values_in.shape[-1] // 2
    return jnp.concatenate([-values_in[..., half_size:], values_in[..., :half_size]], axis=-1)


def apply_rotation(values_in, cosine_table, sine_values):
    return values_in * cosine_table[:, None, :] + turn_half(values_in) * sine_values[:, None, :]


def reverse_rotation(grads_in, cosine_table, sine_values):
    return grads_in * cosine_table[:, None, :] - turn_half(grads_in * sine_values[:, None, :])


def norm_forward(values_in, gain):
    row_scale = lax.rsqrt(jnp.mean(values_in * values_in, axis=-1, keepdims=True) + EPS)
    return (values_in * row_scale * gain, row_scale)


def norm_backward(values_in, row_scale, gain, grad_normed):
    scaled = grad_normed * gain
    inner_mean = jnp.mean(scaled * values_in, axis=-1, keepdims=True)
    value_gradient_rows = row_scale * scaled - values_in * row_scale**3 * inner_mean
    grad_gain = jnp.sum(grad_normed * values_in * row_scale, axis=(0, 1))
    return (value_gradient_rows, grad_gain)


def apply_projection(acts_low, weight_full):
    return jnp.einsum("std,df->stf", acts_low, weight_full, preferred_element_type=jnp.float32)


def project_back(grads_low, weight_full):
    return jnp.einsum("sta,ba->stb", grads_low, weight_full, preferred_element_type=jnp.float32)


def weight_grad(acts_low, grads_low):
    return jnp.einsum("std,stf->df", acts_low, grads_low, preferred_element_type=jnp.float32)


def gather_all(shards, gain_shards):
    wide = (
        lax.all_gather(shards[0], "dp", axis=1, tiled=True),
        lax.all_gather(shards[1], "dp", axis=1, tiled=True),
        lax.all_gather(shards[2], "dp", axis=1, tiled=True),
        lax.all_gather(shards[3], "dp", axis=1, tiled=True),
        lax.all_gather(shards[4], "dp", axis=1, tiled=True),
        lax.all_gather(shards[5], "dp", axis=1, tiled=True),
        lax.all_gather(shards[6], "dp", axis=1, tiled=True),
    )
    return (
        lax.all_gather(wide[0], "seq", axis=0, tiled=True),
        lax.all_gather(wide[1], "seq", axis=0, tiled=True),
        lax.all_gather(wide[2], "seq", axis=0, tiled=True),
        lax.all_gather(wide[3], "seq", axis=0, tiled=True),
        lax.all_gather(wide[4], "seq", axis=0, tiled=True),
        lax.all_gather(wide[5], "seq", axis=0, tiled=True),
        lax.all_gather(wide[6], "seq", axis=0, tiled=True),
        lax.all_gather(gain_shards[0], "seq", axis=0, tiled=True),
        lax.all_gather(gain_shards[1], "seq", axis=0, tiled=True),
    )


def gather_keys(key_low, value_low, seg_low):
    return (
        lax.all_gather(key_low, "seq", axis=1, tiled=True),
        lax.all_gather(value_low, "seq", axis=1, tiled=True),
        lax.all_gather(seg_low, "seq", axis=1, tiled=True),
    )


def reduce_grads(grads):
    rows = [
        lax.psum_scatter(g.astype(jnp.bfloat16), "seq", scatter_dimension=0, tiled=True)
        for g in grads
    ]
    return tuple(
        lax.psum_scatter(r, "dp", scatter_dimension=1, tiled=True).astype(jnp.float32)
        for r in rows
    )


def block_view(gathered, block_index, key_tile_block):
    block_offset = block_index * key_tile_block
    key_portion = lax.dynamic_slice_in_dim(gathered[0], block_offset, key_tile_block, 1)
    value_portion = lax.dynamic_slice_in_dim(gathered[1], block_offset, key_tile_block, 1)
    seg_part = lax.dynamic_slice_in_dim(gathered[2], block_offset, key_tile_block, 1).astype(
        jnp.float32
    )
    sequence_count = key_portion.shape[0]
    key_portion = key_portion.reshape(
        sequence_count, key_tile_block, KEY_VALUE_HEADS, HEAD_DIMENSION
    )
    value_portion = value_portion.reshape(
        sequence_count, key_tile_block, KEY_VALUE_HEADS, HEAD_DIMENSION
    )
    col_pos = block_offset + jnp.arange(key_tile_block, dtype=jnp.int32)
    return (key_portion, value_portion, seg_part, col_pos)


def masked_scores(query_block_list, key_portion, seg_rows, seg_part, row_pos, col_pos, score_scale):
    raw_scores = jnp.einsum(
        "skgtd,sjkd->skgtj", query_block_list, key_portion, preferred_element_type=jnp.float32
    )
    allowed = (seg_rows[:, :, None] == seg_part[:, None, :]) & (
        col_pos[None, None, :] <= row_pos[None, :, None]
    )
    allowed = allowed[:, None, None, :, :]
    return (jnp.where(allowed, raw_scores * score_scale, NEGATIVE), allowed)


def log_sum(
    query_block_list, gathered, seg_rows, row_pos, block_count, key_tile_block, score_scale
):
    lead_shape = query_block_list.shape[:4]

    def log_step_fn(block_index, carried):
        row_top, row_total = carried
        key_portion, value_portion, seg_part, col_pos = block_view(
            gathered, block_index, key_tile_block
        )
        scores, allowed = masked_scores(
            query_block_list, key_portion, seg_rows, seg_part, row_pos, col_pos, score_scale
        )
        new_top = jnp.maximum(row_top, jnp.max(scores, axis=-1))
        exponent = jnp.where(allowed, jnp.exp(scores - new_top[..., None]), 0.0)
        row_total = row_total * jnp.exp(row_top - new_top) + jnp.sum(exponent, axis=-1)
        return (new_top, row_total)

    start_state = (jnp.full(lead_shape, NEGATIVE, jnp.float32), jnp.zeros(lead_shape, jnp.float32))
    row_top, row_total = lax.fori_loop(0, block_count, log_step_fn, start_state)
    return row_top + jnp.log(row_total)


def attend(
    query_block_list,
    gathered,
    seg_rows,
    row_pos,
    block_count,
    key_tile_block,
    score_scale,
    log_total,
):

    def attend_step_fn(block_index, mixed_heads):
        key_portion, value_portion, seg_part, col_pos = block_view(
            gathered, block_index, key_tile_block
        )
        scores, allowed = masked_scores(
            query_block_list, key_portion, seg_rows, seg_part, row_pos, col_pos, score_scale
        )
        probabilities = jnp.where(allowed, jnp.exp(scores - log_total[..., None]), 0.0).astype(
            jnp.bfloat16
        )
        return mixed_heads + jnp.einsum(
            "skgtj,sjkd->skgtd", probabilities, value_portion, preferred_element_type=jnp.float32
        )

    return lax.fori_loop(
        0, block_count, attend_step_fn, jnp.zeros(query_block_list.shape, jnp.float32)
    )


def query_back(
    query_block_list,
    gathered,
    seg_rows,
    row_pos,
    block_count,
    key_tile_block,
    score_scale,
    log_total,
    gradient_reduced,
    row_delta,
):

    def query_step_fn(block_index, grad_query):
        key_portion, value_portion, seg_part, col_pos = block_view(
            gathered, block_index, key_tile_block
        )
        scores, allowed = masked_scores(
            query_block_list, key_portion, seg_rows, seg_part, row_pos, col_pos, score_scale
        )
        probabilities = jnp.where(allowed, jnp.exp(scores - log_total[..., None]), 0.0)
        grad_probs = jnp.einsum(
            "skgtd,sjkd->skgtj", gradient_reduced, value_portion, preferred_element_type=jnp.float32
        )
        grad_scores = (probabilities * (grad_probs - row_delta[..., None]) * score_scale).astype(
            jnp.bfloat16
        )
        return grad_query + jnp.einsum(
            "skgtj,sjkd->skgtd", grad_scores, key_portion, preferred_element_type=jnp.float32
        )

    return lax.fori_loop(
        0, block_count, query_step_fn, jnp.zeros(query_block_list.shape, jnp.float32)
    )


def key_back(
    key_local,
    value_local,
    seg_rows,
    row_pos,
    query_whole,
    grads_whole,
    stats_whole,
    seg_whole,
    first_block,
    block_count,
    query_tile,
    score_scale,
):
    sequence_count = key_local.shape[0]
    group_width = QUERY_HEADS // KEY_VALUE_HEADS

    def key_step_fn(block_index, carried):
        key_total, value_total = carried
        block_offset = block_index * query_tile
        query_rows = lax.dynamic_slice_in_dim(query_whole, block_offset, query_tile, 1).reshape(
            sequence_count, query_tile, KEY_VALUE_HEADS, group_width, HEAD_DIMENSION
        )
        grad_rows = lax.dynamic_slice_in_dim(grads_whole, block_offset, query_tile, 1).reshape(
            sequence_count, query_tile, KEY_VALUE_HEADS, group_width, HEAD_DIMENSION
        )
        log_rows = lax.dynamic_slice_in_dim(stats_whole[0], block_offset, query_tile, 3)
        delta_rows = lax.dynamic_slice_in_dim(stats_whole[1], block_offset, query_tile, 3)
        seg_query = lax.dynamic_slice_in_dim(seg_whole, block_offset, query_tile, 1).astype(
            jnp.float32
        )
        query_pos = block_offset + jnp.arange(query_tile, dtype=jnp.int32)
        raw_scores = jnp.einsum(
            "stkgd,sjkd->skgtj", query_rows, key_local, preferred_element_type=jnp.float32
        )
        allowed = (seg_query[:, :, None] == seg_rows[:, None, :]) & (
            row_pos[None, None, :] <= query_pos[None, :, None]
        )
        allowed = allowed[:, None, None, :, :]
        scores = jnp.where(allowed, raw_scores * score_scale, NEGATIVE)
        probabilities = jnp.where(allowed, jnp.exp(scores - log_rows[..., None]), 0.0)
        grad_probs = jnp.einsum(
            "stkgd,sjkd->skgtj", grad_rows, value_local, preferred_element_type=jnp.float32
        )
        grad_scores = (probabilities * (grad_probs - delta_rows[..., None]) * score_scale).astype(
            jnp.bfloat16
        )
        key_total = key_total + jnp.einsum(
            "skgtj,stkgd->sjkd", grad_scores, query_rows, preferred_element_type=jnp.float32
        )
        value_total = value_total + jnp.einsum(
            "skgtj,stkgd->sjkd",
            probabilities.astype(jnp.bfloat16),
            grad_rows,
            preferred_element_type=jnp.float32,
        )
        return (key_total, value_total)

    start_state = (jnp.zeros(key_local.shape, jnp.float32), jnp.zeros(key_local.shape, jnp.float32))
    return lax.fori_loop(first_block, block_count, key_step_fn, start_state)


def per_device(
    inputs,
    segments,
    weight_query,
    key_weight_matrix,
    value_weight_matrix,
    weight_out,
    weight_gate,
    weight_up,
    weight_down,
    gain_attention,
    gain_feed,
    cotangent,
):
    shards = (
        weight_query,
        key_weight_matrix,
        value_weight_matrix,
        weight_out,
        weight_gate,
        weight_up,
        weight_down,
    )
    gain_shards = (gain_attention, gain_feed)
    micro_count, sequence_count, token_count, model_width = inputs.shape
    group_width = QUERY_HEADS // KEY_VALUE_HEADS
    score_scale = 1.0 / math.sqrt(HEAD_DIMENSION)
    row_pos = lax.axis_index("seq") * token_count + jnp.arange(token_count, dtype=jnp.int32)
    cosine_table, sine_values = rope_tables(row_pos, HEAD_DIMENSION)
    key_span_length = token_count * lax.axis_size("seq")
    key_tile_block = min(512, key_span_length)
    total_blocks = key_span_length // key_tile_block
    block_count = row_pos[token_count - 1] // key_tile_block + 1
    first_block = row_pos[0] // key_tile_block
    outputs = []
    grad_list = []
    totals = jnp.zeros((4,), jnp.float32)
    gain_grads = jnp.zeros((2, model_width), jnp.float32)
    summed = None
    weights_complete = gather_all(shards, gain_shards)
    for batch_index in range(micro_count):
        tokens = inputs[batch_index].astype(jnp.float32)
        seg_local = segments[batch_index]
        seg_rows = seg_local.astype(jnp.float32)
        seg_low = seg_local.astype(jnp.bfloat16)
        gain_first = weights_complete[7].astype(jnp.float32)
        gain_second = weights_complete[8].astype(jnp.float32)
        norm_first, scale_first = norm_forward(tokens, gain_first)
        normalized = norm_first.astype(jnp.bfloat16)
        query_raw = apply_projection(normalized, weights_complete[0]).reshape(
            sequence_count, token_count, QUERY_HEADS, HEAD_DIMENSION
        )
        query_reduced = apply_rotation(query_raw, cosine_table, sine_values).astype(jnp.bfloat16)
        key_unrotated = apply_projection(normalized, weights_complete[1]).reshape(
            sequence_count, token_count, KEY_VALUE_HEADS, HEAD_DIMENSION
        )
        key_low = (
            apply_rotation(key_unrotated, cosine_table, sine_values)
            .astype(jnp.bfloat16)
            .reshape(sequence_count, token_count, KEY_VALUE_HEADS * HEAD_DIMENSION)
        )
        value_low = apply_projection(normalized, weights_complete[2]).astype(jnp.bfloat16)
        gathered = gather_keys(key_low, value_low, seg_low)
        query_block_list = query_reduced.reshape(
            sequence_count, token_count, KEY_VALUE_HEADS, group_width, HEAD_DIMENSION
        ).transpose(0, 2, 3, 1, 4)
        log_total = log_sum(
            query_block_list, gathered, seg_rows, row_pos, block_count, key_tile_block, score_scale
        )
        mixed_heads = attend(
            query_block_list,
            gathered,
            seg_rows,
            row_pos,
            block_count,
            key_tile_block,
            score_scale,
            log_total,
        )
        attn_low = (
            mixed_heads.transpose(0, 3, 1, 2, 4)
            .reshape(sequence_count, token_count, QUERY_HEADS * HEAD_DIMENSION)
            .astype(jnp.bfloat16)
        )
        branch_attn = apply_projection(attn_low, weights_complete[3])
        hidden = tokens + branch_attn
        norm_second, scale_second = norm_forward(hidden, gain_second)
        normed_second = norm_second.astype(jnp.bfloat16)
        gate_values = apply_projection(normed_second, weights_complete[4])
        up_values = apply_projection(normed_second, weights_complete[5])
        gate_sigmoid = jax.nn.sigmoid(gate_values)
        inner_low = (gate_values * gate_sigmoid * up_values).astype(jnp.bfloat16)
        branch_feed = apply_projection(inner_low, weights_complete[6])
        result = hidden + branch_feed
        outputs.append(result.astype(jnp.bfloat16))
        valid_rows = (seg_local != 0).astype(jnp.float32)[:, :, None]
        totals = totals + jnp.stack(
            [
                jnp.sum(valid_rows * branch_attn * branch_attn),
                jnp.sum(valid_rows * branch_feed * branch_feed),
                jnp.sum(valid_rows * result * result),
                jnp.sum(valid_rows),
            ]
        )
        back_weights = weights_complete
        back_keys = gathered
        grad_result = cotangent[batch_index].astype(jnp.float32)
        grad_feed = grad_result.astype(jnp.bfloat16)
        grad_down = weight_grad(inner_low, grad_feed)
        grad_inner = project_back(grad_feed, back_weights[6])
        grad_up = (grad_inner * gate_values * gate_sigmoid).astype(jnp.bfloat16)
        grad_gate = (
            grad_inner * up_values * gate_sigmoid * (1.0 + gate_values * (1.0 - gate_sigmoid))
        ).astype(jnp.bfloat16)
        grad_gate_w = weight_grad(normed_second, grad_gate)
        grad_up_w = weight_grad(normed_second, grad_up)
        grad_normed_second = project_back(grad_gate, back_weights[4]) + project_back(
            grad_up, back_weights[5]
        )
        grad_hidden_norm, grad_gain_second = norm_backward(
            hidden, scale_second, gain_second, grad_normed_second
        )
        grad_hidden = grad_result + grad_hidden_norm
        grad_branch = grad_hidden.astype(jnp.bfloat16)
        grad_out_w = weight_grad(attn_low, grad_branch)
        mixed_gradient = project_back(grad_branch, back_weights[3]).astype(jnp.bfloat16)
        gradient_reduced = mixed_gradient.reshape(
            sequence_count, token_count, KEY_VALUE_HEADS, group_width, HEAD_DIMENSION
        ).transpose(0, 2, 3, 1, 4)
        row_delta = jnp.sum(gradient_reduced.astype(jnp.float32) * mixed_heads, axis=-1)
        grad_query = query_back(
            query_block_list,
            back_keys,
            seg_rows,
            row_pos,
            block_count,
            key_tile_block,
            score_scale,
            log_total,
            gradient_reduced,
            row_delta,
        )
        query_flat = query_reduced.reshape(
            sequence_count, token_count, QUERY_HEADS * HEAD_DIMENSION
        )
        query_whole, grads_whole = (
            lax.all_gather(query_flat, "seq", axis=1, tiled=True),
            lax.all_gather(mixed_gradient, "seq", axis=1, tiled=True),
        )
        stats_whole = (
            lax.all_gather(log_total, "seq", axis=3, tiled=True),
            lax.all_gather(row_delta, "seq", axis=3, tiled=True),
        )
        key_local = key_low.reshape(sequence_count, token_count, KEY_VALUE_HEADS, HEAD_DIMENSION)
        value_local = value_low.reshape(
            sequence_count, token_count, KEY_VALUE_HEADS, HEAD_DIMENSION
        )
        key_total, value_total = key_back(
            key_local,
            value_local,
            seg_rows,
            row_pos,
            query_whole,
            grads_whole,
            stats_whole,
            back_keys[2],
            first_block,
            total_blocks,
            key_tile_block,
            score_scale,
        )
        key_grad_low = (
            reverse_rotation(key_total, cosine_table, sine_values)
            .reshape(sequence_count, token_count, KEY_VALUE_HEADS * HEAD_DIMENSION)
            .astype(jnp.bfloat16)
        )
        value_grad_low = value_total.reshape(
            sequence_count, token_count, KEY_VALUE_HEADS * HEAD_DIMENSION
        ).astype(jnp.bfloat16)
        query_grad = grad_query.transpose(0, 3, 1, 2, 4).reshape(
            sequence_count, token_count, QUERY_HEADS, HEAD_DIMENSION
        )
        query_grad_low = (
            reverse_rotation(query_grad, cosine_table, sine_values)
            .reshape(sequence_count, token_count, QUERY_HEADS * HEAD_DIMENSION)
            .astype(jnp.bfloat16)
        )
        grad_normed = (
            project_back(query_grad_low, back_weights[0])
            + project_back(key_grad_low, back_weights[1])
            + project_back(value_grad_low, back_weights[2])
        )
        grad_token_norm, grad_gain_first = norm_backward(
            tokens, scale_first, gain_first, grad_normed
        )
        grad_list.append((grad_hidden + grad_token_norm).astype(jnp.bfloat16))
        gain_grads = gain_grads + jnp.stack([grad_gain_first, grad_gain_second])
        batch_grads = (
            weight_grad(normalized, query_grad_low),
            weight_grad(normalized, key_grad_low),
            weight_grad(normalized, value_grad_low),
            grad_out_w,
            grad_gate_w,
            grad_up_w,
            grad_down,
        )
        summed = batch_grads if summed is None else jax.tree.map(jnp.add, summed, batch_grads)
    reduced = reduce_grads(summed)
    gain_total, totals = lax.psum((gain_grads, totals), ("dp", "seq"))
    piece_width = model_width // lax.axis_size("seq")
    gain_part = lax.dynamic_slice_in_dim(
        gain_total, lax.axis_index("seq") * piece_width, piece_width, 1
    )
    root_means = jnp.sqrt(totals[:3] / (totals[3] * model_width))
    return (
        jnp.stack(outputs),
        jnp.stack(grad_list),
        reduced[0],
        reduced[1],
        reduced[2],
        reduced[3],
        reduced[4],
        reduced[5],
        reduced[6],
        gain_part[0],
        gain_part[1],
        root_means,
    )


LANES = 128


def roll64(values):
    return pltpu.roll(values, 64, 1)


def prepare(
    ga, gf, seg, wq, wk, wv, wo, gate, up, wd, meta_o, wq_o, wo_o, gu_o, wd_o
):
    f32, bf16 = jnp.float32, jnp.bfloat16
    first = lax.axis_index("dp") == 0
    rows = wq.shape[0]
    low = lax.broadcasted_iota(jnp.int32, (1, LANES), 1) < 64
    meta_o[...] = jnp.zeros(meta_o.shape, f32)
    meta_o[0:1, 0:rows] = ga[...].astype(f32)
    meta_o[1:2, 0:rows] = gf[...].astype(f32)
    meta_o[2:4, 0:64] = seg[...].astype(f32)

    def part(ref, at, size=LANES):
        values = ref[:, at : at + size].astype(f32)
        if size < LANES:
            values = jnp.concatenate(
                [values, jnp.zeros((values.shape[0], LANES - size), f32)], axis=1
            )
        return values

    q = [part(wq, LANES * n) for n in range(4)] + [part(wq, 512, 64)]
    k = [part(wk, 0), part(wk, LANES, 64)]
    v = [part(wv, 0), part(wv, LANES, 64)]
    slabs = (
        (q[0], jnp.where(low, q[1], roll64(k[0])), jnp.where(low, v[0], 0.0)),
        (
            jnp.where(low, roll64(q[1]), roll64(q[2])),
            jnp.where(low, roll64(q[2]), k[0]),
            jnp.where(low, roll64(v[0]), 0.0),
        ),
        (q[3], jnp.where(low, q[4], roll64(k[1])), v[1]),
    )
    for head in range(3):
        for place in range(3):
            wq_o[head, :, LANES * place : LANES * (place + 1)] = slabs[head][place].astype(bf16)

    def window(ref, out):
        pieces = [part(ref, LANES * n) for n in range(4)] + [part(ref, 512, 64)]
        before = jnp.zeros_like(pieces[0])
        for n in range(5):
            moved = jnp.where(low, roll64(before), roll64(pieces[n]))
            out[:, LANES * n : LANES * (n + 1)] = jnp.where(first, pieces[n], moved).astype(bf16)
            before = pieces[n]

    window(wo, wo_o)
    window(wd, wd_o)
    for pair in range(4):
        g = [part(gate, 384 * pair + LANES * n) for n in range(3)]
        u = [part(up, 384 * pair + LANES * n) for n in range(3)]
        slabs = (
            (g[0], jnp.where(low, g[1], roll64(u[1])), u[0]),
            (
                jnp.where(low, roll64(g[1]), roll64(g[2])),
                jnp.where(low, roll64(g[2]), u[2]),
                jnp.where(low, roll64(u[1]), roll64(u[2])),
            ),
        )
        for odd in range(2):
            for place in range(3):
                gu_o[2 * pair + odd, :, LANES * place : LANES * (place + 1)] = slabs[odd][
                    place
                ].astype(bf16)


def fast_kernel(
    x_in,
    cot_in,
    ga,
    gf,
    seg,
    wq,
    wk,
    wv,
    wo,
    gate,
    up,
    wd,
    turn_in,
    out_o,
    gin_o,
    gq_o,
    go_o,
    ggu_o,
    gd_o,
    small_o,
    meta_in,
    wq_in,
    wo_in,
    meta_r,
    xo,
    co,
    n1g,
    gfg,
    n2g,
    wq_r,
    wq_w,
    wo_r,
    wo_w,
    gu_r,
    gu_w,
    wd_r,
    wd_w,
    acc,
    qk,
    qt,
    dat,
    kw,
    vw,
    pb0,
    pb1,
    pb2,
    pb3,
    mx,
    segr,
    segc,
    gains,
    at_s,
    at_r,
    hid,
    dhid,
    inner_s,
    dgu_s,
    part_e,
    e2r1,
    e2r2,
    bfr1,
    bfr2,
    da_s,
    da_r,
    d_s,
    dkvt,
    gux_r,
    guz_r,
    guf_r,
    gd_s,
    gdx_r,
    gdz_r,
    gor1,
    gox_r,
    goq_r,
    goz_r,
    gq_r,
    small_s,
    small_r,
    rows_s,
    rows_r,
    ssem,
    rsem,
):
    f32, bf16 = jnp.float32, jnp.bfloat16
    part_f = n2g
    gu_in, wd_in = guf_r, gd_s.at[0, 0]
    e1r1, e1r2 = gfg.at[0], gfg.at[1]
    x = lax.axis_index("dp")
    s = lax.axis_index("seq")
    zh, j = s // 8, s % 8
    zl, y, c = j // 4, (j // 2) % 2, j % 2
    own_chip = zl * 2 + y
    attends = (j != 3) & (j != 5)

    def head_of(device_index):
        high = device_index // 4
        return device_index - high * (1 + (device_index - 2) // 3)

    head_own = head_of(j)
    width = x_in.shape[2]
    counter = [0]
    everyone = pltpu.get_barrier_semaphore()
    for other in range(1, 32):
        there = (x * 16 + s + other) % 32
        pl.semaphore_signal(
            everyone,
            inc=1,
            device_id=(there // 16, there % 16),
            device_id_type=pl.DeviceIdType.MESH,
        )
    prepare(ga, gf, seg, wq, wk, wv, wo, gate, up, wd, meta_in, wq_in, wo_in, gu_in, wd_in)
    pl.semaphore_wait(everyone, 31)
    pending = []

    def index_of(mask):
        return (
            ((1 - zl) if mask & 4 else zl) * 4
            + ((1 - y) if mask & 2 else y) * 2
            + ((1 - c) if mask & 1 else c)
        )

    def device(mask=0, flip_x=False, flip_z=False):
        return (
            (1 - x) if flip_x else x,
            ((1 - zh) if flip_z else zh) * 8 + index_of(mask),
        )

    def fresh():
        counter[0] += 1
        return counter[0] - 1

    def send(src, dst, target, keep=True):
        n = fresh()
        copy = pltpu.make_async_remote_copy(
            src_ref=src,
            dst_ref=dst,
            send_sem=ssem.at[n],
            recv_sem=rsem.at[n],
            device_id=target,
            device_id_type=pl.DeviceIdType.MESH,
        )
        copy.start()
        if keep:
            pending.append(copy)
        return copy

    def mm(a, b):
        return jnp.dot(a, b, preferred_element_type=f32)

    def mm_t(a, b):
        return lax.dot_general(a, b, (((1,), (1,)), ((), ())), preferred_element_type=f32)

    def mm_w(a, b):
        return lax.dot_general(a, b, (((0,), (0,)), ((), ())), preferred_element_type=f32)

    chip_y, chip_z, chip_d = zl * 2 + 1 - y, (1 - zl) * 2 + y, (1 - zl) * 2 + 1 - y

    class Gather:
        def __init__(self, view, pair=True, halves=(True, True)):
            self.view, self.pair, self.halves = view, pair, halves
            self.copies, self.cores = [], []

        def start(self, source=None):
            own = self.view(own_chip)
            source = own if source is None else source
            self.z = self.put(source, own, 4)
            self.y = self.put(source, own, 2)
            if self.pair:
                self.cores.append(self.put(source, own, 1))

        def put(self, source, place, mask):
            copy = send(source, place, device(mask))
            self.copies.append(copy)
            return copy

        def part(self, chip, half):
            view = self.view(chip)
            return view if self.halves[0] != self.halves[1] else view.at[half]

        def from_z(self):
            self.z.wait_recv()
            if self.halves[0]:
                self.zy = self.put(self.part(chip_z, 0), self.part(chip_z, 0), 2)
            if self.pair:
                self.cores.append(self.put(self.view(chip_z), self.view(chip_z), 1))

        def from_y(self):
            self.y.wait_recv()
            if self.halves[1]:
                self.yz = self.put(self.part(chip_y, 1), self.part(chip_y, 1), 4)
            if self.pair:
                self.cores.append(self.put(self.view(chip_y), self.view(chip_y), 1))

        def from_far(self):
            if self.halves[0]:
                self.zy.wait_recv()
            if self.halves[1]:
                self.yz.wait_recv()
            if self.pair:
                self.cores.append(self.put(self.view(chip_d), self.view(chip_d), 1))

        def finish(self):
            for copy in self.cores:
                copy.wait_recv()

        def sent(self):
            for copy in self.copies:
                copy.wait_send()

    def tokens_of(half):
        return lambda chip: n1g.at[half, chip, c]

    x_a = Gather(tokens_of(zh), True, (True, False))
    x_b = Gather(tokens_of(1 - zh), True, (True, False))
    x_a.start(x_in.at[zh])
    x_copy = send(x_in.at[1 - zh], n1g.at[zh, own_chip, c], device(0, False, True))
    meta_copies = []
    for mask in range(8):
        for far in (False, True):
            if mask or far:
                meta_copies.append(send(meta_in, meta_r.at[s], device(mask, False, far)))

    qkv_sem = fresh()
    qkv_first = []
    for far_x in (False, True):
        for far_z in (False, True):
            for piece in range(3):
                n = fresh()
                tx = (1 - x) if far_x else x
                tz = (1 - zh) if far_z else zh
                target = (tx, tz * 8 + 4 * x + piece + x * ((piece + 1) // 2))
                copy = pltpu.make_async_remote_copy(
                    src_ref=wq_in.at[piece],
                    dst_ref=wq_r.at[s],
                    send_sem=ssem.at[n],
                    recv_sem=rsem.at[qkv_sem],
                    device_id=target,
                    device_id_type=pl.DeviceIdType.MESH,
                )
                if far_x or far_z:
                    copy.start()
                    pending.append(copy)
                else:
                    here = j == 4 * x + piece + x * ((piece + 1) // 2)
                    local = pltpu.make_async_copy(
                        wq_in.at[piece], wq_r.at[s], rsem.at[qkv_sem]
                    )
                    pl.when(here)(local.start)
                    pl.when(jnp.logical_not(here))(copy.start)
                    qkv_first.append((here, copy))
    wo_z = send(wo_in, wo_r.at[x, zh, own_chip, c], device(0, False, True))
    wo_r[x, zh, own_chip, c] = wo_in[...]
    wd_r[x, zh] = wd_in[...]
    gu_r[x, zh, j] = gu_in[j]
    meta_r[s] = meta_in[...]
    n1g[zh, own_chip, c] = x_in[zh]
    xo[zh] = x_in[zh]
    co[zh] = cot_in[zh]
    gfg[zh, own_chip, c] = cot_in[zh]
    da_s[...] = jnp.zeros(da_s.shape, bf16)
    wd_w[...] = jnp.zeros(wd_w.shape, bf16)

    def norm_rows(values, gain):
        scale = lax.rsqrt(jnp.mean(values * values, axis=-1, keepdims=True) + EPS)
        return values * scale * gain, scale

    x_copy.wait_recv()
    x_b.start()
    xo[1 - zh] = n1g[1 - zh, own_chip, c]
    x_a.from_z()
    x_a.from_y()
    for copy in meta_copies:
        copy.wait_recv()
    gain_rows = jnp.zeros((8, width), f32)
    seg_rows = jnp.zeros((8, 1024), f32)
    for slot in range(16):
        piece = meta_r[slot]
        wide = jnp.concatenate([piece, jnp.zeros((8, width - LANES), f32)], axis=1)
        gain_rows = gain_rows + pltpu.roll(wide, 72 * slot, 1)
        wide = jnp.concatenate([piece, jnp.zeros((8, 1024 - LANES), f32)], axis=1)
        seg_rows = seg_rows + pltpu.roll(wide, 64 * slot, 1)
    gains[...] = gain_rows
    seg_own = jnp.where(zh == 0, seg_rows[2:3, :], seg_rows[3:4, :])
    seg_wide = jnp.broadcast_to(seg_own, (8, 1024))
    segr[...] = seg_wide
    segc[...] = seg_wide.T

    x_a.from_far()
    x_b.from_z()
    x_b.from_y()
    x_b.from_far()

    def wo_view(chip):
        return wo_r.at[x, :, chip, c]

    def gf_view(chip):
        return gfg.at[:, chip, c]

    def n2_view(chip):
        return n2g.at[:, chip, c]

    wo_z.wait_recv()
    wo_q = Gather(wo_view, False)
    wo_q.start()
    wo_x = [send(wo_view(own_chip), wo_view(own_chip), device(0, True))]

    def spread_rows(read, columns):
        def step(slot, carry):
            acc[pl.ds(pl.multiple_of(slot * 72, 8), 72), 0:columns] = read(slot).astype(f32)
            return carry

        lax.fori_loop(0, 16, step, 0)

    def to_low(store, columns):
        def step(block, carry):
            at = pl.multiple_of(block * 128, 128)
            store(at, acc[pl.ds(at, 128), 0:columns].astype(bf16))
            return carry

        lax.fori_loop(0, 9, step, 0)

    def from_rows(store):
        def step(slot, carry):
            store(slot, pl.multiple_of(slot * 72, 8))
            return carry

        lax.fori_loop(0, 16, step, 0)


    @pl.when(attends)
    def _():
        pltpu.make_async_copy(wq_r, wq_r, rsem.at[qkv_sem]).wait()
        spread_rows(lambda slot: wq_r[slot], 384)

        def store(at, value):
            wq_w[pl.ds(at, 128), :] = value

        to_low(store, 384)

    x_a.finish()
    x_b.finish()
    x_a.sent()
    x_b.sent()
    cot_copy = send(cot_in.at[1 - zh], co.at[zh], device(0, False, True))
    gu_first = []
    for mask in range(1, 8):
        gu_first.append(send(gu_in.at[index_of(mask)], gu_r.at[x, zh, j], device(mask)))
    wd_z = send(wd_in, wd_r.at[x, zh], device(0, False, True))
    wd_x = send(wd_in, wd_r.at[x, zh], device(0, True))

    lane256 = lax.broadcasted_iota(jnp.int32, (1, 256), 1)
    low_half = (lane256 % 64) < 32

    def swap_half(values):
        return jnp.where(low_half, pltpu.roll(values, 256 - 32, 1), pltpu.roll(values, 32, 1))

    def tables(at, rows):
        both = turn_in[pl.ds(at, rows), :]
        first_half = lane256[:, 0:128] < 64
        cosine = jnp.where(first_half, both, roll64(both))
        sine = jnp.where(first_half, roll64(both), both)
        return (
            jnp.concatenate([cosine, cosine], axis=1),
            jnp.concatenate([sine, sine], axis=1),
        )

    @pl.when(attends)
    def _():
        def step(block, carry):
            at = pl.multiple_of(block * 256, 256)
            rows = n1g[block // 2, pl.ds((block % 2) * 2, 2)].reshape(256, width)
            rows, _ = norm_rows(rows.astype(f32), gains[0:1, :])
            rows = rows.astype(bf16)
            n1g[block // 2, pl.ds((block % 2) * 2, 2)] = rows.reshape(2, 2, 64, width)
            raw = mm(rows, wq_w[...])
            cosine, sine = tables(at, 256)
            pair = raw[:, 0:256]
            turned = pair * cosine + swap_half(pair) * sine
            turned = turned.astype(bf16).astype(f32)
            qk[pl.ds(at, 256), :] = turned.astype(bf16)
            qt[:, pl.ds(at, 256)] = turned.T[0:192].astype(bf16)
            values = raw[:, 256:384].astype(bf16).astype(f32)
            values = jnp.concatenate([values, jnp.zeros((256, 128), f32)], axis=1)
            for head in range(3):
                mine = (lane256 // 64) == head
                shift = (64 * (head + 1)) % 256
                kw[head, pl.ds(at, 256), :] = jnp.where(
                    mine, pltpu.roll(turned, shift, 1), 0.0
                ).astype(bf16)
                placed = pltpu.roll(values, 64 * head, 1) if head else values
                vw[head, pl.ds(at, 256), :] = placed.astype(bf16)
            return carry

        lax.fori_loop(0, 4, step, 0)

    pbs = (pb0, pb1, pb2, pb3)
    scale = 1.0 / math.sqrt(HEAD_DIMENSION)

    def attend_block(quarter):
        length = 256 * (quarter + 1)

        def step(sub, carry):
            at = pl.multiple_of(quarter * 256 + sub * 128, 128)
            query = qk[pl.ds(at, 128), :]
            key_pos = lax.broadcasted_iota(jnp.int32, (128, length), 1)
            row_pos = lax.broadcasted_iota(jnp.int32, (128, length), 0) + at
            allowed = (segc[pl.ds(at, 128), 0:1] == segr[0:1, 0:length]) & (key_pos <= row_pos)
            mixed = jnp.zeros((128, 256), f32)
            for head in range(3):
                scores = mm_t(query, kw[head, 0:length, :])
                scores = jnp.where(allowed, scores * scale, NEGATIVE)
                top = jnp.max(scores, axis=-1, keepdims=True)
                weight = jnp.exp(scores - top)
                weight = weight / jnp.sum(weight, axis=-1, keepdims=True)
                low_p = weight.astype(bf16)
                pbs[quarter][head, pl.ds(pl.multiple_of(sub * 128, 128), 128), :] = low_p
                mixed = mixed + mm(low_p, vw[head, 0:length, :])
            mx[pl.ds(at, 128), :] = mixed
            at_s[quarter // 2, pl.ds((quarter % 2) * 4 + sub * 2, 2)] = mixed.astype(
                bf16
            ).reshape(2, 64, 256)
            return carry

        lax.fori_loop(0, 2, step, 0)

    wo_q.from_z()
    wo_x.append(send(wo_view(chip_z), wo_view(chip_z), device(0, True)))
    pl.when(attends)(lambda: attend_block(0))
    wo_q.from_y()
    wo_x.append(send(wo_view(chip_y), wo_view(chip_y), device(0, True)))
    pl.when(attends)(lambda: attend_block(1))
    for copy in gu_first:
        copy.wait_recv()
        copy.wait_send()
    gu_z = []
    for part in range(2):
        rows = gu_r.at[x, zh, 4 * part : 4 * part + 4]
        gu_z.append(send(rows, rows, device(0, False, True)))
    gu_x = [send(gu_r.at[x, zh], gu_r.at[x, zh], device(0, True))]
    pl.when(attends)(lambda: attend_block(2))
    wo_q.from_far()
    wo_x.append(send(wo_view(chip_d), wo_view(chip_d), device(0, True)))
    wo_c = [send(wo_r.at[x, :, :, c], wo_r.at[x, :, :, c], device(1))]
    pl.when(attends)(lambda: attend_block(3))

    at_copies = []
    for mask in range(1, 8):
        n = fresh()
        there = index_of(mask)
        copy = pltpu.make_async_remote_copy(
            src_ref=at_s.at[:, there],
            dst_ref=at_r.at[head_own],
            send_sem=ssem.at[n],
            recv_sem=rsem.at[n],
            device_id=device(mask),
            device_id_type=pl.DeviceIdType.MESH,
        )
        pl.when(attends)(copy.start)
        at_copies.append(((there != 3) & (there != 5), copy))

    @pl.when(attends)
    def _():
        at_r[head_own] = at_s[:, j]

    cot_copy.wait_recv()
    gfg[1 - zh, own_chip, c] = co[1 - zh]
    gf_all = Gather(gf_view)
    gf_all.start()
    for copy in wo_x:
        copy.wait_recv()
    wo_c.append(send(wo_r.at[1 - x, :, :, c], wo_r.at[1 - x, :, :, c], device(1)))
    wd_z.wait_recv()
    wd_f = send(wd_r.at[x, 1 - zh], wd_r.at[x, 1 - zh], device(0, True))
    for copy in wo_c:
        copy.wait_recv()

    def spread_left(slot):
        z_half, chip, core = slot // 8, (slot % 8) // 2, slot % 2
        left = wo_r[0, z_half, chip, core].astype(f32)
        right = wo_r[1, z_half, chip, core, :, 0:128].astype(f32)
        return jnp.concatenate([left[:, 0:512], left[:, 512:640] + right], axis=1)

    def store_left(at, value):
        wo_w[pl.ds(at, 128), 0:640] = value

    spread_rows(spread_left, 640)
    to_low(store_left, 640)

    def store_right(at, value):
        wo_w[pl.ds(at, 128), 640:1152] = value

    spread_rows(lambda slot: wo_r[1, slot // 8, (slot % 8) // 2, slot % 2, :, 128:640], 512)
    to_low(store_right, 512)

    for theirs, copy in at_copies:
        pl.when(theirs)(copy.wait_recv)

    def branch_of():
        total = jnp.zeros((128, width), f32)
        for head in range(6):
            piece = at_r[head].reshape(128, 256)[:, 0:192]
            total = total + mm(piece, wo_w[192 * head : 192 * head + 192, :])
        return total

    branch = branch_of()
    valid = jnp.concatenate(
        [
            (segc[pl.ds(pl.multiple_of(64 * j, 64), 64), 0:1] != 0).astype(f32),
            (segc[pl.ds(pl.multiple_of(512 + 64 * j, 64), 64), 0:1] != 0).astype(f32),
        ],
        axis=0,
    )
    lane1 = lax.broadcasted_iota(jnp.int32, (1, LANES), 1)
    square_attn = jnp.sum(jnp.sum(valid * branch * branch, axis=0, keepdims=True), axis=1, keepdims=True)
    count = jnp.sum(valid, axis=0, keepdims=True)
    hidden = xo[...].reshape(128, width).astype(f32) + branch
    hid[...] = hidden
    normed, _ = norm_rows(hidden, gains[1:2, :])
    n2g[:, own_chip, c] = normed.astype(bf16).reshape(2, 64, width)
    n2_all = Gather(n2_view)
    n2_all.start()
    gf_all.from_z()
    gf_all.from_y()
    for part in range(2):
        gu_z[part].wait_recv()
        rows = gu_r.at[x, 1 - zh, 4 * part : 4 * part + 4]
        gu_x.append(send(rows, rows, device(0, True)))
    gf_all.from_far()
    n2_all.from_z()
    n2_all.from_y()

    wd_x.wait_recv()
    wd_f.wait_recv()
    for copy in gu_x:
        copy.wait_recv()
    for chunk in range(2):
        spread_rows(lambda slot: gu_r[chunk, slot // 8, slot % 8], 384)

        def store_gu(at, value):
            gu_w[chunk, pl.ds(at, 128), :] = value

        to_low(store_gu, 384)
        left, right = wd_r[0, chunk], wd_r[1, chunk]
        wd_w[chunk, 0:192, 0:512] = left[:, 0:512]
        wd_w[chunk, 0:192, 512:640] = (
            left[:, 512:640].astype(f32) + right[:, 0:128].astype(f32)
        ).astype(bf16)
        wd_w[chunk, 0:192, 640:1152] = right[:, 128:640]
    n2_all.from_far()
    gf_all.finish()
    n2_all.finish()

    def chip_at(step):
        return ((zl + step + 1) % 2) * 2 + (y + (3 - step) // 2) % 2

    def pair_copy(ref, got, base, step):
        chip = chip_at(step)
        return pltpu.make_async_remote_copy(
            src_ref=ref.at[:, chip, 1 - c],
            dst_ref=got.at[step],
            send_sem=ssem.at[base + step],
            recv_sem=rsem.at[base + step],
            device_id=device(1),
            device_id_type=pl.DeviceIdType.MESH,
        )

    def side_copy(ref, got2, base, kind):
        step, half, slot, mask = (
            (0, 0, 0, 2),
            (0, 1, 0, 4),
            (1, 0, 1, 2),
            (2, 1, 2, 4),
            (1, 1, 1, 2),
            (2, 0, 2, 4),
        )[kind]
        return pltpu.make_async_remote_copy(
            src_ref=ref.at[half, chip_at(step), c],
            dst_ref=got2.at[slot, half],
            send_sem=ssem.at[base + 4 + kind],
            recv_sem=rsem.at[base + 4 + kind],
            device_id=device(mask),
            device_id_type=pl.DeviceIdType.MESH,
        )

    def pair_sum(ref, got, step):
        chip = chip_at(step)
        return ref[:, chip, c].astype(f32) + got[step].astype(f32)

    def scatter_side(ref, got, got2, base, step):
        pair_copy(ref, got, base, step).wait_recv()
        ref[:, chip_at(step), c] = pair_sum(ref, got, step).astype(bf16)
        for kind in ((0, 1), (2,), (3,))[step]:
            side_copy(ref, got2, base, kind).start()

    def scatter_first(ref, got, got2, compute, sides=True):
        base = counter[0]
        counter[0] += 10

        def step_fn(step, carry):
            chip = chip_at(step)
            block = compute(chip).astype(bf16).reshape(2, 2, 64, width)
            ref[:, chip] = block
            pair_copy(ref, got, base, step).start()
            for done in range(3 if sides else 0):
                pl.when(step == done + 1)(
                    functools.partial(scatter_side, ref, got, got2, base, done)
                )
            return carry

        lax.fori_loop(0, 4, step_fn, 0)
        return base

    def scatter_second(ref, got, got2, base):
        for kind, step, half in ((5, 2, 0), (4, 1, 1)):
            side_copy(ref, got2, base, half).wait_recv()
            chip = chip_at(step)
            total = ref[half, chip, c].astype(f32) + got2[0, half].astype(f32)
            ref[half, chip, c] = total.astype(bf16)
            side_copy(ref, got2, base, kind).start()

    def scatter_finish(ref, got, got2, base):
        pair_copy(ref, got, base, 3).wait_recv()
        total = pair_sum(ref, got, 3)
        for kind in (2, 3, 4, 5):
            side_copy(ref, got2, base, kind).wait_recv()
        total = total + got2[1].astype(f32) + got2[2].astype(f32)
        return total.reshape(128, width)

    def scatter_sent(ref, got, got2, base):
        for step in range(4):
            pair_copy(ref, got, base, step).wait_send()
        for kind in range(6):
            side_copy(ref, got2, base, kind).wait_send()

    lane128 = lax.broadcasted_iota(jnp.int32, (1, LANES), 1)

    def feed_block(chip):
        rows = n2g[:, chip].reshape(256, width)
        grads = gfg[:, chip].reshape(256, width)
        total = jnp.zeros((256, width), f32)
        for chunk in range(2):
            both = mm(rows, gu_w[chunk])
            d_inner = mm_t(grads, wd_w[chunk])
            gate_a, mid, up_a = both[:, 0:128], both[:, 128:256], both[:, 256:384]
            turned = pltpu.roll(mid, 64, 1)
            pieces = []
            for gate, up, back in (
                (gate_a, up_a, d_inner[:, 0:128]),
                (mid, turned, d_inner[:, 128:256]),
            ):
                sig = jax.nn.sigmoid(gate)
                silu = gate * sig
                pieces.append(
                    (silu * up, back * silu, back * up * sig * (1.0 + gate * (1.0 - sig)))
                )
            inner_s[chunk, :, pl.ds(chip * 2, 2), :, 0:128] = (
                pieces[0][0].astype(bf16).reshape(2, 2, 64, 128)
            )
            inner_s[chunk, :, pl.ds(chip * 2, 2), :, 128:256] = (
                jnp.where(lane128 < 64, pieces[1][0], 0.0).astype(bf16).reshape(2, 2, 64, 128)
            )
            gate_low = jnp.where(lane128 < 64, pieces[1][2], 0.0)
            up_low = jnp.where(lane128 < 64, pieces[1][1], 0.0)
            middle = (gate_low + pltpu.roll(up_low, 64, 1)).astype(bf16)
            d_both = jnp.concatenate(
                [pieces[0][2].astype(bf16), middle, pieces[0][1].astype(bf16)], axis=1
            )
            dgu_s[chunk, :, pl.ds(chip * 2, 2)] = d_both.reshape(2, 2, 64, 384)
            total = total + mm_t(d_both, gu_w[chunk])
        return total

    e2_base = scatter_first(part_e, e2r1, e2r2, feed_block)
    scatter_second(part_e, e2r1, e2r2, e2_base)

    for copy in gu_x + gu_z:
        copy.wait_send()
    gf_all.sent()
    for chunk in range(2):
        grads = dgu_s[chunk].reshape(1024, 384)

        def wide_step(block, carry):
            at = pl.multiple_of(block * 128, 128)
            rows = n2g[:, :, :, :, pl.ds(at, 128)].reshape(1024, 128)
            acc[pl.ds(at, 128), 0:384] = mm_w(rows, grads)
            return carry

        lax.fori_loop(0, 9, wide_step, 0)

        def cut(slot, at):
            gu_r[chunk, slot // 8, slot % 8] = acc[pl.ds(at, 72), 0:384].astype(bf16)

        from_rows(cut)
    ggu_x = send(gu_r.at[1 - x], gux_r, device(0, True))

    wd_z.wait_send()
    wd_x.wait_send()

    def down_step(chunk, carry):
        grads = gfg[...].reshape(1024, width)
        piece = mm_w(inner_s[chunk].reshape(1024, 256), grads)
        gd_s[chunk, 0] = piece[0:192, 0:640].astype(bf16)
        gd_s[chunk, 1] = piece[0:192, 512:1152].astype(bf16)
        return carry

    lax.fori_loop(0, 2, down_step, 0)
    ggd_x = send(gd_s.at[:, 1 - x], gdx_r, device(0, True))

    def result_block(chip):
        total = mm(
            inner_s[0, :, pl.ds(chip * 2, 2)].reshape(256, 256), wd_w[0]
        )
        return total + mm(inner_s[1, :, pl.ds(chip * 2, 2)].reshape(256, 256), wd_w[1])

    n2_all.sent()
    bf_base = scatter_first(part_f, bfr1, bfr2, result_block, False)

    e2 = scatter_finish(part_e, e2r1, e2r2, e2_base)
    hidden = hid[...]
    scale2 = lax.rsqrt(jnp.mean(hidden * hidden, axis=-1, keepdims=True) + EPS)
    scaled = e2 * gains[1:2, :]
    inner_mean = jnp.mean(scaled * hidden, axis=-1, keepdims=True)
    gain_feed_row = jnp.sum(e2 * hidden * scale2, axis=0, keepdims=True)
    d_hidden = (
        co[...].reshape(128, width).astype(f32)
        + scale2 * scaled
        - hidden * (scale2 * scale2 * scale2) * inner_mean
    )
    dhid[...] = d_hidden
    d_low = d_hidden.astype(bf16)
    for head in range(6):
        piece = mm_t(d_low, wo_w[192 * head : 192 * head + 192, :])
        da_s[head, :, :, 0:192] = piece.astype(bf16).reshape(2, 64, 192)
    da_copies = []
    for mask in range(1, 8):
        n = fresh()
        there = index_of(mask)
        copy = pltpu.make_async_remote_copy(
            src_ref=da_s.at[head_of(there)],
            dst_ref=da_r.at[:, j],
            send_sem=ssem.at[n],
            recv_sem=rsem.at[n],
            device_id=device(mask),
            device_id_type=pl.DeviceIdType.MESH,
        )
        pl.when((there != 3) & (there != 5))(copy.start)
        da_copies.append(((there != 3) & (there != 5), copy))

    @pl.when(attends)
    def _():
        da_r[:, j] = da_s[head_own]

    for step in range(3):
        scatter_side(part_f, bfr1, bfr2, bf_base, step)
    for copy in wo_c + wo_x:
        copy.wait_send()
    wo_q.sent()
    for plane in range(2):
        for head in range(6):
            piece = at_r[head].reshape(128, 256)[:, 0:192]
            acc[192 * head : 192 * head + 192, :] = mm_w(
                piece, d_low[:, 512 * plane : 512 * plane + 640]
            )

        def cut_out(slot, at):
            wo_r[plane, slot // 8, (slot % 8) // 2, slot % 2] = acc[pl.ds(at, 72), :].astype(bf16)

        from_rows(cut_out)
    go_c = send(wo_r.at[:, :, :, 1 - c], gor1, device(1))

    dkvt[...] = jnp.zeros(dkvt.shape, f32)
    for _, copy in da_copies:
        pl.when(attends)(copy.wait_recv)

    @pl.when(attends)
    def _():
        def step(block, carry):
            at = pl.multiple_of(block * 256, 256)
            rows = da_r[block // 2, pl.ds((block % 2) * 4, 4)].reshape(256, 256)
            dat[:, pl.ds(at, 256)] = rows.astype(f32).T[0:192].astype(bf16)
            return carry

        lax.fori_loop(0, 4, step, 0)

    def back_block(quarter):
        length = 256 * (quarter + 1)

        def step(sub, carry):
            at = pl.multiple_of(quarter * 256 + sub * 128, 128)
            grads = da_r[quarter // 2, pl.ds((quarter % 2) * 4 + sub * 2, 2)].reshape(128, 256)
            products = grads.astype(f32) * mx[pl.ds(at, 128), :]
            d_query = jnp.zeros((128, 256), f32)
            d_key = jnp.zeros((64, length), f32)
            d_value = jnp.zeros((64, length), f32)
            for head in range(3):
                delta = jnp.sum(
                    jnp.where((lane256 // 64) == head, products, 0.0), axis=-1, keepdims=True
                )
                low_p = pbs[quarter][head, pl.ds(pl.multiple_of(sub * 128, 128), 128), :]
                d_p = mm_t(grads, vw[head, 0:length, :])
                d_s_low = (low_p.astype(f32) * (d_p - delta) * scale).astype(bf16)
                d_query = d_query + mm(d_s_low, kw[head, 0:length, :])
                d_key = d_key + mm(qt[64 * head : 64 * head + 64, pl.ds(at, 128)], d_s_low)
                d_value = d_value + mm(dat[64 * head : 64 * head + 64, pl.ds(at, 128)], low_p)
            mx[pl.ds(at, 128), :] = d_query
            dkvt[0:64, 0:length] += d_value
            dkvt[64:128, 0:length] += d_key
            return carry

        lax.fori_loop(0, 2, step, 0)

    pl.when(attends)(lambda: back_block(0))
    scatter_second(part_f, bfr1, bfr2, bf_base)
    go_c.wait_recv()

    def go_add(chip, carry):
        for half in range(2):
            for plane in range(2):
                wo_r[plane, half, chip, c] = (
                    wo_r[plane, half, chip, c].astype(f32) + gor1[plane, half, chip].astype(f32)
                ).astype(bf16)
        return carry

    lax.fori_loop(0, 4, go_add, 0)

    def go_side(chip, half, slot, mask):
        return send(wo_r.at[:, half, chip, c], goq_r.at[slot, half], device(mask))

    def go_sum(half, chip, slot):
        for plane in range(2):
            wo_r[plane, half, chip, c] = (
                wo_r[plane, half, chip, c].astype(f32) + goq_r[slot, half, plane].astype(f32)
            ).astype(bf16)

    go_first = [
        go_side(chip_d, 0, 0, 2),
        go_side(chip_d, 1, 0, 4),
        go_side(chip_y, 0, 1, 2),
        go_side(chip_z, 1, 2, 4),
    ]
    pl.when(attends)(lambda: back_block(1))
    ggu_x.wait_recv()

    def gu_add(slot, carry):
        gu_r[x, slot // 8, slot % 8] = (
            gu_r[x, slot // 8, slot % 8].astype(f32) + gux_r[slot // 8, slot % 8].astype(f32)
        ).astype(bf16)
        return carry

    lax.fori_loop(0, 16, gu_add, 0)
    ggu_z = send(gu_r.at[x, 1 - zh], guz_r, device(0, False, True))
    pl.when(attends)(lambda: back_block(2))
    pl.when(attends)(lambda: back_block(3))

    @pl.when(attends)
    def _():
        def step(block, carry):
            at = pl.multiple_of(block * 256, 256)
            cosine, sine = tables(at, 256)
            turned = dkvt[:, pl.ds(at, 256)].T
            query = mx[pl.ds(at, 256), :]
            pair = jnp.concatenate(
                [query[:, 0:128], jnp.where(lane128 < 64, query[:, 128:256], turned)], axis=1
            )
            back = pair * cosine - swap_half(pair) * sine
            values = jnp.where(lane128 < 64, turned, 0.0)
            both = jnp.concatenate([back.astype(bf16), values.astype(bf16)], axis=1)
            d_s[block // 2, pl.ds((block % 2) * 4, 4)] = both.reshape(4, 64, 384)
            return carry

        lax.fori_loop(0, 4, step, 0)

    @pl.when(jnp.logical_not(attends))
    def _():
        d_s[...] = jnp.zeros(d_s.shape, bf16)
        wq_w[...] = jnp.zeros(wq_w.shape, bf16)

    def input_block(chip):
        return mm_t(d_s[:, pl.ds(chip * 2, 2)].reshape(256, 384), wq_w[...])

    scatter_sent(part_e, e2r1, e2r2, e2_base)
    e1_base = scatter_first(part_e, e1r1, e1r2, input_block)
    gq_send, gq_sem = fresh(), fresh()
    plane_to = zl
    piece_own = head_own - 3 * zl

    def gq_copy(slot):
        return pltpu.make_async_remote_copy(
            src_ref=wq_r.at[slot],
            dst_ref=gq_r.at[x * 2 + zh, piece_own],
            send_sem=ssem.at[gq_send],
            recv_sem=rsem.at[gq_sem],
            device_id=(plane_to, slot),
            device_id_type=pl.DeviceIdType.MESH,
        )

    @pl.when(attends)
    def _():
        grads = d_s[...].reshape(1024, 384)

        def wide_step(block, carry):
            at = pl.multiple_of(block * 128, 128)
            rows = n1g[:, :, :, :, pl.ds(at, 128)].reshape(1024, 128)
            acc[pl.ds(at, 128), 0:384] = mm_w(rows, grads)
            return carry

        lax.fori_loop(0, 9, wide_step, 0)

        def step(slot, carry):
            wq_r[slot] = acc[pl.ds(pl.multiple_of(slot * 72, 8), 72), 0:384].astype(bf16)
            here = (plane_to == x) & (slot == s)

            @pl.when(here)
            def _():
                pltpu.make_async_copy(
                    wq_r.at[slot], gq_r.at[x * 2 + zh, piece_own], rsem.at[gq_sem]
                ).start()

            pl.when(jnp.logical_not(here))(lambda: gq_copy(slot).start())
            return carry

        lax.fori_loop(0, 16, step, 0)

    scatter_second(part_e, e1r1, e1r2, e1_base)

    ggd_x.wait_recv()
    for half in range(2):
        gd_s[half, x] = (gd_s[half, x].astype(f32) + gdx_r[half].astype(f32)).astype(bf16)
    ggd_z = send(gd_s.at[1 - zh, x], gdz_r, device(0, False, True))
    for n, half, chip, mask, slot in ((0, 0, chip_z, 4, 2), (1, 1, chip_y, 2, 1)):
        go_first[n].wait_recv()
        go_sum(half, chip, 0)
        go_first.append(go_side(chip, half, slot, mask))

    branch_feed = scatter_finish(part_f, bfr1, bfr2, bf_base)
    result = hid[...] + branch_feed
    square_feed = jnp.sum(
        jnp.sum(valid * branch_feed * branch_feed, axis=0, keepdims=True), axis=1, keepdims=True
    )
    square_out = jnp.sum(
        jnp.sum(valid * result * result, axis=0, keepdims=True), axis=1, keepdims=True
    )
    rows_s[0] = result.astype(bf16).reshape(2, 64, width)
    ret_out = send(rows_s.at[0, 1 - zh], rows_r.at[0], device(0, False, True))
    out_o[zh] = rows_s[0, zh]

    ggu_z.wait_recv()

    def gu_add2(slot, carry):
        gu_r[x, zh, slot] = (
            gu_r[x, zh, slot].astype(f32) + guz_r[slot].astype(f32)
        ).astype(bf16)
        return carry

    lax.fori_loop(0, 8, gu_add2, 0)
    e1 = scatter_finish(part_e, e1r1, e1r2, e1_base)
    tokens = xo[...].reshape(128, width).astype(f32)
    scale1 = lax.rsqrt(jnp.mean(tokens * tokens, axis=-1, keepdims=True) + EPS)
    scaled = e1 * gains[0:1, :]
    inner_mean = jnp.mean(scaled * tokens, axis=-1, keepdims=True)
    gain_attn_row = jnp.sum(e1 * tokens * scale1, axis=0, keepdims=True)
    grad_rows = (
        dhid[...] + scale1 * scaled - tokens * (scale1 * scale1 * scale1) * inner_mean
    )
    rows_s[1] = grad_rows.astype(bf16).reshape(2, 64, width)
    ret_in = send(rows_s.at[1, 1 - zh], rows_r.at[1], device(0, False, True))
    gin_o[zh] = rows_s[1, zh]

    ggu_q = [
        send(gu_r.at[x, zh, index_of(mask)], guf_r.at[j], device(mask)) for mask in range(1, 8)
    ]
    guf_r[j] = gu_r[x, zh, j]
    total_row = jnp.where(
        lane1 == 0,
        square_attn,
        jnp.where(lane1 == 1, square_feed, jnp.where(lane1 == 2, square_out, count)),
    )
    row8 = lax.broadcasted_iota(jnp.int32, (8, 1), 0)
    both_gains = jnp.where(
        row8 == 0,
        jnp.broadcast_to(gain_attn_row, (8, width)),
        jnp.broadcast_to(gain_feed_row, (8, width)),
    )
    for slot in range(16):
        moved = pltpu.roll(both_gains, (width - 72 * slot) % width, 1) if slot else both_gains
        small_s[slot] = jnp.where(row8 == 2, total_row, moved[:, 0:LANES])
    small_copies = []
    for flip_x in (False, True):
        for flip_z in (False, True):
            for mask in range(8):
                if flip_x or flip_z or mask:
                    target = device(mask, flip_x, flip_z)
                    small_copies.append(
                        send(small_s.at[target[1]], small_r.at[x * 16 + s], target)
                    )
    small_r[x * 16 + s] = small_s[s]

    for copy in go_first[2:]:
        copy.wait_recv()
    for slot in (1, 2):
        for half in range(2):
            go_sum(half, own_chip, slot)
    go_x = send(wo_r.at[1 - x, :, own_chip, c], gox_r, device(0, True))

    go_x.wait_recv()
    for half in range(2):
        wo_r[x, half, own_chip, c] = (
            wo_r[x, half, own_chip, c].astype(f32) + gox_r[half].astype(f32)
        ).astype(bf16)
    go_z = send(wo_r.at[x, 1 - zh, own_chip, c], goz_r, device(0, False, True))
    ggd_z.wait_recv()
    gd_o[...] = gd_s[zh, x].astype(f32) + gdz_r[...].astype(f32)
    for copy in ggu_q:
        copy.wait_recv()
    ggu_o[...] = guf_r[...]
    go_z.wait_recv()
    go_o[...] = wo_r[x, zh, own_chip, c].astype(f32) + goz_r[...].astype(f32)
    ret_out.wait_recv()
    out_o[1 - zh] = rows_r[0]
    pltpu.make_async_copy(gq_r, gq_r, rsem.at[gq_sem]).wait()
    gq_o[...] = (
        (gq_r[0].astype(f32) + gq_r[1].astype(f32)) + (gq_r[2].astype(f32) + gq_r[3].astype(f32))
    )
    for copy in small_copies:
        copy.wait_recv()
    total = small_r[0]
    for slot in range(1, 32):
        total = total + small_r[slot]
    small_o[...] = total
    ret_in.wait_recv()
    gin_o[1 - zh] = rows_r[1]

    waited = {id(copy) for copy in wo_c + wo_x + gu_x + gu_z + gu_first + [wd_z, wd_x]}
    for gather in (wo_q, gf_all, n2_all, x_a, x_b):
        waited |= {id(copy) for copy in gather.copies}
    for copy in pending:
        if id(copy) not in waited:
            copy.wait_send()
    for here, copy in qkv_first:
        pl.when(jnp.logical_not(here))(copy.wait_send)
    for theirs, copy in at_copies:
        pl.when(attends)(copy.wait_send)
    for theirs, copy in da_copies:
        pl.when(theirs)(copy.wait_send)
    scatter_sent(part_f, bfr1, bfr2, bf_base)
    scatter_sent(part_e, e1r1, e1r2, e1_base)

    @pl.when(attends)
    def _():
        def step(slot, carry):
            here = (plane_to == x) & (slot == s)
            pl.when(jnp.logical_not(here))(lambda: gq_copy(slot).wait_send())
            return carry

        lax.fori_loop(0, 16, step, 0)


def finish_kernel(
    out, gin, gq, go, ggu, gd, small,
    out_o, gin_o, gq_o, gk_o, gv_o, go_o, gg_o, gu_o, gd_o, ga_o, gf_o, rm_o,
):
    f32 = jnp.float32
    first = lax.axis_index("dp") == 0
    rows = gq.shape[1]
    low = lax.broadcasted_iota(jnp.int32, (1, LANES), 1) < 64
    out_o[...] = out[...]
    gin_o[...] = gin[...]
    p = [[gq[head, :, LANES * n : LANES * (n + 1)].astype(f32) for n in range(3)] for head in range(3)]
    gq_o[:, 0:128] = p[0][0]
    gq_o[:, 128:256] = jnp.where(low, p[0][1], roll64(p[1][0]))
    gq_o[:, 256:384] = jnp.where(low, roll64(p[1][0]), roll64(p[1][1]))
    gq_o[:, 384:512] = p[2][0]
    gq_o[:, 512:576] = p[2][1][:, 0:64]
    gk_o[:, 0:128] = jnp.where(low, roll64(p[0][1]), p[1][1])
    gk_o[:, 128:192] = roll64(p[2][1])[:, 0:64]
    gv_o[:, 0:128] = jnp.where(low, p[0][2], roll64(p[1][2]))
    gv_o[:, 128:192] = p[2][2][:, 0:64]

    def unwindow(ref, res):
        pieces = [ref[:, LANES * n : LANES * (n + 1)].astype(f32) for n in range(5)]
        for n in range(5):
            after = pieces[min(n + 1, 4)]
            moved = jnp.where(low, roll64(pieces[n]), roll64(after))
            value = jnp.where(first, pieces[n], moved)
            if n < 4:
                res[:, LANES * n : LANES * (n + 1)] = value
            else:
                res[:, 512:576] = value[:, 0:64]

    unwindow(go, go_o)
    unwindow(gd, gd_o)
    for pair in range(4):
        a, b = [
            [ggu[2 * pair + odd, :, LANES * n : LANES * (n + 1)].astype(f32) for n in range(3)]
            for odd in range(2)
        ]
        at = 384 * pair
        gg_o[:, at : at + 128] = a[0]
        gg_o[:, at + 128 : at + 256] = jnp.where(low, a[1], roll64(b[0]))
        gg_o[:, at + 256 : at + 384] = jnp.where(low, roll64(b[0]), roll64(b[1]))
        gu_o[:, at : at + 128] = a[2]
        gu_o[:, at + 128 : at + 256] = jnp.where(low, roll64(a[1]), roll64(b[2]))
        gu_o[:, at + 256 : at + 384] = jnp.where(low, roll64(b[2]), b[1])
    ga_o[...] = small[0:1, 0:rows]
    gf_o[...] = small[1:2, 0:rows]
    width = out.shape[2]
    rm_o[...] = jnp.sqrt(small[2:3, 0:3] / (small[2:3, 3:4] * width))


def fast_device(
    inputs,
    segments,
    weight_query,
    key_weight_matrix,
    value_weight_matrix,
    weight_out,
    weight_gate,
    weight_up,
    weight_down,
    gain_attention,
    gain_feed,
    cotangent,
):
    f32, bf16 = jnp.float32, jnp.bfloat16
    micro, _, rows, width = inputs.shape
    dp = lax.axis_index("dp")
    length = rows * 16
    piece = width // 16

    whole = pl.BlockSpec(memory_space=pltpu.VMEM)
    half = HEAD_DIMENSION // 2
    frequency = THETA ** (-np.arange(half, dtype=np.float32) * np.float32(2.0) / HEAD_DIMENSION)
    angles = np.arange(length, dtype=np.float32)[:, None] * frequency.astype(np.float32)[None, :]
    cosine, sine = np.cos(angles), np.sin(angles)
    turns = np.concatenate([cosine, cosine, -sine, sine], axis=1).astype(np.float32)

    v = pltpu.VMEM
    tok = (2, 4, 2, 64, width)
    scratch = [
        v((8, LANES), f32),
        v((3, piece, 384), bf16),
        v((piece, 640), bf16),
        v((16, 8, LANES), f32),
        v((2, 64, width), bf16),
        v((2, 64, width), bf16),
        v(tok, bf16),
        v(tok, bf16),
        v(tok, bf16),
        v((16, 72, 384), bf16),
        v((width, 384), bf16),
        v((2, 2, 4, 2, 72, 640), bf16),
        v((width, width), bf16),
        v((2, 2, 8, 72, 384), bf16),
        v((2, width, 384), bf16),
        v((2, 2, 192, 640), bf16),
        v((2, 256, width), bf16),
        v((width, 640), f32),
        v((1024, 256), bf16),
        v((192, 1024), bf16),
        v((192, 1024), bf16),
        v((3, 1024, 256), bf16),
        v((3, 1024, 256), bf16),
        v((3, 256, 256), bf16),
        v((3, 256, 512), bf16),
        v((3, 256, 768), bf16),
        v((3, 256, 1024), bf16),
        v((1024, 256), f32),
        v((8, 1024), f32),
        v((1024, 8), f32),
        v((8, width), f32),
        v((2, 8, 64, 256), bf16),
        v((6, 2, 64, 256), bf16),
        v((128, width), f32),
        v((128, width), f32),
        v((2, 2, 8, 64, 256), bf16),
        v((2, 2, 8, 64, 384), bf16),
        v((2, 4, 2, 64, width), bf16),
        v((4, 2, 64, width), bf16),
        v((3, 2, 64, width), bf16),
        v((4, 2, 64, width), bf16),
        v((3, 2, 64, width), bf16),
        v((6, 2, 64, 256), bf16),
        v((2, 8, 64, 256), bf16),
        v((2, 8, 64, 384), bf16),
        v((128, 1024), f32),
        v((2, 8, 72, 384), bf16),
        v((8, 72, 384), bf16),
        v((8, 72, 384), bf16),
        v((2, 2, 192, 640), bf16),
        v((2, 192, 640), bf16),
        v((192, 640), bf16),
        v((2, 2, 4, 72, 640), bf16),
        v((2, 72, 640), bf16),
        v((3, 2, 2, 72, 640), bf16),
        v((72, 640), bf16),
        v((4, 3, 72, 384), bf16),
        v((16, 8, LANES), f32),
        v((32, 8, LANES), f32),
        v((2, 2, 64, width), bf16),
        v((2, 64, width), bf16),
        pltpu.SemaphoreType.DMA((256,)),
        pltpu.SemaphoreType.DMA((256,)),
    ]
    out, gin, gq, go, ggu, gd, small = pl.pallas_call(
        fast_kernel,
        out_shape=(
            jax.ShapeDtypeStruct((2, rows, width), bf16),
            jax.ShapeDtypeStruct((2, rows, width), bf16),
            jax.ShapeDtypeStruct((3, piece, 384), f32),
            jax.ShapeDtypeStruct((piece, 640), f32),
            jax.ShapeDtypeStruct((8, piece, 384), bf16),
            jax.ShapeDtypeStruct((192, 640), f32),
            jax.ShapeDtypeStruct((8, LANES), f32),
        ),
        in_specs=[whole] * 13,
        out_specs=[whole] * 7,
        scratch_shapes=scratch,
        compiler_params=pltpu.CompilerParams(
            has_side_effects=True, collective_id=0, vmem_limit_bytes=62 * 1024 * 1024
        ),
        name="layer",
    )(
        inputs[:, 0],
        cotangent[:, 0],
        gain_attention.reshape(1, piece),
        gain_feed.reshape(1, piece),
        segments[:, 0],
        weight_query,
        key_weight_matrix,
        value_weight_matrix,
        weight_out,
        weight_gate,
        weight_up,
        weight_down,
        jnp.asarray(turns),
    )

    grads = pl.pallas_call(
        finish_kernel,
        out_shape=(
            jax.ShapeDtypeStruct((2, rows, width), bf16),
            jax.ShapeDtypeStruct((2, rows, width), bf16),
            jax.ShapeDtypeStruct(weight_query.shape, f32),
            jax.ShapeDtypeStruct(key_weight_matrix.shape, f32),
            jax.ShapeDtypeStruct(value_weight_matrix.shape, f32),
            jax.ShapeDtypeStruct(weight_out.shape, f32),
            jax.ShapeDtypeStruct(weight_gate.shape, f32),
            jax.ShapeDtypeStruct(weight_up.shape, f32),
            jax.ShapeDtypeStruct(weight_down.shape, f32),
            jax.ShapeDtypeStruct((1, piece), f32),
            jax.ShapeDtypeStruct((1, piece), f32),
            jax.ShapeDtypeStruct((1, 3), f32),
        ),
        in_specs=[whole] * 7,
        out_specs=[whole] * 12,
        name="finish",
    )(out, gin, gq, go, ggu, gd, small)
    return (
        grads[0][:, None],
        grads[1][:, None],
        *grads[2:9],
        grads[9].reshape(piece),
        grads[10].reshape(piece),
        grads[11].reshape(3),
    )


def solution(mesh):
    placed = (
        P(None, "dp", "seq", None),
        P(None, "dp", "seq"),
        P("seq", "dp"),
        P("seq", "dp"),
        P("seq", "dp"),
        P("seq", "dp"),
        P("seq", "dp"),
        P("seq", "dp"),
        P("seq", "dp"),
        P("seq"),
        P("seq"),
        P(None, "dp", "seq", None),
    )
    body = fast_device if dict(mesh.shape) == {"dp": 2, "seq": 16} else per_device
    return jax.shard_map(
        body,
        mesh=mesh,
        in_specs=placed,
        out_specs=(
            P(None, "dp", "seq", None),
            P(None, "dp", "seq", None),
            P("seq", "dp"),
            P("seq", "dp"),
            P("seq", "dp"),
            P("seq", "dp"),
            P("seq", "dp"),
            P("seq", "dp"),
            P("seq", "dp"),
            P("seq"),
            P("seq"),
            P(),
        ),
        check_vma=False,
    )
```

```python
import functools
import math

import jax
import jax.numpy as jnp
import numpy as np
from jax import lax
from jax.experimental import pallas as pl
from jax.experimental.pallas import tpu as pltpu
from jax.sharding import PartitionSpec as P

QUERY_HEADS = 18
KEY_VALUE_HEADS = 6
HEAD_DIMENSION = 64


EPS = 1e-05
THETA = 10000.0
NEGATIVE = -1e30


def rope_tables(positions, head_size):
    half_size = head_size // 2
    frequency = THETA ** (-jnp.arange(half_size, dtype=jnp.float32) * 2.0 / head_size)
    angles = positions.astype(jnp.float32)[:, None] * frequency[None, :]
    angles = jnp.concatenate([angles, angles], axis=1)
    return (jnp.cos(angles), jnp.sin(angles))


def turn_half(values_in):
    half_size = values_in.shape[-1] // 2
    return jnp.concatenate([-values_in[..., half_size:], values_in[..., :half_size]], axis=-1)


def apply_rotation(values_in, cosine_table, sine_values):
    return values_in * cosine_table[:, None, :] + turn_half(values_in) * sine_values[:, None, :]


def reverse_rotation(grads_in, cosine_table, sine_values):
    return grads_in * cosine_table[:, None, :] - turn_half(grads_in * sine_values[:, None, :])


def norm_forward(values_in, gain):
    row_scale = lax.rsqrt(jnp.mean(values_in * values_in, axis=-1, keepdims=True) + EPS)
    return (values_in * row_scale * gain, row_scale)


def norm_backward(values_in, row_scale, gain, grad_normed):
    scaled = grad_normed * gain
    inner_mean = jnp.mean(scaled * values_in, axis=-1, keepdims=True)
    value_gradient_rows = row_scale * scaled - values_in * row_scale**3 * inner_mean
    grad_gain = jnp.sum(grad_normed * values_in * row_scale, axis=(0, 1))
    return (value_gradient_rows, grad_gain)


def apply_projection(acts_low, weight_full):
    return jnp.einsum("std,df->stf", acts_low, weight_full, preferred_element_type=jnp.float32)


def project_back(grads_low, weight_full):
    return jnp.einsum("sta,ba->stb", grads_low, weight_full, preferred_element_type=jnp.float32)


def weight_grad(acts_low, grads_low):
    return jnp.einsum("std,stf->df", acts_low, grads_low, preferred_element_type=jnp.float32)


def gather_all(shards, gain_shards):
    wide = (
        lax.all_gather(shards[0], "dp", axis=1, tiled=True),
        lax.all_gather(shards[1], "dp", axis=1, tiled=True),
        lax.all_gather(shards[2], "dp", axis=1, tiled=True),
        lax.all_gather(shards[3], "dp", axis=1, tiled=True),
        lax.all_gather(shards[4], "dp", axis=1, tiled=True),
        lax.all_gather(shards[5], "dp", axis=1, tiled=True),
        lax.all_gather(shards[6], "dp", axis=1, tiled=True),
    )
    return (
        lax.all_gather(wide[0], "seq", axis=0, tiled=True),
        lax.all_gather(wide[1], "seq", axis=0, tiled=True),
        lax.all_gather(wide[2], "seq", axis=0, tiled=True),
        lax.all_gather(wide[3], "seq", axis=0, tiled=True),
        lax.all_gather(wide[4], "seq", axis=0, tiled=True),
        lax.all_gather(wide[5], "seq", axis=0, tiled=True),
        lax.all_gather(wide[6], "seq", axis=0, tiled=True),
        lax.all_gather(gain_shards[0], "seq", axis=0, tiled=True),
        lax.all_gather(gain_shards[1], "seq", axis=0, tiled=True),
    )


def gather_keys(key_low, value_low, seg_low):
    return (
        lax.all_gather(key_low, "seq", axis=1, tiled=True),
        lax.all_gather(value_low, "seq", axis=1, tiled=True),
        lax.all_gather(seg_low, "seq", axis=1, tiled=True),
    )


def reduce_grads(grads):
    rows = [
        lax.psum_scatter(g.astype(jnp.bfloat16), "seq", scatter_dimension=0, tiled=True)
        for g in grads
    ]
    return tuple(
        lax.psum_scatter(r, "dp", scatter_dimension=1, tiled=True).astype(jnp.float32)
        for r in rows
    )


def block_view(gathered, block_index, key_tile_block):
    block_offset = block_index * key_tile_block
    key_portion = lax.dynamic_slice_in_dim(gathered[0], block_offset, key_tile_block, 1)
    value_portion = lax.dynamic_slice_in_dim(gathered[1], block_offset, key_tile_block, 1)
    seg_part = lax.dynamic_slice_in_dim(gathered[2], block_offset, key_tile_block, 1).astype(
        jnp.float32
    )
    sequence_count = key_portion.shape[0]
    key_portion = key_portion.reshape(
        sequence_count, key_tile_block, KEY_VALUE_HEADS, HEAD_DIMENSION
    )
    value_portion = value_portion.reshape(
        sequence_count, key_tile_block, KEY_VALUE_HEADS, HEAD_DIMENSION
    )
    col_pos = block_offset + jnp.arange(key_tile_block, dtype=jnp.int32)
    return (key_portion, value_portion, seg_part, col_pos)


def masked_scores(query_block_list, key_portion, seg_rows, seg_part, row_pos, col_pos, score_scale):
    raw_scores = jnp.einsum(
        "skgtd,sjkd->skgtj", query_block_list, key_portion, preferred_element_type=jnp.float32
    )
    allowed = (seg_rows[:, :, None] == seg_part[:, None, :]) & (
        col_pos[None, None, :] <= row_pos[None, :, None]
    )
    allowed = allowed[:, None, None, :, :]
    return (jnp.where(allowed, raw_scores * score_scale, NEGATIVE), allowed)


def log_sum(
    query_block_list, gathered, seg_rows, row_pos, block_count, key_tile_block, score_scale
):
    lead_shape = query_block_list.shape[:4]

    def log_step_fn(block_index, carried):
        row_top, row_total = carried
        key_portion, value_portion, seg_part, col_pos = block_view(
            gathered, block_index, key_tile_block
        )
        scores, allowed = masked_scores(
            query_block_list, key_portion, seg_rows, seg_part, row_pos, col_pos, score_scale
        )
        new_top = jnp.maximum(row_top, jnp.max(scores, axis=-1))
        exponent = jnp.where(allowed, jnp.exp(scores - new_top[..., None]), 0.0)
        row_total = row_total * jnp.exp(row_top - new_top) + jnp.sum(exponent, axis=-1)
        return (new_top, row_total)

    start_state = (jnp.full(lead_shape, NEGATIVE, jnp.float32), jnp.zeros(lead_shape, jnp.float32))
    row_top, row_total = lax.fori_loop(0, block_count, log_step_fn, start_state)
    return row_top + jnp.log(row_total)


def attend(
    query_block_list,
    gathered,
    seg_rows,
    row_pos,
    block_count,
    key_tile_block,
    score_scale,
    log_total,
):

    def attend_step_fn(block_index, mixed_heads):
        key_portion, value_portion, seg_part, col_pos = block_view(
            gathered, block_index, key_tile_block
        )
        scores, allowed = masked_scores(
            query_block_list, key_portion, seg_rows, seg_part, row_pos, col_pos, score_scale
        )
        probabilities = jnp.where(allowed, jnp.exp(scores - log_total[..., None]), 0.0).astype(
            jnp.bfloat16
        )
        return mixed_heads + jnp.einsum(
            "skgtj,sjkd->skgtd", probabilities, value_portion, preferred_element_type=jnp.float32
        )

    return lax.fori_loop(
        0, block_count, attend_step_fn, jnp.zeros(query_block_list.shape, jnp.float32)
    )


def query_back(
    query_block_list,
    gathered,
    seg_rows,
    row_pos,
    block_count,
    key_tile_block,
    score_scale,
    log_total,
    gradient_reduced,
    row_delta,
):

    def query_step_fn(block_index, grad_query):
        key_portion, value_portion, seg_part, col_pos = block_view(
            gathered, block_index, key_tile_block
        )
        scores, allowed = masked_scores(
            query_block_list, key_portion, seg_rows, seg_part, row_pos, col_pos, score_scale
        )
        probabilities = jnp.where(allowed, jnp.exp(scores - log_total[..., None]), 0.0)
        grad_probs = jnp.einsum(
            "skgtd,sjkd->skgtj", gradient_reduced, value_portion, preferred_element_type=jnp.float32
        )
        grad_scores = (probabilities * (grad_probs - row_delta[..., None]) * score_scale).astype(
            jnp.bfloat16
        )
        return grad_query + jnp.einsum(
            "skgtj,sjkd->skgtd", grad_scores, key_portion, preferred_element_type=jnp.float32
        )

    return lax.fori_loop(
        0, block_count, query_step_fn, jnp.zeros(query_block_list.shape, jnp.float32)
    )


def key_back(
    key_local,
    value_local,
    seg_rows,
    row_pos,
    query_whole,
    grads_whole,
    stats_whole,
    seg_whole,
    first_block,
    block_count,
    query_tile,
    score_scale,
):
    sequence_count = key_local.shape[0]
    group_width = QUERY_HEADS // KEY_VALUE_HEADS

    def key_step_fn(block_index, carried):
        key_total, value_total = carried
        block_offset = block_index * query_tile
        query_rows = lax.dynamic_slice_in_dim(query_whole, block_offset, query_tile, 1).reshape(
            sequence_count, query_tile, KEY_VALUE_HEADS, group_width, HEAD_DIMENSION
        )
        grad_rows = lax.dynamic_slice_in_dim(grads_whole, block_offset, query_tile, 1).reshape(
            sequence_count, query_tile, KEY_VALUE_HEADS, group_width, HEAD_DIMENSION
        )
        log_rows = lax.dynamic_slice_in_dim(stats_whole[0], block_offset, query_tile, 3)
        delta_rows = lax.dynamic_slice_in_dim(stats_whole[1], block_offset, query_tile, 3)
        seg_query = lax.dynamic_slice_in_dim(seg_whole, block_offset, query_tile, 1).astype(
            jnp.float32
        )
        query_pos = block_offset + jnp.arange(query_tile, dtype=jnp.int32)
        raw_scores = jnp.einsum(
            "stkgd,sjkd->skgtj", query_rows, key_local, preferred_element_type=jnp.float32
        )
        allowed = (seg_query[:, :, None] == seg_rows[:, None, :]) & (
            row_pos[None, None, :] <= query_pos[None, :, None]
        )
        allowed = allowed[:, None, None, :, :]
        scores = jnp.where(allowed, raw_scores * score_scale, NEGATIVE)
        probabilities = jnp.where(allowed, jnp.exp(scores - log_rows[..., None]), 0.0)
        grad_probs = jnp.einsum(
            "stkgd,sjkd->skgtj", grad_rows, value_local, preferred_element_type=jnp.float32
        )
        grad_scores = (probabilities * (grad_probs - delta_rows[..., None]) * score_scale).astype(
            jnp.bfloat16
        )
        key_total = key_total + jnp.einsum(
            "skgtj,stkgd->sjkd", grad_scores, query_rows, preferred_element_type=jnp.float32
        )
        value_total = value_total + jnp.einsum(
            "skgtj,stkgd->sjkd",
            probabilities.astype(jnp.bfloat16),
            grad_rows,
            preferred_element_type=jnp.float32,
        )
        return (key_total, value_total)

    start_state = (jnp.zeros(key_local.shape, jnp.float32), jnp.zeros(key_local.shape, jnp.float32))
    return lax.fori_loop(first_block, block_count, key_step_fn, start_state)


def per_device(
    inputs,
    segments,
    weight_query,
    key_weight_matrix,
    value_weight_matrix,
    weight_out,
    weight_gate,
    weight_up,
    weight_down,
    gain_attention,
    gain_feed,
    cotangent,
):
    shards = (
        weight_query,
        key_weight_matrix,
        value_weight_matrix,
        weight_out,
        weight_gate,
        weight_up,
        weight_down,
    )
    gain_shards = (gain_attention, gain_feed)
    micro_count, sequence_count, token_count, model_width = inputs.shape
    group_width = QUERY_HEADS // KEY_VALUE_HEADS
    score_scale = 1.0 / math.sqrt(HEAD_DIMENSION)
    row_pos = lax.axis_index("seq") * token_count + jnp.arange(token_count, dtype=jnp.int32)
    cosine_table, sine_values = rope_tables(row_pos, HEAD_DIMENSION)
    key_span_length = token_count * lax.axis_size("seq")
    key_tile_block = min(512, key_span_length)
    total_blocks = key_span_length // key_tile_block
    block_count = row_pos[token_count - 1] // key_tile_block + 1
    first_block = row_pos[0] // key_tile_block
    outputs = []
    grad_list = []
    totals = jnp.zeros((4,), jnp.float32)
    gain_grads = jnp.zeros((2, model_width), jnp.float32)
    summed = None
    weights_complete = gather_all(shards, gain_shards)
    for batch_index in range(micro_count):
        tokens = inputs[batch_index].astype(jnp.float32)
        seg_local = segments[batch_index]
        seg_rows = seg_local.astype(jnp.float32)
        seg_low = seg_local.astype(jnp.bfloat16)
        gain_first = weights_complete[7].astype(jnp.float32)
        gain_second = weights_complete[8].astype(jnp.float32)
        norm_first, scale_first = norm_forward(tokens, gain_first)
        normalized = norm_first.astype(jnp.bfloat16)
        query_raw = apply_projection(normalized, weights_complete[0]).reshape(
            sequence_count, token_count, QUERY_HEADS, HEAD_DIMENSION
        )
        query_reduced = apply_rotation(query_raw, cosine_table, sine_values).astype(jnp.bfloat16)
        key_unrotated = apply_projection(normalized, weights_complete[1]).reshape(
            sequence_count, token_count, KEY_VALUE_HEADS, HEAD_DIMENSION
        )
        key_low = (
            apply_rotation(key_unrotated, cosine_table, sine_values)
            .astype(jnp.bfloat16)
            .reshape(sequence_count, token_count, KEY_VALUE_HEADS * HEAD_DIMENSION)
        )
        value_low = apply_projection(normalized, weights_complete[2]).astype(jnp.bfloat16)
        gathered = gather_keys(key_low, value_low, seg_low)
        query_block_list = query_reduced.reshape(
            sequence_count, token_count, KEY_VALUE_HEADS, group_width, HEAD_DIMENSION
        ).transpose(0, 2, 3, 1, 4)
        log_total = log_sum(
            query_block_list, gathered, seg_rows, row_pos, block_count, key_tile_block, score_scale
        )
        mixed_heads = attend(
            query_block_list,
            gathered,
            seg_rows,
            row_pos,
            block_count,
            key_tile_block,
            score_scale,
            log_total,
        )
        attn_low = (
            mixed_heads.transpose(0, 3, 1, 2, 4)
            .reshape(sequence_count, token_count, QUERY_HEADS * HEAD_DIMENSION)
            .astype(jnp.bfloat16)
        )
        branch_attn = apply_projection(attn_low, weights_complete[3])
        hidden = tokens + branch_attn
        norm_second, scale_second = norm_forward(hidden, gain_second)
        normed_second = norm_second.astype(jnp.bfloat16)
        gate_values = apply_projection(normed_second, weights_complete[4])
        up_values = apply_projection(normed_second, weights_complete[5])
        gate_sigmoid = jax.nn.sigmoid(gate_values)
        inner_low = (gate_values * gate_sigmoid * up_values).astype(jnp.bfloat16)
        branch_feed = apply_projection(inner_low, weights_complete[6])
        result = hidden + branch_feed
        outputs.append(result.astype(jnp.bfloat16))
        valid_rows = (seg_local != 0).astype(jnp.float32)[:, :, None]
        totals = totals + jnp.stack(
            [
                jnp.sum(valid_rows * branch_attn * branch_attn),
                jnp.sum(valid_rows * branch_feed * branch_feed),
                jnp.sum(valid_rows * result * result),
                jnp.sum(valid_rows),
            ]
        )
        back_weights = weights_complete
        back_keys = gathered
        grad_result = cotangent[batch_index].astype(jnp.float32)
        grad_feed = grad_result.astype(jnp.bfloat16)
        grad_down = weight_grad(inner_low, grad_feed)
        grad_inner = project_back(grad_feed, back_weights[6])
        grad_up = (grad_inner * gate_values * gate_sigmoid).astype(jnp.bfloat16)
        grad_gate = (
            grad_inner * up_values * gate_sigmoid * (1.0 + gate_values * (1.0 - gate_sigmoid))
        ).astype(jnp.bfloat16)
        grad_gate_w = weight_grad(normed_second, grad_gate)
        grad_up_w = weight_grad(normed_second, grad_up)
        grad_normed_second = project_back(grad_gate, back_weights[4]) + project_back(
            grad_up, back_weights[5]
        )
        grad_hidden_norm, grad_gain_second = norm_backward(
            hidden, scale_second, gain_second, grad_normed_second
        )
        grad_hidden = grad_result + grad_hidden_norm
        grad_branch = grad_hidden.astype(jnp.bfloat16)
        grad_out_w = weight_grad(attn_low, grad_branch)
        mixed_gradient = project_back(grad_branch, back_weights[3]).astype(jnp.bfloat16)
        gradient_reduced = mixed_gradient.reshape(
            sequence_count, token_count, KEY_VALUE_HEADS, group_width, HEAD_DIMENSION
        ).transpose(0, 2, 3, 1, 4)
        row_delta = jnp.sum(gradient_reduced.astype(jnp.float32) * mixed_heads, axis=-1)
        grad_query = query_back(
            query_block_list,
            back_keys,
            seg_rows,
            row_pos,
            block_count,
            key_tile_block,
            score_scale,
            log_total,
            gradient_reduced,
            row_delta,
        )
        query_flat = query_reduced.reshape(
            sequence_count, token_count, QUERY_HEADS * HEAD_DIMENSION
        )
        query_whole, grads_whole = (
            lax.all_gather(query_flat, "seq", axis=1, tiled=True),
            lax.all_gather(mixed_gradient, "seq", axis=1, tiled=True),
        )
        stats_whole = (
            lax.all_gather(log_total, "seq", axis=3, tiled=True),
            lax.all_gather(row_delta, "seq", axis=3, tiled=True),
        )
        key_local = key_low.reshape(sequence_count, token_count, KEY_VALUE_HEADS, HEAD_DIMENSION)
        value_local = value_low.reshape(
            sequence_count, token_count, KEY_VALUE_HEADS, HEAD_DIMENSION
        )
        key_total, value_total = key_back(
            key_local,
            value_local,
            seg_rows,
            row_pos,
            query_whole,
            grads_whole,
            stats_whole,
            back_keys[2],
            first_block,
            total_blocks,
            key_tile_block,
            score_scale,
        )
        key_grad_low = (
            reverse_rotation(key_total, cosine_table, sine_values)
            .reshape(sequence_count, token_count, KEY_VALUE_HEADS * HEAD_DIMENSION)
            .astype(jnp.bfloat16)
        )
        value_grad_low = value_total.reshape(
            sequence_count, token_count, KEY_VALUE_HEADS * HEAD_DIMENSION
        ).astype(jnp.bfloat16)
        query_grad = grad_query.transpose(0, 3, 1, 2, 4).reshape(
            sequence_count, token_count, QUERY_HEADS, HEAD_DIMENSION
        )
        query_grad_low = (
            reverse_rotation(query_grad, cosine_table, sine_values)
            .reshape(sequence_count, token_count, QUERY_HEADS * HEAD_DIMENSION)
            .astype(jnp.bfloat16)
        )
        grad_normed = (
            project_back(query_grad_low, back_weights[0])
            + project_back(key_grad_low, back_weights[1])
            + project_back(value_grad_low, back_weights[2])
        )
        grad_token_norm, grad_gain_first = norm_backward(
            tokens, scale_first, gain_first, grad_normed
        )
        grad_list.append((grad_hidden + grad_token_norm).astype(jnp.bfloat16))
        gain_grads = gain_grads + jnp.stack([grad_gain_first, grad_gain_second])
        batch_grads = (
            weight_grad(normalized, query_grad_low),
            weight_grad(normalized, key_grad_low),
            weight_grad(normalized, value_grad_low),
            grad_out_w,
            grad_gate_w,
            grad_up_w,
            grad_down,
        )
        summed = batch_grads if summed is None else jax.tree.map(jnp.add, summed, batch_grads)
    reduced = reduce_grads(summed)
    gain_total, totals = lax.psum((gain_grads, totals), ("dp", "seq"))
    piece_width = model_width // lax.axis_size("seq")
    gain_part = lax.dynamic_slice_in_dim(
        gain_total, lax.axis_index("seq") * piece_width, piece_width, 1
    )
    root_means = jnp.sqrt(totals[:3] / (totals[3] * model_width))
    return (
        jnp.stack(outputs),
        jnp.stack(grad_list),
        reduced[0],
        reduced[1],
        reduced[2],
        reduced[3],
        reduced[4],
        reduced[5],
        reduced[6],
        gain_part[0],
        gain_part[1],
        root_means,
    )


LANES = 128


def roll64(values):
    return pltpu.roll(values, 64, 1)


def prepare(
    ga, gf, seg, wq, wk, wv, wo, gate, up, wd, meta_o, wq_o, wo_o, gu_o, wd_o
):
    f32, bf16 = jnp.float32, jnp.bfloat16
    first = lax.axis_index("dp") == 0
    rows = wq.shape[0]
    low = lax.broadcasted_iota(jnp.int32, (1, LANES), 1) < 64
    meta_o[...] = jnp.zeros(meta_o.shape, f32)
    meta_o[0:1, 0:rows] = ga[...].astype(f32)
    meta_o[1:2, 0:rows] = gf[...].astype(f32)
    meta_o[2:4, 0:64] = seg[...].astype(f32)

    def part(ref, at, size=LANES):
        values = ref[:, at : at + size].astype(f32)
        if size < LANES:
            values = jnp.concatenate(
                [values, jnp.zeros((values.shape[0], LANES - size), f32)], axis=1
            )
        return values

    q = [part(wq, LANES * n) for n in range(4)] + [part(wq, 512, 64)]
    k = [part(wk, 0), part(wk, LANES, 64)]
    v = [part(wv, 0), part(wv, LANES, 64)]
    slabs = (
        (q[0], jnp.where(low, q[1], roll64(k[0])), jnp.where(low, v[0], 0.0)),
        (
            jnp.where(low, roll64(q[1]), roll64(q[2])),
            jnp.where(low, roll64(q[2]), k[0]),
            jnp.where(low, roll64(v[0]), 0.0),
        ),
        (q[3], jnp.where(low, q[4], roll64(k[1])), v[1]),
    )
    for head in range(3):
        for place in range(3):
            wq_o[head, :, LANES * place : LANES * (place + 1)] = slabs[head][place].astype(bf16)

    def window(ref, out):
        pieces = [part(ref, LANES * n) for n in range(4)] + [part(ref, 512, 64)]
        before = jnp.zeros_like(pieces[0])
        for n in range(5):
            moved = jnp.where(low, roll64(before), roll64(pieces[n]))
            out[:, LANES * n : LANES * (n + 1)] = jnp.where(first, pieces[n], moved).astype(bf16)
            before = pieces[n]

    window(wo, wo_o)
    window(wd, wd_o)
    for pair in range(4):
        g = [part(gate, 384 * pair + LANES * n) for n in range(3)]
        u = [part(up, 384 * pair + LANES * n) for n in range(3)]
        slabs = (
            (g[0], jnp.where(low, g[1], roll64(u[1])), u[0]),
            (
                jnp.where(low, roll64(g[1]), roll64(g[2])),
                jnp.where(low, roll64(g[2]), u[2]),
                jnp.where(low, roll64(u[1]), roll64(u[2])),
            ),
        )
        for odd in range(2):
            for place in range(3):
                gu_o[2 * pair + odd, :, LANES * place : LANES * (place + 1)] = slabs[odd][
                    place
                ].astype(bf16)


def fast_kernel(
    x_in,
    cot_in,
    ga,
    gf,
    seg,
    wq,
    wk,
    wv,
    wo,
    gate,
    up,
    wd,
    turn_in,
    out_o,
    gin_o,
    gq_o,
    go_o,
    ggu_o,
    gd_o,
    small_o,
    meta_in,
    wq_in,
    wo_in,
    meta_r,
    xo,
    co,
    n1g,
    gfg,
    n2g,
    wq_r,
    wq_w,
    wo_r,
    wo_w,
    gu_r,
    gu_w,
    wd_r,
    wd_w,
    acc,
    qk,
    qt,
    dat,
    kw,
    vw,
    pb0,
    pb1,
    pb2,
    pb3,
    mx,
    segr,
    segc,
    gains,
    at_s,
    at_r,
    hid,
    dhid,
    inner_s,
    dgu_s,
    part_e,
    e2r1,
    e2r2,
    bfr1,
    bfr2,
    da_s,
    da_r,
    d_s,
    dkvt,
    gux_r,
    guz_r,
    guf_r,
    gd_s,
    gdx_r,
    gdz_r,
    gor1,
    gox_r,
    goq_r,
    goz_r,
    gq_r,
    small_s,
    small_r,
    rows_s,
    rows_r,
    ssem,
    rsem,
):
    f32, bf16 = jnp.float32, jnp.bfloat16
    part_f = n2g
    gu_in, wd_in = guf_r, gd_s.at[0, 0]
    e1r1, e1r2 = gfg.at[0], gfg.at[1]
    x = lax.axis_index("dp")
    s = lax.axis_index("seq")
    zh, j = s // 8, s % 8
    zl, y, c = j // 4, (j // 2) % 2, j % 2
    own_chip = zl * 2 + y
    attends = (j != 3) & (j != 5)

    def head_of(device_index):
        high = device_index // 4
        return device_index - high * (1 + (device_index - 2) // 3)

    head_own = head_of(j)
    width = x_in.shape[2]
    counter = [0]
    everyone = pltpu.get_barrier_semaphore()
    for other in range(1, 32):
        there = (x * 16 + s + other) % 32
        pl.semaphore_signal(
            everyone,
            inc=1,
            device_id=(there // 16, there % 16),
            device_id_type=pl.DeviceIdType.MESH,
        )
    prepare(ga, gf, seg, wq, wk, wv, wo, gate, up, wd, meta_in, wq_in, wo_in, gu_in, wd_in)
    pl.semaphore_wait(everyone, 31)
    pending = []

    def index_of(mask):
        return (
            ((1 - zl) if mask & 4 else zl) * 4
            + ((1 - y) if mask & 2 else y) * 2
            + ((1 - c) if mask & 1 else c)
        )

    def device(mask=0, flip_x=False, flip_z=False):
        return (
            (1 - x) if flip_x else x,
            ((1 - zh) if flip_z else zh) * 8 + index_of(mask),
        )

    def fresh():
        counter[0] += 1
        return counter[0] - 1

    def send(src, dst, target, keep=True):
        n = fresh()
        copy = pltpu.make_async_remote_copy(
            src_ref=src,
            dst_ref=dst,
            send_sem=ssem.at[n],
            recv_sem=rsem.at[n],
            device_id=target,
            device_id_type=pl.DeviceIdType.MESH,
        )
        copy.start()
        if keep:
            pending.append(copy)
        return copy

    def mm(a, b):
        return jnp.dot(a, b, preferred_element_type=f32)

    def mm_t(a, b):
        return lax.dot_general(a, b, (((1,), (1,)), ((), ())), preferred_element_type=f32)

    def mm_w(a, b):
        return lax.dot_general(a, b, (((0,), (0,)), ((), ())), preferred_element_type=f32)

    chip_y, chip_z, chip_d = zl * 2 + 1 - y, (1 - zl) * 2 + y, (1 - zl) * 2 + 1 - y

    class Gather:
        def __init__(self, view, pair=True, halves=(True, True)):
            self.view, self.pair, self.halves = view, pair, halves
            self.copies, self.cores = [], []

        def start(self, source=None):
            own = self.view(own_chip)
            source = own if source is None else source
            self.z = self.put(source, own, 4)
            self.y = self.put(source, own, 2)
            if self.pair:
                self.cores.append(self.put(source, own, 1))

        def put(self, source, place, mask):
            copy = send(source, place, device(mask))
            self.copies.append(copy)
            return copy

        def part(self, chip, half):
            view = self.view(chip)
            return view if self.halves[0] != self.halves[1] else view.at[half]

        def from_z(self):
            self.z.wait_recv()
            if self.halves[0]:
                self.zy = self.put(self.part(chip_z, 0), self.part(chip_z, 0), 2)
            if self.pair:
                self.cores.append(self.put(self.view(chip_z), self.view(chip_z), 1))

        def from_y(self):
            self.y.wait_recv()
            if self.halves[1]:
                self.yz = self.put(self.part(chip_y, 1), self.part(chip_y, 1), 4)
            if self.pair:
                self.cores.append(self.put(self.view(chip_y), self.view(chip_y), 1))

        def from_far(self):
            if self.halves[0]:
                self.zy.wait_recv()
            if self.halves[1]:
                self.yz.wait_recv()
            if self.pair:
                self.cores.append(self.put(self.view(chip_d), self.view(chip_d), 1))

        def finish(self):
            for copy in self.cores:
                copy.wait_recv()

        def sent(self):
            for copy in self.copies:
                copy.wait_send()

    def tokens_of(half):
        return lambda chip: n1g.at[half, chip, c]

    x_a = Gather(tokens_of(zh), True, (True, False))
    x_b = Gather(tokens_of(1 - zh), True, (True, False))
    x_a.start(x_in.at[zh])
    x_copy = send(x_in.at[1 - zh], n1g.at[zh, own_chip, c], device(0, False, True))
    meta_copies = []
    for mask in range(8):
        for far in (False, True):
            if mask or far:
                meta_copies.append(send(meta_in, meta_r.at[s], device(mask, False, far)))

    qkv_sem = fresh()
    qkv_first = []
    for far_x in (False, True):
        for far_z in (False, True):
            for piece in range(3):
                n = fresh()
                tx = (1 - x) if far_x else x
                tz = (1 - zh) if far_z else zh
                target = (tx, tz * 8 + 4 * x + piece + x * ((piece + 1) // 2))
                copy = pltpu.make_async_remote_copy(
                    src_ref=wq_in.at[piece],
                    dst_ref=wq_r.at[s],
                    send_sem=ssem.at[n],
                    recv_sem=rsem.at[qkv_sem],
                    device_id=target,
                    device_id_type=pl.DeviceIdType.MESH,
                )
                if far_x or far_z:
                    copy.start()
                    pending.append(copy)
                else:
                    here = j == 4 * x + piece + x * ((piece + 1) // 2)
                    local = pltpu.make_async_copy(
                        wq_in.at[piece], wq_r.at[s], rsem.at[qkv_sem]
                    )
                    pl.when(here)(local.start)
                    pl.when(jnp.logical_not(here))(copy.start)
                    qkv_first.append((here, copy))
    wo_z = send(wo_in, wo_r.at[x, zh, own_chip, c], device(0, False, True))
    wo_r[x, zh, own_chip, c] = wo_in[...]
    wd_r[x, zh] = wd_in[...]
    gu_r[x, zh, j] = gu_in[j]
    meta_r[s] = meta_in[...]
    n1g[zh, own_chip, c] = x_in[zh]
    xo[zh] = x_in[zh]
    co[zh] = cot_in[zh]
    gfg[zh, own_chip, c] = cot_in[zh]
    da_s[...] = jnp.zeros(da_s.shape, bf16)
    wd_w[...] = jnp.zeros(wd_w.shape, bf16)

    def norm_rows(values, gain):
        scale = lax.rsqrt(jnp.mean(values * values, axis=-1, keepdims=True) + EPS)
        return values * scale * gain, scale

    x_copy.wait_recv()
    x_b.start()
    xo[1 - zh] = n1g[1 - zh, own_chip, c]
    x_a.from_z()
    x_a.from_y()
    for copy in meta_copies:
        copy.wait_recv()
    gain_rows = jnp.zeros((8, width), f32)
    seg_rows = jnp.zeros((8, 1024), f32)
    for slot in range(16):
        piece = meta_r[slot]
        wide = jnp.concatenate([piece, jnp.zeros((8, width - LANES), f32)], axis=1)
        gain_rows = gain_rows + pltpu.roll(wide, 72 * slot, 1)
        wide = jnp.concatenate([piece, jnp.zeros((8, 1024 - LANES), f32)], axis=1)
        seg_rows = seg_rows + pltpu.roll(wide, 64 * slot, 1)
    gains[...] = gain_rows
    seg_own = jnp.where(zh == 0, seg_rows[2:3, :], seg_rows[3:4, :])
    seg_wide = jnp.broadcast_to(seg_own, (8, 1024))
    segr[...] = seg_wide
    segc[...] = seg_wide.T

    x_a.from_far()
    x_b.from_z()
    x_b.from_y()
    x_b.from_far()

    def wo_view(chip):
        return wo_r.at[x, :, chip, c]

    def gf_view(chip):
        return gfg.at[:, chip, c]

    def n2_view(chip):
        return n2g.at[:, chip, c]

    wo_z.wait_recv()
    wo_q = Gather(wo_view, False)
    wo_q.start()
    wo_x = [send(wo_view(own_chip), wo_view(own_chip), device(0, True))]

    def spread_rows(read, columns):
        def step(slot, carry):
            acc[pl.ds(pl.multiple_of(slot * 72, 8), 72), 0:columns] = read(slot).astype(f32)
            return carry

        lax.fori_loop(0, 16, step, 0)

    def to_low(store, columns):
        def step(block, carry):
            at = pl.multiple_of(block * 128, 128)
            store(at, acc[pl.ds(at, 128), 0:columns].astype(bf16))
            return carry

        lax.fori_loop(0, 9, step, 0)

    def from_rows(store):
        def step(slot, carry):
            store(slot, pl.multiple_of(slot * 72, 8))
            return carry

        lax.fori_loop(0, 16, step, 0)


    @pl.when(attends)
    def _():
        pltpu.make_async_copy(wq_r, wq_r, rsem.at[qkv_sem]).wait()
        spread_rows(lambda slot: wq_r[slot], 384)

        def store(at, value):
            wq_w[pl.ds(at, 128), :] = value

        to_low(store, 384)

    x_a.finish()
    x_b.finish()
    x_a.sent()
    x_b.sent()
    cot_copy = send(cot_in.at[1 - zh], co.at[zh], device(0, False, True))
    gu_first = []
    for mask in range(1, 8):
        gu_first.append(send(gu_in.at[index_of(mask)], gu_r.at[x, zh, j], device(mask)))
    wd_z = send(wd_in, wd_r.at[x, zh], device(0, False, True))
    wd_x = send(wd_in, wd_r.at[x, zh], device(0, True))

    lane256 = lax.broadcasted_iota(jnp.int32, (1, 256), 1)
    low_half = (lane256 % 64) < 32

    def swap_half(values):
        return jnp.where(low_half, pltpu.roll(values, 256 - 32, 1), pltpu.roll(values, 32, 1))

    def tables(at, rows):
        both = turn_in[pl.ds(at, rows), :]
        first_half = lane256[:, 0:128] < 64
        cosine = jnp.where(first_half, both, roll64(both))
        sine = jnp.where(first_half, roll64(both), both)
        return (
            jnp.concatenate([cosine, cosine], axis=1),
            jnp.concatenate([sine, sine], axis=1),
        )

    @pl.when(attends)
    def _():
        def step(block, carry):
            at = pl.multiple_of(block * 256, 256)
            rows = n1g[block // 2, pl.ds((block % 2) * 2, 2)].reshape(256, width)
            rows, _ = norm_rows(rows.astype(f32), gains[0:1, :])
            rows = rows.astype(bf16)
            n1g[block // 2, pl.ds((block % 2) * 2, 2)] = rows.reshape(2, 2, 64, width)
            raw = mm(rows, wq_w[...])
            cosine, sine = tables(at, 256)
            pair = raw[:, 0:256]
            turned = pair * cosine + swap_half(pair) * sine
            turned = turned.astype(bf16).astype(f32)
            qk[pl.ds(at, 256), :] = turned.astype(bf16)
            qt[:, pl.ds(at, 256)] = turned.T[0:192].astype(bf16)
            values = raw[:, 256:384].astype(bf16).astype(f32)
            values = jnp.concatenate([values, jnp.zeros((256, 128), f32)], axis=1)
            for head in range(3):
                mine = (lane256 // 64) == head
                shift = (64 * (head + 1)) % 256
                kw[head, pl.ds(at, 256), :] = jnp.where(
                    mine, pltpu.roll(turned, shift, 1), 0.0
                ).astype(bf16)
                placed = pltpu.roll(values, 64 * head, 1) if head else values
                vw[head, pl.ds(at, 256), :] = placed.astype(bf16)
            return carry

        lax.fori_loop(0, 4, step, 0)

    pbs = (pb0, pb1, pb2, pb3)
    scale = 1.0 / math.sqrt(HEAD_DIMENSION)

    def attend_block(quarter):
        length = 256 * (quarter + 1)

        def step(sub, carry):
            at = pl.multiple_of(quarter * 256 + sub * 128, 128)
            query = qk[pl.ds(at, 128), :]
            key_pos = lax.broadcasted_iota(jnp.int32, (128, length), 1)
            row_pos = lax.broadcasted_iota(jnp.int32, (128, length), 0) + at
            allowed = (segc[pl.ds(at, 128), 0:1] == segr[0:1, 0:length]) & (key_pos <= row_pos)
            mixed = jnp.zeros((128, 256), f32)
            for head in range(3):
                scores = mm_t(query, kw[head, 0:length, :])
                scores = jnp.where(allowed, scores * scale, NEGATIVE)
                top = jnp.max(scores, axis=-1, keepdims=True)
                weight = jnp.exp(scores - top)
                weight = weight / jnp.sum(weight, axis=-1, keepdims=True)
                low_p = weight.astype(bf16)
                pbs[quarter][head, pl.ds(pl.multiple_of(sub * 128, 128), 128), :] = low_p
                mixed = mixed + mm(low_p, vw[head, 0:length, :])
            mx[pl.ds(at, 128), :] = mixed
            at_s[quarter // 2, pl.ds((quarter % 2) * 4 + sub * 2, 2)] = mixed.astype(
                bf16
            ).reshape(2, 64, 256)
            return carry

        lax.fori_loop(0, 2, step, 0)

    wo_q.from_z()
    wo_x.append(send(wo_view(chip_z), wo_view(chip_z), device(0, True)))
    pl.when(attends)(lambda: attend_block(0))
    wo_q.from_y()
    wo_x.append(send(wo_view(chip_y), wo_view(chip_y), device(0, True)))
    pl.when(attends)(lambda: attend_block(1))
    for copy in gu_first:
        copy.wait_recv()
        copy.wait_send()
    gu_z = []
    for part in range(2):
        rows = gu_r.at[x, zh, 4 * part : 4 * part + 4]
        gu_z.append(send(rows, rows, device(0, False, True)))
    gu_x = [send(gu_r.at[x, zh], gu_r.at[x, zh], device(0, True))]
    pl.when(attends)(lambda: attend_block(2))
    wo_q.from_far()
    wo_x.append(send(wo_view(chip_d), wo_view(chip_d), device(0, True)))
    wo_c = [send(wo_r.at[x, :, :, c], wo_r.at[x, :, :, c], device(1))]
    pl.when(attends)(lambda: attend_block(3))

    at_copies = []
    for mask in (6, 7, 4, 5, 2, 3, 1):
        n = fresh()
        there = index_of(mask)
        copy = pltpu.make_async_remote_copy(
            src_ref=at_s.at[:, there],
            dst_ref=at_r.at[head_own],
            send_sem=ssem.at[n],
            recv_sem=rsem.at[n],
            device_id=device(mask),
            device_id_type=pl.DeviceIdType.MESH,
        )
        pl.when(attends)(copy.start)
        at_copies.append(((there != 3) & (there != 5), copy))

    @pl.when(attends)
    def _():
        at_r[head_own] = at_s[:, j]

    cot_copy.wait_recv()
    gfg[1 - zh, own_chip, c] = co[1 - zh]
    gf_all = Gather(gf_view)
    gf_all.start()
    for copy in wo_x:
        copy.wait_recv()
    wo_c.append(send(wo_r.at[1 - x, :, :, c], wo_r.at[1 - x, :, :, c], device(1)))
    wd_z.wait_recv()
    wd_f = send(wd_r.at[x, 1 - zh], wd_r.at[x, 1 - zh], device(0, True))
    for copy in wo_c:
        copy.wait_recv()

    def spread_left(slot):
        z_half, chip, core = slot // 8, (slot % 8) // 2, slot % 2
        left = wo_r[0, z_half, chip, core].astype(f32)
        right = wo_r[1, z_half, chip, core, :, 0:128].astype(f32)
        return jnp.concatenate([left[:, 0:512], left[:, 512:640] + right], axis=1)

    def store_left(at, value):
        wo_w[pl.ds(at, 128), 0:640] = value

    spread_rows(spread_left, 640)
    to_low(store_left, 640)

    def store_right(at, value):
        wo_w[pl.ds(at, 128), 640:1152] = value

    spread_rows(lambda slot: wo_r[1, slot // 8, (slot % 8) // 2, slot % 2, :, 128:640], 512)
    to_low(store_right, 512)

    for theirs, copy in at_copies:
        pl.when(theirs)(copy.wait_recv)

    def branch_of():
        total = jnp.zeros((128, width), f32)
        for head in range(6):
            piece = at_r[head].reshape(128, 256)[:, 0:192]
            total = total + mm(piece, wo_w[192 * head : 192 * head + 192, :])
        return total

    branch = branch_of()
    valid = jnp.concatenate(
        [
            (segc[pl.ds(pl.multiple_of(64 * j, 64), 64), 0:1] != 0).astype(f32),
            (segc[pl.ds(pl.multiple_of(512 + 64 * j, 64), 64), 0:1] != 0).astype(f32),
        ],
        axis=0,
    )
    lane1 = lax.broadcasted_iota(jnp.int32, (1, LANES), 1)
    square_attn = jnp.sum(jnp.sum(valid * branch * branch, axis=0, keepdims=True), axis=1, keepdims=True)
    count = jnp.sum(valid, axis=0, keepdims=True)
    hidden = xo[...].reshape(128, width).astype(f32) + branch
    hid[...] = hidden
    normed, _ = norm_rows(hidden, gains[1:2, :])
    n2g[:, own_chip, c] = normed.astype(bf16).reshape(2, 64, width)
    n2_all = Gather(n2_view)
    n2_all.start()
    gf_all.from_z()
    gf_all.from_y()
    for part in range(2):
        gu_z[part].wait_recv()
        rows = gu_r.at[x, 1 - zh, 4 * part : 4 * part + 4]
        gu_x.append(send(rows, rows, device(0, True)))
    gf_all.from_far()
    n2_all.from_z()
    n2_all.from_y()

    wd_x.wait_recv()
    wd_f.wait_recv()
    for copy in gu_x:
        copy.wait_recv()
    for chunk in range(2):
        spread_rows(lambda slot: gu_r[chunk, slot // 8, slot % 8], 384)

        def store_gu(at, value):
            gu_w[chunk, pl.ds(at, 128), :] = value

        to_low(store_gu, 384)
        left, right = wd_r[0, chunk], wd_r[1, chunk]
        wd_w[chunk, 0:192, 0:512] = left[:, 0:512]
        wd_w[chunk, 0:192, 512:640] = (
            left[:, 512:640].astype(f32) + right[:, 0:128].astype(f32)
        ).astype(bf16)
        wd_w[chunk, 0:192, 640:1152] = right[:, 128:640]
    n2_all.from_far()
    gf_all.finish()
    n2_all.finish()

    def chip_at(step):
        return ((zl + step + 1) % 2) * 2 + (y + (3 - step) // 2) % 2

    def pair_copy(ref, got, base, step):
        chip = chip_at(step)
        return pltpu.make_async_remote_copy(
            src_ref=ref.at[:, chip, 1 - c],
            dst_ref=got.at[step],
            send_sem=ssem.at[base + step],
            recv_sem=rsem.at[base + step],
            device_id=device(1),
            device_id_type=pl.DeviceIdType.MESH,
        )

    def side_copy(ref, got2, base, kind):
        step, half, slot, mask = (
            (0, 0, 0, 2),
            (0, 1, 0, 4),
            (1, 0, 1, 2),
            (2, 1, 2, 4),
            (1, 1, 1, 2),
            (2, 0, 2, 4),
        )[kind]
        return pltpu.make_async_remote_copy(
            src_ref=ref.at[half, chip_at(step), c],
            dst_ref=got2.at[slot, half],
            send_sem=ssem.at[base + 4 + kind],
            recv_sem=rsem.at[base + 4 + kind],
            device_id=device(mask),
            device_id_type=pl.DeviceIdType.MESH,
        )

    def pair_sum(ref, got, step):
        chip = chip_at(step)
        return ref[:, chip, c].astype(f32) + got[step].astype(f32)

    def scatter_side(ref, got, got2, base, step):
        pair_copy(ref, got, base, step).wait_recv()
        ref[:, chip_at(step), c] = pair_sum(ref, got, step).astype(bf16)
        for kind in ((0, 1), (2,), (3,))[step]:
            side_copy(ref, got2, base, kind).start()

    def scatter_first(ref, got, got2, compute, sides=True):
        base = counter[0]
        counter[0] += 10

        def step_fn(step, carry):
            chip = chip_at(step)
            block = compute(chip).astype(bf16).reshape(2, 2, 64, width)
            ref[:, chip] = block
            pair_copy(ref, got, base, step).start()
            for done in range(3 if sides else 0):
                pl.when(step == done + 1)(
                    functools.partial(scatter_side, ref, got, got2, base, done)
                )
            return carry

        lax.fori_loop(0, 4, step_fn, 0)
        return base

    def scatter_second(ref, got, got2, base):
        for kind, step, half in ((5, 2, 0), (4, 1, 1)):
            side_copy(ref, got2, base, half).wait_recv()
            chip = chip_at(step)
            total = ref[half, chip, c].astype(f32) + got2[0, half].astype(f32)
            ref[half, chip, c] = total.astype(bf16)
            side_copy(ref, got2, base, kind).start()

    def scatter_finish(ref, got, got2, base):
        pair_copy(ref, got, base, 3).wait_recv()
        total = pair_sum(ref, got, 3)
        for kind in (2, 3, 4, 5):
            side_copy(ref, got2, base, kind).wait_recv()
        total = total + got2[1].astype(f32) + got2[2].astype(f32)
        return total.reshape(128, width)

    def scatter_sent(ref, got, got2, base):
        for step in range(4):
            pair_copy(ref, got, base, step).wait_send()
        for kind in range(6):
            side_copy(ref, got2, base, kind).wait_send()

    lane128 = lax.broadcasted_iota(jnp.int32, (1, LANES), 1)

    def feed_block(chip):
        rows = n2g[:, chip].reshape(256, width)
        grads = gfg[:, chip].reshape(256, width)
        total = jnp.zeros((256, width), f32)
        for chunk in range(2):
            both = mm(rows, gu_w[chunk])
            d_inner = mm_t(grads, wd_w[chunk])
            gate_a, mid, up_a = both[:, 0:128], both[:, 128:256], both[:, 256:384]
            turned = pltpu.roll(mid, 64, 1)
            pieces = []
            for gate, up, back in (
                (gate_a, up_a, d_inner[:, 0:128]),
                (mid, turned, d_inner[:, 128:256]),
            ):
                sig = jax.nn.sigmoid(gate)
                silu = gate * sig
                pieces.append(
                    (silu * up, back * silu, back * up * sig * (1.0 + gate * (1.0 - sig)))
                )
            inner_s[chunk, :, pl.ds(chip * 2, 2), :, 0:128] = (
                pieces[0][0].astype(bf16).reshape(2, 2, 64, 128)
            )
            inner_s[chunk, :, pl.ds(chip * 2, 2), :, 128:256] = (
                jnp.where(lane128 < 64, pieces[1][0], 0.0).astype(bf16).reshape(2, 2, 64, 128)
            )
            gate_low = jnp.where(lane128 < 64, pieces[1][2], 0.0)
            up_low = jnp.where(lane128 < 64, pieces[1][1], 0.0)
            middle = (gate_low + pltpu.roll(up_low, 64, 1)).astype(bf16)
            d_both = jnp.concatenate(
                [pieces[0][2].astype(bf16), middle, pieces[0][1].astype(bf16)], axis=1
            )
            dgu_s[chunk, :, pl.ds(chip * 2, 2)] = d_both.reshape(2, 2, 64, 384)
            total = total + mm_t(d_both, gu_w[chunk])
        return total

    e2_base = scatter_first(part_e, e2r1, e2r2, feed_block)
    scatter_second(part_e, e2r1, e2r2, e2_base)

    for copy in gu_x + gu_z:
        copy.wait_send()
    gf_all.sent()
    for chunk in range(2):
        grads = dgu_s[chunk].reshape(1024, 384)

        def wide_step(block, carry):
            at = pl.multiple_of(block * 128, 128)
            rows = n2g[:, :, :, :, pl.ds(at, 128)].reshape(1024, 128)
            acc[pl.ds(at, 128), 0:384] = mm_w(rows, grads)
            return carry

        lax.fori_loop(0, 9, wide_step, 0)

        def cut(slot, at):
            gu_r[chunk, slot // 8, slot % 8] = acc[pl.ds(at, 72), 0:384].astype(bf16)

        from_rows(cut)
    ggu_x = send(gu_r.at[1 - x], gux_r, device(0, True))

    wd_z.wait_send()
    wd_x.wait_send()

    def down_step(chunk, carry):
        grads = gfg[...].reshape(1024, width)
        piece = mm_w(inner_s[chunk].reshape(1024, 256), grads)
        gd_s[chunk, 0] = piece[0:192, 0:640].astype(bf16)
        gd_s[chunk, 1] = piece[0:192, 512:1152].astype(bf16)
        return carry

    lax.fori_loop(0, 2, down_step, 0)
    ggd_x = send(gd_s.at[:, 1 - x], gdx_r, device(0, True))

    def result_block(chip):
        total = mm(
            inner_s[0, :, pl.ds(chip * 2, 2)].reshape(256, 256), wd_w[0]
        )
        return total + mm(inner_s[1, :, pl.ds(chip * 2, 2)].reshape(256, 256), wd_w[1])

    n2_all.sent()
    bf_base = scatter_first(part_f, bfr1, bfr2, result_block, False)

    e2 = scatter_finish(part_e, e2r1, e2r2, e2_base)
    hidden = hid[...]
    scale2 = lax.rsqrt(jnp.mean(hidden * hidden, axis=-1, keepdims=True) + EPS)
    scaled = e2 * gains[1:2, :]
    inner_mean = jnp.mean(scaled * hidden, axis=-1, keepdims=True)
    gain_feed_row = jnp.sum(e2 * hidden * scale2, axis=0, keepdims=True)
    d_hidden = (
        co[...].reshape(128, width).astype(f32)
        + scale2 * scaled
        - hidden * (scale2 * scale2 * scale2) * inner_mean
    )
    dhid[...] = d_hidden
    d_low = d_hidden.astype(bf16)
    for head in range(6):
        piece = mm_t(d_low, wo_w[192 * head : 192 * head + 192, :])
        da_s[head, :, :, 0:192] = piece.astype(bf16).reshape(2, 64, 192)
    da_copies = []
    for mask in (6, 7, 4, 5, 2, 3, 1):
        n = fresh()
        there = index_of(mask)
        copy = pltpu.make_async_remote_copy(
            src_ref=da_s.at[head_of(there)],
            dst_ref=da_r.at[:, j],
            send_sem=ssem.at[n],
            recv_sem=rsem.at[n],
            device_id=device(mask),
            device_id_type=pl.DeviceIdType.MESH,
        )
        pl.when((there != 3) & (there != 5))(copy.start)
        da_copies.append(((there != 3) & (there != 5), copy))

    @pl.when(attends)
    def _():
        da_r[:, j] = da_s[head_own]

    for step in range(3):
        scatter_side(part_f, bfr1, bfr2, bf_base, step)
    for copy in wo_c + wo_x:
        copy.wait_send()
    wo_q.sent()
    for plane in range(2):
        for head in range(6):
            piece = at_r[head].reshape(128, 256)[:, 0:192]
            acc[192 * head : 192 * head + 192, :] = mm_w(
                piece, d_low[:, 512 * plane : 512 * plane + 640]
            )

        def cut_out(slot, at):
            wo_r[plane, slot // 8, (slot % 8) // 2, slot % 2] = acc[pl.ds(at, 72), :].astype(bf16)

        from_rows(cut_out)
    go_c = send(wo_r.at[:, :, :, 1 - c], gor1, device(1))

    dkvt[...] = jnp.zeros(dkvt.shape, f32)
    for _, copy in da_copies:
        pl.when(attends)(copy.wait_recv)

    @pl.when(attends)
    def _():
        def step(block, carry):
            at = pl.multiple_of(block * 256, 256)
            rows = da_r[block // 2, pl.ds((block % 2) * 4, 4)].reshape(256, 256)
            dat[:, pl.ds(at, 256)] = rows.astype(f32).T[0:192].astype(bf16)
            return carry

        lax.fori_loop(0, 4, step, 0)

    def back_block(quarter):
        length = 256 * (quarter + 1)

        def step(sub, carry):
            at = pl.multiple_of(quarter * 256 + sub * 128, 128)
            grads = da_r[quarter // 2, pl.ds((quarter % 2) * 4 + sub * 2, 2)].reshape(128, 256)
            products = grads.astype(f32) * mx[pl.ds(at, 128), :]
            d_query = jnp.zeros((128, 256), f32)
            d_key = jnp.zeros((64, length), f32)
            d_value = jnp.zeros((64, length), f32)
            for head in range(3):
                delta = jnp.sum(
                    jnp.where((lane256 // 64) == head, products, 0.0), axis=-1, keepdims=True
                )
                low_p = pbs[quarter][head, pl.ds(pl.multiple_of(sub * 128, 128), 128), :]
                d_p = mm_t(grads, vw[head, 0:length, :])
                d_s_low = (low_p.astype(f32) * (d_p - delta) * scale).astype(bf16)
                d_query = d_query + mm(d_s_low, kw[head, 0:length, :])
                d_key = d_key + mm(qt[64 * head : 64 * head + 64, pl.ds(at, 128)], d_s_low)
                d_value = d_value + mm(dat[64 * head : 64 * head + 64, pl.ds(at, 128)], low_p)
            mx[pl.ds(at, 128), :] = d_query
            dkvt[0:64, 0:length] += d_value
            dkvt[64:128, 0:length] += d_key
            return carry

        lax.fori_loop(0, 2, step, 0)

    pl.when(attends)(lambda: back_block(0))
    scatter_second(part_f, bfr1, bfr2, bf_base)
    go_c.wait_recv()

    def go_add(chip, carry):
        for half in range(2):
            for plane in range(2):
                wo_r[plane, half, chip, c] = (
                    wo_r[plane, half, chip, c].astype(f32) + gor1[plane, half, chip].astype(f32)
                ).astype(bf16)
        return carry

    lax.fori_loop(0, 4, go_add, 0)

    def go_side(chip, half, slot, mask):
        return send(wo_r.at[:, half, chip, c], goq_r.at[slot, half], device(mask))

    def go_sum(half, chip, slot):
        for plane in range(2):
            wo_r[plane, half, chip, c] = (
                wo_r[plane, half, chip, c].astype(f32) + goq_r[slot, half, plane].astype(f32)
            ).astype(bf16)

    go_first = [
        go_side(chip_d, 0, 0, 2),
        go_side(chip_d, 1, 0, 4),
        go_side(chip_y, 0, 1, 2),
        go_side(chip_z, 1, 2, 4),
    ]
    pl.when(attends)(lambda: back_block(1))
    ggu_x.wait_recv()

    def gu_add(slot, carry):
        gu_r[x, slot // 8, slot % 8] = (
            gu_r[x, slot // 8, slot % 8].astype(f32) + gux_r[slot // 8, slot % 8].astype(f32)
        ).astype(bf16)
        return carry

    lax.fori_loop(0, 16, gu_add, 0)
    ggu_z = send(gu_r.at[x, 1 - zh], guz_r, device(0, False, True))
    pl.when(attends)(lambda: back_block(2))
    pl.when(attends)(lambda: back_block(3))

    @pl.when(attends)
    def _():
        def step(block, carry):
            at = pl.multiple_of(block * 256, 256)
            cosine, sine = tables(at, 256)
            turned = dkvt[:, pl.ds(at, 256)].T
            query = mx[pl.ds(at, 256), :]
            pair = jnp.concatenate(
                [query[:, 0:128], jnp.where(lane128 < 64, query[:, 128:256], turned)], axis=1
            )
            back = pair * cosine - swap_half(pair) * sine
            values = jnp.where(lane128 < 64, turned, 0.0)
            both = jnp.concatenate([back.astype(bf16), values.astype(bf16)], axis=1)
            d_s[block // 2, pl.ds((block % 2) * 4, 4)] = both.reshape(4, 64, 384)
            return carry

        lax.fori_loop(0, 4, step, 0)

    @pl.when(jnp.logical_not(attends))
    def _():
        d_s[...] = jnp.zeros(d_s.shape, bf16)
        wq_w[...] = jnp.zeros(wq_w.shape, bf16)

    def input_block(chip):
        return mm_t(d_s[:, pl.ds(chip * 2, 2)].reshape(256, 384), wq_w[...])

    scatter_sent(part_e, e2r1, e2r2, e2_base)
    e1_base = scatter_first(part_e, e1r1, e1r2, input_block)
    gq_send, gq_sem = fresh(), fresh()
    plane_to = zl
    piece_own = head_own - 3 * zl

    def gq_copy(slot):
        return pltpu.make_async_remote_copy(
            src_ref=wq_r.at[slot],
            dst_ref=gq_r.at[x * 2 + zh, piece_own],
            send_sem=ssem.at[gq_send],
            recv_sem=rsem.at[gq_sem],
            device_id=(plane_to, slot),
            device_id_type=pl.DeviceIdType.MESH,
        )

    @pl.when(attends)
    def _():
        grads = d_s[...].reshape(1024, 384)

        def wide_step(block, carry):
            at = pl.multiple_of(block * 128, 128)
            rows = n1g[:, :, :, :, pl.ds(at, 128)].reshape(1024, 128)
            acc[pl.ds(at, 128), 0:384] = mm_w(rows, grads)
            return carry

        lax.fori_loop(0, 9, wide_step, 0)

        def step(slot, carry):
            wq_r[slot] = acc[pl.ds(pl.multiple_of(slot * 72, 8), 72), 0:384].astype(bf16)
            here = (plane_to == x) & (slot == s)

            @pl.when(here)
            def _():
                pltpu.make_async_copy(
                    wq_r.at[slot], gq_r.at[x * 2 + zh, piece_own], rsem.at[gq_sem]
                ).start()

            pl.when(jnp.logical_not(here))(lambda: gq_copy(slot).start())
            return carry

        lax.fori_loop(0, 16, step, 0)

    scatter_second(part_e, e1r1, e1r2, e1_base)

    ggd_x.wait_recv()
    for half in range(2):
        gd_s[half, x] = (gd_s[half, x].astype(f32) + gdx_r[half].astype(f32)).astype(bf16)
    ggd_z = send(gd_s.at[1 - zh, x], gdz_r, device(0, False, True))
    for n, half, chip, mask, slot in ((0, 0, chip_z, 4, 2), (1, 1, chip_y, 2, 1)):
        go_first[n].wait_recv()
        go_sum(half, chip, 0)
        go_first.append(go_side(chip, half, slot, mask))

    branch_feed = scatter_finish(part_f, bfr1, bfr2, bf_base)
    result = hid[...] + branch_feed
    square_feed = jnp.sum(
        jnp.sum(valid * branch_feed * branch_feed, axis=0, keepdims=True), axis=1, keepdims=True
    )
    square_out = jnp.sum(
        jnp.sum(valid * result * result, axis=0, keepdims=True), axis=1, keepdims=True
    )
    rows_s[0] = result.astype(bf16).reshape(2, 64, width)
    ret_out = send(rows_s.at[0, 1 - zh], rows_r.at[0], device(0, False, True))
    out_o[zh] = rows_s[0, zh]

    ggu_z.wait_recv()

    def gu_add2(slot, carry):
        gu_r[x, zh, slot] = (
            gu_r[x, zh, slot].astype(f32) + guz_r[slot].astype(f32)
        ).astype(bf16)
        return carry

    lax.fori_loop(0, 8, gu_add2, 0)
    e1 = scatter_finish(part_e, e1r1, e1r2, e1_base)
    tokens = xo[...].reshape(128, width).astype(f32)
    scale1 = lax.rsqrt(jnp.mean(tokens * tokens, axis=-1, keepdims=True) + EPS)
    scaled = e1 * gains[0:1, :]
    inner_mean = jnp.mean(scaled * tokens, axis=-1, keepdims=True)
    gain_attn_row = jnp.sum(e1 * tokens * scale1, axis=0, keepdims=True)
    grad_rows = (
        dhid[...] + scale1 * scaled - tokens * (scale1 * scale1 * scale1) * inner_mean
    )
    rows_s[1] = grad_rows.astype(bf16).reshape(2, 64, width)
    ret_in = send(rows_s.at[1, 1 - zh], rows_r.at[1], device(0, False, True))
    gin_o[zh] = rows_s[1, zh]

    ggu_q = [
        send(gu_r.at[x, zh, index_of(mask)], guf_r.at[j], device(mask)) for mask in range(1, 8)
    ]
    guf_r[j] = gu_r[x, zh, j]
    total_row = jnp.where(
        lane1 == 0,
        square_attn,
        jnp.where(lane1 == 1, square_feed, jnp.where(lane1 == 2, square_out, count)),
    )
    row8 = lax.broadcasted_iota(jnp.int32, (8, 1), 0)
    both_gains = jnp.where(
        row8 == 0,
        jnp.broadcast_to(gain_attn_row, (8, width)),
        jnp.broadcast_to(gain_feed_row, (8, width)),
    )
    for slot in range(16):
        moved = pltpu.roll(both_gains, (width - 72 * slot) % width, 1) if slot else both_gains
        small_s[slot] = jnp.where(row8 == 2, total_row, moved[:, 0:LANES])
    small_copies = []
    for flip_z in (True, False):
        for flip_x in (True, False):
            for mask in (6, 7, 4, 5, 2, 3, 1, 0):
                if flip_x or flip_z or mask:
                    target = device(mask, flip_x, flip_z)
                    small_copies.append(
                        send(small_s.at[target[1]], small_r.at[x * 16 + s], target)
                    )
    small_r[x * 16 + s] = small_s[s]

    for copy in go_first[2:]:
        copy.wait_recv()
    for slot in (1, 2):
        for half in range(2):
            go_sum(half, own_chip, slot)
    go_x = send(wo_r.at[1 - x, :, own_chip, c], gox_r, device(0, True))

    go_x.wait_recv()
    for half in range(2):
        wo_r[x, half, own_chip, c] = (
            wo_r[x, half, own_chip, c].astype(f32) + gox_r[half].astype(f32)
        ).astype(bf16)
    go_z = send(wo_r.at[x, 1 - zh, own_chip, c], goz_r, device(0, False, True))
    ggd_z.wait_recv()
    gd_o[...] = gd_s[zh, x].astype(f32) + gdz_r[...].astype(f32)
    for copy in ggu_q:
        copy.wait_recv()
    ggu_o[...] = guf_r[...]
    go_z.wait_recv()
    go_o[...] = wo_r[x, zh, own_chip, c].astype(f32) + goz_r[...].astype(f32)
    ret_out.wait_recv()
    out_o[1 - zh] = rows_r[0]
    pltpu.make_async_copy(gq_r, gq_r, rsem.at[gq_sem]).wait()
    gq_o[...] = (
        (gq_r[0].astype(f32) + gq_r[1].astype(f32)) + (gq_r[2].astype(f32) + gq_r[3].astype(f32))
    )
    for copy in small_copies:
        copy.wait_recv()
    total = small_r[0]
    for slot in range(1, 32):
        total = total + small_r[slot]
    small_o[...] = total
    ret_in.wait_recv()
    gin_o[1 - zh] = rows_r[1]

    waited = {id(copy) for copy in wo_c + wo_x + gu_x + gu_z + gu_first + [wd_z, wd_x]}
    for gather in (wo_q, gf_all, n2_all, x_a, x_b):
        waited |= {id(copy) for copy in gather.copies}
    for copy in pending:
        if id(copy) not in waited:
            copy.wait_send()
    for here, copy in qkv_first:
        pl.when(jnp.logical_not(here))(copy.wait_send)
    for theirs, copy in at_copies:
        pl.when(attends)(copy.wait_send)
    for theirs, copy in da_copies:
        pl.when(theirs)(copy.wait_send)
    scatter_sent(part_f, bfr1, bfr2, bf_base)
    scatter_sent(part_e, e1r1, e1r2, e1_base)

    @pl.when(attends)
    def _():
        def step(slot, carry):
            here = (plane_to == x) & (slot == s)
            pl.when(jnp.logical_not(here))(lambda: gq_copy(slot).wait_send())
            return carry

        lax.fori_loop(0, 16, step, 0)


def finish_kernel(
    out, gin, gq, go, ggu, gd, small,
    out_o, gin_o, gq_o, gk_o, gv_o, go_o, gg_o, gu_o, gd_o, ga_o, gf_o, rm_o,
):
    f32 = jnp.float32
    first = lax.axis_index("dp") == 0
    rows = gq.shape[1]
    low = lax.broadcasted_iota(jnp.int32, (1, LANES), 1) < 64
    out_o[...] = out[...]
    gin_o[...] = gin[...]
    p = [[gq[head, :, LANES * n : LANES * (n + 1)].astype(f32) for n in range(3)] for head in range(3)]
    gq_o[:, 0:128] = p[0][0]
    gq_o[:, 128:256] = jnp.where(low, p[0][1], roll64(p[1][0]))
    gq_o[:, 256:384] = jnp.where(low, roll64(p[1][0]), roll64(p[1][1]))
    gq_o[:, 384:512] = p[2][0]
    gq_o[:, 512:576] = p[2][1][:, 0:64]
    gk_o[:, 0:128] = jnp.where(low, roll64(p[0][1]), p[1][1])
    gk_o[:, 128:192] = roll64(p[2][1])[:, 0:64]
    gv_o[:, 0:128] = jnp.where(low, p[0][2], roll64(p[1][2]))
    gv_o[:, 128:192] = p[2][2][:, 0:64]

    def unwindow(ref, res):
        pieces = [ref[:, LANES * n : LANES * (n + 1)].astype(f32) for n in range(5)]
        for n in range(5):
            after = pieces[min(n + 1, 4)]
            moved = jnp.where(low, roll64(pieces[n]), roll64(after))
            value = jnp.where(first, pieces[n], moved)
            if n < 4:
                res[:, LANES * n : LANES * (n + 1)] = value
            else:
                res[:, 512:576] = value[:, 0:64]

    unwindow(go, go_o)
    unwindow(gd, gd_o)
    for pair in range(4):
        a, b = [
            [ggu[2 * pair + odd, :, LANES * n : LANES * (n + 1)].astype(f32) for n in range(3)]
            for odd in range(2)
        ]
        at = 384 * pair
        gg_o[:, at : at + 128] = a[0]
        gg_o[:, at + 128 : at + 256] = jnp.where(low, a[1], roll64(b[0]))
        gg_o[:, at + 256 : at + 384] = jnp.where(low, roll64(b[0]), roll64(b[1]))
        gu_o[:, at : at + 128] = a[2]
        gu_o[:, at + 128 : at + 256] = jnp.where(low, roll64(a[1]), roll64(b[2]))
        gu_o[:, at + 256 : at + 384] = jnp.where(low, roll64(b[2]), b[1])
    ga_o[...] = small[0:1, 0:rows]
    gf_o[...] = small[1:2, 0:rows]
    width = out.shape[2]
    rm_o[...] = jnp.sqrt(small[2:3, 0:3] / (small[2:3, 3:4] * width))


def fast_device(
    inputs,
    segments,
    weight_query,
    key_weight_matrix,
    value_weight_matrix,
    weight_out,
    weight_gate,
    weight_up,
    weight_down,
    gain_attention,
    gain_feed,
    cotangent,
):
    f32, bf16 = jnp.float32, jnp.bfloat16
    micro, _, rows, width = inputs.shape
    dp = lax.axis_index("dp")
    length = rows * 16
    piece = width // 16

    whole = pl.BlockSpec(memory_space=pltpu.VMEM)
    half = HEAD_DIMENSION // 2
    frequency = THETA ** (-np.arange(half, dtype=np.float32) * np.float32(2.0) / HEAD_DIMENSION)
    angles = np.arange(length, dtype=np.float32)[:, None] * frequency.astype(np.float32)[None, :]
    cosine, sine = np.cos(angles), np.sin(angles)
    turns = np.concatenate([cosine, cosine, -sine, sine], axis=1).astype(np.float32)

    v = pltpu.VMEM
    tok = (2, 4, 2, 64, width)
    scratch = [
        v((8, LANES), f32),
        v((3, piece, 384), bf16),
        v((piece, 640), bf16),
        v((16, 8, LANES), f32),
        v((2, 64, width), bf16),
        v((2, 64, width), bf16),
        v(tok, bf16),
        v(tok, bf16),
        v(tok, bf16),
        v((16, 72, 384), bf16),
        v((width, 384), bf16),
        v((2, 2, 4, 2, 72, 640), bf16),
        v((width, width), bf16),
        v((2, 2, 8, 72, 384), bf16),
        v((2, width, 384), bf16),
        v((2, 2, 192, 640), bf16),
        v((2, 256, width), bf16),
        v((width, 640), f32),
        v((1024, 256), bf16),
        v((192, 1024), bf16),
        v((192, 1024), bf16),
        v((3, 1024, 256), bf16),
        v((3, 1024, 256), bf16),
        v((3, 256, 256), bf16),
        v((3, 256, 512), bf16),
        v((3, 256, 768), bf16),
        v((3, 256, 1024), bf16),
        v((1024, 256), f32),
        v((8, 1024), f32),
        v((1024, 8), f32),
        v((8, width), f32),
        v((2, 8, 64, 256), bf16),
        v((6, 2, 64, 256), bf16),
        v((128, width), f32),
        v((128, width), f32),
        v((2, 2, 8, 64, 256), bf16),
        v((2, 2, 8, 64, 384), bf16),
        v((2, 4, 2, 64, width), bf16),
        v((4, 2, 64, width), bf16),
        v((3, 2, 64, width), bf16),
        v((4, 2, 64, width), bf16),
        v((3, 2, 64, width), bf16),
        v((6, 2, 64, 256), bf16),
        v((2, 8, 64, 256), bf16),
        v((2, 8, 64, 384), bf16),
        v((128, 1024), f32),
        v((2, 8, 72, 384), bf16),
        v((8, 72, 384), bf16),
        v((8, 72, 384), bf16),
        v((2, 2, 192, 640), bf16),
        v((2, 192, 640), bf16),
        v((192, 640), bf16),
        v((2, 2, 4, 72, 640), bf16),
        v((2, 72, 640), bf16),
        v((3, 2, 2, 72, 640), bf16),
        v((72, 640), bf16),
        v((4, 3, 72, 384), bf16),
        v((16, 8, LANES), f32),
        v((32, 8, LANES), f32),
        v((2, 2, 64, width), bf16),
        v((2, 64, width), bf16),
        pltpu.SemaphoreType.DMA((256,)),
        pltpu.SemaphoreType.DMA((256,)),
    ]
    out, gin, gq, go, ggu, gd, small = pl.pallas_call(
        fast_kernel,
        out_shape=(
            jax.ShapeDtypeStruct((2, rows, width), bf16),
            jax.ShapeDtypeStruct((2, rows, width), bf16),
            jax.ShapeDtypeStruct((3, piece, 384), f32),
            jax.ShapeDtypeStruct((piece, 640), f32),
            jax.ShapeDtypeStruct((8, piece, 384), bf16),
            jax.ShapeDtypeStruct((192, 640), f32),
            jax.ShapeDtypeStruct((8, LANES), f32),
        ),
        in_specs=[whole] * 13,
        out_specs=[whole] * 7,
        scratch_shapes=scratch,
        compiler_params=pltpu.CompilerParams(
            has_side_effects=True, collective_id=0, vmem_limit_bytes=62 * 1024 * 1024
        ),
        name="layer",
    )(
        inputs[:, 0],
        cotangent[:, 0],
        gain_attention.reshape(1, piece),
        gain_feed.reshape(1, piece),
        segments[:, 0],
        weight_query,
        key_weight_matrix,
        value_weight_matrix,
        weight_out,
        weight_gate,
        weight_up,
        weight_down,
        jnp.asarray(turns),
    )

    grads = pl.pallas_call(
        finish_kernel,
        out_shape=(
            jax.ShapeDtypeStruct((2, rows, width), bf16),
            jax.ShapeDtypeStruct((2, rows, width), bf16),
            jax.ShapeDtypeStruct(weight_query.shape, f32),
            jax.ShapeDtypeStruct(key_weight_matrix.shape, f32),
            jax.ShapeDtypeStruct(value_weight_matrix.shape, f32),
            jax.ShapeDtypeStruct(weight_out.shape, f32),
            jax.ShapeDtypeStruct(weight_gate.shape, f32),
            jax.ShapeDtypeStruct(weight_up.shape, f32),
            jax.ShapeDtypeStruct(weight_down.shape, f32),
            jax.ShapeDtypeStruct((1, piece), f32),
            jax.ShapeDtypeStruct((1, piece), f32),
            jax.ShapeDtypeStruct((1, 3), f32),
        ),
        in_specs=[whole] * 7,
        out_specs=[whole] * 12,
        name="finish",
    )(out, gin, gq, go, ggu, gd, small)
    return (
        grads[0][:, None],
        grads[1][:, None],
        *grads[2:9],
        grads[9].reshape(piece),
        grads[10].reshape(piece),
        grads[11].reshape(3),
    )


def solution(mesh):
    placed = (
        P(None, "dp", "seq", None),
        P(None, "dp", "seq"),
        P("seq", "dp"),
        P("seq", "dp"),
        P("seq", "dp"),
        P("seq", "dp"),
        P("seq", "dp"),
        P("seq", "dp"),
        P("seq", "dp"),
        P("seq"),
        P("seq"),
        P(None, "dp", "seq", None),
    )
    body = fast_device if dict(mesh.shape) == {"dp": 2, "seq": 16} else per_device
    return jax.shard_map(
        body,
        mesh=mesh,
        in_specs=placed,
        out_specs=(
            P(None, "dp", "seq", None),
            P(None, "dp", "seq", None),
            P("seq", "dp"),
            P("seq", "dp"),
            P("seq", "dp"),
            P("seq", "dp"),
            P("seq", "dp"),
            P("seq", "dp"),
            P("seq", "dp"),
            P("seq"),
            P("seq"),
            P(),
        ),
        check_vma=False,
    )
```

```python
import functools
import math

import jax
import jax.numpy as jnp
import numpy as np
from jax import lax
from jax.experimental import pallas as pl
from jax.experimental.pallas import tpu as pltpu
from jax.sharding import PartitionSpec as P

QUERY_HEADS = 18
KEY_VALUE_HEADS = 6
HEAD_DIMENSION = 64


EPS = 1e-05
THETA = 10000.0
NEGATIVE = -1e30


def rope_tables(positions, head_size):
    half_size = head_size // 2
    frequency = THETA ** (-jnp.arange(half_size, dtype=jnp.float32) * 2.0 / head_size)
    angles = positions.astype(jnp.float32)[:, None] * frequency[None, :]
    angles = jnp.concatenate([angles, angles], axis=1)
    return (jnp.cos(angles), jnp.sin(angles))


def turn_half(values_in):
    half_size = values_in.shape[-1] // 2
    return jnp.concatenate([-values_in[..., half_size:], values_in[..., :half_size]], axis=-1)


def apply_rotation(values_in, cosine_table, sine_values):
    return values_in * cosine_table[:, None, :] + turn_half(values_in) * sine_values[:, None, :]


def reverse_rotation(grads_in, cosine_table, sine_values):
    return grads_in * cosine_table[:, None, :] - turn_half(grads_in * sine_values[:, None, :])


def norm_forward(values_in, gain):
    row_scale = lax.rsqrt(jnp.mean(values_in * values_in, axis=-1, keepdims=True) + EPS)
    return (values_in * row_scale * gain, row_scale)


def norm_backward(values_in, row_scale, gain, grad_normed):
    scaled = grad_normed * gain
    inner_mean = jnp.mean(scaled * values_in, axis=-1, keepdims=True)
    value_gradient_rows = row_scale * scaled - values_in * row_scale**3 * inner_mean
    grad_gain = jnp.sum(grad_normed * values_in * row_scale, axis=(0, 1))
    return (value_gradient_rows, grad_gain)


def apply_projection(acts_low, weight_full):
    return jnp.einsum("std,df->stf", acts_low, weight_full, preferred_element_type=jnp.float32)


def project_back(grads_low, weight_full):
    return jnp.einsum("sta,ba->stb", grads_low, weight_full, preferred_element_type=jnp.float32)


def weight_grad(acts_low, grads_low):
    return jnp.einsum("std,stf->df", acts_low, grads_low, preferred_element_type=jnp.float32)


def gather_all(shards, gain_shards):
    wide = (
        lax.all_gather(shards[0], "dp", axis=1, tiled=True),
        lax.all_gather(shards[1], "dp", axis=1, tiled=True),
        lax.all_gather(shards[2], "dp", axis=1, tiled=True),
        lax.all_gather(shards[3], "dp", axis=1, tiled=True),
        lax.all_gather(shards[4], "dp", axis=1, tiled=True),
        lax.all_gather(shards[5], "dp", axis=1, tiled=True),
        lax.all_gather(shards[6], "dp", axis=1, tiled=True),
    )
    return (
        lax.all_gather(wide[0], "seq", axis=0, tiled=True),
        lax.all_gather(wide[1], "seq", axis=0, tiled=True),
        lax.all_gather(wide[2], "seq", axis=0, tiled=True),
        lax.all_gather(wide[3], "seq", axis=0, tiled=True),
        lax.all_gather(wide[4], "seq", axis=0, tiled=True),
        lax.all_gather(wide[5], "seq", axis=0, tiled=True),
        lax.all_gather(wide[6], "seq", axis=0, tiled=True),
        lax.all_gather(gain_shards[0], "seq", axis=0, tiled=True),
        lax.all_gather(gain_shards[1], "seq", axis=0, tiled=True),
    )


def gather_keys(key_low, value_low, seg_low):
    return (
        lax.all_gather(key_low, "seq", axis=1, tiled=True),
        lax.all_gather(value_low, "seq", axis=1, tiled=True),
        lax.all_gather(seg_low, "seq", axis=1, tiled=True),
    )


def reduce_grads(grads):
    rows = [
        lax.psum_scatter(g.astype(jnp.bfloat16), "seq", scatter_dimension=0, tiled=True)
        for g in grads
    ]
    return tuple(
        lax.psum_scatter(r, "dp", scatter_dimension=1, tiled=True).astype(jnp.float32)
        for r in rows
    )


def block_view(gathered, block_index, key_tile_block):
    block_offset = block_index * key_tile_block
    key_portion = lax.dynamic_slice_in_dim(gathered[0], block_offset, key_tile_block, 1)
    value_portion = lax.dynamic_slice_in_dim(gathered[1], block_offset, key_tile_block, 1)
    seg_part = lax.dynamic_slice_in_dim(gathered[2], block_offset, key_tile_block, 1).astype(
        jnp.float32
    )
    sequence_count = key_portion.shape[0]
    key_portion = key_portion.reshape(
        sequence_count, key_tile_block, KEY_VALUE_HEADS, HEAD_DIMENSION
    )
    value_portion = value_portion.reshape(
        sequence_count, key_tile_block, KEY_VALUE_HEADS, HEAD_DIMENSION
    )
    col_pos = block_offset + jnp.arange(key_tile_block, dtype=jnp.int32)
    return (key_portion, value_portion, seg_part, col_pos)


def masked_scores(query_block_list, key_portion, seg_rows, seg_part, row_pos, col_pos, score_scale):
    raw_scores = jnp.einsum(
        "skgtd,sjkd->skgtj", query_block_list, key_portion, preferred_element_type=jnp.float32
    )
    allowed = (seg_rows[:, :, None] == seg_part[:, None, :]) & (
        col_pos[None, None, :] <= row_pos[None, :, None]
    )
    allowed = allowed[:, None, None, :, :]
    return (jnp.where(allowed, raw_scores * score_scale, NEGATIVE), allowed)


def log_sum(
    query_block_list, gathered, seg_rows, row_pos, block_count, key_tile_block, score_scale
):
    lead_shape = query_block_list.shape[:4]

    def log_step_fn(block_index, carried):
        row_top, row_total = carried
        key_portion, value_portion, seg_part, col_pos = block_view(
            gathered, block_index, key_tile_block
        )
        scores, allowed = masked_scores(
            query_block_list, key_portion, seg_rows, seg_part, row_pos, col_pos, score_scale
        )
        new_top = jnp.maximum(row_top, jnp.max(scores, axis=-1))
        exponent = jnp.where(allowed, jnp.exp(scores - new_top[..., None]), 0.0)
        row_total = row_total * jnp.exp(row_top - new_top) + jnp.sum(exponent, axis=-1)
        return (new_top, row_total)

    start_state = (jnp.full(lead_shape, NEGATIVE, jnp.float32), jnp.zeros(lead_shape, jnp.float32))
    row_top, row_total = lax.fori_loop(0, block_count, log_step_fn, start_state)
    return row_top + jnp.log(row_total)


def attend(
    query_block_list,
    gathered,
    seg_rows,
    row_pos,
    block_count,
    key_tile_block,
    score_scale,
    log_total,
):

    def attend_step_fn(block_index, mixed_heads):
        key_portion, value_portion, seg_part, col_pos = block_view(
            gathered, block_index, key_tile_block
        )
        scores, allowed = masked_scores(
            query_block_list, key_portion, seg_rows, seg_part, row_pos, col_pos, score_scale
        )
        probabilities = jnp.where(allowed, jnp.exp(scores - log_total[..., None]), 0.0).astype(
            jnp.bfloat16
        )
        return mixed_heads + jnp.einsum(
            "skgtj,sjkd->skgtd", probabilities, value_portion, preferred_element_type=jnp.float32
        )

    return lax.fori_loop(
        0, block_count, attend_step_fn, jnp.zeros(query_block_list.shape, jnp.float32)
    )


def query_back(
    query_block_list,
    gathered,
    seg_rows,
    row_pos,
    block_count,
    key_tile_block,
    score_scale,
    log_total,
    gradient_reduced,
    row_delta,
):

    def query_step_fn(block_index, grad_query):
        key_portion, value_portion, seg_part, col_pos = block_view(
            gathered, block_index, key_tile_block
        )
        scores, allowed = masked_scores(
            query_block_list, key_portion, seg_rows, seg_part, row_pos, col_pos, score_scale
        )
        probabilities = jnp.where(allowed, jnp.exp(scores - log_total[..., None]), 0.0)
        grad_probs = jnp.einsum(
            "skgtd,sjkd->skgtj", gradient_reduced, value_portion, preferred_element_type=jnp.float32
        )
        grad_scores = (probabilities * (grad_probs - row_delta[..., None]) * score_scale).astype(
            jnp.bfloat16
        )
        return grad_query + jnp.einsum(
            "skgtj,sjkd->skgtd", grad_scores, key_portion, preferred_element_type=jnp.float32
        )

    return lax.fori_loop(
        0, block_count, query_step_fn, jnp.zeros(query_block_list.shape, jnp.float32)
    )


def key_back(
    key_local,
    value_local,
    seg_rows,
    row_pos,
    query_whole,
    grads_whole,
    stats_whole,
    seg_whole,
    first_block,
    block_count,
    query_tile,
    score_scale,
):
    sequence_count = key_local.shape[0]
    group_width = QUERY_HEADS // KEY_VALUE_HEADS

    def key_step_fn(block_index, carried):
        key_total, value_total = carried
        block_offset = block_index * query_tile
        query_rows = lax.dynamic_slice_in_dim(query_whole, block_offset, query_tile, 1).reshape(
            sequence_count, query_tile, KEY_VALUE_HEADS, group_width, HEAD_DIMENSION
        )
        grad_rows = lax.dynamic_slice_in_dim(grads_whole, block_offset, query_tile, 1).reshape(
            sequence_count, query_tile, KEY_VALUE_HEADS, group_width, HEAD_DIMENSION
        )
        log_rows = lax.dynamic_slice_in_dim(stats_whole[0], block_offset, query_tile, 3)
        delta_rows = lax.dynamic_slice_in_dim(stats_whole[1], block_offset, query_tile, 3)
        seg_query = lax.dynamic_slice_in_dim(seg_whole, block_offset, query_tile, 1).astype(
            jnp.float32
        )
        query_pos = block_offset + jnp.arange(query_tile, dtype=jnp.int32)
        raw_scores = jnp.einsum(
            "stkgd,sjkd->skgtj", query_rows, key_local, preferred_element_type=jnp.float32
        )
        allowed = (seg_query[:, :, None] == seg_rows[:, None, :]) & (
            row_pos[None, None, :] <= query_pos[None, :, None]
        )
        allowed = allowed[:, None, None, :, :]
        scores = jnp.where(allowed, raw_scores * score_scale, NEGATIVE)
        probabilities = jnp.where(allowed, jnp.exp(scores - log_rows[..., None]), 0.0)
        grad_probs = jnp.einsum(
            "stkgd,sjkd->skgtj", grad_rows, value_local, preferred_element_type=jnp.float32
        )
        grad_scores = (probabilities * (grad_probs - delta_rows[..., None]) * score_scale).astype(
            jnp.bfloat16
        )
        key_total = key_total + jnp.einsum(
            "skgtj,stkgd->sjkd", grad_scores, query_rows, preferred_element_type=jnp.float32
        )
        value_total = value_total + jnp.einsum(
            "skgtj,stkgd->sjkd",
            probabilities.astype(jnp.bfloat16),
            grad_rows,
            preferred_element_type=jnp.float32,
        )
        return (key_total, value_total)

    start_state = (jnp.zeros(key_local.shape, jnp.float32), jnp.zeros(key_local.shape, jnp.float32))
    return lax.fori_loop(first_block, block_count, key_step_fn, start_state)


def per_device(
    inputs,
    segments,
    weight_query,
    key_weight_matrix,
    value_weight_matrix,
    weight_out,
    weight_gate,
    weight_up,
    weight_down,
    gain_attention,
    gain_feed,
    cotangent,
):
    shards = (
        weight_query,
        key_weight_matrix,
        value_weight_matrix,
        weight_out,
        weight_gate,
        weight_up,
        weight_down,
    )
    gain_shards = (gain_attention, gain_feed)
    micro_count, sequence_count, token_count, model_width = inputs.shape
    group_width = QUERY_HEADS // KEY_VALUE_HEADS
    score_scale = 1.0 / math.sqrt(HEAD_DIMENSION)
    row_pos = lax.axis_index("seq") * token_count + jnp.arange(token_count, dtype=jnp.int32)
    cosine_table, sine_values = rope_tables(row_pos, HEAD_DIMENSION)
    key_span_length = token_count * lax.axis_size("seq")
    key_tile_block = min(512, key_span_length)
    total_blocks = key_span_length // key_tile_block
    block_count = row_pos[token_count - 1] // key_tile_block + 1
    first_block = row_pos[0] // key_tile_block
    outputs = []
    grad_list = []
    totals = jnp.zeros((4,), jnp.float32)
    gain_grads = jnp.zeros((2, model_width), jnp.float32)
    summed = None
    weights_complete = gather_all(shards, gain_shards)
    for batch_index in range(micro_count):
        tokens = inputs[batch_index].astype(jnp.float32)
        seg_local = segments[batch_index]
        seg_rows = seg_local.astype(jnp.float32)
        seg_low = seg_local.astype(jnp.bfloat16)
        gain_first = weights_complete[7].astype(jnp.float32)
        gain_second = weights_complete[8].astype(jnp.float32)
        norm_first, scale_first = norm_forward(tokens, gain_first)
        normalized = norm_first.astype(jnp.bfloat16)
        query_raw = apply_projection(normalized, weights_complete[0]).reshape(
            sequence_count, token_count, QUERY_HEADS, HEAD_DIMENSION
        )
        query_reduced = apply_rotation(query_raw, cosine_table, sine_values).astype(jnp.bfloat16)
        key_unrotated = apply_projection(normalized, weights_complete[1]).reshape(
            sequence_count, token_count, KEY_VALUE_HEADS, HEAD_DIMENSION
        )
        key_low = (
            apply_rotation(key_unrotated, cosine_table, sine_values)
            .astype(jnp.bfloat16)
            .reshape(sequence_count, token_count, KEY_VALUE_HEADS * HEAD_DIMENSION)
        )
        value_low = apply_projection(normalized, weights_complete[2]).astype(jnp.bfloat16)
        gathered = gather_keys(key_low, value_low, seg_low)
        query_block_list = query_reduced.reshape(
            sequence_count, token_count, KEY_VALUE_HEADS, group_width, HEAD_DIMENSION
        ).transpose(0, 2, 3, 1, 4)
        log_total = log_sum(
            query_block_list, gathered, seg_rows, row_pos, block_count, key_tile_block, score_scale
        )
        mixed_heads = attend(
            query_block_list,
            gathered,
            seg_rows,
            row_pos,
            block_count,
            key_tile_block,
            score_scale,
            log_total,
        )
        attn_low = (
            mixed_heads.transpose(0, 3, 1, 2, 4)
            .reshape(sequence_count, token_count, QUERY_HEADS * HEAD_DIMENSION)
            .astype(jnp.bfloat16)
        )
        branch_attn = apply_projection(attn_low, weights_complete[3])
        hidden = tokens + branch_attn
        norm_second, scale_second = norm_forward(hidden, gain_second)
        normed_second = norm_second.astype(jnp.bfloat16)
        gate_values = apply_projection(normed_second, weights_complete[4])
        up_values = apply_projection(normed_second, weights_complete[5])
        gate_sigmoid = jax.nn.sigmoid(gate_values)
        inner_low = (gate_values * gate_sigmoid * up_values).astype(jnp.bfloat16)
        branch_feed = apply_projection(inner_low, weights_complete[6])
        result = hidden + branch_feed
        outputs.append(result.astype(jnp.bfloat16))
        valid_rows = (seg_local != 0).astype(jnp.float32)[:, :, None]
        totals = totals + jnp.stack(
            [
                jnp.sum(valid_rows * branch_attn * branch_attn),
                jnp.sum(valid_rows * branch_feed * branch_feed),
                jnp.sum(valid_rows * result * result),
                jnp.sum(valid_rows),
            ]
        )
        back_weights = weights_complete
        back_keys = gathered
        grad_result = cotangent[batch_index].astype(jnp.float32)
        grad_feed = grad_result.astype(jnp.bfloat16)
        grad_down = weight_grad(inner_low, grad_feed)
        grad_inner = project_back(grad_feed, back_weights[6])
        grad_up = (grad_inner * gate_values * gate_sigmoid).astype(jnp.bfloat16)
        grad_gate = (
            grad_inner * up_values * gate_sigmoid * (1.0 + gate_values * (1.0 - gate_sigmoid))
        ).astype(jnp.bfloat16)
        grad_gate_w = weight_grad(normed_second, grad_gate)
        grad_up_w = weight_grad(normed_second, grad_up)
        grad_normed_second = project_back(grad_gate, back_weights[4]) + project_back(
            grad_up, back_weights[5]
        )
        grad_hidden_norm, grad_gain_second = norm_backward(
            hidden, scale_second, gain_second, grad_normed_second
        )
        grad_hidden = grad_result + grad_hidden_norm
        grad_branch = grad_hidden.astype(jnp.bfloat16)
        grad_out_w = weight_grad(attn_low, grad_branch)
        mixed_gradient = project_back(grad_branch, back_weights[3]).astype(jnp.bfloat16)
        gradient_reduced = mixed_gradient.reshape(
            sequence_count, token_count, KEY_VALUE_HEADS, group_width, HEAD_DIMENSION
        ).transpose(0, 2, 3, 1, 4)
        row_delta = jnp.sum(gradient_reduced.astype(jnp.float32) * mixed_heads, axis=-1)
        grad_query = query_back(
            query_block_list,
            back_keys,
            seg_rows,
            row_pos,
            block_count,
            key_tile_block,
            score_scale,
            log_total,
            gradient_reduced,
            row_delta,
        )
        query_flat = query_reduced.reshape(
            sequence_count, token_count, QUERY_HEADS * HEAD_DIMENSION
        )
        query_whole, grads_whole = (
            lax.all_gather(query_flat, "seq", axis=1, tiled=True),
            lax.all_gather(mixed_gradient, "seq", axis=1, tiled=True),
        )
        stats_whole = (
            lax.all_gather(log_total, "seq", axis=3, tiled=True),
            lax.all_gather(row_delta, "seq", axis=3, tiled=True),
        )
        key_local = key_low.reshape(sequence_count, token_count, KEY_VALUE_HEADS, HEAD_DIMENSION)
        value_local = value_low.reshape(
            sequence_count, token_count, KEY_VALUE_HEADS, HEAD_DIMENSION
        )
        key_total, value_total = key_back(
            key_local,
            value_local,
            seg_rows,
            row_pos,
            query_whole,
            grads_whole,
            stats_whole,
            back_keys[2],
            first_block,
            total_blocks,
            key_tile_block,
            score_scale,
        )
        key_grad_low = (
            reverse_rotation(key_total, cosine_table, sine_values)
            .reshape(sequence_count, token_count, KEY_VALUE_HEADS * HEAD_DIMENSION)
            .astype(jnp.bfloat16)
        )
        value_grad_low = value_total.reshape(
            sequence_count, token_count, KEY_VALUE_HEADS * HEAD_DIMENSION
        ).astype(jnp.bfloat16)
        query_grad = grad_query.transpose(0, 3, 1, 2, 4).reshape(
            sequence_count, token_count, QUERY_HEADS, HEAD_DIMENSION
        )
        query_grad_low = (
            reverse_rotation(query_grad, cosine_table, sine_values)
            .reshape(sequence_count, token_count, QUERY_HEADS * HEAD_DIMENSION)
            .astype(jnp.bfloat16)
        )
        grad_normed = (
            project_back(query_grad_low, back_weights[0])
            + project_back(key_grad_low, back_weights[1])
            + project_back(value_grad_low, back_weights[2])
        )
        grad_token_norm, grad_gain_first = norm_backward(
            tokens, scale_first, gain_first, grad_normed
        )
        grad_list.append((grad_hidden + grad_token_norm).astype(jnp.bfloat16))
        gain_grads = gain_grads + jnp.stack([grad_gain_first, grad_gain_second])
        batch_grads = (
            weight_grad(normalized, query_grad_low),
            weight_grad(normalized, key_grad_low),
            weight_grad(normalized, value_grad_low),
            grad_out_w,
            grad_gate_w,
            grad_up_w,
            grad_down,
        )
        summed = batch_grads if summed is None else jax.tree.map(jnp.add, summed, batch_grads)
    reduced = reduce_grads(summed)
    gain_total, totals = lax.psum((gain_grads, totals), ("dp", "seq"))
    piece_width = model_width // lax.axis_size("seq")
    gain_part = lax.dynamic_slice_in_dim(
        gain_total, lax.axis_index("seq") * piece_width, piece_width, 1
    )
    root_means = jnp.sqrt(totals[:3] / (totals[3] * model_width))
    return (
        jnp.stack(outputs),
        jnp.stack(grad_list),
        reduced[0],
        reduced[1],
        reduced[2],
        reduced[3],
        reduced[4],
        reduced[5],
        reduced[6],
        gain_part[0],
        gain_part[1],
        root_means,
    )


LANES = 128


def roll64(values):
    return pltpu.roll(values, 64, 1)


def prepare(
    ga, gf, seg, wq, wk, wv, wo, gate, up, wd, meta_o, wq_o, wo_o, gu_o, wd_o
):
    f32, bf16 = jnp.float32, jnp.bfloat16
    first = lax.axis_index("dp") == 0
    rows = wq.shape[0]
    low = lax.broadcasted_iota(jnp.int32, (1, LANES), 1) < 64
    meta_o[...] = jnp.zeros(meta_o.shape, f32)
    meta_o[0:1, 0:rows] = ga[...].astype(f32)
    meta_o[1:2, 0:rows] = gf[...].astype(f32)
    meta_o[2:4, 0:64] = seg[...].astype(f32)

    def part(ref, at, size=LANES):
        values = ref[:, at : at + size].astype(f32)
        if size < LANES:
            values = jnp.concatenate(
                [values, jnp.zeros((values.shape[0], LANES - size), f32)], axis=1
            )
        return values

    q = [part(wq, LANES * n) for n in range(4)] + [part(wq, 512, 64)]
    k = [part(wk, 0), part(wk, LANES, 64)]
    v = [part(wv, 0), part(wv, LANES, 64)]
    slabs = (
        (q[0], jnp.where(low, q[1], roll64(k[0])), jnp.where(low, v[0], 0.0)),
        (
            jnp.where(low, roll64(q[1]), roll64(q[2])),
            jnp.where(low, roll64(q[2]), k[0]),
            jnp.where(low, roll64(v[0]), 0.0),
        ),
        (q[3], jnp.where(low, q[4], roll64(k[1])), v[1]),
    )
    for head in range(3):
        for place in range(3):
            wq_o[head, :, LANES * place : LANES * (place + 1)] = slabs[head][place].astype(bf16)

    def window(ref, out):
        pieces = [part(ref, LANES * n) for n in range(4)] + [part(ref, 512, 64)]
        before = jnp.zeros_like(pieces[0])
        for n in range(5):
            moved = jnp.where(low, roll64(before), roll64(pieces[n]))
            out[:, LANES * n : LANES * (n + 1)] = jnp.where(first, pieces[n], moved).astype(bf16)
            before = pieces[n]

    window(wo, wo_o)
    window(wd, wd_o)
    for pair in range(4):
        g = [part(gate, 384 * pair + LANES * n) for n in range(3)]
        u = [part(up, 384 * pair + LANES * n) for n in range(3)]
        slabs = (
            (g[0], jnp.where(low, g[1], roll64(u[1])), u[0]),
            (
                jnp.where(low, roll64(g[1]), roll64(g[2])),
                jnp.where(low, roll64(g[2]), u[2]),
                jnp.where(low, roll64(u[1]), roll64(u[2])),
            ),
        )
        for odd in range(2):
            for place in range(3):
                gu_o[2 * pair + odd, :, LANES * place : LANES * (place + 1)] = slabs[odd][
                    place
                ].astype(bf16)


def fast_kernel(
    x_in,
    cot_in,
    ga,
    gf,
    seg,
    wq,
    wk,
    wv,
    wo,
    gate,
    up,
    wd,
    turn_in,
    out_o,
    gin_o,
    gq_o,
    go_o,
    ggu_o,
    gd_o,
    small_o,
    meta_in,
    wq_in,
    wo_in,
    meta_r,
    xo,
    co,
    n1g,
    gfg,
    n2g,
    wq_r,
    wq_w,
    wo_r,
    wo_w,
    gu_r,
    gu_w,
    wd_r,
    wd_w,
    acc,
    qk,
    qt,
    dat,
    kw,
    vw,
    pb0,
    pb1,
    pb2,
    pb3,
    mx,
    segr,
    segc,
    gains,
    at_s,
    at_r,
    hid,
    dhid,
    inner_s,
    dgu_s,
    part_e,
    e2r1,
    e2r2,
    bfr1,
    bfr2,
    da_s,
    da_r,
    d_s,
    dkvt,
    gux_r,
    guz_r,
    guf_r,
    gd_s,
    gdx_r,
    gdz_r,
    gor1,
    gox_r,
    goq_r,
    goz_r,
    gq_r,
    small_s,
    small_r,
    rows_s,
    rows_r,
    ssem,
    rsem,
):
    f32, bf16 = jnp.float32, jnp.bfloat16
    part_f = n2g
    gu_in, wd_in = guf_r, gd_s.at[0, 0]
    e1r1, e1r2 = gfg.at[0], gfg.at[1]
    x = lax.axis_index("dp")
    s = lax.axis_index("seq")
    zh, j = s // 8, s % 8
    zl, y, c = j // 4, (j // 2) % 2, j % 2
    own_chip = zl * 2 + y
    attends = (j != 3) & (j != 5)

    def head_of(device_index):
        high = device_index // 4
        return device_index - high * (1 + (device_index - 2) // 3)

    head_own = head_of(j)
    width = x_in.shape[2]
    counter = [0]
    everyone = pltpu.get_barrier_semaphore()
    for other in range(1, 32):
        there = (x * 16 + s + other) % 32
        pl.semaphore_signal(
            everyone,
            inc=1,
            device_id=(there // 16, there % 16),
            device_id_type=pl.DeviceIdType.MESH,
        )
    prepare(ga, gf, seg, wq, wk, wv, wo, gate, up, wd, meta_in, wq_in, wo_in, gu_in, wd_in)
    pl.semaphore_wait(everyone, 31)
    pending = []

    def index_of(mask):
        return (
            ((1 - zl) if mask & 4 else zl) * 4
            + ((1 - y) if mask & 2 else y) * 2
            + ((1 - c) if mask & 1 else c)
        )

    def device(mask=0, flip_x=False, flip_z=False):
        return (
            (1 - x) if flip_x else x,
            ((1 - zh) if flip_z else zh) * 8 + index_of(mask),
        )

    def fresh():
        counter[0] += 1
        return counter[0] - 1

    def send(src, dst, target, keep=True):
        n = fresh()
        copy = pltpu.make_async_remote_copy(
            src_ref=src,
            dst_ref=dst,
            send_sem=ssem.at[n],
            recv_sem=rsem.at[n],
            device_id=target,
            device_id_type=pl.DeviceIdType.MESH,
        )
        copy.start()
        if keep:
            pending.append(copy)
        return copy

    def mm(a, b):
        return jnp.dot(a, b, preferred_element_type=f32)

    def mm_t(a, b):
        return lax.dot_general(a, b, (((1,), (1,)), ((), ())), preferred_element_type=f32)

    def mm_w(a, b):
        return lax.dot_general(a, b, (((0,), (0,)), ((), ())), preferred_element_type=f32)

    chip_y, chip_z, chip_d = zl * 2 + 1 - y, (1 - zl) * 2 + y, (1 - zl) * 2 + 1 - y

    class Gather:
        def __init__(self, view, pair=True, halves=(True, True)):
            self.view, self.pair, self.halves = view, pair, halves
            self.copies, self.cores = [], []

        def start(self, source=None):
            own = self.view(own_chip)
            source = own if source is None else source
            self.z = self.put(source, own, 4)
            self.y = self.put(source, own, 2)
            if self.pair:
                self.cores.append(self.put(source, own, 1))

        def put(self, source, place, mask):
            copy = send(source, place, device(mask))
            self.copies.append(copy)
            return copy

        def part(self, chip, half):
            view = self.view(chip)
            return view if self.halves[0] != self.halves[1] else view.at[half]

        def from_z(self):
            self.z.wait_recv()
            if self.halves[0]:
                self.zy = self.put(self.part(chip_z, 0), self.part(chip_z, 0), 2)
            if self.pair:
                self.cores.append(self.put(self.view(chip_z), self.view(chip_z), 1))

        def from_y(self):
            self.y.wait_recv()
            if self.halves[1]:
                self.yz = self.put(self.part(chip_y, 1), self.part(chip_y, 1), 4)
            if self.pair:
                self.cores.append(self.put(self.view(chip_y), self.view(chip_y), 1))

        def from_far(self):
            if self.halves[0]:
                self.zy.wait_recv()
            if self.halves[1]:
                self.yz.wait_recv()
            if self.pair:
                self.cores.append(self.put(self.view(chip_d), self.view(chip_d), 1))

        def finish(self):
            for copy in self.cores:
                copy.wait_recv()

        def sent(self):
            for copy in self.copies:
                copy.wait_send()

    def tokens_of(half):
        return lambda chip: n1g.at[half, chip, c]

    x_a = Gather(tokens_of(zh), True, (True, False))
    x_b = Gather(tokens_of(1 - zh), True, (True, False))
    x_copy = send(x_in.at[1 - zh], n1g.at[zh, own_chip, c], device(0, False, True))
    x_a.start(x_in.at[zh])
    meta_copies = []
    for mask in range(8):
        for far in (False, True):
            if mask or far:
                meta_copies.append(send(meta_in, meta_r.at[s], device(mask, False, far)))

    qkv_sem = fresh()
    qkv_first = []
    for far_x in (False, True):
        for far_z in (False, True):
            for piece in range(3):
                n = fresh()
                tx = (1 - x) if far_x else x
                tz = (1 - zh) if far_z else zh
                target = (tx, tz * 8 + 4 * x + piece + x * ((piece + 1) // 2))
                copy = pltpu.make_async_remote_copy(
                    src_ref=wq_in.at[piece],
                    dst_ref=wq_r.at[s],
                    send_sem=ssem.at[n],
                    recv_sem=rsem.at[qkv_sem],
                    device_id=target,
                    device_id_type=pl.DeviceIdType.MESH,
                )
                if far_x or far_z:
                    copy.start()
                    pending.append(copy)
                else:
                    here = j == 4 * x + piece + x * ((piece + 1) // 2)
                    local = pltpu.make_async_copy(
                        wq_in.at[piece], wq_r.at[s], rsem.at[qkv_sem]
                    )
                    pl.when(here)(local.start)
                    pl.when(jnp.logical_not(here))(copy.start)
                    qkv_first.append((here, copy))
    wo_z = send(wo_in, wo_r.at[x, zh, own_chip, c], device(0, False, True))
    wo_r[x, zh, own_chip, c] = wo_in[...]
    wd_r[x, zh] = wd_in[...]
    gu_r[x, zh, j] = gu_in[j]
    meta_r[s] = meta_in[...]
    n1g[zh, own_chip, c] = x_in[zh]
    xo[zh] = x_in[zh]
    co[zh] = cot_in[zh]
    gfg[zh, own_chip, c] = cot_in[zh]
    da_s[...] = jnp.zeros(da_s.shape, bf16)
    wd_w[...] = jnp.zeros(wd_w.shape, bf16)

    def norm_rows(values, gain):
        scale = lax.rsqrt(jnp.mean(values * values, axis=-1, keepdims=True) + EPS)
        return values * scale * gain, scale

    x_copy.wait_recv()
    x_b.start()
    xo[1 - zh] = n1g[1 - zh, own_chip, c]
    x_a.from_z()
    x_a.from_y()
    for copy in meta_copies:
        copy.wait_recv()
    gain_rows = jnp.zeros((8, width), f32)
    seg_rows = jnp.zeros((8, 1024), f32)
    for slot in range(16):
        piece = meta_r[slot]
        wide = jnp.concatenate([piece, jnp.zeros((8, width - LANES), f32)], axis=1)
        gain_rows = gain_rows + pltpu.roll(wide, 72 * slot, 1)
        wide = jnp.concatenate([piece, jnp.zeros((8, 1024 - LANES), f32)], axis=1)
        seg_rows = seg_rows + pltpu.roll(wide, 64 * slot, 1)
    gains[...] = gain_rows
    seg_own = jnp.where(zh == 0, seg_rows[2:3, :], seg_rows[3:4, :])
    seg_wide = jnp.broadcast_to(seg_own, (8, 1024))
    segr[...] = seg_wide
    segc[...] = seg_wide.T

    x_a.from_far()
    x_b.from_z()
    x_b.from_y()
    x_b.from_far()

    def wo_view(chip):
        return wo_r.at[x, :, chip, c]

    def gf_view(chip):
        return gfg.at[:, chip, c]

    def n2_view(chip):
        return n2g.at[:, chip, c]

    wo_z.wait_recv()
    wo_q = Gather(wo_view, False)
    wo_q.start()
    wo_x = [send(wo_view(own_chip), wo_view(own_chip), device(0, True))]

    def spread_rows(read, columns):
        def step(slot, carry):
            acc[pl.ds(pl.multiple_of(slot * 72, 8), 72), 0:columns] = read(slot).astype(f32)
            return carry

        lax.fori_loop(0, 16, step, 0)

    def to_low(store, columns):
        def step(block, carry):
            at = pl.multiple_of(block * 128, 128)
            store(at, acc[pl.ds(at, 128), 0:columns].astype(bf16))
            return carry

        lax.fori_loop(0, 9, step, 0)

    def from_rows(store):
        def step(slot, carry):
            store(slot, pl.multiple_of(slot * 72, 8))
            return carry

        lax.fori_loop(0, 16, step, 0)


    @pl.when(attends)
    def _():
        pltpu.make_async_copy(wq_r, wq_r, rsem.at[qkv_sem]).wait()
        spread_rows(lambda slot: wq_r[slot], 384)

        def store(at, value):
            wq_w[pl.ds(at, 128), :] = value

        to_low(store, 384)

    x_a.finish()
    x_b.finish()
    x_a.sent()
    x_b.sent()
    cot_copy = send(cot_in.at[1 - zh], co.at[zh], device(0, False, True))
    gu_first = []
    for mask in range(1, 8):
        gu_first.append(send(gu_in.at[index_of(mask)], gu_r.at[x, zh, j], device(mask)))
    wd_z = send(wd_in, wd_r.at[x, zh], device(0, False, True))
    wd_x = send(wd_in, wd_r.at[x, zh], device(0, True))

    lane256 = lax.broadcasted_iota(jnp.int32, (1, 256), 1)
    low_half = (lane256 % 64) < 32

    def swap_half(values):
        return jnp.where(low_half, pltpu.roll(values, 256 - 32, 1), pltpu.roll(values, 32, 1))

    def tables(at, rows):
        both = turn_in[pl.ds(at, rows), :]
        first_half = lane256[:, 0:128] < 64
        cosine = jnp.where(first_half, both, roll64(both))
        sine = jnp.where(first_half, roll64(both), both)
        return (
            jnp.concatenate([cosine, cosine], axis=1),
            jnp.concatenate([sine, sine], axis=1),
        )

    @pl.when(attends)
    def _():
        def step(block, carry):
            at = pl.multiple_of(block * 256, 256)
            rows = n1g[block // 2, pl.ds((block % 2) * 2, 2)].reshape(256, width)
            rows, _ = norm_rows(rows.astype(f32), gains[0:1, :])
            rows = rows.astype(bf16)
            n1g[block // 2, pl.ds((block % 2) * 2, 2)] = rows.reshape(2, 2, 64, width)
            raw = mm(rows, wq_w[...])
            cosine, sine = tables(at, 256)
            pair = raw[:, 0:256]
            turned = pair * cosine + swap_half(pair) * sine
            turned = turned.astype(bf16).astype(f32)
            qk[pl.ds(at, 256), :] = turned.astype(bf16)
            qt[:, pl.ds(at, 256)] = turned.T[0:192].astype(bf16)
            values = raw[:, 256:384].astype(bf16).astype(f32)
            values = jnp.concatenate([values, jnp.zeros((256, 128), f32)], axis=1)
            for head in range(3):
                mine = (lane256 // 64) == head
                shift = (64 * (head + 1)) % 256
                kw[head, pl.ds(at, 256), :] = jnp.where(
                    mine, pltpu.roll(turned, shift, 1), 0.0
                ).astype(bf16)
                placed = pltpu.roll(values, 64 * head, 1) if head else values
                vw[head, pl.ds(at, 256), :] = placed.astype(bf16)
            return carry

        lax.fori_loop(0, 4, step, 0)

    pbs = (pb0, pb1, pb2, pb3)
    scale = 1.0 / math.sqrt(HEAD_DIMENSION)

    def attend_block(quarter):
        length = 256 * (quarter + 1)

        def step(sub, carry):
            at = pl.multiple_of(quarter * 256 + sub * 128, 128)
            query = qk[pl.ds(at, 128), :]
            key_pos = lax.broadcasted_iota(jnp.int32, (128, length), 1)
            row_pos = lax.broadcasted_iota(jnp.int32, (128, length), 0) + at
            allowed = (segc[pl.ds(at, 128), 0:1] == segr[0:1, 0:length]) & (key_pos <= row_pos)
            mixed = jnp.zeros((128, 256), f32)
            for head in range(3):
                scores = mm_t(query, kw[head, 0:length, :])
                scores = jnp.where(allowed, scores * scale, NEGATIVE)
                top = jnp.max(scores, axis=-1, keepdims=True)
                weight = jnp.exp(scores - top)
                weight = weight * (1.0 / jnp.sum(weight, axis=-1, keepdims=True))
                low_p = weight.astype(bf16)
                pbs[quarter][head, pl.ds(pl.multiple_of(sub * 128, 128), 128), :] = low_p
                mixed = mixed + mm(low_p, vw[head, 0:length, :])
            mx[pl.ds(at, 128), :] = mixed
            at_s[quarter // 2, pl.ds((quarter % 2) * 4 + sub * 2, 2)] = mixed.astype(
                bf16
            ).reshape(2, 64, 256)
            return carry

        lax.fori_loop(0, 2, step, 0)

    wo_q.from_z()
    wo_x.append(send(wo_view(chip_z), wo_view(chip_z), device(0, True)))
    pl.when(attends)(lambda: attend_block(0))
    wo_q.from_y()
    wo_x.append(send(wo_view(chip_y), wo_view(chip_y), device(0, True)))
    pl.when(attends)(lambda: attend_block(1))
    for copy in gu_first:
        copy.wait_recv()
        copy.wait_send()
    gu_z = []
    for part in range(2):
        rows = gu_r.at[x, zh, 4 * part : 4 * part + 4]
        gu_z.append(send(rows, rows, device(0, False, True)))
    gu_x = [send(gu_r.at[x, zh], gu_r.at[x, zh], device(0, True))]
    pl.when(attends)(lambda: attend_block(2))
    wo_q.from_far()
    wo_x.append(send(wo_view(chip_d), wo_view(chip_d), device(0, True)))
    wo_c = [send(wo_r.at[x, :, :, c], wo_r.at[x, :, :, c], device(1))]
    pl.when(attends)(lambda: attend_block(3))

    at_copies = []
    for mask in (6, 7, 4, 5, 2, 3, 1):
        n = fresh()
        there = index_of(mask)
        copy = pltpu.make_async_remote_copy(
            src_ref=at_s.at[:, there],
            dst_ref=at_r.at[head_own],
            send_sem=ssem.at[n],
            recv_sem=rsem.at[n],
            device_id=device(mask),
            device_id_type=pl.DeviceIdType.MESH,
        )
        pl.when(attends)(copy.start)
        at_copies.append(((there != 3) & (there != 5), copy))

    @pl.when(attends)
    def _():
        at_r[head_own] = at_s[:, j]

    cot_copy.wait_recv()
    gfg[1 - zh, own_chip, c] = co[1 - zh]
    gf_all = Gather(gf_view)
    gf_all.start()
    for copy in wo_x:
        copy.wait_recv()
    wo_c.append(send(wo_r.at[1 - x, :, :, c], wo_r.at[1 - x, :, :, c], device(1)))
    wd_z.wait_recv()
    wd_f = send(wd_r.at[x, 1 - zh], wd_r.at[x, 1 - zh], device(0, True))
    for copy in wo_c:
        copy.wait_recv()

    def spread_left(slot):
        z_half, chip, core = slot // 8, (slot % 8) // 2, slot % 2
        left = wo_r[0, z_half, chip, core].astype(f32)
        right = wo_r[1, z_half, chip, core, :, 0:128].astype(f32)
        return jnp.concatenate([left[:, 0:512], left[:, 512:640] + right], axis=1)

    def store_left(at, value):
        wo_w[pl.ds(at, 128), 0:640] = value

    spread_rows(spread_left, 640)
    to_low(store_left, 640)

    def store_right(at, value):
        wo_w[pl.ds(at, 128), 640:1152] = value

    spread_rows(lambda slot: wo_r[1, slot // 8, (slot % 8) // 2, slot % 2, :, 128:640], 512)
    to_low(store_right, 512)

    for theirs, copy in at_copies:
        pl.when(theirs)(copy.wait_recv)

    def branch_of():
        total = jnp.zeros((128, width), f32)
        for head in range(6):
            piece = at_r[head].reshape(128, 256)[:, 0:192]
            total = total + mm(piece, wo_w[192 * head : 192 * head + 192, :])
        return total

    branch = branch_of()
    valid = jnp.concatenate(
        [
            (segc[pl.ds(pl.multiple_of(64 * j, 64), 64), 0:1] != 0).astype(f32),
            (segc[pl.ds(pl.multiple_of(512 + 64 * j, 64), 64), 0:1] != 0).astype(f32),
        ],
        axis=0,
    )
    lane1 = lax.broadcasted_iota(jnp.int32, (1, LANES), 1)
    square_attn = jnp.sum(jnp.sum(valid * branch * branch, axis=0, keepdims=True), axis=1, keepdims=True)
    count = jnp.sum(valid, axis=0, keepdims=True)
    hidden = xo[...].reshape(128, width).astype(f32) + branch
    hid[...] = hidden
    normed, _ = norm_rows(hidden, gains[1:2, :])
    n2g[:, own_chip, c] = normed.astype(bf16).reshape(2, 64, width)
    n2_all = Gather(n2_view)
    n2_all.start()
    gf_all.from_z()
    gf_all.from_y()
    for part in range(2):
        gu_z[part].wait_recv()
        rows = gu_r.at[x, 1 - zh, 4 * part : 4 * part + 4]
        gu_x.append(send(rows, rows, device(0, True)))
    gf_all.from_far()
    n2_all.from_z()
    n2_all.from_y()

    wd_x.wait_recv()
    wd_f.wait_recv()
    for copy in gu_x:
        copy.wait_recv()
    for chunk in range(2):
        spread_rows(lambda slot: gu_r[chunk, slot // 8, slot % 8], 384)

        def store_gu(at, value):
            gu_w[chunk, pl.ds(at, 128), :] = value

        to_low(store_gu, 384)
        left, right = wd_r[0, chunk], wd_r[1, chunk]
        wd_w[chunk, 0:192, 0:512] = left[:, 0:512]
        wd_w[chunk, 0:192, 512:640] = (
            left[:, 512:640].astype(f32) + right[:, 0:128].astype(f32)
        ).astype(bf16)
        wd_w[chunk, 0:192, 640:1152] = right[:, 128:640]
    n2_all.from_far()
    gf_all.finish()
    n2_all.finish()

    def chip_at(step):
        return ((zl + step + 1) % 2) * 2 + (y + (3 - step) // 2) % 2

    def pair_copy(ref, got, base, step):
        chip = chip_at(step)
        return pltpu.make_async_remote_copy(
            src_ref=ref.at[:, chip, 1 - c],
            dst_ref=got.at[step],
            send_sem=ssem.at[base + step],
            recv_sem=rsem.at[base + step],
            device_id=device(1),
            device_id_type=pl.DeviceIdType.MESH,
        )

    def side_copy(ref, got2, base, kind):
        step, half, slot, mask = (
            (0, 0, 0, 2),
            (0, 1, 0, 4),
            (1, 0, 1, 2),
            (2, 1, 2, 4),
            (1, 1, 1, 2),
            (2, 0, 2, 4),
        )[kind]
        return pltpu.make_async_remote_copy(
            src_ref=ref.at[half, chip_at(step), c],
            dst_ref=got2.at[slot, half],
            send_sem=ssem.at[base + 4 + kind],
            recv_sem=rsem.at[base + 4 + kind],
            device_id=device(mask),
            device_id_type=pl.DeviceIdType.MESH,
        )

    def pair_sum(ref, got, step):
        chip = chip_at(step)
        return ref[:, chip, c].astype(f32) + got[step].astype(f32)

    def scatter_side(ref, got, got2, base, step):
        pair_copy(ref, got, base, step).wait_recv()
        ref[:, chip_at(step), c] = pair_sum(ref, got, step).astype(bf16)
        for kind in ((0, 1), (2,), (3,))[step]:
            side_copy(ref, got2, base, kind).start()

    def scatter_first(ref, got, got2, compute, sides=True):
        base = counter[0]
        counter[0] += 10

        def step_fn(step, carry):
            chip = chip_at(step)
            block = compute(chip).astype(bf16).reshape(2, 2, 64, width)
            ref[:, chip] = block
            pair_copy(ref, got, base, step).start()
            for done in range(3 if sides else 0):
                pl.when(step == done + 1)(
                    functools.partial(scatter_side, ref, got, got2, base, done)
                )
            return carry

        lax.fori_loop(0, 4, step_fn, 0)
        return base

    def scatter_second(ref, got, got2, base):
        for kind, step, half in ((5, 2, 0), (4, 1, 1)):
            side_copy(ref, got2, base, half).wait_recv()
            chip = chip_at(step)
            total = ref[half, chip, c].astype(f32) + got2[0, half].astype(f32)
            ref[half, chip, c] = total.astype(bf16)
            side_copy(ref, got2, base, kind).start()

    def scatter_finish(ref, got, got2, base):
        pair_copy(ref, got, base, 3).wait_recv()
        total = pair_sum(ref, got, 3)
        for kind in (2, 3, 4, 5):
            side_copy(ref, got2, base, kind).wait_recv()
        total = total + got2[1].astype(f32) + got2[2].astype(f32)
        return total.reshape(128, width)

    def scatter_sent(ref, got, got2, base):
        for step in range(4):
            pair_copy(ref, got, base, step).wait_send()
        for kind in range(6):
            side_copy(ref, got2, base, kind).wait_send()

    lane128 = lax.broadcasted_iota(jnp.int32, (1, LANES), 1)

    def feed_block(chip):
        rows = n2g[:, chip].reshape(256, width)
        grads = gfg[:, chip].reshape(256, width)
        total = jnp.zeros((256, width), f32)
        for chunk in range(2):
            both = mm(rows, gu_w[chunk])
            d_inner = mm_t(grads, wd_w[chunk])
            gate_a, mid, up_a = both[:, 0:128], both[:, 128:256], both[:, 256:384]
            turned = pltpu.roll(mid, 64, 1)
            pieces = []
            for gate, up, back in (
                (gate_a, up_a, d_inner[:, 0:128]),
                (mid, turned, d_inner[:, 128:256]),
            ):
                sig = jax.nn.sigmoid(gate)
                silu = gate * sig
                pieces.append(
                    (silu * up, back * silu, back * up * sig * (1.0 + gate * (1.0 - sig)))
                )
            inner_s[chunk, :, pl.ds(chip * 2, 2), :, 0:128] = (
                pieces[0][0].astype(bf16).reshape(2, 2, 64, 128)
            )
            inner_s[chunk, :, pl.ds(chip * 2, 2), :, 128:256] = (
                jnp.where(lane128 < 64, pieces[1][0], 0.0).astype(bf16).reshape(2, 2, 64, 128)
            )
            gate_low = jnp.where(lane128 < 64, pieces[1][2], 0.0)
            up_low = jnp.where(lane128 < 64, pieces[1][1], 0.0)
            middle = (gate_low + pltpu.roll(up_low, 64, 1)).astype(bf16)
            d_both = jnp.concatenate(
                [pieces[0][2].astype(bf16), middle, pieces[0][1].astype(bf16)], axis=1
            )
            dgu_s[chunk, :, pl.ds(chip * 2, 2)] = d_both.reshape(2, 2, 64, 384)
            total = total + mm_t(d_both, gu_w[chunk])
        return total

    e2_base = scatter_first(part_e, e2r1, e2r2, feed_block)
    scatter_second(part_e, e2r1, e2r2, e2_base)

    for copy in gu_x + gu_z:
        copy.wait_send()
    gf_all.sent()
    for chunk in range(2):
        grads = dgu_s[chunk].reshape(1024, 384)

        def wide_step(block, carry):
            at = pl.multiple_of(block * 128, 128)
            rows = n2g[:, :, :, :, pl.ds(at, 128)].reshape(1024, 128)
            acc[pl.ds(at, 128), 0:384] = mm_w(rows, grads)
            return carry

        lax.fori_loop(0, 9, wide_step, 0)

        def cut(slot, at):
            gu_r[chunk, slot // 8, slot % 8] = acc[pl.ds(at, 72), 0:384].astype(bf16)

        from_rows(cut)
    ggu_x = send(gu_r.at[1 - x], gux_r, device(0, True))

    wd_z.wait_send()
    wd_x.wait_send()

    def down_step(chunk, carry):
        grads = gfg[...].reshape(1024, width)
        piece = mm_w(inner_s[chunk].reshape(1024, 256), grads)
        gd_s[chunk, 0] = piece[0:192, 0:640].astype(bf16)
        gd_s[chunk, 1] = piece[0:192, 512:1152].astype(bf16)
        return carry

    lax.fori_loop(0, 2, down_step, 0)
    ggd_x = send(gd_s.at[:, 1 - x], gdx_r, device(0, True))

    def result_block(chip):
        total = mm(
            inner_s[0, :, pl.ds(chip * 2, 2)].reshape(256, 256), wd_w[0]
        )
        return total + mm(inner_s[1, :, pl.ds(chip * 2, 2)].reshape(256, 256), wd_w[1])

    n2_all.sent()
    bf_base = scatter_first(part_f, bfr1, bfr2, result_block, False)

    e2 = scatter_finish(part_e, e2r1, e2r2, e2_base)
    hidden = hid[...]
    scale2 = lax.rsqrt(jnp.mean(hidden * hidden, axis=-1, keepdims=True) + EPS)
    scaled = e2 * gains[1:2, :]
    inner_mean = jnp.mean(scaled * hidden, axis=-1, keepdims=True)
    gain_feed_row = jnp.sum(e2 * hidden * scale2, axis=0, keepdims=True)
    d_hidden = (
        co[...].reshape(128, width).astype(f32)
        + scale2 * scaled
        - hidden * (scale2 * scale2 * scale2) * inner_mean
    )
    dhid[...] = d_hidden
    d_low = d_hidden.astype(bf16)
    for head in range(6):
        piece = mm_t(d_low, wo_w[192 * head : 192 * head + 192, :])
        da_s[head, :, :, 0:192] = piece.astype(bf16).reshape(2, 64, 192)
    da_copies = []
    for mask in (6, 7, 4, 5, 2, 3, 1):
        n = fresh()
        there = index_of(mask)
        copy = pltpu.make_async_remote_copy(
            src_ref=da_s.at[head_of(there)],
            dst_ref=da_r.at[:, j],
            send_sem=ssem.at[n],
            recv_sem=rsem.at[n],
            device_id=device(mask),
            device_id_type=pl.DeviceIdType.MESH,
        )
        pl.when((there != 3) & (there != 5))(copy.start)
        da_copies.append(((there != 3) & (there != 5), copy))

    @pl.when(attends)
    def _():
        da_r[:, j] = da_s[head_own]

    for step in range(3):
        scatter_side(part_f, bfr1, bfr2, bf_base, step)
    for copy in wo_c + wo_x:
        copy.wait_send()
    wo_q.sent()
    for plane in range(2):
        for head in range(6):
            piece = at_r[head].reshape(128, 256)[:, 0:192]
            acc[192 * head : 192 * head + 192, :] = mm_w(
                piece, d_low[:, 512 * plane : 512 * plane + 640]
            )

        def cut_out(slot, at):
            wo_r[plane, slot // 8, (slot % 8) // 2, slot % 2] = acc[pl.ds(at, 72), :].astype(bf16)

        from_rows(cut_out)
    go_c = send(wo_r.at[:, :, :, 1 - c], gor1, device(1))

    dkvt[...] = jnp.zeros(dkvt.shape, f32)
    for _, copy in da_copies:
        pl.when(attends)(copy.wait_recv)

    @pl.when(attends)
    def _():
        def step(block, carry):
            at = pl.multiple_of(block * 256, 256)
            rows = da_r[block // 2, pl.ds((block % 2) * 4, 4)].reshape(256, 256)
            dat[:, pl.ds(at, 256)] = rows.astype(f32).T[0:192].astype(bf16)
            return carry

        lax.fori_loop(0, 4, step, 0)

    def back_block(quarter):
        length = 256 * (quarter + 1)

        def step(sub, carry):
            at = pl.multiple_of(quarter * 256 + sub * 128, 128)
            grads = da_r[quarter // 2, pl.ds((quarter % 2) * 4 + sub * 2, 2)].reshape(128, 256)
            products = grads.astype(f32) * mx[pl.ds(at, 128), :]
            d_query = jnp.zeros((128, 256), f32)
            d_key = jnp.zeros((64, length), f32)
            d_value = jnp.zeros((64, length), f32)
            for head in range(3):
                delta = jnp.sum(
                    jnp.where((lane256 // 64) == head, products, 0.0), axis=-1, keepdims=True
                )
                low_p = pbs[quarter][head, pl.ds(pl.multiple_of(sub * 128, 128), 128), :]
                d_p = mm_t(grads, vw[head, 0:length, :])
                d_s_low = (low_p.astype(f32) * (d_p - delta) * scale).astype(bf16)
                d_query = d_query + mm(d_s_low, kw[head, 0:length, :])
                d_key = d_key + mm(qt[64 * head : 64 * head + 64, pl.ds(at, 128)], d_s_low)
                d_value = d_value + mm(dat[64 * head : 64 * head + 64, pl.ds(at, 128)], low_p)
            mx[pl.ds(at, 128), :] = d_query
            dkvt[0:64, 0:length] += d_value
            dkvt[64:128, 0:length] += d_key
            return carry

        lax.fori_loop(0, 2, step, 0)

    pl.when(attends)(lambda: back_block(0))
    scatter_second(part_f, bfr1, bfr2, bf_base)
    go_c.wait_recv()

    def go_add(chip, carry):
        for half in range(2):
            for plane in range(2):
                wo_r[plane, half, chip, c] = (
                    wo_r[plane, half, chip, c].astype(f32) + gor1[plane, half, chip].astype(f32)
                ).astype(bf16)
        return carry

    lax.fori_loop(0, 4, go_add, 0)

    def go_side(chip, half, slot, mask):
        return send(wo_r.at[:, half, chip, c], goq_r.at[slot, half], device(mask))

    def go_sum(half, chip, slot):
        for plane in range(2):
            wo_r[plane, half, chip, c] = (
                wo_r[plane, half, chip, c].astype(f32) + goq_r[slot, half, plane].astype(f32)
            ).astype(bf16)

    go_first = [
        go_side(chip_d, 0, 0, 2),
        go_side(chip_d, 1, 0, 4),
        go_side(chip_y, 0, 1, 2),
        go_side(chip_z, 1, 2, 4),
    ]
    pl.when(attends)(lambda: back_block(1))
    ggu_x.wait_recv()

    def gu_add(slot, carry):
        gu_r[x, slot // 8, slot % 8] = (
            gu_r[x, slot // 8, slot % 8].astype(f32) + gux_r[slot // 8, slot % 8].astype(f32)
        ).astype(bf16)
        return carry

    lax.fori_loop(0, 16, gu_add, 0)
    ggu_z = send(gu_r.at[x, 1 - zh], guz_r, device(0, False, True))
    pl.when(attends)(lambda: back_block(2))
    pl.when(attends)(lambda: back_block(3))

    @pl.when(attends)
    def _():
        def step(block, carry):
            at = pl.multiple_of(block * 256, 256)
            cosine, sine = tables(at, 256)
            turned = dkvt[:, pl.ds(at, 256)].T
            query = mx[pl.ds(at, 256), :]
            pair = jnp.concatenate(
                [query[:, 0:128], jnp.where(lane128 < 64, query[:, 128:256], turned)], axis=1
            )
            back = pair * cosine - swap_half(pair) * sine
            values = jnp.where(lane128 < 64, turned, 0.0)
            both = jnp.concatenate([back.astype(bf16), values.astype(bf16)], axis=1)
            d_s[block // 2, pl.ds((block % 2) * 4, 4)] = both.reshape(4, 64, 384)
            return carry

        lax.fori_loop(0, 4, step, 0)

    @pl.when(jnp.logical_not(attends))
    def _():
        d_s[...] = jnp.zeros(d_s.shape, bf16)
        wq_w[...] = jnp.zeros(wq_w.shape, bf16)

    def input_block(chip):
        return mm_t(d_s[:, pl.ds(chip * 2, 2)].reshape(256, 384), wq_w[...])

    scatter_sent(part_e, e2r1, e2r2, e2_base)
    e1_base = scatter_first(part_e, e1r1, e1r2, input_block)
    gq_send, gq_sem = fresh(), fresh()
    plane_to = zl
    piece_own = head_own - 3 * zl

    def gq_copy(slot):
        return pltpu.make_async_remote_copy(
            src_ref=wq_r.at[slot],
            dst_ref=gq_r.at[x * 2 + zh, piece_own],
            send_sem=ssem.at[gq_send],
            recv_sem=rsem.at[gq_sem],
            device_id=(plane_to, slot),
            device_id_type=pl.DeviceIdType.MESH,
        )

    @pl.when(attends)
    def _():
        grads = d_s[...].reshape(1024, 384)

        def wide_step(block, carry):
            at = pl.multiple_of(block * 128, 128)
            rows = n1g[:, :, :, :, pl.ds(at, 128)].reshape(1024, 128)
            acc[pl.ds(at, 128), 0:384] = mm_w(rows, grads)
            return carry

        lax.fori_loop(0, 9, wide_step, 0)

        def step(slot, carry):
            wq_r[slot] = acc[pl.ds(pl.multiple_of(slot * 72, 8), 72), 0:384].astype(bf16)
            here = (plane_to == x) & (slot == s)

            @pl.when(here)
            def _():
                pltpu.make_async_copy(
                    wq_r.at[slot], gq_r.at[x * 2 + zh, piece_own], rsem.at[gq_sem]
                ).start()

            pl.when(jnp.logical_not(here))(lambda: gq_copy(slot).start())
            return carry

        lax.fori_loop(0, 16, step, 0)

    scatter_second(part_e, e1r1, e1r2, e1_base)

    ggd_x.wait_recv()
    for half in range(2):
        gd_s[half, x] = (gd_s[half, x].astype(f32) + gdx_r[half].astype(f32)).astype(bf16)
    ggd_z = send(gd_s.at[1 - zh, x], gdz_r, device(0, False, True))
    for n, half, chip, mask, slot in ((0, 0, chip_z, 4, 2), (1, 1, chip_y, 2, 1)):
        go_first[n].wait_recv()
        go_sum(half, chip, 0)
        go_first.append(go_side(chip, half, slot, mask))

    branch_feed = scatter_finish(part_f, bfr1, bfr2, bf_base)
    result = hid[...] + branch_feed
    square_feed = jnp.sum(
        jnp.sum(valid * branch_feed * branch_feed, axis=0, keepdims=True), axis=1, keepdims=True
    )
    square_out = jnp.sum(
        jnp.sum(valid * result * result, axis=0, keepdims=True), axis=1, keepdims=True
    )
    rows_s[0] = result.astype(bf16).reshape(2, 64, width)
    ret_out = send(rows_s.at[0, 1 - zh], rows_r.at[0], device(0, False, True))
    out_o[zh] = rows_s[0, zh]

    ggu_z.wait_recv()

    def gu_add2(slot, carry):
        gu_r[x, zh, slot] = (
            gu_r[x, zh, slot].astype(f32) + guz_r[slot].astype(f32)
        ).astype(bf16)
        return carry

    lax.fori_loop(0, 8, gu_add2, 0)
    e1 = scatter_finish(part_e, e1r1, e1r2, e1_base)
    tokens = xo[...].reshape(128, width).astype(f32)
    scale1 = lax.rsqrt(jnp.mean(tokens * tokens, axis=-1, keepdims=True) + EPS)
    scaled = e1 * gains[0:1, :]
    inner_mean = jnp.mean(scaled * tokens, axis=-1, keepdims=True)
    gain_attn_row = jnp.sum(e1 * tokens * scale1, axis=0, keepdims=True)
    grad_rows = (
        dhid[...] + scale1 * scaled - tokens * (scale1 * scale1 * scale1) * inner_mean
    )
    rows_s[1] = grad_rows.astype(bf16).reshape(2, 64, width)
    ret_in = send(rows_s.at[1, 1 - zh], rows_r.at[1], device(0, False, True))
    gin_o[zh] = rows_s[1, zh]

    ggu_q = [
        send(gu_r.at[x, zh, index_of(mask)], guf_r.at[j], device(mask)) for mask in range(1, 8)
    ]
    guf_r[j] = gu_r[x, zh, j]
    total_row = jnp.where(
        lane1 == 0,
        square_attn,
        jnp.where(lane1 == 1, square_feed, jnp.where(lane1 == 2, square_out, count)),
    )
    row8 = lax.broadcasted_iota(jnp.int32, (8, 1), 0)
    both_gains = jnp.where(
        row8 == 0,
        jnp.broadcast_to(gain_attn_row, (8, width)),
        jnp.broadcast_to(gain_feed_row, (8, width)),
    )
    for slot in range(16):
        moved = pltpu.roll(both_gains, (width - 72 * slot) % width, 1) if slot else both_gains
        small_s[slot] = jnp.where(row8 == 2, total_row, moved[:, 0:LANES])
    small_copies = []
    for flip_z in (True, False):
        for flip_x in (True, False):
            for mask in (6, 7, 4, 5, 2, 3, 1, 0):
                if flip_x or flip_z or mask:
                    target = device(mask, flip_x, flip_z)
                    small_copies.append(
                        send(small_s.at[target[1]], small_r.at[x * 16 + s], target)
                    )
    small_r[x * 16 + s] = small_s[s]

    for copy in go_first[2:]:
        copy.wait_recv()
    for slot in (1, 2):
        for half in range(2):
            go_sum(half, own_chip, slot)
    go_x = send(wo_r.at[1 - x, :, own_chip, c], gox_r, device(0, True))

    go_x.wait_recv()
    for half in range(2):
        wo_r[x, half, own_chip, c] = (
            wo_r[x, half, own_chip, c].astype(f32) + gox_r[half].astype(f32)
        ).astype(bf16)
    go_z = send(wo_r.at[x, 1 - zh, own_chip, c], goz_r, device(0, False, True))
    ggd_z.wait_recv()
    gd_o[...] = gd_s[zh, x].astype(f32) + gdz_r[...].astype(f32)
    for copy in ggu_q:
        copy.wait_recv()
    ggu_o[...] = guf_r[...]
    go_z.wait_recv()
    go_o[...] = wo_r[x, zh, own_chip, c].astype(f32) + goz_r[...].astype(f32)
    ret_out.wait_recv()
    out_o[1 - zh] = rows_r[0]
    pltpu.make_async_copy(gq_r, gq_r, rsem.at[gq_sem]).wait()
    gq_o[...] = (
        (gq_r[0].astype(f32) + gq_r[1].astype(f32)) + (gq_r[2].astype(f32) + gq_r[3].astype(f32))
    )
    for copy in small_copies:
        copy.wait_recv()
    total = small_r[0]
    for slot in range(1, 32):
        total = total + small_r[slot]
    small_o[...] = total
    ret_in.wait_recv()
    gin_o[1 - zh] = rows_r[1]

    waited = {id(copy) for copy in wo_c + wo_x + gu_x + gu_z + gu_first + [wd_z, wd_x]}
    for gather in (wo_q, gf_all, n2_all, x_a, x_b):
        waited |= {id(copy) for copy in gather.copies}
    for copy in pending:
        if id(copy) not in waited:
            copy.wait_send()
    for here, copy in qkv_first:
        pl.when(jnp.logical_not(here))(copy.wait_send)
    for theirs, copy in at_copies:
        pl.when(attends)(copy.wait_send)
    for theirs, copy in da_copies:
        pl.when(theirs)(copy.wait_send)
    scatter_sent(part_f, bfr1, bfr2, bf_base)
    scatter_sent(part_e, e1r1, e1r2, e1_base)

    @pl.when(attends)
    def _():
        def step(slot, carry):
            here = (plane_to == x) & (slot == s)
            pl.when(jnp.logical_not(here))(lambda: gq_copy(slot).wait_send())
            return carry

        lax.fori_loop(0, 16, step, 0)


def finish_kernel(
    out, gin, gq, go, ggu, gd, small,
    out_o, gin_o, gq_o, gk_o, gv_o, go_o, gg_o, gu_o, gd_o, ga_o, gf_o, rm_o,
):
    f32 = jnp.float32
    first = lax.axis_index("dp") == 0
    rows = gq.shape[1]
    low = lax.broadcasted_iota(jnp.int32, (1, LANES), 1) < 64
    out_o[...] = out[...]
    gin_o[...] = gin[...]
    p = [[gq[head, :, LANES * n : LANES * (n + 1)].astype(f32) for n in range(3)] for head in range(3)]
    gq_o[:, 0:128] = p[0][0]
    gq_o[:, 128:256] = jnp.where(low, p[0][1], roll64(p[1][0]))
    gq_o[:, 256:384] = jnp.where(low, roll64(p[1][0]), roll64(p[1][1]))
    gq_o[:, 384:512] = p[2][0]
    gq_o[:, 512:576] = p[2][1][:, 0:64]
    gk_o[:, 0:128] = jnp.where(low, roll64(p[0][1]), p[1][1])
    gk_o[:, 128:192] = roll64(p[2][1])[:, 0:64]
    gv_o[:, 0:128] = jnp.where(low, p[0][2], roll64(p[1][2]))
    gv_o[:, 128:192] = p[2][2][:, 0:64]

    def unwindow(ref, res):
        pieces = [ref[:, LANES * n : LANES * (n + 1)].astype(f32) for n in range(5)]
        for n in range(5):
            after = pieces[min(n + 1, 4)]
            moved = jnp.where(low, roll64(pieces[n]), roll64(after))
            value = jnp.where(first, pieces[n], moved)
            if n < 4:
                res[:, LANES * n : LANES * (n + 1)] = value
            else:
                res[:, 512:576] = value[:, 0:64]

    unwindow(go, go_o)
    unwindow(gd, gd_o)
    for pair in range(4):
        a, b = [
            [ggu[2 * pair + odd, :, LANES * n : LANES * (n + 1)].astype(f32) for n in range(3)]
            for odd in range(2)
        ]
        at = 384 * pair
        gg_o[:, at : at + 128] = a[0]
        gg_o[:, at + 128 : at + 256] = jnp.where(low, a[1], roll64(b[0]))
        gg_o[:, at + 256 : at + 384] = jnp.where(low, roll64(b[0]), roll64(b[1]))
        gu_o[:, at : at + 128] = a[2]
        gu_o[:, at + 128 : at + 256] = jnp.where(low, roll64(a[1]), roll64(b[2]))
        gu_o[:, at + 256 : at + 384] = jnp.where(low, roll64(b[2]), b[1])
    ga_o[...] = small[0:1, 0:rows]
    gf_o[...] = small[1:2, 0:rows]
    width = out.shape[2]
    rm_o[...] = jnp.sqrt(small[2:3, 0:3] / (small[2:3, 3:4] * width))


def fast_device(
    inputs,
    segments,
    weight_query,
    key_weight_matrix,
    value_weight_matrix,
    weight_out,
    weight_gate,
    weight_up,
    weight_down,
    gain_attention,
    gain_feed,
    cotangent,
):
    f32, bf16 = jnp.float32, jnp.bfloat16
    micro, _, rows, width = inputs.shape
    dp = lax.axis_index("dp")
    length = rows * 16
    piece = width // 16

    whole = pl.BlockSpec(memory_space=pltpu.VMEM)
    half = HEAD_DIMENSION // 2
    frequency = THETA ** (-np.arange(half, dtype=np.float32) * np.float32(2.0) / HEAD_DIMENSION)
    angles = np.arange(length, dtype=np.float32)[:, None] * frequency.astype(np.float32)[None, :]
    cosine, sine = np.cos(angles), np.sin(angles)
    turns = np.concatenate([cosine, cosine, -sine, sine], axis=1).astype(np.float32)

    v = pltpu.VMEM
    tok = (2, 4, 2, 64, width)
    scratch = [
        v((8, LANES), f32),
        v((3, piece, 384), bf16),
        v((piece, 640), bf16),
        v((16, 8, LANES), f32),
        v((2, 64, width), bf16),
        v((2, 64, width), bf16),
        v(tok, bf16),
        v(tok, bf16),
        v(tok, bf16),
        v((16, 72, 384), bf16),
        v((width, 384), bf16),
        v((2, 2, 4, 2, 72, 640), bf16),
        v((width, width), bf16),
        v((2, 2, 8, 72, 384), bf16),
        v((2, width, 384), bf16),
        v((2, 2, 192, 640), bf16),
        v((2, 256, width), bf16),
        v((width, 640), f32),
        v((1024, 256), bf16),
        v((192, 1024), bf16),
        v((192, 1024), bf16),
        v((3, 1024, 256), bf16),
        v((3, 1024, 256), bf16),
        v((3, 256, 256), bf16),
        v((3, 256, 512), bf16),
        v((3, 256, 768), bf16),
        v((3, 256, 1024), bf16),
        v((1024, 256), f32),
        v((8, 1024), f32),
        v((1024, 8), f32),
        v((8, width), f32),
        v((2, 8, 64, 256), bf16),
        v((6, 2, 64, 256), bf16),
        v((128, width), f32),
        v((128, width), f32),
        v((2, 2, 8, 64, 256), bf16),
        v((2, 2, 8, 64, 384), bf16),
        v((2, 4, 2, 64, width), bf16),
        v((4, 2, 64, width), bf16),
        v((3, 2, 64, width), bf16),
        v((4, 2, 64, width), bf16),
        v((3, 2, 64, width), bf16),
        v((6, 2, 64, 256), bf16),
        v((2, 8, 64, 256), bf16),
        v((2, 8, 64, 384), bf16),
        v((128, 1024), f32),
        v((2, 8, 72, 384), bf16),
        v((8, 72, 384), bf16),
        v((8, 72, 384), bf16),
        v((2, 2, 192, 640), bf16),
        v((2, 192, 640), bf16),
        v((192, 640), bf16),
        v((2, 2, 4, 72, 640), bf16),
        v((2, 72, 640), bf16),
        v((3, 2, 2, 72, 640), bf16),
        v((72, 640), bf16),
        v((4, 3, 72, 384), bf16),
        v((16, 8, LANES), f32),
        v((32, 8, LANES), f32),
        v((2, 2, 64, width), bf16),
        v((2, 64, width), bf16),
        pltpu.SemaphoreType.DMA((256,)),
        pltpu.SemaphoreType.DMA((256,)),
    ]
    out, gin, gq, go, ggu, gd, small = pl.pallas_call(
        fast_kernel,
        out_shape=(
            jax.ShapeDtypeStruct((2, rows, width), bf16),
            jax.ShapeDtypeStruct((2, rows, width), bf16),
            jax.ShapeDtypeStruct((3, piece, 384), f32),
            jax.ShapeDtypeStruct((piece, 640), f32),
            jax.ShapeDtypeStruct((8, piece, 384), bf16),
            jax.ShapeDtypeStruct((192, 640), f32),
            jax.ShapeDtypeStruct((8, LANES), f32),
        ),
        in_specs=[whole] * 13,
        out_specs=[whole] * 7,
        scratch_shapes=scratch,
        compiler_params=pltpu.CompilerParams(
            has_side_effects=True, collective_id=0, vmem_limit_bytes=62 * 1024 * 1024
        ),
        name="layer",
    )(
        inputs[:, 0],
        cotangent[:, 0],
        gain_attention.reshape(1, piece),
        gain_feed.reshape(1, piece),
        segments[:, 0],
        weight_query,
        key_weight_matrix,
        value_weight_matrix,
        weight_out,
        weight_gate,
        weight_up,
        weight_down,
        jnp.asarray(turns),
    )

    grads = pl.pallas_call(
        finish_kernel,
        out_shape=(
            jax.ShapeDtypeStruct((2, rows, width), bf16),
            jax.ShapeDtypeStruct((2, rows, width), bf16),
            jax.ShapeDtypeStruct(weight_query.shape, f32),
            jax.ShapeDtypeStruct(key_weight_matrix.shape, f32),
            jax.ShapeDtypeStruct(value_weight_matrix.shape, f32),
            jax.ShapeDtypeStruct(weight_out.shape, f32),
            jax.ShapeDtypeStruct(weight_gate.shape, f32),
            jax.ShapeDtypeStruct(weight_up.shape, f32),
            jax.ShapeDtypeStruct(weight_down.shape, f32),
            jax.ShapeDtypeStruct((1, piece), f32),
            jax.ShapeDtypeStruct((1, piece), f32),
            jax.ShapeDtypeStruct((1, 3), f32),
        ),
        in_specs=[whole] * 7,
        out_specs=[whole] * 12,
        name="finish",
    )(out, gin, gq, go, ggu, gd, small)
    return (
        grads[0][:, None],
        grads[1][:, None],
        *grads[2:9],
        grads[9].reshape(piece),
        grads[10].reshape(piece),
        grads[11].reshape(3),
    )


def solution(mesh):
    placed = (
        P(None, "dp", "seq", None),
        P(None, "dp", "seq"),
        P("seq", "dp"),
        P("seq", "dp"),
        P("seq", "dp"),
        P("seq", "dp"),
        P("seq", "dp"),
        P("seq", "dp"),
        P("seq", "dp"),
        P("seq"),
        P("seq"),
        P(None, "dp", "seq", None),
    )
    body = fast_device if dict(mesh.shape) == {"dp": 2, "seq": 16} else per_device
    return jax.shard_map(
        body,
        mesh=mesh,
        in_specs=placed,
        out_specs=(
            P(None, "dp", "seq", None),
            P(None, "dp", "seq", None),
            P("seq", "dp"),
            P("seq", "dp"),
            P("seq", "dp"),
            P("seq", "dp"),
            P("seq", "dp"),
            P("seq", "dp"),
            P("seq", "dp"),
            P("seq"),
            P("seq"),
            P(),
        ),
        check_vma=False,
    )
```
